32 devices in a mesh: grp: 2 (over y), sta: 4 (over z), hr: 2 (over x), sub: 2 (over core).
Axes of the slice: x: 2, y: 2, z: 4, core: 2. Of those that a mesh axis runs over, the one named last changes fastest.
Arguments:
- spectra: bfloat16 [4, 1000, 2, 4096], P(('grp', 'hr'), 'sub', None, 'sta'), parts along dimension 0, may hold values from -400 to 400
- pair_blocks: int32 [4, 2], replicated, may hold values from 0 to 31, as said below
- pair_owner: int32 [4], replicated, may hold values from 0 to 3, as said below
- block_members: int32 [32, 128], P('sta'), may hold values from 0 to 1023, as said below
Outputs:
- correlations: bfloat16 [32, 12, 128, 128], P(('grp', 'hr', 'sub'), 'sta'), parts along dimension 0
The draws below stay inside these ranges and needn't reach their ends.
There are 2 independent parts, one for each index of `grp`. The reference program is written for one: setup_inputs(seed, part) draws one part's arguments, and reference() takes and returns one part's arrays. A program takes and returns all parts, laid end to end along the dimension named above; an argument that names none is the same for every part. Nothing has to cross between parts.
Inputs may be any that keep to these rules, and one draw needn't show every extreme that they name: `pair_blocks`: each row names two different blocks; block g holds stations of index g // 8 of sta. The blocks of the pairs of owner o lie on indices o, o + 1, o + 2 or o + 3 (mod 4) of sta, and the distinct blocks named by the pairs of one owner lie on distinct indices of sta. `pair_owner`: at most 3 pairs share an owner, and some owner has exactly 3. `block_members`: the 8 rows of the blocks of one index of sta hold each of 0 to 1023 once.
All inputs are finite; a program needn't handle non-finite values.
Results may differ from the reference program's by a relative error of at most 0.0063.
Values may be sent and summed in bfloat16 or wider, within the bound.
No kernel may reach another device: no remote copies, remote signals or barrier semaphores. Data moves between devices by JAX's collectives and lax.ppermute only.
A program may use at most 64 MiB of HBM per device.

```python
import math
import jax
import jax.numpy as jnp
import numpy as np
from jax import lax

SB = 128
F = 1000
BAND = 50
LAGS = 16
CAP = 3
BLK_DEV = 8
STA_DEV = 1024
STATIONS = 4096
NBLK = 32
NPAIR = 4
SLOTS = 12
HOURS = 2
N_STA = 4


COMBOS = np.array([[0, 1], [0, 2], [0, 3], [1, 2], [1, 3], [2, 3]], dtype=np.int32)


def pair_tables(key):
    split_keys = jax.random.split(key, 6)
    pair_total = NPAIR
    spare_count = pair_total - 3
    halves = spare_count // 2
    shares = jax.random.randint(split_keys[0], (halves,), 0, 3).astype(jnp.int32)
    owner_loads = jnp.concatenate([jnp.array([3, 0, 0], jnp.int32), jnp.stack([shares, 2 - shares], 1).reshape(-1).astype(jnp.int32), jnp.ones((spare_count % 2,), jnp.int32)])
    owners_order = jax.random.permutation(split_keys[1], pair_total).astype(jnp.int32)
    last_owner = N_STA - 1
    last_pos = jnp.argmax(owners_order == last_owner).astype(jnp.int32)
    target_pos = jnp.where(owner_loads[3] > 0, 3, 4).astype(jnp.int32)
    need_swap = owner_loads[last_pos] == 0
    other_owner = owners_order[target_pos]
    swapped = owners_order.at[last_pos].set(other_owner).at[target_pos].set(last_owner)
    owners_order = jnp.where(need_swap, swapped, owners_order).astype(jnp.int32)
    group_of = jnp.repeat(jnp.arange(pair_total, dtype=jnp.int32), owner_loads, total_repeat_length=pair_total)
    group_starts = jnp.cumsum(owner_loads) - owner_loads
    within = jnp.arange(pair_total, dtype=jnp.int32) - group_starts[group_of]
    owner_sorted = owners_order[group_of]
    block_pick = jax.random.randint(split_keys[2], (pair_total, 4), 0, BLK_DEV).astype(jnp.int32)
    block_pick = block_pick.at[last_owner, 0].set(BLK_DEV - 1)
    scores = jax.random.randint(split_keys[3], (pair_total, 6), 0, 4096).astype(jnp.int32) * 8 + jnp.arange(6, dtype=jnp.int32)
    row_ids = jnp.arange(pair_total, dtype=jnp.int32)[:, None]
    col_ids = jnp.arange(6, dtype=jnp.int32)[None, :]
    scores = scores + jnp.where((row_ids == last_owner) & (col_ids >= 3), 8 * 4096, 0).astype(jnp.int32)
    orders = jnp.argsort(scores, axis=1).astype(jnp.int32)
    combo_row = orders[owner_sorted, within]
    offsets = jnp.asarray(COMBOS)[combo_row]
    home_ids = jnp.mod(owner_sorted[:, None] + offsets, N_STA)
    chosen_blocks = home_ids * BLK_DEV + block_pick[owner_sorted[:, None], offsets]
    flip_bits = jax.random.randint(split_keys[4], (pair_total,), 0, 2).astype(jnp.int32)
    first_block = jnp.where(flip_bits == 1, chosen_blocks[:, 1], chosen_blocks[:, 0])
    second = jnp.where(flip_bits == 1, chosen_blocks[:, 0], chosen_blocks[:, 1])
    shuffle = jax.random.permutation(split_keys[5], pair_total)
    listed = jnp.stack([first_block, second], 1)[shuffle].astype(jnp.int32)
    return (listed, owner_sorted[shuffle].astype(jnp.int32))


def draw_pair_blocks(key, part):
    tables = pair_tables(key)
    return tables[0]


def draw_pair_owner(key, part):
    tables = pair_tables(key)
    return tables[1]


def draw_block_members(key, part):
    key = jax.random.fold_in(key, 11)

    def one_home(home_id):
        return jax.random.permutation(jax.random.fold_in(key, home_id), STA_DEV).astype(jnp.int32)
    orders = jax.vmap(one_home)(jnp.arange(N_STA, dtype=jnp.int32))
    return orders.reshape(NBLK, SB)


def draw_spectra(key, part):
    key = jax.random.fold_in(key, 23)
    base_key, hour_key, freq_key = jax.random.split(key, 3)
    full_shape = (HOURS, F, 2, STATIONS)
    base_values = jnp.clip(jax.random.normal(base_key, full_shape, jnp.float32), -4.0, 4.0)
    station_scale = jnp.exp(jax.random.uniform(hour_key, (HOURS, 1, 1, STATIONS), jnp.float32, 0.0, math.log(10.0)))
    freq_scale = jnp.exp(jax.random.uniform(freq_key, (1, F, 1, STATIONS), jnp.float32, 0.0, math.log(10.0)))
    return (base_values * station_scale * freq_scale).astype(jnp.bfloat16)


def setup_inputs(seed: int = 0, part: int = 0) -> dict:
    keys = jax.random.split(jax.random.key(seed), 5)
    part_keys = jax.random.split(jax.random.fold_in(keys[4], part), 5)
    spectra = draw_spectra(jax.random.fold_in(jax.random.fold_in(keys[4], part), 71), part)
    pair_blocks = draw_pair_blocks(jax.random.fold_in(keys[4], 71), part)
    pair_owner = draw_pair_owner(jax.random.fold_in(keys[4], 71), part)
    block_members = draw_block_members(jax.random.fold_in(keys[4], 71), part)
    return {"spectra": spectra, "pair_blocks": pair_blocks, "pair_owner": pair_owner, "block_members": block_members}


EPSILON = 1e-05

def whiten(spectra):
    values = spectra.astype(jnp.float32)
    hour_count, freq_count, part_count, station_count = values.shape
    banded = values.reshape(hour_count, freq_count // BAND, BAND, part_count, station_count)
    band_power = lax.optimization_barrier(jnp.mean(banded * banded, axis=(2, 3), keepdims=True))
    whitened = banded / jnp.sqrt(band_power + EPSILON)
    return whitened.reshape(hour_count, freq_count, part_count, station_count).astype(jnp.bfloat16)

def lag_phases(freq_ids, lag_shift):
    angle_turns = jnp.mod(freq_ids * lag_shift, F).astype(jnp.float32) * (2.0 * math.pi / F)
    return (jnp.cos(angle_turns), jnp.sin(angle_turns))

def rotate(block, cosine, sine_part):
    real_part = block[..., 0, :].astype(jnp.float32)
    imag_part = block[..., 1, :].astype(jnp.float32)
    cos_col = cosine[:, None]
    sin_col = sine_part[:, None]
    turned = jnp.stack([real_part * cos_col - imag_part * sin_col, real_part * sin_col + imag_part * cos_col], axis=-2)
    return turned.astype(jnp.bfloat16)

def reference(spectra, pair_blocks, pair_owner, block_members):
    whitened = whiten(spectra)
    home_ids = jnp.arange(NBLK, dtype=jnp.int32) // BLK_DEV
    station_ids = (home_ids * STA_DEV)[:, None] + block_members
    pair_ids = jnp.arange(NPAIR, dtype=jnp.int32)
    earlier = pair_ids[:, None] > pair_ids[None, :]
    same_owner = pair_owner[:, None] == pair_owner[None, :]
    owner_rank = lax.optimization_barrier(jnp.sum((earlier & same_owner).astype(jnp.int32), axis=1)).astype(jnp.int32)
    slot_index = pair_owner * CAP + owner_rank
    freq_ids = jnp.arange(F, dtype=jnp.int32)
    norming = 1.0 / math.sqrt(HOURS * F)
    lag_shifts = jnp.arange(LAGS, dtype=jnp.int32) - LAGS // 2

    def one_pair(pair_row):
        left_block = jnp.take(whitened, station_ids[pair_row[0]], axis=3)
        right_flat = jnp.take(whitened, station_ids[pair_row[1]], axis=3).reshape(-1, SB)

        def one_lag(lag_shift):
            cosine, sine_part = lag_phases(freq_ids, lag_shift)
            turned = rotate(left_block, cosine, sine_part).reshape(-1, SB)
            return jnp.dot(turned.T, right_flat, preferred_element_type=jnp.float32)
        return lax.map(one_lag, lag_shifts) * norming
    lagged = lax.map(one_pair, pair_blocks)
    result = jnp.zeros((LAGS, SLOTS, SB, SB), jnp.float32)
    result = result.at[:, slot_index].set(jnp.transpose(lagged, (1, 0, 2, 3)))
    return result.astype(jnp.bfloat16)
```

```python
import functools
import math

import jax
import jax.numpy as jnp
import numpy as np
from jax import lax
from jax.experimental import pallas as pl
from jax.experimental.pallas import tpu as pltpu
from jax.sharding import PartitionSpec as P

BAND = 50
LAGS = 16
CAP = 3
REACH = 4
EPSILON = 1e-05
LANES = 128
F32 = jnp.float32
BF16 = jnp.bfloat16
VMEM_LIMIT = 48 * 1024 * 1024

NT = (((1,), (1,)), ((), ()))


def dot_nt(left, right):
    return lax.dot_general(left, right, NT, preferred_element_type=F32)


def iota(shape, dim):
    return lax.broadcasted_iota(jnp.int32, shape, dim)


def band_matrix(chunk, freqs):
    row, col = iota((2 * LANES, LANES), 0), iota((2 * LANES, LANES), 1)
    freq = chunk * LANES + row % LANES
    low = (col % 16) * BAND
    hit = (freq >= low) & (freq < low + BAND) & (freq < freqs) & (col < 48)
    return jnp.where(hit, 1.0, 0.0).astype(BF16)


def pick_kernel(sta_axis, pair_ref, owner_ref, member_ref, x_ref, *rest):
    outs, (x_buf, y_buf, z_buf, sems) = rest[:REACH], rest[REACH:]
    tiles, freqs = x_buf.shape[0], x_buf.shape[1]
    block_count, width = member_ref.shape
    chunks = y_buf.shape[1] // (2 * LANES)

    def fetch(tile):
        return pltpu.make_async_copy(
            x_ref.at[0, :, :, pl.ds(tile * LANES, LANES)], x_buf.at[tile], sems.at[tile]
        )

    for tile in range(tiles):
        fetch(tile).start()

    my_sta = lax.axis_index(sta_axis)
    sta_count = lax.axis_size(sta_axis)
    members = jnp.transpose(member_ref[...].astype(F32))
    block_col = iota(members.shape, 1)
    station = []
    for reach in range(REACH):
        owner = lax.rem(my_sta - reach + REACH * sta_count, sta_count)
        chosen = jnp.int32(0)
        for pair in range(owner_ref.shape[0]):
            for side in range(2):
                block = pair_ref[side, pair]
                hit = (owner_ref[pair] == owner) & (block // block_count == my_sta)
                chosen = jnp.where(hit, lax.rem(block, block_count), chosen)
        picked = jnp.where(block_col == chosen, members, 0.0)
        station.append(jnp.sum(picked, axis=1, keepdims=True).astype(jnp.int32))
    station = jnp.concatenate(station, axis=0)

    lane = iota((REACH * width, LANES), 1)

    def one_hot(tile):
        return jnp.where(station == lane + tile * LANES, 1.0, 0.0).astype(BF16)

    half = tiles // 2
    y_buf[...] = jnp.zeros_like(y_buf)
    total = None
    for first in (0, half):
        span = range(first, first + half)
        hot = jnp.concatenate([one_hot(tile) for tile in span], axis=1)
        for tile in span:
            fetch(tile).wait()
        x = jnp.concatenate(
            [x_buf.at[tile].reshape(2 * freqs, LANES)[...] for tile in span], axis=1
        )
        part = dot_nt(hot, x)
        total = part if total is None else total + part
    y_buf[:, : 2 * freqs] = total.astype(BF16)

    row, col = iota((2 * LANES, 2 * LANES), 0), iota((2 * LANES, 2 * LANES), 1)
    split = jnp.where(row == 2 * (col % LANES) + col // LANES, 1.0, 0.0).astype(BF16)
    power = None
    for chunk in range(chunks):
        z = jnp.dot(
            y_buf[:, chunk * 2 * LANES : (chunk + 1) * 2 * LANES],
            split,
            preferred_element_type=F32,
        )
        z_buf[chunk] = z
        square = z * z
        high = square.astype(BF16)
        low = (square - high.astype(F32)).astype(BF16)
        bands = band_matrix(chunk, freqs)
        part = jnp.dot(high, bands, preferred_element_type=F32) + jnp.dot(
            low, bands, preferred_element_type=F32
        )
        power = part if power is None else power + part
    scale = lax.rsqrt(power * (1.0 / (2 * BAND)) + EPSILON)
    high = scale.astype(BF16)
    rest1 = scale - high.astype(F32)
    mid = rest1.astype(BF16)
    low = rest1 - mid.astype(F32)
    third = iota(scale.shape, 1) // 16
    pieces = jnp.where(
        third == 0, high.astype(F32), jnp.where(third == 1, mid.astype(F32), low)
    ).astype(BF16)
    for chunk in range(chunks):
        white = (z_buf[chunk] * dot_nt(pieces, band_matrix(chunk, freqs))).astype(BF16)
        for reach in range(REACH):
            rows = slice(reach * width, (reach + 1) * width)
            outs[reach][:, chunk * LANES : (chunk + 1) * LANES] = white[rows, :LANES]
            outs[reach][:, (chunks + chunk) * LANES : (chunks + chunk + 1) * LANES] = white[
                rows, LANES:
            ]


def pick_blocks(spectra, pair_sides, pair_owner, block_members):
    _, freqs, parts, stations = spectra.shape
    block_count, width = block_members.shape
    tiles = stations // LANES
    chunks = -(-freqs // LANES)
    rows = REACH * width
    smem = pl.BlockSpec(memory_space=pltpu.SMEM)
    vmem = pl.BlockSpec(memory_space=pltpu.VMEM)
    return pl.pallas_call(
        functools.partial(pick_kernel, "sta"),
        out_shape=[jax.ShapeDtypeStruct((width, chunks * 2 * LANES), BF16)] * REACH,
        in_specs=[smem, smem, vmem, pl.BlockSpec(memory_space=pltpu.HBM)],
        out_specs=[vmem] * REACH,
        scratch_shapes=[
            pltpu.VMEM((tiles, freqs, parts, LANES), BF16),
            pltpu.VMEM((rows, chunks * 2 * LANES), BF16),
            pltpu.VMEM((chunks, rows, 2 * LANES), F32),
            pltpu.SemaphoreType.DMA((tiles,)),
        ],
        compiler_params=pltpu.CompilerParams(vmem_limit_bytes=VMEM_LIMIT),
        cost_estimate=pl.CostEstimate(
            flops=2 * rows * stations * freqs * parts,
            bytes_accessed=2 * spectra.size + 4 * rows * chunks * LANES,
            transcendentals=0,
        ),
        name="pick_and_whiten",
    )(pair_sides, pair_owner, block_members, spectra)


def phase_table(sub_count, sub_freqs, groups, lag_rows):
    chunks = -(-sub_freqs // LANES)
    freq = np.arange(sub_count * sub_freqs, dtype=np.int64).reshape(sub_count, 1, sub_freqs)
    total = sub_count * sub_freqs
    middle = [2 * (group * lag_rows - LAGS // 2) + lag_rows - 1 for group in range(groups)]
    away = [step for step in range(1, lag_rows) if step % 2 != lag_rows % 2]
    twice = np.array(middle + away, dtype=np.int64).reshape(1, -1, 1)
    angle = np.mod(freq * twice, 2 * total) * (math.pi / total)
    table = np.stack([np.cos(angle), np.sin(angle)], axis=2)
    table = table.reshape(sub_count, -1, sub_freqs)
    pad = ((0, 0), (0, -table.shape[1] % 8), (0, chunks * LANES - sub_freqs))
    return np.pad(table, pad).astype(np.float32), len(away)


def lag_kernel(hops, lag_rows, away, block_count, pair_ref, owner_ref, table_ref, *rest):
    sub_count = lax.axis_size("sub")
    hr_count = lax.axis_size("hr")
    blocks = rest[: REACH * sub_count]
    outs = rest[REACH * sub_count : REACH * sub_count + len(hops)]
    left_buf, right_buf, turned_buf, versions = rest[REACH * sub_count + len(hops) :]
    width = left_buf.shape[1]
    span = left_buf.shape[2] // 2
    middle_lag = lag_rows % 2
    my_sta = lax.axis_index("sta")
    my_sub = lax.axis_index("sub")
    my_hr = lax.axis_index("hr")
    sta_count = lax.axis_size("sta")
    pair_count = owner_ref.shape[0]
    groups = hr_count * sub_count

    for slot in range(CAP):
        count = jnp.int32(0)
        left, right = jnp.int32(-1), jnp.int32(-1)
        for pair in range(pair_count):
            mine = owner_ref[pair] == my_sta
            hit = mine & (count == slot)
            ends = [
                lax.rem(pair_ref[side, pair] // block_count - my_sta + sta_count, sta_count)
                for side in range(2)
            ]
            left = jnp.where(hit, ends[0], left)
            right = jnp.where(hit, ends[1], right)
            count = count + mine.astype(jnp.int32)

        @pl.when(left < 0)
        def _():
            for out in outs:
                out[:, slot] = jnp.zeros((lag_rows, width, width), out.dtype)

        for reach in range(REACH):

            @pl.when(left == reach)
            def _():
                for step in range(sub_count):
                    left_buf[step] = blocks[reach * sub_count + step][...]

            @pl.when(right == reach)
            def _():
                for step in range(sub_count):
                    right_buf[step] = blocks[reach * sub_count + step][...]

        @pl.when(left >= 0)
        def _():
            for step in range(sub_count):
                sub = lax.rem(my_sub + step, sub_count)
                base = step * 2 * span
                real = right_buf[step, :, :span].astype(F32)
                imag = right_buf[step, :, span:].astype(F32)
                if middle_lag:
                    versions[:width, base : base + 2 * span] = right_buf[step]
                for index in range(away):
                    row = 2 * (groups + index)
                    cosine = table_ref[sub, row : row + 1, :]
                    sine = table_ref[sub, row + 1 : row + 2, :]
                    top = (middle_lag + 2 * index) * width
                    versions[top : top + width, base : base + span] = (real * cosine).astype(BF16)
                    versions[top : top + width, base + span : base + 2 * span] = (
                        imag * cosine
                    ).astype(BF16)
                    top += width
                    versions[top : top + width, base : base + span] = (imag * sine).astype(BF16)
                    versions[top : top + width, base + span : base + 2 * span] = (
                        -(real * sine)
                    ).astype(BF16)
            for out, hop in zip(outs, hops):
                group = lax.rem(my_hr + hop, hr_count) * sub_count + my_sub
                for step in range(sub_count):
                    sub = lax.rem(my_sub + step, sub_count)
                    base = step * 2 * span
                    real = left_buf[step, :, :span].astype(F32)
                    imag = left_buf[step, :, span:].astype(F32)
                    cosine = table_ref[sub, pl.ds(2 * group, 1), :]
                    sine = table_ref[sub, pl.ds(2 * group + 1, 1), :]
                    turned_buf[:, base : base + span] = (real * cosine - imag * sine).astype(BF16)
                    turned_buf[:, base + span : base + 2 * span] = (
                        real * sine + imag * cosine
                    ).astype(BF16)
                product = dot_nt(turned_buf[...], versions[...])
                if middle_lag:
                    out[lag_rows // 2, slot] = product[:, :width].astype(out.dtype)
                for index in range(away):
                    start = (middle_lag + 2 * index) * width
                    even = product[:, start : start + width]
                    odd = product[:, start + width : start + 2 * width]
                    below = (lag_rows - 1) // 2 - index - middle_lag
                    above = lag_rows - 1 - below
                    out[above, slot] = (even + odd).astype(out.dtype)
                    out[below, slot] = (even - odd).astype(out.dtype)


def on_device(spectra, pair_blocks, pair_owner, block_members):
    hour_count, sub_freqs, _, _ = spectra.shape
    block_count, width = block_members.shape
    sta_count, hr_count, sub_count = (lax.axis_size(axis) for axis in ("sta", "hr", "sub"))
    groups = hr_count * sub_count
    lag_rows = LAGS // groups
    norming = 1.0 / math.sqrt(hour_count * hr_count * sub_count * sub_freqs)
    pair_sides = pair_blocks.T
    table, away = phase_table(sub_count, sub_freqs, groups, lag_rows)
    table = jnp.asarray(table)

    picked = pick_blocks(spectra, pair_sides, pair_owner, block_members)
    arrived = [picked[0]]
    for reach in range(1, REACH):
        to_owner = [(home, (home - reach) % sta_count) for home in range(sta_count)]
        arrived.append(lax.ppermute(picked[reach], "sta", to_owner))
    blocks = []
    for block in arrived:
        blocks.append(block)
        for step in range(1, sub_count):
            swap = [((sub + step) % sub_count, sub) for sub in range(sub_count)]
            blocks.append(lax.ppermute(block, "sub", swap))

    smem = pl.BlockSpec(memory_space=pltpu.SMEM)
    vmem = pl.BlockSpec(memory_space=pltpu.VMEM)
    depth = sub_count * picked[0].shape[1]
    versions = (lag_rows % 2 + 2 * away) * width

    def products(hops, dtype, name):
        flops = 2 * CAP * len(hops) * versions * width * depth
        return pl.pallas_call(
            functools.partial(lag_kernel, hops, lag_rows, away, block_count),
            out_shape=[jax.ShapeDtypeStruct((lag_rows, CAP, width, width), dtype)] * len(hops),
            in_specs=[smem, smem] + [vmem] * (1 + len(blocks)),
            out_specs=[vmem] * len(hops),
            scratch_shapes=[
                pltpu.VMEM((sub_count, width, depth // sub_count), BF16),
                pltpu.VMEM((sub_count, width, depth // sub_count), BF16),
                pltpu.VMEM((width, depth), BF16),
                pltpu.VMEM((versions, depth), BF16),
            ],
            compiler_params=pltpu.CompilerParams(vmem_limit_bytes=VMEM_LIMIT),
            cost_estimate=pl.CostEstimate(
                flops=flops, bytes_accessed=2 * REACH * width * depth, transcendentals=0
            ),
            name=name,
        )(pair_sides, pair_owner, table, *blocks)

    hops = tuple(range(1, hr_count))
    sent = products(hops, BF16, "lags_to_send")
    received = []
    for hop, part in zip(hops, sent):
        to_device = [(hr, (hr + hop) % hr_count) for hr in range(hr_count)]
        received.append(lax.ppermute(part, "hr", to_device))
    (summed,) = products((0,), F32, "lags_to_keep")
    for part in received:
        summed = summed + part.astype(F32)
    return (summed * norming).astype(BF16)


def solution(mesh):
    placed = (P(("grp", "hr"), "sub", None, "sta"), P(), P(), P("sta", None))
    return jax.shard_map(
        on_device,
        mesh=mesh,
        in_specs=placed,
        out_specs=P(("grp", "hr", "sub"), "sta", None, None),
        check_vma=False,
    )
```

```python
import functools
import math

import jax
import jax.numpy as jnp
import numpy as np
from jax import lax
from jax.experimental import pallas as pl
from jax.experimental.pallas import tpu as pltpu
from jax.sharding import PartitionSpec as P

BAND = 50
LAGS = 16
CAP = 3
REACH = 4
EPSILON = 1e-05
LANES = 128
F32 = jnp.float32
BF16 = jnp.bfloat16
VMEM_LIMIT = 48 * 1024 * 1024
PICK_VMEM_LIMIT = 59 * 1024 * 1024

NT = (((1,), (1,)), ((), ()))


def dot_nt(left, right):
    return lax.dot_general(left, right, NT, preferred_element_type=F32)


def iota(shape, dim):
    return lax.broadcasted_iota(jnp.int32, shape, dim)


def band_matrix(chunk, freqs):
    row, col = iota((2 * LANES, LANES), 0), iota((2 * LANES, LANES), 1)
    freq = chunk * LANES + row % LANES
    low = (col % 16) * BAND
    hit = (freq >= low) & (freq < low + BAND) & (freq < freqs) & (col < 48)
    return jnp.where(hit, 1.0, 0.0).astype(BF16)


def pick_kernel(kept, branched, sta_axis, pair_ref, owner_ref, member_ref, x_ref, *rest):
    outs = rest[:REACH]
    branch_ref = rest[REACH] if branched else None
    x_buf, y_buf, z_buf, sems = rest[REACH + branched :]
    tiles, freqs = x_buf.shape[0], x_buf.shape[1]
    block_count, width = member_ref.shape
    chunks = y_buf.shape[1] // (2 * LANES)

    def fetch(tile):
        return pltpu.make_async_copy(
            x_ref.at[0, :, :, pl.ds(tile * LANES, LANES)], x_buf.at[tile], sems.at[tile]
        )

    for tile in range(tiles):
        fetch(tile).start()

    my_sta = lax.axis_index(sta_axis)
    sta_count = lax.axis_size(sta_axis)
    pair_count = owner_ref.shape[0]
    members = jnp.transpose(member_ref[...].astype(F32))
    block_col = iota(members.shape, 1)
    found, wanted = jnp.int32(0), []
    for reach in range(REACH):
        owner = lax.rem(my_sta - reach + REACH * sta_count, sta_count)
        chosen = jnp.int32(-1)
        for pair in range(pair_count):
            for side in range(2):
                block = pair_ref[side, pair]
                hit = (owner_ref[pair] == owner) & (block // block_count == my_sta)
                chosen = jnp.where(hit, lax.rem(block, block_count), chosen)
        wanted.append((found, chosen))
        found = found + (chosen >= 0).astype(jnp.int32)
    places, station = [], []
    for place in range(kept):
        reach_here, block_here = jnp.int32(-1), jnp.int32(0)
        for reach, (rank, chosen) in enumerate(wanted):
            hit = (rank == place) & (chosen >= 0)
            reach_here = jnp.where(hit, reach, reach_here)
            block_here = jnp.where(hit, chosen, block_here)
        places.append(reach_here)
        column = jnp.where(block_col == block_here, members, 0.0)
        station.append(jnp.sum(column, axis=1, keepdims=True).astype(jnp.int32))
    station = jnp.concatenate(station, axis=0)

    lane = iota((kept * width, LANES), 1)

    def one_hot(tile):
        return jnp.where(station == lane + tile * LANES, 1.0, 0.0).astype(BF16)

    half = tiles // 2
    y_buf[...] = jnp.zeros_like(y_buf)
    total = None
    for first in (0, half):
        span = range(first, first + half)
        hot = jnp.concatenate([one_hot(tile) for tile in span], axis=1)
        for tile in span:
            fetch(tile).wait()
        x = jnp.concatenate(
            [x_buf.at[tile].reshape(2 * freqs, LANES)[...] for tile in span], axis=1
        )
        part = dot_nt(hot, x)
        total = part if total is None else total + part
    y_buf[:, : 2 * freqs] = total.astype(BF16)

    row, col = iota((2 * LANES, 2 * LANES), 0), iota((2 * LANES, 2 * LANES), 1)
    split = jnp.where(row == 2 * (col % LANES) + col // LANES, 1.0, 0.0).astype(BF16)
    power = None
    for chunk in range(chunks):
        z = jnp.dot(
            y_buf[:, chunk * 2 * LANES : (chunk + 1) * 2 * LANES],
            split,
            preferred_element_type=F32,
        )
        z_buf[chunk] = z
        square = z * z
        high = square.astype(BF16)
        low = (square - high.astype(F32)).astype(BF16)
        bands = band_matrix(chunk, freqs)
        part = jnp.dot(high, bands, preferred_element_type=F32) + jnp.dot(
            low, bands, preferred_element_type=F32
        )
        power = part if power is None else power + part
    scale = lax.rsqrt(power * (1.0 / (2 * BAND)) + EPSILON)
    high = scale.astype(BF16)
    rest1 = scale - high.astype(F32)
    mid = rest1.astype(BF16)
    low = rest1 - mid.astype(F32)
    third = iota(scale.shape, 1) // 16
    pieces = jnp.where(
        third == 0, high.astype(F32), jnp.where(third == 1, mid.astype(F32), low)
    ).astype(BF16)
    for chunk in range(chunks):
        white = (z_buf[chunk] * dot_nt(pieces, band_matrix(chunk, freqs))).astype(BF16)
        y_buf[:, chunk * LANES : (chunk + 1) * LANES] = white[:, :LANES]
        y_buf[:, (chunks + chunk) * LANES : (chunks + chunk + 1) * LANES] = white[:, LANES:]
    for place, reach_here in enumerate(places):
        for reach in range(REACH):

            @pl.when(reach_here == reach)
            def _():
                outs[reach][...] = y_buf[place * width : (place + 1) * width]

    if branch_ref is not None:
        first = second = jnp.int32(0)
        for pair in range(pair_count):
            owner = owner_ref[pair]
            count = jnp.int32(0)
            for other in range(pair_count):
                count = count + (owner_ref[other] == owner).astype(jnp.int32)
            first = jnp.where(count == CAP, owner, first)
            second = jnp.where(count < CAP, owner, second)
        branch_ref[0] = first * (sta_count - 1) + second - (second > first).astype(jnp.int32)


def pick_blocks(kept, branched, spectra, pair_sides, pair_owner, block_members):
    _, freqs, parts, stations = spectra.shape
    block_count, width = block_members.shape
    tiles = stations // LANES
    chunks = -(-freqs // LANES)
    rows = kept * width
    smem = pl.BlockSpec(memory_space=pltpu.SMEM)
    vmem = pl.BlockSpec(memory_space=pltpu.VMEM)
    blocks = [jax.ShapeDtypeStruct((width, chunks * 2 * LANES), BF16)] * REACH
    branch = [jax.ShapeDtypeStruct((1,), jnp.int32)] * branched
    return pl.pallas_call(
        functools.partial(pick_kernel, kept, branched, "sta"),
        out_shape=blocks + branch,
        in_specs=[smem, smem, vmem, pl.BlockSpec(memory_space=pltpu.HBM)],
        out_specs=[vmem] * REACH + [smem] * branched,
        scratch_shapes=[
            pltpu.VMEM((tiles, freqs, parts, LANES), BF16),
            pltpu.VMEM((rows, chunks * 2 * LANES), BF16),
            pltpu.VMEM((chunks, rows, 2 * LANES), F32),
            pltpu.SemaphoreType.DMA((tiles,)),
        ],
        compiler_params=pltpu.CompilerParams(vmem_limit_bytes=PICK_VMEM_LIMIT),
        cost_estimate=pl.CostEstimate(
            flops=2 * rows * stations * freqs * parts,
            bytes_accessed=2 * spectra.size + 4 * rows * chunks * LANES,
            transcendentals=0,
        ),
        name="pick_and_whiten",
    )(pair_sides, pair_owner, block_members, spectra)


def phase_table(sub_count, sub_freqs, groups, lag_rows):
    chunks = -(-sub_freqs // LANES)
    freq = np.arange(sub_count * sub_freqs, dtype=np.int64).reshape(sub_count, 1, sub_freqs)
    total = sub_count * sub_freqs
    middle = [2 * (group * lag_rows - LAGS // 2) + lag_rows - 1 for group in range(groups)]
    away = [step for step in range(1, lag_rows) if step % 2 != lag_rows % 2]
    twice = np.array(middle + away, dtype=np.int64).reshape(1, -1, 1)
    angle = np.mod(freq * twice, 2 * total) * (math.pi / total)
    table = np.stack([np.cos(angle), np.sin(angle)], axis=2)
    table = table.reshape(sub_count, -1, sub_freqs)
    pad = ((0, 0), (0, -table.shape[1] % 8), (0, chunks * LANES - sub_freqs))
    return np.pad(table, pad).astype(np.float32), len(away)


def lag_kernel(hops, lag_rows, away, block_count, pair_ref, owner_ref, table_ref, *rest):
    sub_count = lax.axis_size("sub")
    hr_count = lax.axis_size("hr")
    blocks = rest[: REACH * sub_count]
    outs = rest[REACH * sub_count : REACH * sub_count + len(hops)]
    left_buf, right_buf, turned_buf, versions = rest[REACH * sub_count + len(hops) :]
    width = left_buf.shape[1]
    span = left_buf.shape[2] // 2
    middle_lag = lag_rows % 2
    my_sta = lax.axis_index("sta")
    my_sub = lax.axis_index("sub")
    my_hr = lax.axis_index("hr")
    sta_count = lax.axis_size("sta")
    pair_count = owner_ref.shape[0]
    groups = hr_count * sub_count

    for slot in range(CAP):
        count = jnp.int32(0)
        left, right = jnp.int32(-1), jnp.int32(-1)
        for pair in range(pair_count):
            mine = owner_ref[pair] == my_sta
            hit = mine & (count == slot)
            ends = [
                lax.rem(pair_ref[side, pair] // block_count - my_sta + sta_count, sta_count)
                for side in range(2)
            ]
            left = jnp.where(hit, ends[0], left)
            right = jnp.where(hit, ends[1], right)
            count = count + mine.astype(jnp.int32)

        @pl.when(left < 0)
        def _():
            for out in outs:
                out[:, slot] = jnp.zeros((lag_rows, width, width), out.dtype)

        for reach in range(REACH):

            @pl.when(left == reach)
            def _():
                for step in range(sub_count):
                    left_buf[step] = blocks[reach * sub_count + step][...]

            @pl.when(right == reach)
            def _():
                for step in range(sub_count):
                    right_buf[step] = blocks[reach * sub_count + step][...]

        @pl.when(left >= 0)
        def _():
            for step in range(sub_count):
                sub = lax.rem(my_sub + step, sub_count)
                base = step * 2 * span
                real = right_buf[step, :, :span].astype(F32)
                imag = right_buf[step, :, span:].astype(F32)
                if middle_lag:
                    versions[:width, base : base + 2 * span] = right_buf[step]
                for index in range(away):
                    row = 2 * (groups + index)
                    cosine = table_ref[sub, row : row + 1, :]
                    sine = table_ref[sub, row + 1 : row + 2, :]
                    top = (middle_lag + 2 * index) * width
                    versions[top : top + width, base : base + span] = (real * cosine).astype(BF16)
                    versions[top : top + width, base + span : base + 2 * span] = (
                        imag * cosine
                    ).astype(BF16)
                    top += width
                    versions[top : top + width, base : base + span] = (imag * sine).astype(BF16)
                    versions[top : top + width, base + span : base + 2 * span] = (
                        -(real * sine)
                    ).astype(BF16)
            for out, hop in zip(outs, hops):
                group = lax.rem(my_hr + hop, hr_count) * sub_count + my_sub
                for step in range(sub_count):
                    sub = lax.rem(my_sub + step, sub_count)
                    base = step * 2 * span
                    real = left_buf[step, :, :span].astype(F32)
                    imag = left_buf[step, :, span:].astype(F32)
                    cosine = table_ref[sub, pl.ds(2 * group, 1), :]
                    sine = table_ref[sub, pl.ds(2 * group + 1, 1), :]
                    turned_buf[:, base : base + span] = (real * cosine - imag * sine).astype(BF16)
                    turned_buf[:, base + span : base + 2 * span] = (
                        real * sine + imag * cosine
                    ).astype(BF16)
                product = dot_nt(turned_buf[...], versions[...])
                if middle_lag:
                    out[lag_rows // 2, slot] = product[:, :width].astype(out.dtype)
                for index in range(away):
                    start = (middle_lag + 2 * index) * width
                    even = product[:, start : start + width]
                    odd = product[:, start + width : start + 2 * width]
                    below = (lag_rows - 1) // 2 - index - middle_lag
                    above = lag_rows - 1 - below
                    out[above, slot] = (even + odd).astype(out.dtype)
                    out[below, slot] = (even - odd).astype(out.dtype)


def on_device(spectra, pair_blocks, pair_owner, block_members):
    hour_count, sub_freqs, _, _ = spectra.shape
    block_count, width = block_members.shape
    sta_count, hr_count, sub_count = (lax.axis_size(axis) for axis in ("sta", "hr", "sub"))
    groups = hr_count * sub_count
    lag_rows = LAGS // groups
    norming = 1.0 / math.sqrt(hour_count * hr_count * sub_count * sub_freqs)
    pair_sides = pair_blocks.T
    table, away = phase_table(sub_count, sub_freqs, groups, lag_rows)
    table = jnp.asarray(table)

    owners_at_most = pair_owner.shape[0] - CAP + 1
    branched = owners_at_most == 2 and sta_count == REACH
    kept = min(REACH, owners_at_most)
    picked = pick_blocks(kept, branched, spectra, pair_sides, pair_owner, block_members)

    def exchange(owners, *picked):
        arrived = [picked[0]]
        for reach in range(1, REACH):
            to_owner = [((owner + reach) % sta_count, owner) for owner in owners]
            arrived.append(lax.ppermute(picked[reach], "sta", to_owner))
        blocks = []
        for block in arrived:
            blocks.append(block)
            for step in range(1, sub_count):
                swap = [
                    (owner * sub_count + (sub + step) % sub_count, owner * sub_count + sub)
                    for owner in owners
                    for sub in range(sub_count)
                ]
                blocks.append(lax.ppermute(block, ("sta", "sub"), swap))
        return blocks

    if branched:
        pairs = [(a, b) for a in range(sta_count) for b in range(sta_count) if a != b]
        blocks = lax.switch(
            picked[REACH][0], [functools.partial(exchange, pair) for pair in pairs], *picked[:REACH]
        )
    else:
        blocks = exchange(tuple(range(sta_count)), *picked)

    smem = pl.BlockSpec(memory_space=pltpu.SMEM)
    vmem = pl.BlockSpec(memory_space=pltpu.VMEM)
    depth = sub_count * picked[0].shape[1]
    versions = (lag_rows % 2 + 2 * away) * width

    def products(hops, dtype, name):
        flops = 2 * CAP * len(hops) * versions * width * depth
        return pl.pallas_call(
            functools.partial(lag_kernel, hops, lag_rows, away, block_count),
            out_shape=[jax.ShapeDtypeStruct((lag_rows, CAP, width, width), dtype)] * len(hops),
            in_specs=[smem, smem] + [vmem] * (1 + len(blocks)),
            out_specs=[vmem] * len(hops),
            scratch_shapes=[
                pltpu.VMEM((sub_count, width, depth // sub_count), BF16),
                pltpu.VMEM((sub_count, width, depth // sub_count), BF16),
                pltpu.VMEM((width, depth), BF16),
                pltpu.VMEM((versions, depth), BF16),
            ],
            compiler_params=pltpu.CompilerParams(vmem_limit_bytes=VMEM_LIMIT),
            cost_estimate=pl.CostEstimate(
                flops=flops, bytes_accessed=2 * REACH * width * depth, transcendentals=0
            ),
            name=name,
        )(pair_sides, pair_owner, table, *blocks)

    hops = tuple(range(1, hr_count))
    sent = products(hops, BF16, "lags_to_send")
    received = []
    for hop, part in zip(hops, sent):
        to_device = [(hr, (hr + hop) % hr_count) for hr in range(hr_count)]
        received.append(lax.ppermute(part, "hr", to_device))
    (summed,) = products((0,), F32, "lags_to_keep")
    for part in received:
        summed = summed + part.astype(F32)
    return (summed * norming).astype(BF16)


def solution(mesh):
    placed = (P(("grp", "hr"), "sub", None, "sta"), P(), P(), P("sta", None))
    return jax.shard_map(
        on_device,
        mesh=mesh,
        in_specs=placed,
        out_specs=P(("grp", "hr", "sub"), "sta", None, None),
        check_vma=False,
    )
```

```python
import functools
import math

import jax
import jax.numpy as jnp
import numpy as np
from jax import lax
from jax.experimental import pallas as pl
from jax.experimental.pallas import tpu as pltpu
from jax.sharding import PartitionSpec as P

BAND = 50
LAGS = 16
CAP = 3
REACH = 4
EPSILON = 1e-05
LANES = 128
F32 = jnp.float32
BF16 = jnp.bfloat16
VMEM_LIMIT = 48 * 1024 * 1024
PICK_VMEM_LIMIT = 59 * 1024 * 1024

NT = (((1,), (1,)), ((), ()))


def dot_nt(left, right):
    return lax.dot_general(left, right, NT, preferred_element_type=F32)


def iota(shape, dim):
    return lax.broadcasted_iota(jnp.int32, shape, dim)


def band_matrix(chunk, freqs):
    row, col = iota((2 * LANES, LANES), 0), iota((2 * LANES, LANES), 1)
    freq = chunk * LANES + row % LANES
    low = (col % 16) * BAND
    hit = (freq >= low) & (freq < low + BAND) & (freq < freqs) & (col < 48)
    return jnp.where(hit, 1.0, 0.0).astype(BF16)


def pick_kernel(kept, branched, sta_axis, pair_ref, owner_ref, member_ref, x_ref, *rest):
    outs = rest[:REACH]
    branch_ref = rest[REACH] if branched else None
    x_buf, y_buf, z_buf, sems = rest[REACH + branched :]
    tiles, freqs = x_buf.shape[0], x_buf.shape[1]
    block_count, width = member_ref.shape
    chunks = y_buf.shape[1] // (2 * LANES)

    def fetch(tile):
        return pltpu.make_async_copy(
            x_ref.at[0, :, :, pl.ds(tile * LANES, LANES)], x_buf.at[tile], sems.at[tile]
        )

    for tile in range(tiles):
        fetch(tile).start()

    my_sta = lax.axis_index(sta_axis)
    sta_count = lax.axis_size(sta_axis)
    pair_count = owner_ref.shape[0]
    members = jnp.transpose(member_ref[...].astype(F32))
    block_col = iota(members.shape, 1)
    found, wanted = jnp.int32(0), []
    for reach in range(REACH):
        owner = lax.rem(my_sta - reach + REACH * sta_count, sta_count)
        chosen = jnp.int32(-1)
        for pair in range(pair_count):
            for side in range(2):
                block = pair_ref[side, pair]
                hit = (owner_ref[pair] == owner) & (block // block_count == my_sta)
                chosen = jnp.where(hit, lax.rem(block, block_count), chosen)
        wanted.append((found, chosen))
        found = found + (chosen >= 0).astype(jnp.int32)
    places, station = [], []
    for place in range(kept):
        reach_here, block_here = jnp.int32(-1), jnp.int32(0)
        for reach, (rank, chosen) in enumerate(wanted):
            hit = (rank == place) & (chosen >= 0)
            reach_here = jnp.where(hit, reach, reach_here)
            block_here = jnp.where(hit, chosen, block_here)
        places.append(reach_here)
        column = jnp.where(block_col == block_here, members, 0.0)
        station.append(jnp.sum(column, axis=1, keepdims=True).astype(jnp.int32))
    station = jnp.concatenate(station, axis=0)

    lane = iota((kept * width, LANES), 1)

    def one_hot(tile):
        return jnp.where(station == lane + tile * LANES, 1.0, 0.0).astype(BF16)

    half = tiles // 2
    y_buf[...] = jnp.zeros_like(y_buf)
    total = None
    for first in (0, half):
        span = range(first, first + half)
        hot = jnp.concatenate([one_hot(tile) for tile in span], axis=1)
        for tile in span:
            fetch(tile).wait()
        x = jnp.concatenate(
            [x_buf.at[tile].reshape(2 * freqs, LANES)[...] for tile in span], axis=1
        )
        part = dot_nt(hot, x)
        total = part if total is None else total + part
    y_buf[:, : 2 * freqs] = total.astype(BF16)

    row, col = iota((2 * LANES, 2 * LANES), 0), iota((2 * LANES, 2 * LANES), 1)
    split = jnp.where(row == 2 * (col % LANES) + col // LANES, 1.0, 0.0).astype(BF16)
    power = None
    for chunk in range(chunks):
        z = jnp.dot(
            y_buf[:, chunk * 2 * LANES : (chunk + 1) * 2 * LANES],
            split,
            preferred_element_type=F32,
        )
        z_buf[chunk] = z
        square = z * z
        high = square.astype(BF16)
        low = (square - high.astype(F32)).astype(BF16)
        bands = band_matrix(chunk, freqs)
        part = jnp.dot(high, bands, preferred_element_type=F32) + jnp.dot(
            low, bands, preferred_element_type=F32
        )
        power = part if power is None else power + part
    scale = lax.rsqrt(power * (1.0 / (2 * BAND)) + EPSILON)
    high = scale.astype(BF16)
    rest1 = scale - high.astype(F32)
    mid = rest1.astype(BF16)
    low = rest1 - mid.astype(F32)
    third = iota(scale.shape, 1) // 16
    pieces = jnp.where(
        third == 0, high.astype(F32), jnp.where(third == 1, mid.astype(F32), low)
    ).astype(BF16)
    for chunk in range(chunks):
        white = (z_buf[chunk] * dot_nt(pieces, band_matrix(chunk, freqs))).astype(BF16)
        y_buf[:, chunk * LANES : (chunk + 1) * LANES] = white[:, :LANES]
        y_buf[:, (chunks + chunk) * LANES : (chunks + chunk + 1) * LANES] = white[:, LANES:]
    for place, reach_here in enumerate(places):
        for reach in range(REACH):

            @pl.when(reach_here == reach)
            def _():
                outs[reach][...] = y_buf[place * width : (place + 1) * width]

    if branch_ref is not None:
        first = second = jnp.int32(0)
        for pair in range(pair_count):
            owner = owner_ref[pair]
            count = jnp.int32(0)
            for other in range(pair_count):
                count = count + (owner_ref[other] == owner).astype(jnp.int32)
            first = jnp.where(count == CAP, owner, first)
            second = jnp.where(count < CAP, owner, second)
        branch_ref[0] = first * (sta_count - 1) + second - (second > first).astype(jnp.int32)


def pick_blocks(kept, branched, spectra, pair_sides, pair_owner, block_members):
    _, freqs, parts, stations = spectra.shape
    block_count, width = block_members.shape
    tiles = stations // LANES
    chunks = -(-freqs // LANES)
    rows = kept * width
    smem = pl.BlockSpec(memory_space=pltpu.SMEM)
    vmem = pl.BlockSpec(memory_space=pltpu.VMEM)
    blocks = [jax.ShapeDtypeStruct((width, chunks * 2 * LANES), BF16)] * REACH
    branch = [jax.ShapeDtypeStruct((1,), jnp.int32)] * branched
    return pl.pallas_call(
        functools.partial(pick_kernel, kept, branched, "sta"),
        out_shape=blocks + branch,
        in_specs=[smem, smem, vmem, pl.BlockSpec(memory_space=pltpu.HBM)],
        out_specs=[vmem] * REACH + [smem] * branched,
        scratch_shapes=[
            pltpu.VMEM((tiles, freqs, parts, LANES), BF16),
            pltpu.VMEM((rows, chunks * 2 * LANES), BF16),
            pltpu.VMEM((chunks, rows, 2 * LANES), F32),
            pltpu.SemaphoreType.DMA((tiles,)),
        ],
        compiler_params=pltpu.CompilerParams(vmem_limit_bytes=PICK_VMEM_LIMIT),
        cost_estimate=pl.CostEstimate(
            flops=2 * rows * stations * freqs * parts,
            bytes_accessed=2 * spectra.size + 4 * rows * chunks * LANES,
            transcendentals=0,
        ),
        name="pick_and_whiten",
    )(pair_sides, pair_owner, block_members, spectra)


def phase_table(sub_count, sub_freqs, groups, lag_rows):
    chunks = -(-sub_freqs // LANES)
    freq = np.arange(sub_count * sub_freqs, dtype=np.int64).reshape(sub_count, 1, sub_freqs)
    total = sub_count * sub_freqs
    middle = [2 * (group * lag_rows - LAGS // 2) + lag_rows - 1 for group in range(groups)]
    away = [step for step in range(1, lag_rows) if step % 2 != lag_rows % 2]
    twice = np.array(middle + away, dtype=np.int64).reshape(1, -1, 1)
    angle = np.mod(freq * twice, 2 * total) * (math.pi / total)
    table = np.stack([np.cos(angle), np.sin(angle)], axis=2)
    table = table.reshape(sub_count, -1, sub_freqs)
    pad = ((0, 0), (0, -table.shape[1] % 8), (0, chunks * LANES - sub_freqs))
    return np.pad(table, pad).astype(np.float32), len(away)


def lag_kernel(hops, lag_rows, away, block_count, pair_ref, owner_ref, table_ref, *rest):
    sub_count = lax.axis_size("sub")
    hr_count = lax.axis_size("hr")
    blocks = rest[: REACH * sub_count]
    outs = rest[REACH * sub_count : REACH * sub_count + len(hops)]
    left_buf, right_buf, turned_buf, versions = rest[REACH * sub_count + len(hops) :]
    width = left_buf.shape[1]
    span = left_buf.shape[2] // 2
    middle_lag = lag_rows % 2
    my_sta = lax.axis_index("sta")
    my_sub = lax.axis_index("sub")
    my_hr = lax.axis_index("hr")
    sta_count = lax.axis_size("sta")
    pair_count = owner_ref.shape[0]
    groups = hr_count * sub_count

    for slot in range(CAP):
        count = jnp.int32(0)
        left, right = jnp.int32(-1), jnp.int32(-1)
        for pair in range(pair_count):
            mine = owner_ref[pair] == my_sta
            hit = mine & (count == slot)
            ends = [
                lax.rem(pair_ref[side, pair] // block_count - my_sta + sta_count, sta_count)
                for side in range(2)
            ]
            left = jnp.where(hit, ends[0], left)
            right = jnp.where(hit, ends[1], right)
            count = count + mine.astype(jnp.int32)

        @pl.when(left < 0)
        def _():
            for out in outs:
                out[:, slot] = jnp.zeros((lag_rows, width, width), out.dtype)

        for reach in range(REACH):

            @pl.when(left == reach)
            def _():
                for step in range(sub_count):
                    left_buf[step] = blocks[reach * sub_count + step][...]

            @pl.when(right == reach)
            def _():
                for step in range(sub_count):
                    right_buf[step] = blocks[reach * sub_count + step][...]

        @pl.when(left >= 0)
        def _():
            for step in range(sub_count):
                sub = lax.rem(my_sub + step, sub_count)
                base = step * 2 * span
                real = right_buf[step, :, :span].astype(F32)
                imag = right_buf[step, :, span:].astype(F32)
                if middle_lag:
                    versions[:width, base : base + 2 * span] = right_buf[step]
                for index in range(away):
                    row = 2 * (groups + index)
                    cosine = table_ref[sub, row : row + 1, :]
                    sine = table_ref[sub, row + 1 : row + 2, :]
                    top = (middle_lag + 2 * index) * width
                    versions[top : top + width, base : base + span] = (real * cosine).astype(BF16)
                    versions[top : top + width, base + span : base + 2 * span] = (
                        imag * cosine
                    ).astype(BF16)
                    top += width
                    versions[top : top + width, base : base + span] = (imag * sine).astype(BF16)
                    versions[top : top + width, base + span : base + 2 * span] = (
                        -(real * sine)
                    ).astype(BF16)
            for out, hop in zip(outs, hops):
                group = lax.rem(my_hr + hop, hr_count) * sub_count + my_sub
                for step in range(sub_count):
                    sub = lax.rem(my_sub + step, sub_count)
                    base = step * 2 * span
                    real = left_buf[step, :, :span].astype(F32)
                    imag = left_buf[step, :, span:].astype(F32)
                    cosine = table_ref[sub, pl.ds(2 * group, 1), :]
                    sine = table_ref[sub, pl.ds(2 * group + 1, 1), :]
                    turned_buf[:, base : base + span] = (real * cosine - imag * sine).astype(BF16)
                    turned_buf[:, base + span : base + 2 * span] = (
                        real * sine + imag * cosine
                    ).astype(BF16)
                product = dot_nt(turned_buf[...], versions[...])
                if middle_lag:
                    out[lag_rows // 2, slot] = product[:, :width].astype(out.dtype)
                for index in range(away):
                    start = (middle_lag + 2 * index) * width
                    even = product[:, start : start + width]
                    odd = product[:, start + width : start + 2 * width]
                    below = (lag_rows - 1) // 2 - index - middle_lag
                    above = lag_rows - 1 - below
                    out[above, slot] = (even + odd).astype(out.dtype)
                    out[below, slot] = (even - odd).astype(out.dtype)


def on_device(spectra, pair_blocks, pair_owner, block_members):
    hour_count, sub_freqs, _, _ = spectra.shape
    block_count, width = block_members.shape
    sta_count, hr_count, sub_count = (lax.axis_size(axis) for axis in ("sta", "hr", "sub"))
    groups = hr_count * sub_count
    lag_rows = LAGS // groups
    norming = 1.0 / math.sqrt(hour_count * hr_count * sub_count * sub_freqs)
    pair_sides = pair_blocks.T
    table, away = phase_table(sub_count, sub_freqs, groups, lag_rows)
    table = jnp.asarray(table)

    owners_at_most = pair_owner.shape[0] - CAP + 1
    branched = owners_at_most == 2 and sta_count == REACH
    kept = min(REACH, owners_at_most)
    picked = pick_blocks(kept, branched, spectra, pair_sides, pair_owner, block_members)

    def exchange(owners, *picked):
        arrived = [picked[0]]
        for reach in range(1, REACH):
            to_owner = [((owner + reach) % sta_count, owner) for owner in owners]
            arrived.append(lax.ppermute(picked[reach], "sta", to_owner))
        blocks = []
        for block in arrived:
            blocks.append(block)
            for step in range(1, sub_count):
                swap = [((sub + step) % sub_count, sub) for sub in range(sub_count)]
                blocks.append(lax.ppermute(block, "sub", swap))
        return blocks

    if branched:
        pairs = [(a, b) for a in range(sta_count) for b in range(sta_count) if a != b]
        blocks = lax.switch(
            picked[REACH][0], [functools.partial(exchange, pair) for pair in pairs], *picked[:REACH]
        )
    else:
        blocks = exchange(tuple(range(sta_count)), *picked)

    smem = pl.BlockSpec(memory_space=pltpu.SMEM)
    vmem = pl.BlockSpec(memory_space=pltpu.VMEM)
    depth = sub_count * picked[0].shape[1]
    versions = (lag_rows % 2 + 2 * away) * width

    def products(hops, dtype, name):
        flops = 2 * CAP * len(hops) * versions * width * depth
        return pl.pallas_call(
            functools.partial(lag_kernel, hops, lag_rows, away, block_count),
            out_shape=[jax.ShapeDtypeStruct((lag_rows, CAP, width, width), dtype)] * len(hops),
            in_specs=[smem, smem] + [vmem] * (1 + len(blocks)),
            out_specs=[vmem] * len(hops),
            scratch_shapes=[
                pltpu.VMEM((sub_count, width, depth // sub_count), BF16),
                pltpu.VMEM((sub_count, width, depth // sub_count), BF16),
                pltpu.VMEM((width, depth), BF16),
                pltpu.VMEM((versions, depth), BF16),
            ],
            compiler_params=pltpu.CompilerParams(vmem_limit_bytes=VMEM_LIMIT),
            cost_estimate=pl.CostEstimate(
                flops=flops, bytes_accessed=2 * REACH * width * depth, transcendentals=0
            ),
            name=name,
        )(pair_sides, pair_owner, table, *blocks)

    hops = tuple(range(1, hr_count))
    sent = products(hops, BF16, "lags_to_send")
    received = []
    for hop, part in zip(hops, sent):
        to_device = [(hr, (hr + hop) % hr_count) for hr in range(hr_count)]
        received.append(lax.ppermute(part, "hr", to_device))
    (summed,) = products((0,), F32, "lags_to_keep")
    for part in received:
        summed = summed + part.astype(F32)
    return (summed * norming).astype(BF16)


def solution(mesh):
    placed = (P(("grp", "hr"), "sub", None, "sta"), P(), P(), P("sta", None))
    return jax.shard_map(
        on_device,
        mesh=mesh,
        in_specs=placed,
        out_specs=P(("grp", "hr", "sub"), "sta", None, None),
        check_vma=False,
    )
```

```python
import functools
import itertools
import math

import jax
import jax.numpy as jnp
import numpy as np
from jax import lax
from jax.experimental import pallas as pl
from jax.experimental.pallas import tpu as pltpu
from jax.sharding import PartitionSpec as P

BAND = 50
LAGS = 16
CAP = 3
REACH = 4
EPSILON = 1e-05
LANES = 128
F32 = jnp.float32
BF16 = jnp.bfloat16
VMEM_LIMIT = 59 * 1024 * 1024

NT = (((1,), (1,)), ((), ()))


def dot_nt(left, right):
    return lax.dot_general(left, right, NT, preferred_element_type=F32)


def iota(shape, dim):
    return lax.broadcasted_iota(jnp.int32, shape, dim)


def band_matrix(chunk, freqs):
    row, col = iota((2 * LANES, LANES), 0), iota((2 * LANES, LANES), 1)
    freq = chunk * LANES + row % LANES
    low = (col % 16) * BAND
    hit = (freq >= low) & (freq < low + BAND) & (freq < freqs) & (col < 48)
    return jnp.where(hit, 1.0, 0.0).astype(BF16)


def pick_kernel(kept, choices, sta_axis, pair_hbm, owner_hbm, member_hbm, x_ref, *rest):
    branched = len(choices) > 0
    outs = rest[:REACH]
    branch_ref = rest[REACH] if branched else None
    pair_ref, owner_ref, member_ref, x_buf, y_buf, z_buf, sems = rest[REACH + branched :]
    tiles, freqs = x_buf.shape[0], x_buf.shape[1]
    block_count, width = member_ref.shape
    chunks = y_buf.shape[1] // (2 * LANES)

    def fetch(tile):
        return pltpu.make_async_copy(
            x_ref.at[0, :, :, pl.ds(tile * LANES, LANES)], x_buf.at[tile], sems.at[tile]
        )

    small = [
        pltpu.make_async_copy(source, target, sems.at[tiles + index])
        for index, (source, target) in enumerate(
            ((pair_hbm, pair_ref), (owner_hbm, owner_ref), (member_hbm, member_ref))
        )
    ]
    for copy in small:
        copy.start()
    for tile in range(tiles):
        fetch(tile).start()
    for copy in small:
        copy.wait()

    my_sta = lax.axis_index(sta_axis)
    sta_count = lax.axis_size(sta_axis)
    pair_count = owner_ref.shape[0]
    members = jnp.transpose(member_ref[...].astype(F32))
    block_col = iota(members.shape, 1)
    found, wanted = jnp.int32(0), []
    for reach in range(REACH):
        owner = lax.rem(my_sta - reach + REACH * sta_count, sta_count)
        chosen = jnp.int32(-1)
        for pair in range(pair_count):
            for side in range(2):
                block = pair_ref[side, pair]
                hit = (owner_ref[pair] == owner) & (block // block_count == my_sta)
                chosen = jnp.where(hit, lax.rem(block, block_count), chosen)
        wanted.append((found, chosen))
        found = found + (chosen >= 0).astype(jnp.int32)
    places, station = [], []
    for place in range(kept):
        reach_here, block_here = jnp.int32(-1), jnp.int32(0)
        for reach, (rank, chosen) in enumerate(wanted):
            hit = (rank == place) & (chosen >= 0)
            reach_here = jnp.where(hit, reach, reach_here)
            block_here = jnp.where(hit, chosen, block_here)
        places.append(reach_here)
        column = jnp.where(block_col == block_here, members, 0.0)
        station.append(jnp.sum(column, axis=1, keepdims=True).astype(jnp.int32))
    station = jnp.concatenate(station, axis=0)

    lane = iota((kept * width, LANES), 1)

    def one_hot(tile):
        return jnp.where(station == lane + tile * LANES, 1.0, 0.0).astype(BF16)

    y_buf[:, 2 * freqs :] = jnp.zeros((kept * width, y_buf.shape[1] - 2 * freqs), BF16)
    total = None
    for first in range(0, tiles, 2):
        span = range(first, min(first + 2, tiles))
        hot = jnp.concatenate([one_hot(tile) for tile in span], axis=1)
        for tile in span:
            fetch(tile).wait()
        x = jnp.concatenate(
            [x_buf.at[tile].reshape(2 * freqs, LANES)[...] for tile in span], axis=1
        )
        part = dot_nt(hot, x)
        total = part if total is None else total + part
    y_buf[:, : 2 * freqs] = total.astype(BF16)

    row, col = iota((2 * LANES, 2 * LANES), 0), iota((2 * LANES, 2 * LANES), 1)
    split = jnp.where(row == 2 * (col % LANES) + col // LANES, 1.0, 0.0).astype(BF16)
    power = None
    for chunk in range(chunks):
        z = jnp.dot(
            y_buf[:, chunk * 2 * LANES : (chunk + 1) * 2 * LANES],
            split,
            preferred_element_type=F32,
        )
        z_buf[chunk] = z
        square = z * z
        high = square.astype(BF16)
        low = (square - high.astype(F32)).astype(BF16)
        bands = band_matrix(chunk, freqs)
        part = jnp.dot(high, bands, preferred_element_type=F32) + jnp.dot(
            low, bands, preferred_element_type=F32
        )
        power = part if power is None else power + part
    scale = lax.rsqrt(power * (1.0 / (2 * BAND)) + EPSILON)
    high = scale.astype(BF16)
    rest1 = scale - high.astype(F32)
    mid = rest1.astype(BF16)
    low = rest1 - mid.astype(F32)
    third = iota(scale.shape, 1) // 16
    pieces = jnp.where(
        third == 0, high.astype(F32), jnp.where(third == 1, mid.astype(F32), low)
    ).astype(BF16)
    for chunk in range(chunks):
        white = (z_buf[chunk] * dot_nt(pieces, band_matrix(chunk, freqs))).astype(BF16)
        y_buf[:, chunk * LANES : (chunk + 1) * LANES] = white[:, :LANES]
        y_buf[:, (chunks + chunk) * LANES : (chunks + chunk + 1) * LANES] = white[:, LANES:]
    for place, reach_here in enumerate(places):
        for reach in range(REACH):

            @pl.when(reach_here == reach)
            def _():
                outs[reach][...] = y_buf[place * width : (place + 1) * width]

    if branched:
        first = second = needs = jnp.int32(0)
        for pair in range(pair_count):
            owner = owner_ref[pair]
            count = jnp.int32(0)
            for other in range(pair_count):
                count = count + (owner_ref[other] == owner).astype(jnp.int32)
            ends = [
                lax.rem(pair_ref[side, pair] // block_count - owner + sta_count, sta_count)
                for side in range(2)
            ]
            first = jnp.where(count == CAP, owner, first)
            second = jnp.where(count < CAP, owner, second)
            needs = jnp.where(count < CAP, (1 << ends[0]) | (1 << ends[1]), needs)
        case = (first * sta_count + second) * (1 << REACH) + (needs & ~1)
        branch = jnp.int32(0)
        for known, number in choices:
            branch = jnp.where(case == known, number, branch)
        branch_ref[0] = branch


def pick_blocks(kept, choices, spectra, pair_sides, pair_owner, block_members):
    _, freqs, parts, stations = spectra.shape
    block_count, width = block_members.shape
    tiles = stations // LANES
    chunks = -(-freqs // LANES)
    rows = kept * width
    branched = len(choices) > 0
    vmem = pl.BlockSpec(memory_space=pltpu.VMEM)
    blocks = [jax.ShapeDtypeStruct((width, chunks * 2 * LANES), BF16)] * REACH
    branch = [jax.ShapeDtypeStruct((1,), jnp.int32)] * branched
    return pl.pallas_call(
        functools.partial(pick_kernel, kept, choices, "sta"),
        out_shape=blocks + branch,
        in_specs=[pl.BlockSpec(memory_space=pltpu.HBM)] * 4,
        out_specs=[vmem] * REACH + [pl.BlockSpec(memory_space=pltpu.SMEM)] * branched,
        scratch_shapes=[
            pltpu.SMEM(pair_sides.shape, jnp.int32),
            pltpu.SMEM(pair_owner.shape, jnp.int32),
            pltpu.VMEM(block_members.shape, jnp.int32),
            pltpu.VMEM((tiles, freqs, parts, LANES), BF16),
            pltpu.VMEM((rows, chunks * 2 * LANES), BF16),
            pltpu.VMEM((chunks, rows, 2 * LANES), F32),
            pltpu.SemaphoreType.DMA((tiles + 3,)),
        ],
        compiler_params=pltpu.CompilerParams(vmem_limit_bytes=VMEM_LIMIT),
        cost_estimate=pl.CostEstimate(
            flops=2 * rows * stations * freqs * parts,
            bytes_accessed=2 * spectra.size + 4 * rows * chunks * LANES,
            transcendentals=0,
        ),
        name="pick_and_whiten",
    )(pair_sides, pair_owner, block_members, spectra)


def routes(sta_count):
    def load(first, second, reaches):
        links = {}
        flows = [(first, reach) for reach in range(1, REACH)]
        flows += [(second, reach) for reach in reaches]
        for owner, reach in flows:
            source = (owner + reach) % sta_count
            step = 1 if owner > source else -1
            for place in range(source, owner, step):
                links[place, step] = links.get((place, step), 0) + 1
        return max(links.values())

    every = tuple(range(1, REACH))
    sets = [every] + list(itertools.combinations(every, 2))
    branches, choices = [], []
    for first, second in itertools.permutations(range(sta_count), 2):
        for named in itertools.combinations(range(REACH), 2):
            needs = set(named) - {0}
            fits = [reaches for reaches in sets if needs <= set(reaches)]
            best = min(fits, key=lambda reaches: load(first, second, reaches))
            branch = (first, second, best)
            if branch not in branches:
                branches.append(branch)
            mask = sum(1 << reach for reach in needs)
            case = (first * sta_count + second) * (1 << REACH) + mask
            choices.append((case, branches.index(branch)))
    return branches, choices


def phase_tables(sub_count, sub_freqs, groups, lag_rows):
    chunks = -(-sub_freqs // LANES)
    total = sub_count * sub_freqs
    freq = np.arange(total, dtype=np.int64).reshape(sub_count, 1, sub_freqs)
    middle = [2 * (group * lag_rows - LAGS // 2) + lag_rows - 1 for group in range(groups)]
    away = [step for step in range(1, lag_rows) if step % 2 != lag_rows % 2]

    def table(twice, forms, tile, dtype):
        twice = np.array(twice or [0], dtype=np.int64).reshape(1, -1, 1)
        angle = np.mod(freq * twice, 2 * total) * (math.pi / total)
        rows = np.stack([form(angle) for form in forms], axis=2)
        rows = rows.reshape(sub_count, -1, sub_freqs)
        pad = ((0, 0), (0, -rows.shape[1] % tile), (0, chunks * LANES - sub_freqs))
        return np.pad(rows, pad).astype(np.float32).astype(dtype)

    turns = table(middle, (np.cos, np.sin), 8, np.float32)
    offsets = table(away, (np.cos, np.sin, lambda angle: -np.sin(angle)), 16, BF16)
    return turns, offsets, len(away)


def lag_kernel(hops, slots, lag_rows, away, block_count, *refs):
    sub_count = lax.axis_size("sub")
    hr_count = lax.axis_size("hr")
    pair_ref, owner_ref, turn_ref, offset_ref = refs[:4]
    blocks = refs[4 : 4 + REACH * sub_count]
    outs = refs[4 + REACH * sub_count : 4 + REACH * sub_count + len(hops)]
    buf, sems = refs[4 + REACH * sub_count + len(hops) :]
    width = buf.shape[3]
    span = buf.shape[4] // 2
    middle_lag = lag_rows % 2
    my_sta = lax.axis_index("sta")
    my_sub = lax.axis_index("sub")
    my_hr = lax.axis_index("hr")
    sta_count = lax.axis_size("sta")

    ends = []
    for slot in slots:
        count = jnp.int32(0)
        left, right = jnp.int32(-1), jnp.int32(-1)
        for pair in range(owner_ref.shape[0]):
            mine = owner_ref[pair] == my_sta
            hit = mine & (count == slot)
            place = [
                lax.rem(pair_ref[side, pair] // block_count - my_sta + sta_count, sta_count)
                for side in range(2)
            ]
            left = jnp.where(hit, place[0], left)
            right = jnp.where(hit, place[1], right)
            count = count + mine.astype(jnp.int32)
        ends.append((left, right))

    def fetches(index, act):
        for side in range(2):
            for reach in range(REACH):

                @pl.when(ends[index][side] == reach)
                def _():
                    for step in range(sub_count):
                        act(
                            pltpu.make_async_copy(
                                blocks[reach * sub_count + step],
                                buf.at[index, side, step],
                                sems.at[index, side, step],
                            )
                        )

    for index in range(len(slots)):
        fetches(index, lambda copy: copy.start())

    for index in range(len(slots)):

        @pl.when(ends[index][0] < 0)
        def _():
            for out in outs:
                out[:, index] = jnp.zeros((lag_rows, width, width), out.dtype)

        fetches(index, lambda copy: copy.wait())

        @pl.when(ends[index][0] >= 0)
        def _():
            totals = [None] * len(hops)
            for step in range(sub_count):
                sub = lax.rem(my_sub + step, sub_count)
                real = buf[index, 1, step, :, :span]
                imag = buf[index, 1, step, :, span:]
                real_rows = [real] * middle_lag
                imag_rows = [imag] * middle_lag
                for near in range(away):
                    cosine, sine, minus = (
                        offset_ref[sub, 3 * near + form : 3 * near + form + 1, :]
                        for form in range(3)
                    )
                    real_rows += [real * cosine, imag * sine]
                    imag_rows += [imag * cosine, real * minus]
                real_rows = jnp.concatenate(real_rows, axis=0)
                imag_rows = jnp.concatenate(imag_rows, axis=0)
                real = buf[index, 0, step, :, :span].astype(F32)
                imag = buf[index, 0, step, :, span:].astype(F32)
                for place, hop in enumerate(hops):
                    group = lax.rem(my_hr + hop, hr_count) * sub_count + my_sub
                    cosine = turn_ref[sub, pl.ds(2 * group, 1), :]
                    sine = turn_ref[sub, pl.ds(2 * group + 1, 1), :]
                    part = dot_nt((real * cosine - imag * sine).astype(BF16), real_rows)
                    part += dot_nt((real * sine + imag * cosine).astype(BF16), imag_rows)
                    totals[place] = part if step == 0 else totals[place] + part
            for out, product in zip(outs, totals):
                if middle_lag:
                    out[lag_rows // 2, index] = product[:, :width].astype(out.dtype)
                for near in range(away):
                    start = (middle_lag + 2 * near) * width
                    even = product[:, start : start + width]
                    odd = product[:, start + width : start + 2 * width]
                    below = (lag_rows - 1) // 2 - near - middle_lag
                    above = lag_rows - 1 - below
                    out[above, index] = (even + odd).astype(out.dtype)
                    out[below, index] = (even - odd).astype(out.dtype)


def on_device(spectra, pair_blocks, pair_owner, block_members):
    hour_count, sub_freqs, _, _ = spectra.shape
    block_count, width = block_members.shape
    sta_count, hr_count, sub_count = (lax.axis_size(axis) for axis in ("sta", "hr", "sub"))
    groups = hr_count * sub_count
    lag_rows = LAGS // groups
    norming = 1.0 / math.sqrt(hour_count * hr_count * sub_count * sub_freqs)
    pair_sides = pair_blocks.T
    turns, offsets, away = phase_tables(sub_count, sub_freqs, groups, lag_rows)

    owners_at_most = pair_owner.shape[0] - CAP + 1
    branched = owners_at_most == 2 and sta_count == REACH
    kept = min(REACH, owners_at_most)
    branches, choices = routes(sta_count) if branched else ([], [])
    picked = pick_blocks(kept, choices, spectra, pair_sides, pair_owner, block_members)

    def exchange(owners_of, *picked):
        arrived = [picked[0]]
        for reach in range(1, REACH):
            to_owner = [((owner + reach) % sta_count, owner) for owner in owners_of[reach - 1]]
            arrived.append(lax.ppermute(picked[reach], "sta", to_owner))
        blocks = []
        for block in arrived:
            blocks.append(block)
            for step in range(1, sub_count):
                swap = [((sub + step) % sub_count, sub) for sub in range(sub_count)]
                blocks.append(lax.ppermute(block, "sub", swap))
        return blocks

    if branched:
        plans = [
            [(first, second) if reach in reaches else (first,) for reach in range(1, REACH)]
            for first, second, reaches in branches
        ]
        blocks = lax.switch(
            picked[REACH][0],
            [functools.partial(exchange, plan) for plan in plans],
            *picked[:REACH],
        )
    else:
        blocks = exchange([range(sta_count)] * (REACH - 1), *picked)

    smem = pl.BlockSpec(memory_space=pltpu.SMEM)
    vmem = pl.BlockSpec(memory_space=pltpu.VMEM)
    hbm = pl.BlockSpec(memory_space=pltpu.HBM)
    row = picked[0].shape[1]
    versions = (lag_rows % 2 + 2 * away) * width

    def products(hops, slots, dtype, name):
        return pl.pallas_call(
            functools.partial(lag_kernel, hops, slots, lag_rows, away, block_count),
            out_shape=[jax.ShapeDtypeStruct((lag_rows, len(slots), width, width), dtype)]
            * len(hops),
            in_specs=[smem, smem, vmem, vmem] + [hbm] * len(blocks),
            out_specs=[vmem] * len(hops),
            scratch_shapes=[
                pltpu.VMEM((len(slots), 2, sub_count, width, row), BF16),
                pltpu.SemaphoreType.DMA((len(slots), 2, sub_count)),
            ],
            compiler_params=pltpu.CompilerParams(vmem_limit_bytes=VMEM_LIMIT),
            cost_estimate=pl.CostEstimate(
                flops=2 * len(slots) * len(hops) * versions * width * sub_count * row,
                bytes_accessed=4 * len(slots) * sub_count * width * row,
                transcendentals=0,
            ),
            name=name,
        )(pair_sides, pair_owner, turns, offsets, *blocks)

    hops, slots = tuple(range(1, hr_count)), tuple(range(CAP))
    sent = products(hops, slots, BF16, "lags_to_send")
    received = []
    for hop, part in zip(hops, sent):
        to_device = [(hr, (hr + hop) % hr_count) for hr in range(hr_count)]
        received.append(lax.ppermute(part, "hr", to_device))
    (summed,) = products((0,), slots, F32, "lags_to_keep")
    for part in received:
        summed = summed + part.astype(F32)
    return (summed * norming).astype(BF16)


def solution(mesh):
    placed = (P(("grp", "hr"), "sub", None, "sta"), P(), P(), P("sta", None))
    return jax.shard_map(
        on_device,
        mesh=mesh,
        in_specs=placed,
        out_specs=P(("grp", "hr", "sub"), "sta", None, None),
        check_vma=False,
    )
```

```python
import functools
import itertools
import math

import jax
import jax.numpy as jnp
import numpy as np
from jax import lax
from jax.experimental import pallas as pl
from jax.experimental.pallas import tpu as pltpu
from jax.sharding import PartitionSpec as P

BAND = 50
LAGS = 16
CAP = 3
REACH = 4
EPSILON = 1e-05
LANES = 128
F32 = jnp.float32
BF16 = jnp.bfloat16
PICK_VMEM_LIMIT = 59 * 1024 * 1024
LAG_VMEM_LIMIT = 32 * 1024 * 1024

NT = (((1,), (1,)), ((), ()))


def dot_nt(left, right):
    return lax.dot_general(left, right, NT, preferred_element_type=F32)


def iota(shape, dim):
    return lax.broadcasted_iota(jnp.int32, shape, dim)


def band_matrix(chunk, freqs):
    row, col = iota((2 * LANES, LANES), 0), iota((2 * LANES, LANES), 1)
    freq = chunk * LANES + row % LANES
    low = (col % 16) * BAND
    hit = (freq >= low) & (freq < low + BAND) & (freq < freqs) & (col < 48)
    return jnp.where(hit, 1.0, 0.0).astype(BF16)


def pick_kernel(kept, choices, sta_axis, pair_hbm, owner_hbm, member_hbm, x_ref, *rest):
    branched = len(choices) > 0
    outs = rest[:REACH]
    branch_ref = rest[REACH] if branched else None
    pair_ref, owner_ref, member_ref, x_buf, y_buf, z_buf, sems = rest[REACH + branched :]
    tiles, freqs = x_buf.shape[0], x_buf.shape[1]
    block_count, width = member_ref.shape
    chunks = y_buf.shape[1] // (2 * LANES)

    def fetch(tile):
        return pltpu.make_async_copy(
            x_ref.at[0, :, :, pl.ds(tile * LANES, LANES)], x_buf.at[tile], sems.at[tile]
        )

    small = [
        pltpu.make_async_copy(source, target, sems.at[tiles + index])
        for index, (source, target) in enumerate(
            ((pair_hbm, pair_ref), (owner_hbm, owner_ref), (member_hbm, member_ref))
        )
    ]
    for copy in small:
        copy.start()
    for tile in range(tiles):
        fetch(tile).start()
    for copy in small:
        copy.wait()

    my_sta = lax.axis_index(sta_axis)
    sta_count = lax.axis_size(sta_axis)
    pair_count = owner_ref.shape[0]
    members = jnp.transpose(member_ref[...].astype(F32))
    block_col = iota(members.shape, 1)
    found, wanted = jnp.int32(0), []
    for reach in range(REACH):
        owner = lax.rem(my_sta - reach + REACH * sta_count, sta_count)
        chosen = jnp.int32(-1)
        for pair in range(pair_count):
            for side in range(2):
                block = pair_ref[side, pair]
                hit = (owner_ref[pair] == owner) & (block // block_count == my_sta)
                chosen = jnp.where(hit, lax.rem(block, block_count), chosen)
        wanted.append((found, chosen))
        found = found + (chosen >= 0).astype(jnp.int32)
    places, station = [], []
    for place in range(kept):
        reach_here, block_here = jnp.int32(-1), jnp.int32(0)
        for reach, (rank, chosen) in enumerate(wanted):
            hit = (rank == place) & (chosen >= 0)
            reach_here = jnp.where(hit, reach, reach_here)
            block_here = jnp.where(hit, chosen, block_here)
        places.append(reach_here)
        column = jnp.where(block_col == block_here, members, 0.0)
        station.append(jnp.sum(column, axis=1, keepdims=True).astype(jnp.int32))
    station = jnp.concatenate(station, axis=0)

    lane = iota((kept * width, LANES), 1)

    def one_hot(tile):
        return jnp.where(station == lane + tile * LANES, 1.0, 0.0).astype(BF16)

    y_buf[:, 2 * freqs :] = jnp.zeros((kept * width, y_buf.shape[1] - 2 * freqs), BF16)
    total = None
    for first in range(0, tiles, 2):
        span = range(first, min(first + 2, tiles))
        hot = jnp.concatenate([one_hot(tile) for tile in span], axis=1)
        for tile in span:
            fetch(tile).wait()
        x = jnp.concatenate(
            [x_buf.at[tile].reshape(2 * freqs, LANES)[...] for tile in span], axis=1
        )
        part = dot_nt(hot, x)
        total = part if total is None else total + part
    y_buf[:, : 2 * freqs] = total.astype(BF16)

    row, col = iota((2 * LANES, 2 * LANES), 0), iota((2 * LANES, 2 * LANES), 1)
    split = jnp.where(row == 2 * (col % LANES) + col // LANES, 1.0, 0.0).astype(BF16)
    power = None
    for chunk in range(chunks):
        z = jnp.dot(
            y_buf[:, chunk * 2 * LANES : (chunk + 1) * 2 * LANES],
            split,
            preferred_element_type=F32,
        )
        z_buf[chunk] = z
        square = z * z
        high = square.astype(BF16)
        low = (square - high.astype(F32)).astype(BF16)
        bands = band_matrix(chunk, freqs)
        part = jnp.dot(high, bands, preferred_element_type=F32) + jnp.dot(
            low, bands, preferred_element_type=F32
        )
        power = part if power is None else power + part
    scale = lax.rsqrt(power * (1.0 / (2 * BAND)) + EPSILON)
    high = scale.astype(BF16)
    rest1 = scale - high.astype(F32)
    mid = rest1.astype(BF16)
    low = rest1 - mid.astype(F32)
    third = iota(scale.shape, 1) // 16
    pieces = jnp.where(
        third == 0, high.astype(F32), jnp.where(third == 1, mid.astype(F32), low)
    ).astype(BF16)
    for chunk in range(chunks):
        white = (z_buf[chunk] * dot_nt(pieces, band_matrix(chunk, freqs))).astype(BF16)
        y_buf[:, chunk * LANES : (chunk + 1) * LANES] = white[:, :LANES]
        y_buf[:, (chunks + chunk) * LANES : (chunks + chunk + 1) * LANES] = white[:, LANES:]
    for place, reach_here in enumerate(places):
        for reach in range(REACH):

            @pl.when(reach_here == reach)
            def _():
                outs[reach][...] = y_buf[place * width : (place + 1) * width]

    if branched:
        first = second = needs = jnp.int32(0)
        for pair in range(pair_count):
            owner = owner_ref[pair]
            count = jnp.int32(0)
            for other in range(pair_count):
                count = count + (owner_ref[other] == owner).astype(jnp.int32)
            ends = [
                lax.rem(pair_ref[side, pair] // block_count - owner + sta_count, sta_count)
                for side in range(2)
            ]
            first = jnp.where(count == CAP, owner, first)
            second = jnp.where(count < CAP, owner, second)
            needs = jnp.where(count < CAP, (1 << ends[0]) | (1 << ends[1]), needs)
        case = (first * sta_count + second) * (1 << REACH) + (needs & ~1)
        branch = jnp.int32(0)
        for known, number in choices:
            branch = jnp.where(case == known, number, branch)
        branch_ref[0] = branch


def pick_blocks(kept, choices, spectra, pair_sides, pair_owner, block_members):
    _, freqs, parts, stations = spectra.shape
    block_count, width = block_members.shape
    tiles = stations // LANES
    chunks = -(-freqs // LANES)
    rows = kept * width
    branched = len(choices) > 0
    vmem = pl.BlockSpec(memory_space=pltpu.VMEM)
    blocks = [jax.ShapeDtypeStruct((width, chunks * 2 * LANES), BF16)] * REACH
    branch = [jax.ShapeDtypeStruct((1,), jnp.int32)] * branched
    return pl.pallas_call(
        functools.partial(pick_kernel, kept, choices, "sta"),
        out_shape=blocks + branch,
        in_specs=[pl.BlockSpec(memory_space=pltpu.HBM)] * 4,
        out_specs=[vmem] * REACH + [pl.BlockSpec(memory_space=pltpu.SMEM)] * branched,
        scratch_shapes=[
            pltpu.SMEM(pair_sides.shape, jnp.int32),
            pltpu.SMEM(pair_owner.shape, jnp.int32),
            pltpu.VMEM(block_members.shape, jnp.int32),
            pltpu.VMEM((tiles, freqs, parts, LANES), BF16),
            pltpu.VMEM((rows, chunks * 2 * LANES), BF16),
            pltpu.VMEM((chunks, rows, 2 * LANES), F32),
            pltpu.SemaphoreType.DMA((tiles + 3,)),
        ],
        compiler_params=pltpu.CompilerParams(vmem_limit_bytes=PICK_VMEM_LIMIT),
        cost_estimate=pl.CostEstimate(
            flops=2 * rows * stations * freqs * parts,
            bytes_accessed=2 * spectra.size + 4 * rows * chunks * LANES,
            transcendentals=0,
        ),
        name="pick_and_whiten",
    )(pair_sides, pair_owner, block_members, spectra)


def routes(sta_count):
    def load(first, second, reaches):
        links = {}
        flows = [(first, reach) for reach in range(1, REACH)]
        flows += [(second, reach) for reach in reaches]
        for owner, reach in flows:
            source = (owner + reach) % sta_count
            step = 1 if owner > source else -1
            for place in range(source, owner, step):
                links[place, step] = links.get((place, step), 0) + 1
        return max(links.values())

    every = tuple(range(1, REACH))
    sets = [every] + list(itertools.combinations(every, 2))
    branches, choices = [], []
    for first, second in itertools.permutations(range(sta_count), 2):
        for named in itertools.combinations(range(REACH), 2):
            needs = set(named) - {0}
            fits = [reaches for reaches in sets if needs <= set(reaches)]
            best = min(fits, key=lambda reaches: load(first, second, reaches))
            branch = (first, second, best)
            if branch not in branches:
                branches.append(branch)
            mask = sum(1 << reach for reach in needs)
            case = (first * sta_count + second) * (1 << REACH) + mask
            choices.append((case, branches.index(branch)))
    return branches, choices


def phase_tables(sub_count, sub_freqs, groups, lag_rows):
    chunks = -(-sub_freqs // LANES)
    total = sub_count * sub_freqs
    freq = np.arange(total, dtype=np.int64).reshape(sub_count, 1, sub_freqs)
    middle = [2 * (group * lag_rows - LAGS // 2) + lag_rows - 1 for group in range(groups)]
    away = [step for step in range(1, lag_rows) if step % 2 != lag_rows % 2]

    def table(twice, forms, tile, dtype):
        twice = np.array(twice or [0], dtype=np.int64).reshape(1, -1, 1)
        angle = np.mod(freq * twice, 2 * total) * (math.pi / total)
        rows = np.stack([form(angle) for form in forms], axis=2)
        rows = rows.reshape(sub_count, -1, sub_freqs)
        pad = ((0, 0), (0, -rows.shape[1] % tile), (0, chunks * LANES - sub_freqs))
        return np.pad(rows, pad).astype(np.float32).astype(dtype)

    turns = table(middle, (np.cos, np.sin), 8, np.float32)
    offsets = table(away, (np.cos, np.sin, lambda angle: -np.sin(angle)), 16, BF16)
    return turns, offsets, len(away)


def lag_kernel(hops, slots, lag_rows, away, block_count, *refs):
    sub_count = lax.axis_size("sub")
    hr_count = lax.axis_size("hr")
    pair_ref, owner_ref, turn_ref, offset_ref = refs[:4]
    blocks = refs[4 : 4 + REACH * sub_count]
    outs = refs[4 + REACH * sub_count : 4 + REACH * sub_count + len(hops)]
    buf, sems = refs[4 + REACH * sub_count + len(hops) :]
    width = buf.shape[3]
    span = buf.shape[4] // 2
    middle_lag = lag_rows % 2
    my_sta = lax.axis_index("sta")
    my_sub = lax.axis_index("sub")
    my_hr = lax.axis_index("hr")
    sta_count = lax.axis_size("sta")

    ends = []
    for slot in slots:
        count = jnp.int32(0)
        left, right = jnp.int32(-1), jnp.int32(-1)
        for pair in range(owner_ref.shape[0]):
            mine = owner_ref[pair] == my_sta
            hit = mine & (count == slot)
            place = [
                lax.rem(pair_ref[side, pair] // block_count - my_sta + sta_count, sta_count)
                for side in range(2)
            ]
            left = jnp.where(hit, place[0], left)
            right = jnp.where(hit, place[1], right)
            count = count + mine.astype(jnp.int32)
        ends.append((left, right))

    def fetches(index, act):
        for side in range(2):
            for reach in range(REACH):

                @pl.when(ends[index][side] == reach)
                def _():
                    for step in range(sub_count):
                        act(
                            pltpu.make_async_copy(
                                blocks[reach * sub_count + step],
                                buf.at[index, side, step],
                                sems.at[index, side, step],
                            )
                        )

    for index in range(len(slots)):
        fetches(index, lambda copy: copy.start())

    for index in range(len(slots)):

        @pl.when(ends[index][0] < 0)
        def _():
            for out in outs:
                out[:, index] = jnp.zeros((lag_rows, width, width), out.dtype)

        fetches(index, lambda copy: copy.wait())

        @pl.when(ends[index][0] >= 0)
        def _():
            total = None
            for step in range(sub_count):
                sub = lax.rem(my_sub + step, sub_count)
                real = buf[index, 0, step, :, :span]
                imag = buf[index, 0, step, :, span:]
                scaled_real, scaled_imag = [real] * middle_lag, [imag] * middle_lag
                for near in range(away):
                    cosine, sine, minus = (
                        offset_ref[sub, 3 * near + form : 3 * near + form + 1, :]
                        for form in range(3)
                    )
                    scaled_real += [real * cosine, imag * minus]
                    scaled_imag += [imag * cosine, real * sine]
                real = buf[index, 1, step, :, :span].astype(F32)
                imag = buf[index, 1, step, :, span:].astype(F32)
                turned_real, turned_imag = [], []
                for hop in hops:
                    group = lax.rem(my_hr + hop, hr_count) * sub_count + my_sub
                    cosine = turn_ref[sub, pl.ds(2 * group, 1), :]
                    sine = turn_ref[sub, pl.ds(2 * group + 1, 1), :]
                    turned_real.append((real * cosine + imag * sine).astype(BF16))
                    turned_imag.append((imag * cosine - real * sine).astype(BF16))
                for scaled, turned in ((scaled_real, turned_real), (scaled_imag, turned_imag)):
                    part = dot_nt(jnp.concatenate(scaled, axis=0), jnp.concatenate(turned, axis=0))
                    total = part if total is None else total + part
            for place, out in enumerate(outs):
                columns = slice(place * width, (place + 1) * width)
                if middle_lag:
                    out[lag_rows // 2, index] = total[:width, columns].astype(out.dtype)
                for near in range(away):
                    start = (middle_lag + 2 * near) * width
                    even = total[start : start + width, columns]
                    odd = total[start + width : start + 2 * width, columns]
                    below = (lag_rows - 1) // 2 - near - middle_lag
                    above = lag_rows - 1 - below
                    out[above, index] = (even + odd).astype(out.dtype)
                    out[below, index] = (even - odd).astype(out.dtype)


def on_device(spectra, pair_blocks, pair_owner, block_members):
    hour_count, sub_freqs, _, _ = spectra.shape
    block_count, width = block_members.shape
    sta_count, hr_count, sub_count = (lax.axis_size(axis) for axis in ("sta", "hr", "sub"))
    groups = hr_count * sub_count
    lag_rows = LAGS // groups
    norming = 1.0 / math.sqrt(hour_count * hr_count * sub_count * sub_freqs)
    pair_sides = pair_blocks.T
    turns, offsets, away = phase_tables(sub_count, sub_freqs, groups, lag_rows)

    owners_at_most = pair_owner.shape[0] - CAP + 1
    branched = owners_at_most == 2 and sta_count == REACH
    kept = min(REACH, owners_at_most)
    branches, choices = routes(sta_count) if branched else ([], [])
    picked = pick_blocks(kept, choices, spectra, pair_sides, pair_owner, block_members)

    def exchange(owners_of, *picked):
        arrived = [picked[0]]
        for reach in range(1, REACH):
            to_owner = [((owner + reach) % sta_count, owner) for owner in owners_of[reach - 1]]
            arrived.append(lax.ppermute(picked[reach], "sta", to_owner))
        blocks = []
        for block in arrived:
            blocks.append(block)
            for step in range(1, sub_count):
                swap = [((sub + step) % sub_count, sub) for sub in range(sub_count)]
                blocks.append(lax.ppermute(block, "sub", swap))
        return blocks

    if branched:
        plans = [
            [(first, second) if reach in reaches else (first,) for reach in range(1, REACH)]
            for first, second, reaches in branches
        ]
        blocks = lax.switch(
            picked[REACH][0],
            [functools.partial(exchange, plan) for plan in plans],
            *picked[:REACH],
        )
    else:
        blocks = exchange([range(sta_count)] * (REACH - 1), *picked)

    smem = pl.BlockSpec(memory_space=pltpu.SMEM)
    vmem = pl.BlockSpec(memory_space=pltpu.VMEM)
    hbm = pl.BlockSpec(memory_space=pltpu.HBM)
    row = picked[0].shape[1]
    versions = (lag_rows % 2 + 2 * away) * width

    def products(hops, slots, dtype, name):
        return pl.pallas_call(
            functools.partial(lag_kernel, hops, slots, lag_rows, away, block_count),
            out_shape=[jax.ShapeDtypeStruct((lag_rows, len(slots), width, width), dtype)]
            * len(hops),
            in_specs=[smem, smem, vmem, vmem] + [hbm] * len(blocks),
            out_specs=[vmem] * len(hops),
            scratch_shapes=[
                pltpu.VMEM((len(slots), 2, sub_count, width, row), BF16),
                pltpu.SemaphoreType.DMA((len(slots), 2, sub_count)),
            ],
            compiler_params=pltpu.CompilerParams(vmem_limit_bytes=LAG_VMEM_LIMIT),
            cost_estimate=pl.CostEstimate(
                flops=2 * len(slots) * len(hops) * versions * width * sub_count * row,
                bytes_accessed=4 * len(slots) * sub_count * width * row,
                transcendentals=0,
            ),
            name=name,
        )(pair_sides, pair_owner, turns, offsets, *blocks)

    hops, slots = tuple(range(1, hr_count)), tuple(range(CAP))
    sent = products(hops, slots, BF16, "lags_to_send")
    received = []
    for hop, part in zip(hops, sent):
        to_device = [(hr, (hr + hop) % hr_count) for hr in range(hr_count)]
        received.append(lax.ppermute(part, "hr", to_device))
    (summed,) = products((0,), slots, F32, "lags_to_keep")
    for part in received:
        summed = summed + part.astype(F32)
    return (summed * norming).astype(BF16)


def solution(mesh):
    placed = (P(("grp", "hr"), "sub", None, "sta"), P(), P(), P("sta", None))
    return jax.shard_map(
        on_device,
        mesh=mesh,
        in_specs=placed,
        out_specs=P(("grp", "hr", "sub"), "sta", None, None),
        check_vma=False,
    )
```

```python
import functools
import itertools
import math

import jax
import jax.numpy as jnp
import numpy as np
from jax import lax
from jax.experimental import pallas as pl
from jax.experimental.pallas import tpu as pltpu
from jax.sharding import PartitionSpec as P

BAND = 50
LAGS = 16
CAP = 3
REACH = 4
EPSILON = 1e-05
LANES = 128
F32 = jnp.float32
BF16 = jnp.bfloat16
PICK_VMEM_LIMIT = 59 * 1024 * 1024
LAG_VMEM_LIMIT = 32 * 1024 * 1024

NT = (((1,), (1,)), ((), ()))


def dot_nt(left, right):
    return lax.dot_general(left, right, NT, preferred_element_type=F32)


def iota(shape, dim):
    return lax.broadcasted_iota(jnp.int32, shape, dim)


def band_matrix(chunk, freqs):
    row, col = iota((2 * LANES, LANES), 0), iota((2 * LANES, LANES), 1)
    freq = chunk * LANES + row % LANES
    low = (col % 16) * BAND
    hit = (freq >= low) & (freq < low + BAND) & (freq < freqs) & (col < 48)
    return jnp.where(hit, 1.0, 0.0).astype(BF16)


def pick_kernel(kept, choices, sta_axis, pair_hbm, owner_hbm, member_hbm, x_ref, *rest):
    branched = len(choices) > 0
    outs = rest[:REACH]
    branch_ref = rest[REACH] if branched else None
    pair_ref, owner_ref, member_ref, x_buf, y_buf, z_buf, sems = rest[REACH + branched :]
    tiles, freqs = x_buf.shape[0], x_buf.shape[1]
    block_count, width = member_ref.shape
    chunks = y_buf.shape[1] // (2 * LANES)

    def fetch(tile):
        return pltpu.make_async_copy(
            x_ref.at[0, :, :, pl.ds(tile * LANES, LANES)], x_buf.at[tile], sems.at[tile]
        )

    small = [
        pltpu.make_async_copy(source, target, sems.at[tiles + index])
        for index, (source, target) in enumerate(
            ((pair_hbm, pair_ref), (owner_hbm, owner_ref), (member_hbm, member_ref))
        )
    ]
    for copy in small:
        copy.start()
    for tile in range(tiles):
        fetch(tile).start()
    for copy in small:
        copy.wait()

    my_sta = lax.axis_index(sta_axis)
    sta_count = lax.axis_size(sta_axis)
    pair_count = owner_ref.shape[0]
    members = jnp.transpose(member_ref[...].astype(F32))
    block_col = iota(members.shape, 1)
    found, wanted = jnp.int32(0), []
    for reach in range(REACH):
        owner = lax.rem(my_sta - reach + REACH * sta_count, sta_count)
        chosen = jnp.int32(-1)
        for pair in range(pair_count):
            for side in range(2):
                block = pair_ref[side, pair]
                hit = (owner_ref[pair] == owner) & (block // block_count == my_sta)
                chosen = jnp.where(hit, lax.rem(block, block_count), chosen)
        wanted.append((found, chosen))
        found = found + (chosen >= 0).astype(jnp.int32)
    places, station = [], []
    for place in range(kept):
        reach_here, block_here = jnp.int32(-1), jnp.int32(0)
        for reach, (rank, chosen) in enumerate(wanted):
            hit = (rank == place) & (chosen >= 0)
            reach_here = jnp.where(hit, reach, reach_here)
            block_here = jnp.where(hit, chosen, block_here)
        places.append(reach_here)
        column = jnp.where(block_col == block_here, members, 0.0)
        station.append(jnp.sum(column, axis=1, keepdims=True).astype(jnp.int32))
    station = jnp.concatenate(station, axis=0)

    lane = iota((kept * width, LANES), 1)

    def one_hot(tile):
        return jnp.where(station == lane + tile * LANES, 1.0, 0.0).astype(BF16)

    y_buf[:, 2 * freqs :] = jnp.zeros((kept * width, y_buf.shape[1] - 2 * freqs), BF16)
    total = None
    for first in range(0, tiles, 2):
        span = range(first, min(first + 2, tiles))
        hot = jnp.concatenate([one_hot(tile) for tile in span], axis=1)
        for tile in span:
            fetch(tile).wait()
        x = jnp.concatenate(
            [x_buf.at[tile].reshape(2 * freqs, LANES)[...] for tile in span], axis=1
        )
        part = dot_nt(hot, x)
        total = part if total is None else total + part
    y_buf[:, : 2 * freqs] = total.astype(BF16)

    row, col = iota((2 * LANES, 2 * LANES), 0), iota((2 * LANES, 2 * LANES), 1)
    split = jnp.where(row == 2 * (col % LANES) + col // LANES, 1.0, 0.0).astype(BF16)
    power = None
    for chunk in range(chunks):
        z = jnp.dot(
            y_buf[:, chunk * 2 * LANES : (chunk + 1) * 2 * LANES],
            split,
            preferred_element_type=F32,
        )
        z_buf[chunk] = z
        square = z * z
        high = square.astype(BF16)
        low = (square - high.astype(F32)).astype(BF16)
        bands = band_matrix(chunk, freqs)
        part = jnp.dot(high, bands, preferred_element_type=F32) + jnp.dot(
            low, bands, preferred_element_type=F32
        )
        power = part if power is None else power + part
    scale = lax.rsqrt(power * (1.0 / (2 * BAND)) + EPSILON)
    high = scale.astype(BF16)
    rest1 = scale - high.astype(F32)
    mid = rest1.astype(BF16)
    low = rest1 - mid.astype(F32)
    third = iota(scale.shape, 1) // 16
    pieces = jnp.where(
        third == 0, high.astype(F32), jnp.where(third == 1, mid.astype(F32), low)
    ).astype(BF16)
    for chunk in range(chunks):
        white = (z_buf[chunk] * dot_nt(pieces, band_matrix(chunk, freqs))).astype(BF16)
        y_buf[:, chunk * LANES : (chunk + 1) * LANES] = white[:, :LANES]
        y_buf[:, (chunks + chunk) * LANES : (chunks + chunk + 1) * LANES] = white[:, LANES:]
    for place, reach_here in enumerate(places):
        for reach in range(REACH):

            @pl.when(reach_here == reach)
            def _():
                outs[reach][...] = y_buf[place * width : (place + 1) * width]

    if branched:
        first, second = owners(owner_ref)
        needs = jnp.int32(0)
        for pair in range(pair_count):
            ends = [
                lax.rem(pair_ref[side, pair] // block_count - second + sta_count, sta_count)
                for side in range(2)
            ]
            named = (1 << ends[0]) | (1 << ends[1])
            needs = jnp.where(owner_ref[pair] == second, named, needs)
        case = (first * sta_count + second) * (1 << REACH) + (needs & ~1)
        branch = jnp.int32(0)
        for known, number in choices:
            branch = jnp.where(case == known, number, branch)
        branch_ref[0] = branch


def pick_blocks(kept, choices, spectra, pair_sides, pair_owner, block_members):
    _, freqs, parts, stations = spectra.shape
    block_count, width = block_members.shape
    tiles = stations // LANES
    chunks = -(-freqs // LANES)
    rows = kept * width
    branched = len(choices) > 0
    vmem = pl.BlockSpec(memory_space=pltpu.VMEM)
    blocks = [jax.ShapeDtypeStruct((width, chunks * 2 * LANES), BF16)] * REACH
    branch = [jax.ShapeDtypeStruct((1,), jnp.int32)] * branched
    return pl.pallas_call(
        functools.partial(pick_kernel, kept, choices, "sta"),
        out_shape=blocks + branch,
        in_specs=[pl.BlockSpec(memory_space=pltpu.HBM)] * 4,
        out_specs=[vmem] * REACH + [pl.BlockSpec(memory_space=pltpu.SMEM)] * branched,
        scratch_shapes=[
            pltpu.SMEM(pair_sides.shape, jnp.int32),
            pltpu.SMEM(pair_owner.shape, jnp.int32),
            pltpu.VMEM(block_members.shape, jnp.int32),
            pltpu.VMEM((tiles, freqs, parts, LANES), BF16),
            pltpu.VMEM((rows, chunks * 2 * LANES), BF16),
            pltpu.VMEM((chunks, rows, 2 * LANES), F32),
            pltpu.SemaphoreType.DMA((tiles + 3,)),
        ],
        compiler_params=pltpu.CompilerParams(vmem_limit_bytes=PICK_VMEM_LIMIT),
        cost_estimate=pl.CostEstimate(
            flops=2 * rows * stations * freqs * parts,
            bytes_accessed=2 * spectra.size + 4 * rows * chunks * LANES,
            transcendentals=0,
        ),
        name="pick_and_whiten",
    )(pair_sides, pair_owner, block_members, spectra)


def routes(sta_count):
    def load(first, second, reaches):
        links = {}
        flows = [(first, reach) for reach in range(1, REACH)]
        flows += [(second, reach) for reach in reaches]
        for owner, reach in flows:
            source = (owner + reach) % sta_count
            step = 1 if owner > source else -1
            for place in range(source, owner, step):
                links[place, step] = links.get((place, step), 0) + 1
        return max(links.values())

    every = tuple(range(1, REACH))
    sets = [every] + list(itertools.combinations(every, 2))
    branches, choices = [], []
    for first, second in itertools.permutations(range(sta_count), 2):
        for named in itertools.combinations(range(REACH), 2):
            needs = set(named) - {0}
            fits = [reaches for reaches in sets if needs <= set(reaches)]
            best = min(fits, key=lambda reaches: load(first, second, reaches))
            branch = (first, second, best)
            if branch not in branches:
                branches.append(branch)
            mask = sum(1 << reach for reach in needs)
            case = (first * sta_count + second) * (1 << REACH) + mask
            choices.append((case, branches.index(branch)))
    return branches, choices


def send_ranks(first, second, sta_count, where):
    keys = []
    for reach in range(1, REACH):
        to_first = (second - first - reach) % sta_count == 0
        to_second = (first - second - reach) % sta_count == 0
        keys.append(where(to_second, 2 * REACH, where(to_first, REACH, 0)) + reach)
    return [sum(where(other < key, 1, 0) for other in keys) for key in keys]


def owners(owner_ref):
    first = second = jnp.int32(0)
    for pair in range(owner_ref.shape[0]):
        owner = owner_ref[pair]
        count = jnp.int32(0)
        for other in range(owner_ref.shape[0]):
            count = count + (owner_ref[other] == owner).astype(jnp.int32)
        first = jnp.where(count == CAP, owner, first)
        second = jnp.where(count < CAP, owner, second)
    return first, second


def phase_tables(sub_count, sub_freqs, groups, lag_rows):
    chunks = -(-sub_freqs // LANES)
    total = sub_count * sub_freqs
    freq = np.arange(total, dtype=np.int64).reshape(sub_count, 1, sub_freqs)
    middle = [2 * (group * lag_rows - LAGS // 2) + lag_rows - 1 for group in range(groups)]
    away = [step for step in range(1, lag_rows) if step % 2 != lag_rows % 2]

    def table(twice, forms, tile, dtype):
        twice = np.array(twice or [0], dtype=np.int64).reshape(1, -1, 1)
        angle = np.mod(freq * twice, 2 * total) * (math.pi / total)
        rows = np.stack([form(angle) for form in forms], axis=2)
        rows = rows.reshape(sub_count, -1, sub_freqs)
        pad = ((0, 0), (0, -rows.shape[1] % tile), (0, chunks * LANES - sub_freqs))
        return np.pad(rows, pad).astype(np.float32).astype(dtype)

    turns = table(middle, (np.cos, np.sin), 8, np.float32)
    offsets = table(away, (np.cos, np.sin, lambda angle: -np.sin(angle)), 16, BF16)
    return turns, offsets, len(away)


def lag_kernel(hops, slots, lag_rows, away, block_count, branched, *refs):
    sub_count = lax.axis_size("sub")
    hr_count = lax.axis_size("hr")
    pair_ref, owner_ref, turn_ref, offset_ref = refs[:4]
    blocks = refs[4 : 4 + REACH * sub_count]
    outs = refs[4 + REACH * sub_count : 4 + REACH * sub_count + len(hops)]
    buf, sems = refs[4 + REACH * sub_count + len(hops) :]
    width = buf.shape[3]
    span = buf.shape[4] // 2
    middle_lag = lag_rows % 2
    my_sta = lax.axis_index("sta")
    my_sub = lax.axis_index("sub")
    my_hr = lax.axis_index("hr")
    sta_count = lax.axis_size("sta")

    places = [jnp.int32(reach) for reach in range(REACH)]
    if branched:
        first, second = owners(owner_ref)
        ranks = send_ranks(first + sta_count, second + sta_count, sta_count, jnp.where)
        places[1:] = [1 + rank for rank in ranks]

    def place_of(block):
        reach = lax.rem(block // block_count - my_sta + sta_count, sta_count)
        place = places[0]
        for known in range(1, REACH):
            place = jnp.where(reach == known, places[known], place)
        return place

    ends = []
    for slot in slots:
        count = jnp.int32(0)
        left, right = jnp.int32(-1), jnp.int32(-1)
        for pair in range(owner_ref.shape[0]):
            mine = owner_ref[pair] == my_sta
            hit = mine & (count == slot)
            left = jnp.where(hit, place_of(pair_ref[0, pair]), left)
            right = jnp.where(hit, place_of(pair_ref[1, pair]), right)
            count = count + mine.astype(jnp.int32)
        ends.append((left, right))

    def fetches(index, act):
        for side in range(2):
            for place in range(REACH):

                @pl.when(ends[index][side] == place)
                def _():
                    for step in range(sub_count):
                        act(
                            pltpu.make_async_copy(
                                blocks[place * sub_count + step],
                                buf.at[index, side, step],
                                sems.at[index, side, step],
                            )
                        )

    for index in range(len(slots)):
        fetches(index, lambda copy: copy.start())

    for index in range(len(slots)):

        @pl.when(ends[index][0] < 0)
        def _():
            for out in outs:
                out[:, index] = jnp.zeros((lag_rows, width, width), out.dtype)

        fetches(index, lambda copy: copy.wait())

        @pl.when(ends[index][0] >= 0)
        def _():
            total = None
            for step in range(sub_count):
                sub = lax.rem(my_sub + step, sub_count)
                real = buf[index, 0, step, :, :span]
                imag = buf[index, 0, step, :, span:]
                scaled_real, scaled_imag = [real] * middle_lag, [imag] * middle_lag
                for near in range(away):
                    cosine, sine, minus = (
                        offset_ref[sub, 3 * near + form : 3 * near + form + 1, :]
                        for form in range(3)
                    )
                    scaled_real += [real * cosine, imag * minus]
                    scaled_imag += [imag * cosine, real * sine]
                real = buf[index, 1, step, :, :span].astype(F32)
                imag = buf[index, 1, step, :, span:].astype(F32)
                turned_real, turned_imag = [], []
                for hop in hops:
                    group = lax.rem(my_hr + hop, hr_count) * sub_count + my_sub
                    cosine = turn_ref[sub, pl.ds(2 * group, 1), :]
                    sine = turn_ref[sub, pl.ds(2 * group + 1, 1), :]
                    turned_real.append((real * cosine + imag * sine).astype(BF16))
                    turned_imag.append((imag * cosine - real * sine).astype(BF16))
                for scaled, turned in ((scaled_real, turned_real), (scaled_imag, turned_imag)):
                    part = dot_nt(jnp.concatenate(scaled, axis=0), jnp.concatenate(turned, axis=0))
                    total = part if total is None else total + part
            for place, out in enumerate(outs):
                columns = slice(place * width, (place + 1) * width)
                if middle_lag:
                    out[lag_rows // 2, index] = total[:width, columns].astype(out.dtype)
                for near in range(away):
                    start = (middle_lag + 2 * near) * width
                    even = total[start : start + width, columns]
                    odd = total[start + width : start + 2 * width, columns]
                    below = (lag_rows - 1) // 2 - near - middle_lag
                    above = lag_rows - 1 - below
                    out[above, index] = (even + odd).astype(out.dtype)
                    out[below, index] = (even - odd).astype(out.dtype)


def on_device(spectra, pair_blocks, pair_owner, block_members):
    hour_count, sub_freqs, _, _ = spectra.shape
    block_count, width = block_members.shape
    sta_count, hr_count, sub_count = (lax.axis_size(axis) for axis in ("sta", "hr", "sub"))
    groups = hr_count * sub_count
    lag_rows = LAGS // groups
    norming = 1.0 / math.sqrt(hour_count * hr_count * sub_count * sub_freqs)
    pair_sides = pair_blocks.T
    turns, offsets, away = phase_tables(sub_count, sub_freqs, groups, lag_rows)

    owners_at_most = pair_owner.shape[0] - CAP + 1
    branched = owners_at_most == 2 and sta_count == REACH
    kept = min(REACH, owners_at_most)
    branches, choices = routes(sta_count) if branched else ([], [])
    picked = pick_blocks(kept, choices, spectra, pair_sides, pair_owner, block_members)

    def exchange(owners_of, order, *picked):
        arrived = [picked[0]]
        for reach in order:
            to_owner = [((owner + reach) % sta_count, owner) for owner in owners_of[reach - 1]]
            arrived.append(lax.ppermute(picked[reach], "sta", to_owner))
        blocks = []
        for block in arrived:
            blocks.append(block)
            for step in range(1, sub_count):
                swap = [((sub + step) % sub_count, sub) for sub in range(sub_count)]
                blocks.append(lax.ppermute(block, "sub", swap))
        return blocks

    if branched:
        steps = []
        for first, second, reaches in branches:
            owners_of = [
                (first, second) if reach in reaches else (first,) for reach in range(1, REACH)
            ]
            ranks = send_ranks(first, second, sta_count, lambda hit, yes, no: yes if hit else no)
            order = sorted(range(1, REACH), key=lambda reach: ranks[reach - 1])
            steps.append(functools.partial(exchange, owners_of, order))
        blocks = lax.switch(picked[REACH][0], steps, *picked[:REACH])
    else:
        blocks = exchange([range(sta_count)] * (REACH - 1), range(1, REACH), *picked)

    smem = pl.BlockSpec(memory_space=pltpu.SMEM)
    vmem = pl.BlockSpec(memory_space=pltpu.VMEM)
    hbm = pl.BlockSpec(memory_space=pltpu.HBM)
    row = picked[0].shape[1]
    versions = (lag_rows % 2 + 2 * away) * width

    def products(hops, slots, dtype, name):
        return pl.pallas_call(
            functools.partial(lag_kernel, hops, slots, lag_rows, away, block_count, branched),
            out_shape=[jax.ShapeDtypeStruct((lag_rows, len(slots), width, width), dtype)]
            * len(hops),
            in_specs=[smem, smem, vmem, vmem] + [hbm] * len(blocks),
            out_specs=[vmem] * len(hops),
            scratch_shapes=[
                pltpu.VMEM((len(slots), 2, sub_count, width, row), BF16),
                pltpu.SemaphoreType.DMA((len(slots), 2, sub_count)),
            ],
            compiler_params=pltpu.CompilerParams(vmem_limit_bytes=LAG_VMEM_LIMIT),
            cost_estimate=pl.CostEstimate(
                flops=2 * len(slots) * len(hops) * versions * width * sub_count * row,
                bytes_accessed=4 * len(slots) * sub_count * width * row,
                transcendentals=0,
            ),
            name=name,
        )(pair_sides, pair_owner, turns, offsets, *blocks)

    hops, slots = tuple(range(1, hr_count)), tuple(range(CAP))
    sent = products(hops, slots, BF16, "lags_to_send")
    received = []
    for hop, part in zip(hops, sent):
        to_device = [(hr, (hr + hop) % hr_count) for hr in range(hr_count)]
        received.append(lax.ppermute(part, "hr", to_device))
    (summed,) = products((0,), slots, F32, "lags_to_keep")
    for part in received:
        summed = summed + part.astype(F32)
    return (summed * norming).astype(BF16)


def solution(mesh):
    placed = (P(("grp", "hr"), "sub", None, "sta"), P(), P(), P("sta", None))
    return jax.shard_map(
        on_device,
        mesh=mesh,
        in_specs=placed,
        out_specs=P(("grp", "hr", "sub"), "sta", None, None),
        check_vma=False,
    )
```

```python
import functools
import itertools
import math

import jax
import jax.numpy as jnp
import numpy as np
from jax import lax
from jax.experimental import pallas as pl
from jax.experimental.pallas import tpu as pltpu
from jax.sharding import PartitionSpec as P

BAND = 50
LAGS = 16
CAP = 3
REACH = 4
EPSILON = 1e-05
LANES = 128
F32 = jnp.float32
BF16 = jnp.bfloat16
PICK_VMEM_LIMIT = 59 * 1024 * 1024
LAG_VMEM_LIMIT = 32 * 1024 * 1024

NT = (((1,), (1,)), ((), ()))


def dot_nt(left, right):
    return lax.dot_general(left, right, NT, preferred_element_type=F32)


def iota(shape, dim):
    return lax.broadcasted_iota(jnp.int32, shape, dim)


def send_keys(first, second, needs, sta_count, where):
    keys = []
    for reach in range(1, REACH):
        distance = abs((first + reach) % sta_count - first)
        shared = (needs >> reach) % 2 == 1
        first_sends = (first - second - reach) % sta_count == 0
        late = where(shared, where(first_sends, 2, 1), 0)
        keys.append((late * sta_count + distance) * REACH + reach)
    return keys


def pick_kernel(kept, branched, sta_axis, pair_hbm, owner_hbm, member_hbm, case_hbm, x_ref, *rest):
    outs = rest[:REACH]
    slot_ref = rest[REACH]
    branch_ref = rest[REACH + 1] if branched else None
    pair_ref, owner_ref, member_ref, case_ref, x_buf, hot_buf, band_buf, y_buf, sems = rest[
        REACH + 1 + branched :
    ]
    tiles, freqs = x_buf.shape[0], x_buf.shape[1]
    block_count, width = member_ref.shape
    columns = y_buf.shape[1]
    chunks = columns // (2 * LANES)

    def fetch(tile):
        return pltpu.make_async_copy(
            x_ref.at[0, :, :, pl.ds(tile * LANES, LANES)], x_buf.at[tile], sems.at[tile]
        )

    small = [
        pltpu.make_async_copy(source, target, sems.at[tiles + index])
        for index, (source, target) in enumerate(
            (
                (pair_hbm, pair_ref),
                (owner_hbm, owner_ref),
                (member_hbm, member_ref),
                (case_hbm, case_ref),
            )
        )
    ]
    for copy in small:
        copy.start()
    for tile in range(tiles):
        fetch(tile).start()

    row, col = iota((columns, LANES), 0), iota((columns, LANES), 1)
    low = (col % 16) * (2 * BAND)
    hit = (row >= low) & (row < low + 2 * BAND) & (row < 2 * freqs) & (col < 48)
    band_buf[...] = jnp.where(hit, 1.0, 0.0).astype(BF16)
    row, col = iota((2 * LANES, 2 * LANES), 0), iota((2 * LANES, 2 * LANES), 1)
    split = jnp.where(row == 2 * (col % LANES) + col // LANES, 1.0, 0.0).astype(BF16)
    y_buf[:, 2 * freqs :] = jnp.zeros((kept * width, columns - 2 * freqs), F32)
    for copy in small:
        copy.wait()

    my_sta = lax.axis_index(sta_axis)
    sta_count = lax.axis_size(sta_axis)
    pair_count = owner_ref.shape[0]
    members = jnp.transpose(member_ref[...].astype(F32))
    block_col = iota(members.shape, 1)
    pairs = []
    for pair in range(pair_count):
        blocks = [pair_ref[side, pair] for side in range(2)]
        homes = [lax.div(block, block_count) for block in blocks]
        pairs.append((owner_ref[pair], blocks, homes))
    found, wanted = jnp.int32(0), []
    for reach in range(REACH):
        owner = lax.rem(my_sta - reach + REACH * sta_count, sta_count)
        chosen = jnp.int32(-1)
        for pair_owner, blocks, homes in pairs:
            for block, home in zip(blocks, homes):
                hit = (pair_owner == owner) & (home == my_sta)
                chosen = jnp.where(hit, lax.rem(block, block_count), chosen)
        wanted.append((found, chosen))
        found = found + (chosen >= 0).astype(jnp.int32)
    places, station = [], []
    for place in range(kept):
        reach_here, block_here = jnp.int32(-1), jnp.int32(0)
        for reach, (rank, chosen) in enumerate(wanted):
            hit = (rank == place) & (chosen >= 0)
            reach_here = jnp.where(hit, reach, reach_here)
            block_here = jnp.where(hit, chosen, block_here)
        places.append(reach_here)
        column = jnp.where(block_col == block_here, members, 0.0)
        station.append(jnp.sum(column, axis=1, keepdims=True).astype(jnp.int32))
    station = jnp.concatenate(station, axis=0)
    lane = iota((kept * width, LANES), 1)
    for tile in range(tiles):
        hot = jnp.where(station == lane + tile * LANES, 1.0, 0.0).astype(BF16)
        hot_buf[:, tile * LANES : (tile + 1) * LANES] = hot

    order = [jnp.int32(reach) for reach in range(REACH)]
    if branched:
        first = second = needs = jnp.int32(0)
        for owner, _, homes in pairs:
            count = jnp.int32(0)
            for other, _, _ in pairs:
                count = count + (other == owner).astype(jnp.int32)
            ends = [lax.rem(home - owner + sta_count, sta_count) for home in homes]
            first = jnp.where(count == CAP, owner, first)
            second = jnp.where(count < CAP, owner, second)
            needs = jnp.where(count < CAP, (1 << ends[0]) | (1 << ends[1]), needs)
        branch_ref[0] = case_ref[case_number(first, second, needs, sta_count)]
        keys = send_keys(first, second, needs, sta_count, jnp.where)
        for reach, key in enumerate(keys):
            order[1 + reach] = 1 + sum((other < key).astype(jnp.int32) for other in keys)
    for slot in range(CAP):
        count = jnp.int32(0)
        ends = [jnp.int32(-1)] * 2
        for owner, _, homes in pairs:
            mine = owner == my_sta
            hit = mine & (count == slot)
            count = count + mine.astype(jnp.int32)
            for side, home in enumerate(homes):
                reach_here = lax.rem(home - my_sta + sta_count, sta_count)
                place_here = order[0]
                for reach in range(1, REACH):
                    place_here = jnp.where(reach_here == reach, order[reach], place_here)
                ends[side] = jnp.where(hit, place_here, ends[side])
        for side in range(2):
            slot_ref[2 * slot + side] = ends[side]

    half = -(-tiles // 2)
    total = None
    for first_tile in (0, half):
        span = range(first_tile, min(first_tile + half, tiles))
        for tile in span:
            fetch(tile).wait()
        x = jnp.concatenate(
            [x_buf.at[tile].reshape(2 * freqs, LANES)[...] for tile in span], axis=1
        )
        hot = hot_buf[:, span.start * LANES : span.stop * LANES]
        part = dot_nt(hot, x)
        total = part if total is None else total + part
    y_buf[:, : 2 * freqs] = total

    values = y_buf[...]
    square = values * values
    high = square.astype(BF16)
    low = (square - high.astype(F32)).astype(BF16)
    power = jnp.dot(high, band_buf[...], preferred_element_type=F32)
    power += jnp.dot(low, band_buf[...], preferred_element_type=F32)
    scale = lax.rsqrt(power * (1.0 / (2 * BAND)) + EPSILON)
    high = scale.astype(BF16)
    rest1 = scale - high.astype(F32)
    mid = rest1.astype(BF16)
    low = rest1 - mid.astype(F32)
    third = iota(scale.shape, 1) // 16
    pieces = jnp.where(
        third == 0, high.astype(F32), jnp.where(third == 1, mid.astype(F32), low)
    ).astype(BF16)
    white = (y_buf[...] * dot_nt(pieces, band_buf[...])).astype(BF16)
    parted = []
    for chunk in range(chunks):
        mixed = white[:, chunk * 2 * LANES : (chunk + 1) * 2 * LANES]
        parted.append(jnp.dot(mixed, split, preferred_element_type=F32).astype(BF16))
    white = jnp.concatenate(
        [part[:, :LANES] for part in parted] + [part[:, LANES:] for part in parted], axis=1
    )
    hot_buf[:, :columns] = white
    for place, reach_here in enumerate(places):
        for reach in range(REACH):

            @pl.when(reach_here == reach)
            def _():
                outs[reach][...] = hot_buf[place * width : (place + 1) * width, :columns]


def pick_blocks(kept, cases, spectra, pair_sides, pair_owner, block_members):
    _, freqs, parts, stations = spectra.shape
    block_count, width = block_members.shape
    tiles = stations // LANES
    columns = -(-freqs // LANES) * 2 * LANES
    rows = kept * width
    branched = len(cases) > 0
    case_table = jnp.asarray(np.array(cases or [0], dtype=np.int32))
    vmem = pl.BlockSpec(memory_space=pltpu.VMEM)
    smem = pl.BlockSpec(memory_space=pltpu.SMEM)
    out_shape = [jax.ShapeDtypeStruct((width, columns), BF16)] * REACH
    out_shape += [jax.ShapeDtypeStruct((2 * CAP,), jnp.int32)]
    out_shape += [jax.ShapeDtypeStruct((1,), jnp.int32)] * branched
    return pl.pallas_call(
        functools.partial(pick_kernel, kept, branched, "sta"),
        out_shape=out_shape,
        in_specs=[pl.BlockSpec(memory_space=pltpu.HBM)] * 5,
        out_specs=[vmem] * REACH + [smem] * (1 + branched),
        scratch_shapes=[
            pltpu.SMEM(pair_sides.shape, jnp.int32),
            pltpu.SMEM(pair_owner.shape, jnp.int32),
            pltpu.VMEM(block_members.shape, jnp.int32),
            pltpu.SMEM(case_table.shape, jnp.int32),
            pltpu.VMEM((tiles, freqs, parts, LANES), BF16),
            pltpu.VMEM((rows, max(columns, stations)), BF16),
            pltpu.VMEM((columns, LANES), BF16),
            pltpu.VMEM((rows, columns), F32),
            pltpu.SemaphoreType.DMA((tiles + 4,)),
        ],
        compiler_params=pltpu.CompilerParams(vmem_limit_bytes=PICK_VMEM_LIMIT),
        cost_estimate=pl.CostEstimate(
            flops=2 * rows * stations * freqs * parts,
            bytes_accessed=2 * spectra.size + 4 * rows * columns,
            transcendentals=0,
        ),
        name="pick_and_whiten",
    )(pair_sides, pair_owner, block_members, case_table, spectra)


def case_number(first, second, needs, sta_count):
    return (first * sta_count + second) * (1 << (REACH - 1)) + needs // 2


def routes(sta_count):
    branches = []
    cases = [0] * case_number(sta_count, 0, 0, sta_count)
    for first, second in itertools.permutations(range(sta_count), 2):
        for named in itertools.combinations(range(REACH), 2):
            needs = sum(1 << reach for reach in named)
            cases[case_number(first, second, needs, sta_count)] = len(branches)
            branches.append((first, second, needs))
    return branches, cases


def phase_tables(sub_count, sub_freqs, groups, lag_rows):
    chunks = -(-sub_freqs // LANES)
    total = sub_count * sub_freqs
    freq = np.arange(total, dtype=np.int64).reshape(sub_count, 1, sub_freqs)
    middle = [2 * (group * lag_rows - LAGS // 2) + lag_rows - 1 for group in range(groups)]
    away = [step for step in range(1, lag_rows) if step % 2 != lag_rows % 2]

    def table(twice, forms, tile, dtype):
        twice = np.array(twice or [0], dtype=np.int64).reshape(1, -1, 1)
        angle = np.mod(freq * twice, 2 * total) * (math.pi / total)
        rows = np.stack([form(angle) for form in forms], axis=2)
        rows = rows.reshape(sub_count, -1, sub_freqs)
        pad = ((0, 0), (0, -rows.shape[1] % tile), (0, chunks * LANES - sub_freqs))
        return np.pad(rows, pad).astype(np.float32).astype(dtype)

    turns = table(middle, (np.cos, np.sin), 8, np.float32)
    offsets = table(away, (np.cos, np.sin, lambda angle: -np.sin(angle)), 16, BF16)
    return turns, offsets, len(away)


def lag_kernel(hops, slots, lag_rows, away, slot_ref, turn_ref, offset_ref, *refs):
    sub_count = lax.axis_size("sub")
    hr_count = lax.axis_size("hr")
    blocks = refs[: REACH * sub_count]
    outs = refs[REACH * sub_count : REACH * sub_count + len(hops)]
    buf, sems = refs[REACH * sub_count + len(hops) :]
    width = buf.shape[3]
    span = buf.shape[4] // 2
    middle_lag = lag_rows % 2
    my_sub = lax.axis_index("sub")
    my_hr = lax.axis_index("hr")
    ends = [(slot_ref[2 * slot], slot_ref[2 * slot + 1]) for slot in slots]

    def fetches(index, act):
        for side in range(2):
            for place in range(REACH):

                @pl.when(ends[index][side] == place)
                def _():
                    for step in range(sub_count):
                        act(
                            pltpu.make_async_copy(
                                blocks[place * sub_count + step],
                                buf.at[index, side, step],
                                sems.at[index, side, step],
                            )
                        )

    for index in range(len(slots)):
        fetches(index, lambda copy: copy.start())

    for index in range(len(slots)):

        @pl.when(ends[index][0] < 0)
        def _():
            for out in outs:
                out[:, index] = jnp.zeros((lag_rows, width, width), out.dtype)

        fetches(index, lambda copy: copy.wait())

        @pl.when(ends[index][0] >= 0)
        def _():
            total = None
            for step in range(sub_count):
                sub = lax.rem(my_sub + step, sub_count)
                real = buf[index, 0, step, :, :span]
                imag = buf[index, 0, step, :, span:]
                scaled_real, scaled_imag = [real] * middle_lag, [imag] * middle_lag
                for near in range(away):
                    cosine, sine, minus = (
                        offset_ref[sub, 3 * near + form : 3 * near + form + 1, :]
                        for form in range(3)
                    )
                    scaled_real += [real * cosine, imag * minus]
                    scaled_imag += [imag * cosine, real * sine]
                real = buf[index, 1, step, :, :span].astype(F32)
                imag = buf[index, 1, step, :, span:].astype(F32)
                turned_real, turned_imag = [], []
                for hop in hops:
                    group = lax.rem(my_hr + hop, hr_count) * sub_count + my_sub
                    cosine = turn_ref[sub, pl.ds(2 * group, 1), :]
                    sine = turn_ref[sub, pl.ds(2 * group + 1, 1), :]
                    turned_real.append((real * cosine + imag * sine).astype(BF16))
                    turned_imag.append((imag * cosine - real * sine).astype(BF16))
                for scaled, turned in ((scaled_real, turned_real), (scaled_imag, turned_imag)):
                    part = dot_nt(jnp.concatenate(scaled, axis=0), jnp.concatenate(turned, axis=0))
                    total = part if total is None else total + part
            for place, out in enumerate(outs):
                columns = slice(place * width, (place + 1) * width)
                if middle_lag:
                    out[lag_rows // 2, index] = total[:width, columns].astype(out.dtype)
                for near in range(away):
                    start = (middle_lag + 2 * near) * width
                    even = total[start : start + width, columns]
                    odd = total[start + width : start + 2 * width, columns]
                    below = (lag_rows - 1) // 2 - near - middle_lag
                    above = lag_rows - 1 - below
                    out[above, index] = (even + odd).astype(out.dtype)
                    out[below, index] = (even - odd).astype(out.dtype)


def on_device(spectra, pair_blocks, pair_owner, block_members):
    hour_count, sub_freqs, _, _ = spectra.shape
    block_count, width = block_members.shape
    sta_count, hr_count, sub_count = (lax.axis_size(axis) for axis in ("sta", "hr", "sub"))
    groups = hr_count * sub_count
    lag_rows = LAGS // groups
    norming = 1.0 / math.sqrt(hour_count * hr_count * sub_count * sub_freqs)
    pair_sides = pair_blocks.T
    turns, offsets, away = phase_tables(sub_count, sub_freqs, groups, lag_rows)

    owners_at_most = pair_owner.shape[0] - CAP + 1
    branched = owners_at_most == 2 and sta_count == REACH
    kept = min(REACH, owners_at_most)
    branches, cases = routes(sta_count) if branched else ([], [])
    picked = pick_blocks(kept, cases, spectra, pair_sides, pair_owner, block_members)
    slot_ends = picked[REACH]

    def exchange(owners_of, order, *picked):
        arrived = [picked[0]]
        for reach in order:
            to_owner = [((owner + reach) % sta_count, owner) for owner in owners_of[reach - 1]]
            arrived.append(lax.ppermute(picked[reach], "sta", to_owner))
        blocks = []
        for block in arrived:
            blocks.append(block)
            for step in range(1, sub_count):
                swap = [((sub + step) % sub_count, sub) for sub in range(sub_count)]
                blocks.append(lax.ppermute(block, "sub", swap))
        return blocks

    if branched:
        steps = []
        for first, second, needs in branches:
            owners_of = [
                (first, second) if needs >> reach & 1 else (first,) for reach in range(1, REACH)
            ]
            keys = send_keys(first, second, needs, sta_count, lambda hit, yes, no: yes if hit else no)
            order = sorted(range(1, REACH), key=lambda reach: keys[reach - 1])
            steps.append(functools.partial(exchange, owners_of, order))
        blocks = lax.switch(picked[REACH + 1][0], steps, *picked[:REACH])
    else:
        blocks = exchange([range(sta_count)] * (REACH - 1), range(1, REACH), *picked[:REACH])

    smem = pl.BlockSpec(memory_space=pltpu.SMEM)
    vmem = pl.BlockSpec(memory_space=pltpu.VMEM)
    hbm = pl.BlockSpec(memory_space=pltpu.HBM)
    row = picked[0].shape[1]
    versions = (lag_rows % 2 + 2 * away) * width

    def products(hops, slots, dtype, name):
        return pl.pallas_call(
            functools.partial(lag_kernel, hops, slots, lag_rows, away),
            out_shape=[jax.ShapeDtypeStruct((lag_rows, len(slots), width, width), dtype)]
            * len(hops),
            in_specs=[smem, vmem, vmem] + [hbm] * len(blocks),
            out_specs=[vmem] * len(hops),
            scratch_shapes=[
                pltpu.VMEM((len(slots), 2, sub_count, width, row), BF16),
                pltpu.SemaphoreType.DMA((len(slots), 2, sub_count)),
            ],
            compiler_params=pltpu.CompilerParams(vmem_limit_bytes=LAG_VMEM_LIMIT),
            cost_estimate=pl.CostEstimate(
                flops=2 * len(slots) * len(hops) * versions * width * sub_count * row,
                bytes_accessed=4 * len(slots) * sub_count * width * row,
                transcendentals=0,
            ),
            name=name,
        )(slot_ends, turns, offsets, *blocks)

    hops, slots = tuple(range(1, hr_count)), tuple(range(CAP))
    sent = products(hops, slots, BF16, "lags_to_send")
    received = []
    for hop, part in zip(hops, sent):
        to_device = [(hr, (hr + hop) % hr_count) for hr in range(hr_count)]
        received.append(lax.ppermute(part, "hr", to_device))
    (summed,) = products((0,), slots, F32, "lags_to_keep")
    for part in received:
        summed = summed + part.astype(F32)
    return (summed * norming).astype(BF16)


def solution(mesh):
    placed = (P(("grp", "hr"), "sub", None, "sta"), P(), P(), P("sta", None))
    return jax.shard_map(
        on_device,
        mesh=mesh,
        in_specs=placed,
        out_specs=P(("grp", "hr", "sub"), "sta", None, None),
        check_vma=False,
    )
```

```python
import functools
import itertools
import math

import jax
import jax.numpy as jnp
import numpy as np
from jax import lax
from jax.experimental import pallas as pl
from jax.experimental.pallas import tpu as pltpu
from jax.sharding import PartitionSpec as P

BAND = 50
LAGS = 16
CAP = 3
REACH = 4
EPSILON = 1e-05
LANES = 128
F32 = jnp.float32
BF16 = jnp.bfloat16
PICK_VMEM_LIMIT = 59 * 1024 * 1024
LAG_VMEM_LIMIT = 32 * 1024 * 1024

NT = (((1,), (1,)), ((), ()))


def dot_nt(left, right):
    return lax.dot_general(left, right, NT, preferred_element_type=F32)


def iota(shape, dim):
    return lax.broadcasted_iota(jnp.int32, shape, dim)


def send_keys(first, second, needs, sta_count, where):
    keys = []
    for reach in range(1, REACH):
        distance = abs((first + reach) % sta_count - first)
        shared = (needs >> reach) % 2 == 1
        first_sends = (first - second - reach) % sta_count == 0
        late = where(shared, where(first_sends, 2, 1), 0)
        keys.append((late * sta_count + distance) * REACH + reach)
    return keys


def read_pairs(pair_ref, owner_ref, block_count):
    pairs = []
    for pair in range(owner_ref.shape[0]):
        blocks = [pair_ref[side, pair] for side in range(2)]
        pairs.append((owner_ref[pair], blocks, [lax.div(block, block_count) for block in blocks]))
    return pairs


def case_of(pairs, case_ref, sta_count):
    first = second = needs = jnp.int32(0)
    for owner, _, homes in pairs:
        count = jnp.int32(0)
        for other, _, _ in pairs:
            count = count + (other == owner).astype(jnp.int32)
        ends = [lax.rem(home - owner + sta_count, sta_count) for home in homes]
        first = jnp.where(count == CAP, owner, first)
        second = jnp.where(count < CAP, owner, second)
        needs = jnp.where(count < CAP, (1 << ends[0]) | (1 << ends[1]), needs)
    return first, second, case_ref[case_number(first, second, needs, sta_count)]


def pick_kernel(kept, branched, sta_axis, pair_hbm, owner_hbm, member_hbm, case_hbm, x_ref, *rest):
    outs = rest[:REACH]
    branch_ref = rest[REACH] if branched else None
    pair_ref, owner_ref, member_ref, case_ref, x_buf, hot_buf, band_buf, y_buf, sems = rest[
        REACH + branched :
    ]
    tiles, freqs = x_buf.shape[0], x_buf.shape[1]
    block_count, width = member_ref.shape
    columns = y_buf.shape[1]
    chunks = columns // (2 * LANES)

    def fetch(tile):
        return pltpu.make_async_copy(
            x_ref.at[0, :, :, pl.ds(tile * LANES, LANES)], x_buf.at[tile], sems.at[tile]
        )

    small = [
        pltpu.make_async_copy(source, target, sems.at[tiles + index])
        for index, (source, target) in enumerate(
            (
                (pair_hbm, pair_ref),
                (owner_hbm, owner_ref),
                (member_hbm, member_ref),
                (case_hbm, case_ref),
            )
        )
    ]
    for copy in small:
        copy.start()
    for tile in range(tiles):
        fetch(tile).start()

    row, col = iota((columns, LANES), 0), iota((columns, LANES), 1)
    low = (col % 16) * (2 * BAND)
    hit = (row >= low) & (row < low + 2 * BAND) & (row < 2 * freqs) & (col < 48)
    band_buf[...] = jnp.where(hit, 1.0, 0.0).astype(BF16)
    row, col = iota((2 * LANES, 2 * LANES), 0), iota((2 * LANES, 2 * LANES), 1)
    split = jnp.where(row == 2 * (col % LANES) + col // LANES, 1.0, 0.0).astype(BF16)
    y_buf[:, 2 * freqs :] = jnp.zeros((kept * width, columns - 2 * freqs), F32)
    for copy in small:
        copy.wait()

    my_sta = lax.axis_index(sta_axis)
    sta_count = lax.axis_size(sta_axis)
    members = jnp.transpose(member_ref[...].astype(F32))
    block_col = iota(members.shape, 1)
    pairs = read_pairs(pair_ref, owner_ref, block_count)
    found, wanted = jnp.int32(0), []
    for reach in range(REACH):
        owner = lax.rem(my_sta - reach + REACH * sta_count, sta_count)
        chosen = jnp.int32(-1)
        for pair_owner, blocks, homes in pairs:
            for block, home in zip(blocks, homes):
                hit = (pair_owner == owner) & (home == my_sta)
                chosen = jnp.where(hit, lax.rem(block, block_count), chosen)
        wanted.append((found, chosen))
        found = found + (chosen >= 0).astype(jnp.int32)
    places, station = [], []
    for place in range(kept):
        reach_here, block_here = jnp.int32(-1), jnp.int32(0)
        for reach, (rank, chosen) in enumerate(wanted):
            hit = (rank == place) & (chosen >= 0)
            reach_here = jnp.where(hit, reach, reach_here)
            block_here = jnp.where(hit, chosen, block_here)
        places.append(reach_here)
        column = jnp.where(block_col == block_here, members, 0.0)
        station.append(jnp.sum(column, axis=1, keepdims=True).astype(jnp.int32))
    station = jnp.concatenate(station, axis=0)
    lane = iota((kept * width, LANES), 1)
    for tile in range(tiles):
        hot = jnp.where(station == lane + tile * LANES, 1.0, 0.0).astype(BF16)
        hot_buf[:, tile * LANES : (tile + 1) * LANES] = hot

    if branched:
        branch_ref[0] = case_of(pairs, case_ref, sta_count)[2] >> REACH

    half = -(-tiles // 2)
    total = None
    for first_tile in (0, half):
        span = range(first_tile, min(first_tile + half, tiles))
        for tile in span:
            fetch(tile).wait()
        x = jnp.concatenate(
            [x_buf.at[tile].reshape(2 * freqs, LANES)[...] for tile in span], axis=1
        )
        hot = hot_buf[:, span.start * LANES : span.stop * LANES]
        part = dot_nt(hot, x)
        total = part if total is None else total + part
    y_buf[:, : 2 * freqs] = total

    values = y_buf[...]
    square = values * values
    high = square.astype(BF16)
    low = (square - high.astype(F32)).astype(BF16)
    power = jnp.dot(high, band_buf[...], preferred_element_type=F32)
    power += jnp.dot(low, band_buf[...], preferred_element_type=F32)
    scale = lax.rsqrt(power * (1.0 / (2 * BAND)) + EPSILON)
    high = scale.astype(BF16)
    rest1 = scale - high.astype(F32)
    mid = rest1.astype(BF16)
    low = rest1 - mid.astype(F32)
    third = iota(scale.shape, 1) // 16
    pieces = jnp.where(
        third == 0, high.astype(F32), jnp.where(third == 1, mid.astype(F32), low)
    ).astype(BF16)
    white = (y_buf[...] * dot_nt(pieces, band_buf[...])).astype(BF16)
    parted = []
    for chunk in range(chunks):
        mixed = white[:, chunk * 2 * LANES : (chunk + 1) * 2 * LANES]
        parted.append(jnp.dot(mixed, split, preferred_element_type=F32).astype(BF16))
    white = jnp.concatenate(
        [part[:, :LANES] for part in parted] + [part[:, LANES:] for part in parted], axis=1
    )
    hot_buf[:, :columns] = white
    for place, reach_here in enumerate(places):
        for reach in range(REACH):

            @pl.when(reach_here == reach)
            def _():
                outs[reach][...] = hot_buf[place * width : (place + 1) * width, :columns]


def pick_blocks(kept, branched, spectra, pair_sides, pair_owner, block_members, case_table):
    _, freqs, parts, stations = spectra.shape
    block_count, width = block_members.shape
    tiles = stations // LANES
    columns = -(-freqs // LANES) * 2 * LANES
    rows = kept * width
    vmem = pl.BlockSpec(memory_space=pltpu.VMEM)
    smem = pl.BlockSpec(memory_space=pltpu.SMEM)
    out_shape = [jax.ShapeDtypeStruct((width, columns), BF16)] * REACH
    out_shape += [jax.ShapeDtypeStruct((1,), jnp.int32)] * branched
    return pl.pallas_call(
        functools.partial(pick_kernel, kept, branched, "sta"),
        out_shape=out_shape,
        in_specs=[pl.BlockSpec(memory_space=pltpu.HBM)] * 5,
        out_specs=[vmem] * REACH + [smem] * branched,
        scratch_shapes=[
            pltpu.SMEM(pair_sides.shape, jnp.int32),
            pltpu.SMEM(pair_owner.shape, jnp.int32),
            pltpu.VMEM(block_members.shape, jnp.int32),
            pltpu.SMEM(case_table.shape, jnp.int32),
            pltpu.VMEM((tiles, freqs, parts, LANES), BF16),
            pltpu.VMEM((rows, max(columns, stations)), BF16),
            pltpu.VMEM((columns, LANES), BF16),
            pltpu.VMEM((rows, columns), F32),
            pltpu.SemaphoreType.DMA((tiles + 4,)),
        ],
        compiler_params=pltpu.CompilerParams(vmem_limit_bytes=PICK_VMEM_LIMIT),
        cost_estimate=pl.CostEstimate(
            flops=2 * rows * stations * freqs * parts,
            bytes_accessed=2 * spectra.size + 4 * rows * columns,
            transcendentals=0,
        ),
        name="pick_and_whiten",
    )(pair_sides, pair_owner, block_members, case_table, spectra)


def case_number(first, second, needs, sta_count):
    return (first * sta_count + second) * (1 << (REACH - 1)) + needs // 2


def routes(sta_count):
    def load(first, second, sent):
        links = {}
        flows = [(first, reach) for reach in range(1, REACH)]
        flows += [(second, reach) for reach in range(1, REACH) if sent >> reach & 1]
        for owner, reach in flows:
            source = (owner + reach) % sta_count
            step = 1 if owner > source else -1
            for place in range(source, owner, step):
                links[place, step] = links.get((place, step), 0) + 1
        return max(links.values())

    every = (1 << REACH) - 2
    sets = [every] + [every - (1 << reach) for reach in range(REACH - 1, 0, -1)]
    branches = []
    cases = [0] * case_number(sta_count, 0, 0, sta_count)
    for first, second in itertools.permutations(range(sta_count), 2):
        for named in itertools.combinations(range(REACH), 2):
            needs = sum(1 << reach for reach in named) & every
            fits = [sent for sent in sets if needs & ~sent == 0]
            sent = min(fits, key=lambda sent: load(first, second, sent))
            branch = (first, second, sent)
            if branch not in branches:
                branches.append(branch)
            number = branches.index(branch)
            cases[case_number(first, second, needs, sta_count)] = (number << REACH) + sent
    return branches, cases


def phase_tables(sub_count, sub_freqs, groups, lag_rows):
    chunks = -(-sub_freqs // LANES)
    total = sub_count * sub_freqs
    freq = np.arange(total, dtype=np.int64).reshape(sub_count, 1, sub_freqs)
    middle = [2 * (group * lag_rows - LAGS // 2) + lag_rows - 1 for group in range(groups)]
    away = [step for step in range(1, lag_rows) if step % 2 != lag_rows % 2]

    def table(twice, forms, tile, dtype):
        twice = np.array(twice or [0], dtype=np.int64).reshape(1, -1, 1)
        angle = np.mod(freq * twice, 2 * total) * (math.pi / total)
        rows = np.stack([form(angle) for form in forms], axis=2)
        rows = rows.reshape(sub_count, -1, sub_freqs)
        pad = ((0, 0), (0, -rows.shape[1] % tile), (0, chunks * LANES - sub_freqs))
        return np.pad(rows, pad).astype(np.float32).astype(dtype)

    turns = table(middle, (np.cos, np.sin), 8, np.float32)
    offsets = table(away, (np.cos, np.sin, lambda angle: -np.sin(angle)), 16, BF16)
    return turns, offsets, len(away)


def lag_kernel(hops, slots, lag_rows, away, block_count, branched, pair_ref, owner_ref, case_ref, turn_ref, offset_ref, *refs):
    sub_count = lax.axis_size("sub")
    hr_count = lax.axis_size("hr")
    blocks = refs[: REACH * sub_count]
    outs = refs[REACH * sub_count : REACH * sub_count + len(hops)]
    buf, sems = refs[REACH * sub_count + len(hops) :]
    width = buf.shape[3]
    span = buf.shape[4] // 2
    middle_lag = lag_rows % 2
    my_sub = lax.axis_index("sub")
    my_hr = lax.axis_index("hr")
    my_sta = lax.axis_index("sta")
    sta_count = lax.axis_size("sta")

    pairs = read_pairs(pair_ref, owner_ref, block_count)
    order = [jnp.int32(reach) for reach in range(REACH)]
    if branched:
        first, second, case = case_of(pairs, case_ref, sta_count)
        keys = send_keys(first, second, case, sta_count, jnp.where)
        for reach, key in enumerate(keys):
            order[1 + reach] = 1 + sum((other < key).astype(jnp.int32) for other in keys)
    owned = []
    for owner, _, homes in pairs:
        places = []
        for home in homes:
            reach_here = lax.rem(home - my_sta + sta_count, sta_count)
            place_here = order[0]
            for reach in range(1, REACH):
                place_here = jnp.where(reach_here == reach, order[reach], place_here)
            places.append(place_here)
        owned.append((owner == my_sta, places))
    ends = []
    for slot in slots:
        count = jnp.int32(0)
        slot_ends = [jnp.int32(-1)] * 2
        for mine, places in owned:
            hit = mine & (count == slot)
            count = count + mine.astype(jnp.int32)
            slot_ends = [jnp.where(hit, new, old) for new, old in zip(places, slot_ends)]
        ends.append(slot_ends)

    def fetches(index, act):
        for side in range(2):
            for place in range(REACH):

                @pl.when(ends[index][side] == place)
                def _():
                    for step in range(sub_count):
                        act(
                            pltpu.make_async_copy(
                                blocks[place * sub_count + step],
                                buf.at[index, side, step],
                                sems.at[index, side, step],
                            )
                        )

    for index in range(len(slots)):
        fetches(index, lambda copy: copy.start())

    for index in range(len(slots)):

        @pl.when(ends[index][0] < 0)
        def _():
            for out in outs:
                out[:, index] = jnp.zeros((lag_rows, width, width), out.dtype)

        fetches(index, lambda copy: copy.wait())

        @pl.when(ends[index][0] >= 0)
        def _():
            total = None
            for step in range(sub_count):
                sub = lax.rem(my_sub + step, sub_count)
                real = buf[index, 0, step, :, :span]
                imag = buf[index, 0, step, :, span:]
                scaled_real, scaled_imag = [real] * middle_lag, [imag] * middle_lag
                for near in range(away):
                    cosine, sine, minus = (
                        offset_ref[sub, 3 * near + form : 3 * near + form + 1, :]
                        for form in range(3)
                    )
                    scaled_real += [real * cosine, imag * minus]
                    scaled_imag += [imag * cosine, real * sine]
                real = buf[index, 1, step, :, :span].astype(F32)
                imag = buf[index, 1, step, :, span:].astype(F32)
                turned_real, turned_imag = [], []
                for hop in hops:
                    group = lax.rem(my_hr + hop, hr_count) * sub_count + my_sub
                    cosine = turn_ref[sub, pl.ds(2 * group, 1), :]
                    sine = turn_ref[sub, pl.ds(2 * group + 1, 1), :]
                    turned_real.append((real * cosine + imag * sine).astype(BF16))
                    turned_imag.append((imag * cosine - real * sine).astype(BF16))
                for scaled, turned in ((scaled_real, turned_real), (scaled_imag, turned_imag)):
                    part = dot_nt(jnp.concatenate(scaled, axis=0), jnp.concatenate(turned, axis=0))
                    total = part if total is None else total + part
            for place, out in enumerate(outs):
                columns = slice(place * width, (place + 1) * width)
                if middle_lag:
                    out[lag_rows // 2, index] = total[:width, columns].astype(out.dtype)
                for near in range(away):
                    start = (middle_lag + 2 * near) * width
                    even = total[start : start + width, columns]
                    odd = total[start + width : start + 2 * width, columns]
                    below = (lag_rows - 1) // 2 - near - middle_lag
                    above = lag_rows - 1 - below
                    out[above, index] = (even + odd).astype(out.dtype)
                    out[below, index] = (even - odd).astype(out.dtype)


def on_device(spectra, pair_blocks, pair_owner, block_members):
    hour_count, sub_freqs, _, _ = spectra.shape
    block_count, width = block_members.shape
    sta_count, hr_count, sub_count = (lax.axis_size(axis) for axis in ("sta", "hr", "sub"))
    groups = hr_count * sub_count
    lag_rows = LAGS // groups
    norming = 1.0 / math.sqrt(hour_count * hr_count * sub_count * sub_freqs)
    pair_sides = pair_blocks.T
    turns, offsets, away = phase_tables(sub_count, sub_freqs, groups, lag_rows)

    owners_at_most = pair_owner.shape[0] - CAP + 1
    branched = owners_at_most == 2 and sta_count == REACH
    kept = min(REACH, owners_at_most)
    branches, cases = routes(sta_count) if branched else ([], [])
    case_table = jnp.asarray(np.array(cases or [0], dtype=np.int32))
    picked = pick_blocks(
        kept, branched, spectra, pair_sides, pair_owner, block_members, case_table
    )

    def exchange(owners_of, order, *picked):
        arrived = [picked[0]]
        for reach in order:
            to_owner = [((owner + reach) % sta_count, owner) for owner in owners_of[reach - 1]]
            arrived.append(lax.ppermute(picked[reach], "sta", to_owner))
        blocks = []
        for block in arrived:
            blocks.append(block)
            for step in range(1, sub_count):
                swap = [((sub + step) % sub_count, sub) for sub in range(sub_count)]
                blocks.append(lax.ppermute(block, "sub", swap))
        return blocks

    if branched:
        steps = []
        for first, second, sent in branches:
            owners_of = [
                (first, second) if sent >> reach & 1 else (first,) for reach in range(1, REACH)
            ]
            keys = send_keys(first, second, sent, sta_count, lambda hit, yes, no: yes if hit else no)
            order = sorted(range(1, REACH), key=lambda reach: keys[reach - 1])
            steps.append(functools.partial(exchange, owners_of, order))
        blocks = lax.switch(picked[REACH][0], steps, *picked[:REACH])
    else:
        blocks = exchange([range(sta_count)] * (REACH - 1), range(1, REACH), *picked[:REACH])

    smem = pl.BlockSpec(memory_space=pltpu.SMEM)
    vmem = pl.BlockSpec(memory_space=pltpu.VMEM)
    hbm = pl.BlockSpec(memory_space=pltpu.HBM)
    row = picked[0].shape[1]
    versions = (lag_rows % 2 + 2 * away) * width

    def products(hops, slots, dtype, name):
        return pl.pallas_call(
            functools.partial(
                lag_kernel, hops, slots, lag_rows, away, block_count, branched
            ),
            out_shape=[jax.ShapeDtypeStruct((lag_rows, len(slots), width, width), dtype)]
            * len(hops),
            in_specs=[smem, smem, smem, vmem, vmem] + [hbm] * len(blocks),
            out_specs=[vmem] * len(hops),
            scratch_shapes=[
                pltpu.VMEM((len(slots), 2, sub_count, width, row), BF16),
                pltpu.SemaphoreType.DMA((len(slots), 2, sub_count)),
            ],
            compiler_params=pltpu.CompilerParams(vmem_limit_bytes=LAG_VMEM_LIMIT),
            cost_estimate=pl.CostEstimate(
                flops=2 * len(slots) * len(hops) * versions * width * sub_count * row,
                bytes_accessed=4 * len(slots) * sub_count * width * row,
                transcendentals=0,
            ),
            name=name,
        )(pair_sides, pair_owner, case_table, turns, offsets, *blocks)

    hops, slots = tuple(range(1, hr_count)), tuple(range(CAP))
    sent = products(hops, slots, BF16, "lags_to_send")
    received = []
    for hop, part in zip(hops, sent):
        to_device = [(hr, (hr + hop) % hr_count) for hr in range(hr_count)]
        received.append(lax.ppermute(part, "hr", to_device))
    (summed,) = products((0,), slots, F32, "lags_to_keep")
    for part in received:
        summed = summed + part.astype(F32)
    return (summed * norming).astype(BF16)


def solution(mesh):
    placed = (P(("grp", "hr"), "sub", None, "sta"), P(), P(), P("sta", None))
    return jax.shard_map(
        on_device,
        mesh=mesh,
        in_specs=placed,
        out_specs=P(("grp", "hr", "sub"), "sta", None, None),
        check_vma=False,
    )
```

```python
import functools
import itertools
import math

import jax
import jax.numpy as jnp
import numpy as np
from jax import lax
from jax.experimental import pallas as pl
from jax.experimental.pallas import tpu as pltpu
from jax.sharding import PartitionSpec as P

BAND = 50
LAGS = 16
CAP = 3
REACH = 4
COPIES = 2
EPSILON = 1e-05
LANES = 128
F32 = jnp.float32
BF16 = jnp.bfloat16
PICK_VMEM_LIMIT = 59 * 1024 * 1024
LAG_VMEM_LIMIT = 32 * 1024 * 1024

NT = (((1,), (1,)), ((), ()))


def dot_nt(left, right):
    return lax.dot_general(left, right, NT, preferred_element_type=F32)


def iota(shape, dim):
    return lax.broadcasted_iota(jnp.int32, shape, dim)


def send_keys(first, second, needs, sta_count, where):
    keys = []
    for reach in range(1, REACH):
        distance = abs((first + reach) % sta_count - first)
        shared = (needs >> reach) % 2 == 1
        first_sends = (first - second - reach) % sta_count == 0
        late = where(shared, where(first_sends, 2, 1), 0)
        keys.append((late * sta_count + distance) * REACH + reach)
    return keys


def read_pairs(pair_ref, owner_ref, block_count):
    pairs = []
    for pair in range(owner_ref.shape[0]):
        blocks = [pair_ref[side, pair] for side in range(2)]
        pairs.append((owner_ref[pair], blocks, [lax.div(block, block_count) for block in blocks]))
    return pairs


def case_of(pairs, case_ref, sta_count):
    first = second = needs = jnp.int32(0)
    for owner, _, homes in pairs:
        count = jnp.int32(0)
        for other, _, _ in pairs:
            count = count + (other == owner).astype(jnp.int32)
        ends = [lax.rem(home - owner + sta_count, sta_count) for home in homes]
        first = jnp.where(count == CAP, owner, first)
        second = jnp.where(count < CAP, owner, second)
        needs = jnp.where(count < CAP, (1 << ends[0]) | (1 << ends[1]), needs)
    return first, second, case_ref[case_number(first, second, needs, sta_count)]


def pick_kernel(kept, branched, sta_axis, pair_hbm, owner_hbm, member_hbm, case_hbm, x_ref, *rest):
    outs = rest[:REACH]
    branch_ref = rest[REACH] if branched else None
    pair_ref, owner_ref, member_ref, case_ref, x_buf, hot_buf, band_buf, y_buf, sems = rest[
        REACH + branched :
    ]
    freqs, tiles = x_buf.shape[0], x_buf.shape[2] // LANES
    step = freqs // COPIES
    block_count, width = member_ref.shape
    columns = y_buf.shape[1]
    chunks = columns // (2 * LANES)

    def fetch(part):
        rows = pl.ds(part * step, step)
        return pltpu.make_async_copy(x_ref.at[0, rows], x_buf.at[rows], sems.at[part])

    small = [
        pltpu.make_async_copy(source, target, sems.at[COPIES + index])
        for index, (source, target) in enumerate(
            (
                (pair_hbm, pair_ref),
                (owner_hbm, owner_ref),
                (member_hbm, member_ref),
                (case_hbm, case_ref),
            )
        )
    ]
    for copy in small:
        copy.start()
    for part in range(COPIES):
        fetch(part).start()

    row, col = iota((columns, LANES), 0), iota((columns, LANES), 1)
    low = (col % 16) * (2 * BAND)
    hit = (row >= low) & (row < low + 2 * BAND) & (row < 2 * freqs) & (col < 48)
    band_buf[...] = jnp.where(hit, 1.0, 0.0).astype(BF16)
    row, col = iota((2 * LANES, 2 * LANES), 0), iota((2 * LANES, 2 * LANES), 1)
    split = jnp.where(row == 2 * (col % LANES) + col // LANES, 1.0, 0.0).astype(BF16)
    y_buf[:, 2 * freqs :] = jnp.zeros((kept * width, columns - 2 * freqs), F32)
    for copy in small:
        copy.wait()

    my_sta = lax.axis_index(sta_axis)
    sta_count = lax.axis_size(sta_axis)
    members = jnp.transpose(member_ref[...].astype(F32))
    block_col = iota(members.shape, 1)
    pairs = read_pairs(pair_ref, owner_ref, block_count)
    found, wanted = jnp.int32(0), []
    for reach in range(REACH):
        owner = lax.rem(my_sta - reach + REACH * sta_count, sta_count)
        chosen = jnp.int32(-1)
        for pair_owner, blocks, homes in pairs:
            for block, home in zip(blocks, homes):
                hit = (pair_owner == owner) & (home == my_sta)
                chosen = jnp.where(hit, lax.rem(block, block_count), chosen)
        wanted.append((found, chosen))
        found = found + (chosen >= 0).astype(jnp.int32)
    places, station = [], []
    for place in range(kept):
        reach_here, block_here = jnp.int32(-1), jnp.int32(0)
        for reach, (rank, chosen) in enumerate(wanted):
            hit = (rank == place) & (chosen >= 0)
            reach_here = jnp.where(hit, reach, reach_here)
            block_here = jnp.where(hit, chosen, block_here)
        places.append(reach_here)
        column = jnp.where(block_col == block_here, members, 0.0)
        station.append(jnp.sum(column, axis=1, keepdims=True).astype(jnp.int32))
    station = jnp.concatenate(station, axis=0)
    lane = iota((kept * width, LANES), 1)
    for tile in range(tiles):
        hot = jnp.where(station == lane + tile * LANES, 1.0, 0.0).astype(BF16)
        hot_buf[:, tile * LANES : (tile + 1) * LANES] = hot

    if branched:
        branch_ref[0] = case_of(pairs, case_ref, sta_count)[2] >> REACH

    for part in range(COPIES):
        fetch(part).wait()
    x = jnp.concatenate(
        [
            x_buf[:, :, tile * LANES : (tile + 1) * LANES].reshape(2 * freqs, LANES)
            for tile in range(tiles)
        ],
        axis=1,
    )
    y_buf[:, : 2 * freqs] = dot_nt(hot_buf[:, : tiles * LANES], x)

    values = y_buf[...]
    square = values * values
    high = square.astype(BF16)
    low = (square - high.astype(F32)).astype(BF16)
    power = jnp.dot(high, band_buf[...], preferred_element_type=F32)
    power += jnp.dot(low, band_buf[...], preferred_element_type=F32)
    scale = lax.rsqrt(power * (1.0 / (2 * BAND)) + EPSILON)
    high = scale.astype(BF16)
    rest1 = scale - high.astype(F32)
    mid = rest1.astype(BF16)
    low = rest1 - mid.astype(F32)
    third = iota(scale.shape, 1) // 16
    pieces = jnp.where(
        third == 0, high.astype(F32), jnp.where(third == 1, mid.astype(F32), low)
    ).astype(BF16)
    white = (y_buf[...] * dot_nt(pieces, band_buf[...])).astype(BF16)
    parted = []
    for chunk in range(chunks):
        mixed = white[:, chunk * 2 * LANES : (chunk + 1) * 2 * LANES]
        parted.append(jnp.dot(mixed, split, preferred_element_type=F32).astype(BF16))
    white = jnp.concatenate(
        [part[:, :LANES] for part in parted] + [part[:, LANES:] for part in parted], axis=1
    )
    hot_buf[:, :columns] = white
    for place, reach_here in enumerate(places):
        for reach in range(REACH):

            @pl.when(reach_here == reach)
            def _():
                outs[reach][...] = hot_buf[place * width : (place + 1) * width, :columns]


def pick_blocks(kept, branched, spectra, pair_sides, pair_owner, block_members, case_table):
    _, freqs, parts, stations = spectra.shape
    block_count, width = block_members.shape
    columns = -(-freqs // LANES) * 2 * LANES
    rows = kept * width
    vmem = pl.BlockSpec(memory_space=pltpu.VMEM)
    smem = pl.BlockSpec(memory_space=pltpu.SMEM)
    out_shape = [jax.ShapeDtypeStruct((width, columns), BF16)] * REACH
    out_shape += [jax.ShapeDtypeStruct((1,), jnp.int32)] * branched
    return pl.pallas_call(
        functools.partial(pick_kernel, kept, branched, "sta"),
        out_shape=out_shape,
        in_specs=[pl.BlockSpec(memory_space=pltpu.HBM)] * 5,
        out_specs=[vmem] * REACH + [smem] * branched,
        scratch_shapes=[
            pltpu.SMEM(pair_sides.shape, jnp.int32),
            pltpu.SMEM(pair_owner.shape, jnp.int32),
            pltpu.VMEM(block_members.shape, jnp.int32),
            pltpu.SMEM(case_table.shape, jnp.int32),
            pltpu.VMEM((freqs, parts, stations), BF16),
            pltpu.VMEM((rows, max(columns, stations)), BF16),
            pltpu.VMEM((columns, LANES), BF16),
            pltpu.VMEM((rows, columns), F32),
            pltpu.SemaphoreType.DMA((COPIES + 4,)),
        ],
        compiler_params=pltpu.CompilerParams(vmem_limit_bytes=PICK_VMEM_LIMIT),
        cost_estimate=pl.CostEstimate(
            flops=2 * rows * stations * freqs * parts,
            bytes_accessed=2 * spectra.size + 4 * rows * columns,
            transcendentals=0,
        ),
        name="pick_and_whiten",
    )(pair_sides, pair_owner, block_members, case_table, spectra)


def case_number(first, second, needs, sta_count):
    return (first * sta_count + second) * (1 << (REACH - 1)) + needs // 2


def routes(sta_count):
    def load(first, second, sent):
        links = {}
        flows = [(first, reach) for reach in range(1, REACH)]
        flows += [(second, reach) for reach in range(1, REACH) if sent >> reach & 1]
        for owner, reach in flows:
            source = (owner + reach) % sta_count
            step = 1 if owner > source else -1
            for place in range(source, owner, step):
                links[place, step] = links.get((place, step), 0) + 1
        return max(links.values())

    every = (1 << REACH) - 2
    sets = [every] + [every - (1 << reach) for reach in range(REACH - 1, 0, -1)]
    branches = []
    cases = [0] * case_number(sta_count, 0, 0, sta_count)
    for first, second in itertools.permutations(range(sta_count), 2):
        for named in itertools.combinations(range(REACH), 2):
            needs = sum(1 << reach for reach in named) & every
            fits = [sent for sent in sets if needs & ~sent == 0]
            sent = min(fits, key=lambda sent: load(first, second, sent))
            branch = (first, second, sent)
            if branch not in branches:
                branches.append(branch)
            number = branches.index(branch)
            cases[case_number(first, second, needs, sta_count)] = (number << REACH) + sent
    return branches, cases


def phase_tables(sub_count, sub_freqs, groups, lag_rows):
    chunks = -(-sub_freqs // LANES)
    total = sub_count * sub_freqs
    freq = np.arange(total, dtype=np.int64).reshape(sub_count, 1, sub_freqs)
    middle = [2 * (group * lag_rows - LAGS // 2) + lag_rows - 1 for group in range(groups)]
    away = [step for step in range(1, lag_rows) if step % 2 != lag_rows % 2]

    def table(twice, forms, tile, dtype):
        twice = np.array(twice or [0], dtype=np.int64).reshape(1, -1, 1)
        angle = np.mod(freq * twice, 2 * total) * (math.pi / total)
        rows = np.stack([form(angle) for form in forms], axis=2)
        rows = rows.reshape(sub_count, -1, sub_freqs)
        pad = ((0, 0), (0, -rows.shape[1] % tile), (0, chunks * LANES - sub_freqs))
        return np.pad(rows, pad).astype(np.float32).astype(dtype)

    turns = table(middle, (np.cos, np.sin), 8, np.float32)
    offsets = table(away, (np.cos, np.sin, lambda angle: -np.sin(angle)), 16, BF16)
    return turns, offsets, len(away)


def lag_kernel(hops, slots, lag_rows, away, block_count, branched, pair_ref, owner_ref, case_ref, turn_ref, offset_ref, *refs):
    sub_count = lax.axis_size("sub")
    hr_count = lax.axis_size("hr")
    blocks = refs[: REACH * sub_count]
    outs = refs[REACH * sub_count : REACH * sub_count + len(hops)]
    buf, sems = refs[REACH * sub_count + len(hops) :]
    width = buf.shape[1]
    span = buf.shape[2] // 2
    middle_lag = lag_rows % 2
    my_sub = lax.axis_index("sub")
    my_hr = lax.axis_index("hr")
    my_sta = lax.axis_index("sta")
    sta_count = lax.axis_size("sta")

    pairs = read_pairs(pair_ref, owner_ref, block_count)
    order = [jnp.int32(reach) for reach in range(REACH)]
    if branched:
        first, second, case = case_of(pairs, case_ref, sta_count)
        keys = send_keys(first, second, case, sta_count, jnp.where)
        for reach, key in enumerate(keys):
            order[1 + reach] = 1 + sum((other < key).astype(jnp.int32) for other in keys)
    owned = []
    for owner, _, homes in pairs:
        places = []
        for home in homes:
            reach_here = lax.rem(home - my_sta + sta_count, sta_count)
            place_here = order[0]
            for reach in range(1, REACH):
                place_here = jnp.where(reach_here == reach, order[reach], place_here)
            places.append(place_here)
        owned.append((owner == my_sta, places))
    ends = []
    for slot in slots:
        count = jnp.int32(0)
        slot_ends = [jnp.int32(-1)] * 2
        for mine, places in owned:
            hit = mine & (count == slot)
            count = count + mine.astype(jnp.int32)
            slot_ends = [jnp.where(hit, new, old) for new, old in zip(places, slot_ends)]
        ends.append(slot_ends)

    def fetch(place, step):
        piece = place * sub_count + step
        return pltpu.make_async_copy(blocks[piece], buf.at[piece], sems.at[piece])

    pieces = [(place, step) for step in range(sub_count) for place in range(REACH)]

    @pl.when(ends[0][0] >= 0)
    def _():
        for place, step in pieces:
            fetch(place, step).start()

    for index, (left, right) in enumerate(ends):

        @pl.when(left < 0)
        def _():
            for out in outs:
                out[:, index] = jnp.zeros((lag_rows, width, width), out.dtype)

        @pl.when(left >= 0)
        def _():
            total = None
            for step in range(sub_count):
                if index == 0:
                    for place in range(REACH):
                        fetch(place, step).wait()
                sub = lax.rem(my_sub + step, sub_count)
                real = buf[left * sub_count + step, :, :span]
                imag = buf[left * sub_count + step, :, span:]
                scaled_real, scaled_imag = [real] * middle_lag, [imag] * middle_lag
                for near in range(away):
                    cosine, sine, minus = (
                        offset_ref[sub, 3 * near + form : 3 * near + form + 1, :]
                        for form in range(3)
                    )
                    scaled_real += [real * cosine, imag * minus]
                    scaled_imag += [imag * cosine, real * sine]
                real = buf[right * sub_count + step, :, :span].astype(F32)
                imag = buf[right * sub_count + step, :, span:].astype(F32)
                turned_real, turned_imag = [], []
                for hop in hops:
                    group = lax.rem(my_hr + hop, hr_count) * sub_count + my_sub
                    cosine = turn_ref[sub, pl.ds(2 * group, 1), :]
                    sine = turn_ref[sub, pl.ds(2 * group + 1, 1), :]
                    turned_real.append((real * cosine + imag * sine).astype(BF16))
                    turned_imag.append((imag * cosine - real * sine).astype(BF16))
                for scaled, turned in ((scaled_real, turned_real), (scaled_imag, turned_imag)):
                    part = dot_nt(jnp.concatenate(scaled, axis=0), jnp.concatenate(turned, axis=0))
                    total = part if total is None else total + part
            for place, out in enumerate(outs):
                columns = slice(place * width, (place + 1) * width)
                if middle_lag:
                    out[lag_rows // 2, index] = total[:width, columns].astype(out.dtype)
                for near in range(away):
                    start = (middle_lag + 2 * near) * width
                    even = total[start : start + width, columns]
                    odd = total[start + width : start + 2 * width, columns]
                    below = (lag_rows - 1) // 2 - near - middle_lag
                    above = lag_rows - 1 - below
                    out[above, index] = (even + odd).astype(out.dtype)
                    out[below, index] = (even - odd).astype(out.dtype)


def on_device(spectra, pair_blocks, pair_owner, block_members):
    hour_count, sub_freqs, _, _ = spectra.shape
    block_count, width = block_members.shape
    sta_count, hr_count, sub_count = (lax.axis_size(axis) for axis in ("sta", "hr", "sub"))
    groups = hr_count * sub_count
    lag_rows = LAGS // groups
    norming = 1.0 / math.sqrt(hour_count * hr_count * sub_count * sub_freqs)
    pair_sides = pair_blocks.T
    turns, offsets, away = phase_tables(sub_count, sub_freqs, groups, lag_rows)

    owners_at_most = pair_owner.shape[0] - CAP + 1
    branched = owners_at_most == 2 and sta_count == REACH
    kept = min(REACH, owners_at_most)
    branches, cases = routes(sta_count) if branched else ([], [])
    case_table = jnp.asarray(np.array(cases or [0], dtype=np.int32))
    picked = pick_blocks(
        kept, branched, spectra, pair_sides, pair_owner, block_members, case_table
    )

    def exchange(owners_of, order, *picked):
        arrived = [picked[0]]
        for reach in order:
            to_owner = [((owner + reach) % sta_count, owner) for owner in owners_of[reach - 1]]
            arrived.append(lax.ppermute(picked[reach], "sta", to_owner))
        blocks = []
        for block in arrived:
            blocks.append(block)
            for step in range(1, sub_count):
                swap = [((sub + step) % sub_count, sub) for sub in range(sub_count)]
                blocks.append(lax.ppermute(block, "sub", swap))
        return blocks

    if branched:
        steps = []
        for first, second, sent in branches:
            owners_of = [
                (first, second) if sent >> reach & 1 else (first,) for reach in range(1, REACH)
            ]
            keys = send_keys(first, second, sent, sta_count, lambda hit, yes, no: yes if hit else no)
            order = sorted(range(1, REACH), key=lambda reach: keys[reach - 1])
            steps.append(functools.partial(exchange, owners_of, order))
        blocks = lax.switch(picked[REACH][0], steps, *picked[:REACH])
    else:
        blocks = exchange([range(sta_count)] * (REACH - 1), range(1, REACH), *picked[:REACH])

    smem = pl.BlockSpec(memory_space=pltpu.SMEM)
    vmem = pl.BlockSpec(memory_space=pltpu.VMEM)
    hbm = pl.BlockSpec(memory_space=pltpu.HBM)
    row = picked[0].shape[1]
    versions = (lag_rows % 2 + 2 * away) * width

    def products(hops, slots, dtype, name):
        return pl.pallas_call(
            functools.partial(
                lag_kernel, hops, slots, lag_rows, away, block_count, branched
            ),
            out_shape=[jax.ShapeDtypeStruct((lag_rows, len(slots), width, width), dtype)]
            * len(hops),
            in_specs=[smem, smem, smem, vmem, vmem] + [hbm] * len(blocks),
            out_specs=[vmem] * len(hops),
            scratch_shapes=[
                pltpu.VMEM((len(blocks), width, row), BF16),
                pltpu.SemaphoreType.DMA((len(blocks),)),
            ],
            compiler_params=pltpu.CompilerParams(vmem_limit_bytes=LAG_VMEM_LIMIT),
            cost_estimate=pl.CostEstimate(
                flops=2 * len(slots) * len(hops) * versions * width * sub_count * row,
                bytes_accessed=2 * len(blocks) * width * row,
                transcendentals=0,
            ),
            name=name,
        )(pair_sides, pair_owner, case_table, turns, offsets, *blocks)

    hops, slots = tuple(range(1, hr_count)), tuple(range(CAP))
    sent = products(hops, slots, BF16, "lags_to_send")
    received = []
    for hop, part in zip(hops, sent):
        to_device = [(hr, (hr + hop) % hr_count) for hr in range(hr_count)]
        received.append(lax.ppermute(part, "hr", to_device))
    (summed,) = products((0,), slots, F32, "lags_to_keep")
    for part in received:
        summed = summed + part.astype(F32)
    return (summed * norming).astype(BF16)


def solution(mesh):
    placed = (P(("grp", "hr"), "sub", None, "sta"), P(), P(), P("sta", None))
    return jax.shard_map(
        on_device,
        mesh=mesh,
        in_specs=placed,
        out_specs=P(("grp", "hr", "sub"), "sta", None, None),
        check_vma=False,
    )
```

```python
import functools
import itertools
import math

import jax
import jax.numpy as jnp
import numpy as np
from jax import lax
from jax.experimental import pallas as pl
from jax.experimental.pallas import tpu as pltpu
from jax.sharding import PartitionSpec as P

BAND = 50
LAGS = 16
CAP = 3
REACH = 4
EPSILON = 1e-05
LANES = 128
F32 = jnp.float32
BF16 = jnp.bfloat16
PICK_VMEM_LIMIT = 59 * 1024 * 1024
LAG_VMEM_LIMIT = 32 * 1024 * 1024

NT = (((1,), (1,)), ((), ()))


def dot_nt(left, right):
    return lax.dot_general(left, right, NT, preferred_element_type=F32)


def iota(shape, dim):
    return lax.broadcasted_iota(jnp.int32, shape, dim)


def send_keys(first, second, needs, sta_count, where):
    keys = []
    for reach in range(1, REACH):
        distance = abs((first + reach) % sta_count - first)
        shared = (needs >> reach) % 2 == 1
        first_sends = (first - second - reach) % sta_count == 0
        late = where(shared, where(first_sends, 2, 1), 0)
        keys.append((late * sta_count + distance) * REACH + reach)
    return keys


def read_pairs(pair_ref, owner_ref, block_count):
    pairs = []
    for pair in range(owner_ref.shape[0]):
        blocks = [pair_ref[side, pair] for side in range(2)]
        pairs.append((owner_ref[pair], blocks, [lax.div(block, block_count) for block in blocks]))
    return pairs


def case_of(pairs, case_ref, sta_count):
    first = second = needs = jnp.int32(0)
    for owner, _, homes in pairs:
        count = jnp.int32(0)
        for other, _, _ in pairs:
            count = count + (other == owner).astype(jnp.int32)
        ends = [lax.rem(home - owner + sta_count, sta_count) for home in homes]
        first = jnp.where(count == CAP, owner, first)
        second = jnp.where(count < CAP, owner, second)
        needs = jnp.where(count < CAP, (1 << ends[0]) | (1 << ends[1]), needs)
    return first, second, case_ref[case_number(first, second, needs, sta_count)]


def pick_kernel(kept, branched, sta_axis, pair_hbm, owner_hbm, member_hbm, case_hbm, x_ref, *rest):
    outs = rest[:REACH]
    branch_ref = rest[REACH] if branched else None
    pair_ref, owner_ref, member_ref, case_ref, x_buf, hot_buf, band_buf, y_buf, sems = rest[
        REACH + branched :
    ]
    freqs, tiles = x_buf.shape[0], x_buf.shape[2] // LANES
    block_count, width = member_ref.shape
    columns = y_buf.shape[1]
    chunks = columns // (2 * LANES)

    runs = [(first, min(LANES, freqs - first)) for first in range(0, freqs, LANES)]

    def fetch(part):
        rows = pl.ds(*runs[part])
        return pltpu.make_async_copy(x_ref.at[0, rows], x_buf.at[rows], sems.at[part])

    small = [
        pltpu.make_async_copy(source, target, sems.at[len(runs) + index])
        for index, (source, target) in enumerate(
            (
                (pair_hbm, pair_ref),
                (owner_hbm, owner_ref),
                (member_hbm, member_ref),
                (case_hbm, case_ref),
            )
        )
    ]
    for copy in small:
        copy.start()
    for part in range(len(runs)):
        fetch(part).start()

    row, col = iota((columns, LANES), 0), iota((columns, LANES), 1)
    low = (col % 16) * (2 * BAND)
    hit = (row >= low) & (row < low + 2 * BAND) & (row < 2 * freqs) & (col < 48)
    band_buf[...] = jnp.where(hit, 1.0, 0.0).astype(BF16)
    row, col = iota((2 * LANES, 2 * LANES), 0), iota((2 * LANES, 2 * LANES), 1)
    split = jnp.where(row == 2 * (col % LANES) + col // LANES, 1.0, 0.0).astype(BF16)
    y_buf[:, 2 * freqs :] = jnp.zeros((kept * width, columns - 2 * freqs), F32)
    for copy in small:
        copy.wait()

    my_sta = lax.axis_index(sta_axis)
    sta_count = lax.axis_size(sta_axis)
    members = jnp.transpose(member_ref[...].astype(F32))
    block_col = iota(members.shape, 1)
    pairs = read_pairs(pair_ref, owner_ref, block_count)
    found, wanted = jnp.int32(0), []
    for reach in range(REACH):
        owner = lax.rem(my_sta - reach + REACH * sta_count, sta_count)
        chosen = jnp.int32(-1)
        for pair_owner, blocks, homes in pairs:
            for block, home in zip(blocks, homes):
                hit = (pair_owner == owner) & (home == my_sta)
                chosen = jnp.where(hit, lax.rem(block, block_count), chosen)
        wanted.append((found, chosen))
        found = found + (chosen >= 0).astype(jnp.int32)
    places, station = [], []
    for place in range(kept):
        reach_here, block_here = jnp.int32(-1), jnp.int32(0)
        for reach, (rank, chosen) in enumerate(wanted):
            hit = (rank == place) & (chosen >= 0)
            reach_here = jnp.where(hit, reach, reach_here)
            block_here = jnp.where(hit, chosen, block_here)
        places.append(reach_here)
        column = jnp.where(block_col == block_here, members, 0.0)
        station.append(jnp.sum(column, axis=1, keepdims=True).astype(jnp.int32))
    station = jnp.concatenate(station, axis=0)
    lane = iota((kept * width, LANES), 1)
    for tile in range(tiles):
        hot = jnp.where(station == lane + tile * LANES, 1.0, 0.0).astype(BF16)
        hot_buf[:, tile * LANES : (tile + 1) * LANES] = hot

    if branched:
        branch_ref[0] = case_of(pairs, case_ref, sta_count)[2] >> REACH

    for part, (first, count) in enumerate(runs):
        fetch(part).wait()
        x = jnp.concatenate(
            [
                x_buf[first : first + count, :, tile * LANES : (tile + 1) * LANES].reshape(
                    2 * count, LANES
                )
                for tile in range(tiles)
            ],
            axis=1,
        )
        y_buf[:, 2 * first : 2 * (first + count)] = dot_nt(hot_buf[:, : tiles * LANES], x)

    values = y_buf[...]
    square = values * values
    high = square.astype(BF16)
    low = (square - high.astype(F32)).astype(BF16)
    power = jnp.dot(high, band_buf[...], preferred_element_type=F32)
    power += jnp.dot(low, band_buf[...], preferred_element_type=F32)
    scale = lax.rsqrt(power * (1.0 / (2 * BAND)) + EPSILON)
    high = scale.astype(BF16)
    rest1 = scale - high.astype(F32)
    mid = rest1.astype(BF16)
    low = rest1 - mid.astype(F32)
    third = iota(scale.shape, 1) // 16
    pieces = jnp.where(
        third == 0, high.astype(F32), jnp.where(third == 1, mid.astype(F32), low)
    ).astype(BF16)
    white = (y_buf[...] * dot_nt(pieces, band_buf[...])).astype(BF16)
    parted = []
    for chunk in range(chunks):
        mixed = white[:, chunk * 2 * LANES : (chunk + 1) * 2 * LANES]
        parted.append(jnp.dot(mixed, split, preferred_element_type=F32).astype(BF16))
    white = jnp.concatenate(
        [part[:, :LANES] for part in parted] + [part[:, LANES:] for part in parted], axis=1
    )
    hot_buf[:, :columns] = white
    for place, reach_here in enumerate(places):
        for reach in range(REACH):

            @pl.when(reach_here == reach)
            def _():
                outs[reach][...] = hot_buf[place * width : (place + 1) * width, :columns]


def pick_blocks(kept, branched, spectra, pair_sides, pair_owner, block_members, case_table):
    _, freqs, parts, stations = spectra.shape
    block_count, width = block_members.shape
    columns = -(-freqs // LANES) * 2 * LANES
    rows = kept * width
    vmem = pl.BlockSpec(memory_space=pltpu.VMEM)
    smem = pl.BlockSpec(memory_space=pltpu.SMEM)
    out_shape = [jax.ShapeDtypeStruct((width, columns), BF16)] * REACH
    out_shape += [jax.ShapeDtypeStruct((1,), jnp.int32)] * branched
    return pl.pallas_call(
        functools.partial(pick_kernel, kept, branched, "sta"),
        out_shape=out_shape,
        in_specs=[pl.BlockSpec(memory_space=pltpu.HBM)] * 5,
        out_specs=[vmem] * REACH + [smem] * branched,
        scratch_shapes=[
            pltpu.SMEM(pair_sides.shape, jnp.int32),
            pltpu.SMEM(pair_owner.shape, jnp.int32),
            pltpu.VMEM(block_members.shape, jnp.int32),
            pltpu.SMEM(case_table.shape, jnp.int32),
            pltpu.VMEM((freqs, parts, stations), BF16),
            pltpu.VMEM((rows, max(columns, stations)), BF16),
            pltpu.VMEM((columns, LANES), BF16),
            pltpu.VMEM((rows, columns), F32),
            pltpu.SemaphoreType.DMA((-(-freqs // LANES) + 4,)),
        ],
        compiler_params=pltpu.CompilerParams(vmem_limit_bytes=PICK_VMEM_LIMIT),
        cost_estimate=pl.CostEstimate(
            flops=2 * rows * stations * freqs * parts,
            bytes_accessed=2 * spectra.size + 4 * rows * columns,
            transcendentals=0,
        ),
        name="pick_and_whiten",
    )(pair_sides, pair_owner, block_members, case_table, spectra)


def case_number(first, second, needs, sta_count):
    return (first * sta_count + second) * (1 << (REACH - 1)) + needs // 2


def routes(sta_count):
    def load(first, second, sent):
        links = {}
        flows = [(first, reach) for reach in range(1, REACH)]
        flows += [(second, reach) for reach in range(1, REACH) if sent >> reach & 1]
        for owner, reach in flows:
            source = (owner + reach) % sta_count
            step = 1 if owner > source else -1
            for place in range(source, owner, step):
                links[place, step] = links.get((place, step), 0) + 1
        return max(links.values())

    every = (1 << REACH) - 2
    sets = [every] + [every - (1 << reach) for reach in range(REACH - 1, 0, -1)]
    branches = []
    cases = [0] * case_number(sta_count, 0, 0, sta_count)
    for first, second in itertools.permutations(range(sta_count), 2):
        for named in itertools.combinations(range(REACH), 2):
            needs = sum(1 << reach for reach in named) & every
            fits = [sent for sent in sets if needs & ~sent == 0]
            sent = min(fits, key=lambda sent: load(first, second, sent))
            branch = (first, second, sent)
            if branch not in branches:
                branches.append(branch)
            number = branches.index(branch)
            cases[case_number(first, second, needs, sta_count)] = (number << REACH) + sent
    return branches, cases


def phase_tables(sub_count, sub_freqs, groups, lag_rows):
    chunks = -(-sub_freqs // LANES)
    total = sub_count * sub_freqs
    freq = np.arange(total, dtype=np.int64).reshape(sub_count, 1, sub_freqs)
    middle = [2 * (group * lag_rows - LAGS // 2) + lag_rows - 1 for group in range(groups)]
    away = [step for step in range(1, lag_rows) if step % 2 != lag_rows % 2]

    def table(twice, forms, tile, dtype):
        twice = np.array(twice or [0], dtype=np.int64).reshape(1, -1, 1)
        angle = np.mod(freq * twice, 2 * total) * (math.pi / total)
        rows = np.stack([form(angle) for form in forms], axis=2)
        rows = rows.reshape(sub_count, -1, sub_freqs)
        pad = ((0, 0), (0, -rows.shape[1] % tile), (0, chunks * LANES - sub_freqs))
        return np.pad(rows, pad).astype(np.float32).astype(dtype)

    turns = table(middle, (np.cos, np.sin), 8, np.float32)
    offsets = table(away, (np.cos, np.sin, lambda angle: -np.sin(angle)), 16, BF16)
    return turns, offsets, len(away)


def lag_kernel(hops, slots, lag_rows, away, block_count, branched, pair_ref, owner_ref, case_ref, turn_ref, offset_ref, *refs):
    sub_count = lax.axis_size("sub")
    hr_count = lax.axis_size("hr")
    blocks = refs[: REACH * sub_count]
    outs = refs[REACH * sub_count : REACH * sub_count + len(hops)]
    buf, sems = refs[REACH * sub_count + len(hops) :]
    width = buf.shape[1]
    span = buf.shape[2] // 2
    middle_lag = lag_rows % 2
    my_sub = lax.axis_index("sub")
    my_hr = lax.axis_index("hr")
    my_sta = lax.axis_index("sta")
    sta_count = lax.axis_size("sta")

    pairs = read_pairs(pair_ref, owner_ref, block_count)
    order = [jnp.int32(reach) for reach in range(REACH)]
    if branched:
        first, second, case = case_of(pairs, case_ref, sta_count)
        keys = send_keys(first, second, case, sta_count, jnp.where)
        for reach, key in enumerate(keys):
            order[1 + reach] = 1 + sum((other < key).astype(jnp.int32) for other in keys)
    owned = []
    for owner, _, homes in pairs:
        places = []
        for home in homes:
            reach_here = lax.rem(home - my_sta + sta_count, sta_count)
            place_here = order[0]
            for reach in range(1, REACH):
                place_here = jnp.where(reach_here == reach, order[reach], place_here)
            places.append(place_here)
        owned.append((owner == my_sta, places))
    ends = []
    for slot in slots:
        count = jnp.int32(0)
        slot_ends = [jnp.int32(-1)] * 2
        for mine, places in owned:
            hit = mine & (count == slot)
            count = count + mine.astype(jnp.int32)
            slot_ends = [jnp.where(hit, new, old) for new, old in zip(places, slot_ends)]
        ends.append(slot_ends)

    fresh, seen = [], []
    for place in itertools.chain.from_iterable(ends):
        known = place < 0
        for other in seen:
            known = known | (other == place)
        seen.append(place)
        fresh.append(jnp.logical_not(known))
    for slot_pair in range(0, len(seen), 2):
        for step in range(sub_count):
            for entry in (slot_pair, slot_pair + 1):
                for place in range(REACH):

                    @pl.when(fresh[entry] & (seen[entry] == place))
                    def _():
                        piece = place * sub_count + step
                        pltpu.make_async_copy(
                            blocks[piece], buf.at[piece], sems.at[piece]
                        ).start()

    def arrive(entry, step):
        @pl.when(fresh[entry])
        def _():
            piece = seen[entry] * sub_count + step
            pltpu.make_async_copy(blocks[step], buf.at[piece], sems.at[piece]).wait()

    for index, (left, right) in enumerate(ends):

        @pl.when(left < 0)
        def _():
            for out in outs:
                out[:, index] = jnp.zeros((lag_rows, width, width), out.dtype)

        @pl.when(left >= 0)
        def _():
            total = None
            for step in range(sub_count):
                arrive(2 * index, step)
                arrive(2 * index + 1, step)
                sub = lax.rem(my_sub + step, sub_count)
                real = buf[left * sub_count + step, :, :span]
                imag = buf[left * sub_count + step, :, span:]
                scaled_real, scaled_imag = [real] * middle_lag, [imag] * middle_lag
                for near in range(away):
                    cosine, sine, minus = (
                        offset_ref[sub, 3 * near + form : 3 * near + form + 1, :]
                        for form in range(3)
                    )
                    scaled_real += [real * cosine, imag * minus]
                    scaled_imag += [imag * cosine, real * sine]
                real = buf[right * sub_count + step, :, :span].astype(F32)
                imag = buf[right * sub_count + step, :, span:].astype(F32)
                turned_real, turned_imag = [], []
                for hop in hops:
                    group = lax.rem(my_hr + hop, hr_count) * sub_count + my_sub
                    cosine = turn_ref[sub, pl.ds(2 * group, 1), :]
                    sine = turn_ref[sub, pl.ds(2 * group + 1, 1), :]
                    turned_real.append((real * cosine + imag * sine).astype(BF16))
                    turned_imag.append((imag * cosine - real * sine).astype(BF16))
                for scaled, turned in ((scaled_real, turned_real), (scaled_imag, turned_imag)):
                    part = dot_nt(jnp.concatenate(scaled, axis=0), jnp.concatenate(turned, axis=0))
                    total = part if total is None else total + part
            for place, out in enumerate(outs):
                columns = slice(place * width, (place + 1) * width)
                if middle_lag:
                    out[lag_rows // 2, index] = total[:width, columns].astype(out.dtype)
                for near in range(away):
                    start = (middle_lag + 2 * near) * width
                    even = total[start : start + width, columns]
                    odd = total[start + width : start + 2 * width, columns]
                    below = (lag_rows - 1) // 2 - near - middle_lag
                    above = lag_rows - 1 - below
                    out[above, index] = (even + odd).astype(out.dtype)
                    out[below, index] = (even - odd).astype(out.dtype)


def on_device(spectra, pair_blocks, pair_owner, block_members):
    hour_count, sub_freqs, _, _ = spectra.shape
    block_count, width = block_members.shape
    sta_count, hr_count, sub_count = (lax.axis_size(axis) for axis in ("sta", "hr", "sub"))
    groups = hr_count * sub_count
    lag_rows = LAGS // groups
    norming = 1.0 / math.sqrt(hour_count * hr_count * sub_count * sub_freqs)
    pair_sides = pair_blocks.T
    turns, offsets, away = phase_tables(sub_count, sub_freqs, groups, lag_rows)

    owners_at_most = pair_owner.shape[0] - CAP + 1
    branched = owners_at_most == 2 and sta_count == REACH
    kept = min(REACH, owners_at_most)
    branches, cases = routes(sta_count) if branched else ([], [])
    case_table = jnp.asarray(np.array(cases or [0], dtype=np.int32))
    picked = pick_blocks(
        kept, branched, spectra, pair_sides, pair_owner, block_members, case_table
    )

    def exchange(owners_of, order, *picked):
        arrived = [picked[0]]
        for reach in order:
            to_owner = [((owner + reach) % sta_count, owner) for owner in owners_of[reach - 1]]
            arrived.append(lax.ppermute(picked[reach], "sta", to_owner))
        blocks = []
        for block in arrived:
            blocks.append(block)
            for step in range(1, sub_count):
                swap = [((sub + step) % sub_count, sub) for sub in range(sub_count)]
                blocks.append(lax.ppermute(block, "sub", swap))
        return blocks

    if branched:
        steps = []
        for first, second, sent in branches:
            owners_of = [
                (first, second) if sent >> reach & 1 else (first,) for reach in range(1, REACH)
            ]
            keys = send_keys(first, second, sent, sta_count, lambda hit, yes, no: yes if hit else no)
            order = sorted(range(1, REACH), key=lambda reach: keys[reach - 1])
            steps.append(functools.partial(exchange, owners_of, order))
        blocks = lax.switch(picked[REACH][0], steps, *picked[:REACH])
    else:
        blocks = exchange([range(sta_count)] * (REACH - 1), range(1, REACH), *picked[:REACH])

    smem = pl.BlockSpec(memory_space=pltpu.SMEM)
    vmem = pl.BlockSpec(memory_space=pltpu.VMEM)
    hbm = pl.BlockSpec(memory_space=pltpu.HBM)
    row = picked[0].shape[1]
    versions = (lag_rows % 2 + 2 * away) * width

    def products(hops, slots, dtype, name):
        return pl.pallas_call(
            functools.partial(
                lag_kernel, hops, slots, lag_rows, away, block_count, branched
            ),
            out_shape=[jax.ShapeDtypeStruct((lag_rows, len(slots), width, width), dtype)]
            * len(hops),
            in_specs=[smem, smem, smem, vmem, vmem] + [hbm] * len(blocks),
            out_specs=[vmem] * len(hops),
            scratch_shapes=[
                pltpu.VMEM((len(blocks), width, row), BF16),
                pltpu.SemaphoreType.DMA((len(blocks),)),
            ],
            compiler_params=pltpu.CompilerParams(vmem_limit_bytes=LAG_VMEM_LIMIT),
            cost_estimate=pl.CostEstimate(
                flops=2 * len(slots) * len(hops) * versions * width * sub_count * row,
                bytes_accessed=2 * len(blocks) * width * row,
                transcendentals=0,
            ),
            name=name,
        )(pair_sides, pair_owner, case_table, turns, offsets, *blocks)

    hops, slots = tuple(range(1, hr_count)), tuple(range(CAP))
    sent = products(hops, slots, BF16, "lags_to_send")
    received = []
    for hop, part in zip(hops, sent):
        to_device = [(hr, (hr + hop) % hr_count) for hr in range(hr_count)]
        received.append(lax.ppermute(part, "hr", to_device))
    (summed,) = products((0,), slots, F32, "lags_to_keep")
    for part in received:
        summed = summed + part.astype(F32)
    return (summed * norming).astype(BF16)


def solution(mesh):
    placed = (P(("grp", "hr"), "sub", None, "sta"), P(), P(), P("sta", None))
    return jax.shard_map(
        on_device,
        mesh=mesh,
        in_specs=placed,
        out_specs=P(("grp", "hr", "sub"), "sta", None, None),
        check_vma=False,
    )
```

```python
import functools
import itertools
import math

import jax
import jax.numpy as jnp
import numpy as np
from jax import lax
from jax.experimental import pallas as pl
from jax.experimental.pallas import tpu as pltpu
from jax.sharding import PartitionSpec as P

BAND = 50
LAGS = 16
CAP = 3
REACH = 4
COPIES = 2
EPSILON = 1e-05
LANES = 128
F32 = jnp.float32
BF16 = jnp.bfloat16
PICK_VMEM_LIMIT = 59 * 1024 * 1024
LAG_VMEM_LIMIT = 32 * 1024 * 1024

NT = (((1,), (1,)), ((), ()))


def dot_nt(left, right):
    return lax.dot_general(left, right, NT, preferred_element_type=F32)


def iota(shape, dim):
    return lax.broadcasted_iota(jnp.int32, shape, dim)


def send_keys(first, second, needs, sta_count, where):
    keys = []
    for reach in range(1, REACH):
        distance = abs((first + reach) % sta_count - first)
        shared = (needs >> reach) % 2 == 1
        first_sends = (first - second - reach) % sta_count == 0
        late = where(shared, where(first_sends, 2, 1), 0)
        keys.append((late * sta_count + distance) * REACH + reach)
    return keys


def read_pairs(pair_ref, owner_ref, block_count):
    pairs = []
    for pair in range(owner_ref.shape[0]):
        blocks = [pair_ref[side, pair] for side in range(2)]
        pairs.append((owner_ref[pair], blocks, [lax.div(block, block_count) for block in blocks]))
    return pairs


def case_of(pairs, case_ref, sta_count):
    first = second = needs = jnp.int32(0)
    for owner, _, homes in pairs:
        count = jnp.int32(0)
        for other, _, _ in pairs:
            count = count + (other == owner).astype(jnp.int32)
        ends = [lax.rem(home - owner + sta_count, sta_count) for home in homes]
        first = jnp.where(count == CAP, owner, first)
        second = jnp.where(count < CAP, owner, second)
        needs = jnp.where(count < CAP, (1 << ends[0]) | (1 << ends[1]), needs)
    return first, second, case_ref[case_number(first, second, needs, sta_count)]


def pick_kernel(kept, branched, sta_axis, pair_hbm, owner_hbm, member_hbm, case_hbm, x_ref, *rest):
    outs = rest[:REACH]
    branch_ref = rest[REACH] if branched else None
    pair_ref, owner_ref, member_ref, case_ref, x_buf, y_buf, white_buf, sems = rest[
        REACH + branched :
    ]
    freqs, tiles = x_buf.shape[0], x_buf.shape[2] // LANES
    block_count, width = member_ref.shape
    rows = y_buf.shape[0]
    chunks = rows // (2 * LANES)

    def fetch(part):
        run = pl.ds(part * (freqs // COPIES), freqs // COPIES)
        return pltpu.make_async_copy(x_ref.at[0, run], x_buf.at[run], sems.at[part])

    small = [
        pltpu.make_async_copy(source, target, sems.at[COPIES + index])
        for index, (source, target) in enumerate(
            (
                (pair_hbm, pair_ref),
                (owner_hbm, owner_ref),
                (member_hbm, member_ref),
                (case_hbm, case_ref),
            )
        )
    ]
    for copy in small:
        copy.start()
    for part in range(COPIES):
        fetch(part).start()

    def bands(shape, part_dim):
        part, place = iota(shape, part_dim), iota(shape, 1 - part_dim)
        low = (place % 16) * (2 * BAND)
        hit = (part >= low) & (part < low + 2 * BAND) & (part < 2 * freqs) & (place < 48)
        return jnp.where(hit, 1.0, 0.0).astype(BF16)

    gather_bands, spread_bands = bands((48, rows), 1), bands((rows, LANES), 0)
    row, col = iota((2 * LANES, 2 * LANES), 0), iota((2 * LANES, 2 * LANES), 1)
    split = jnp.where(row == 2 * (col % LANES) + col // LANES, 1.0, 0.0).astype(BF16)
    y_buf[2 * freqs :] = jnp.zeros((rows - 2 * freqs, kept * width), F32)
    for copy in small:
        copy.wait()

    my_sta = lax.axis_index(sta_axis)
    sta_count = lax.axis_size(sta_axis)
    pairs = read_pairs(pair_ref, owner_ref, block_count)
    found, wanted = jnp.int32(0), []
    for reach in range(REACH):
        owner = lax.rem(my_sta - reach + REACH * sta_count, sta_count)
        chosen = jnp.int32(-1)
        for pair_owner, blocks, homes in pairs:
            for block, home in zip(blocks, homes):
                hit = (pair_owner == owner) & (home == my_sta)
                chosen = jnp.where(hit, lax.rem(block, block_count), chosen)
        wanted.append((found, chosen))
        found = found + (chosen >= 0).astype(jnp.int32)
    places, station = [], []
    for place in range(kept):
        reach_here, block_here = jnp.int32(-1), jnp.int32(0)
        for reach, (rank, chosen) in enumerate(wanted):
            hit = (rank == place) & (chosen >= 0)
            reach_here = jnp.where(hit, reach, reach_here)
            block_here = jnp.where(hit, chosen, block_here)
        places.append(reach_here)
        station.append(member_ref[pl.ds(block_here, 1), :])
    station = jnp.concatenate(station, axis=1)
    hot = jnp.where(station == iota((tiles * LANES, kept * width), 0), 1.0, 0.0).astype(BF16)

    if branched:
        branch_ref[0] = case_of(pairs, case_ref, sta_count)[2] >> REACH

    for part in range(COPIES):
        fetch(part).wait()
    x = jnp.concatenate(
        [
            x_buf[:, :, tile * LANES : (tile + 1) * LANES].reshape(2 * freqs, LANES)
            for tile in range(tiles)
        ],
        axis=1,
    )
    y_buf[: 2 * freqs] = jnp.dot(x, hot, preferred_element_type=F32)

    values = y_buf[...]
    square = values * values
    high = square.astype(BF16)
    low = (square - high.astype(F32)).astype(BF16)
    power = jnp.dot(gather_bands, high, preferred_element_type=F32)
    power += jnp.dot(gather_bands, low, preferred_element_type=F32)
    scale = lax.rsqrt(power * (1.0 / (2 * BAND)) + EPSILON)
    high = scale.astype(BF16).astype(F32)
    mid = (scale - high).astype(BF16).astype(F32)
    low = scale - high - mid
    third = iota(scale.shape, 0) // 16
    pieces = jnp.where(third == 0, high, jnp.where(third == 1, mid, low))
    pieces = jnp.concatenate(
        [pieces, jnp.zeros((LANES - pieces.shape[0], pieces.shape[1]), F32)], axis=0
    ).astype(BF16)
    white = y_buf[...] * jnp.dot(spread_bands, pieces, preferred_element_type=F32)
    white = white.astype(BF16)
    parted = []
    for chunk in range(chunks):
        mixed = white[chunk * 2 * LANES : (chunk + 1) * 2 * LANES]
        part = lax.dot_general(
            mixed, split, (((0,), (0,)), ((), ())), preferred_element_type=F32
        )
        parted.append(part.astype(BF16))
    white_buf[...] = jnp.concatenate(
        [part[:, :LANES] for part in parted] + [part[:, LANES:] for part in parted], axis=1
    )
    for place, reach_here in enumerate(places):
        for reach in range(REACH):

            @pl.when(reach_here == reach)
            def _():
                outs[reach][...] = white_buf[place * width : (place + 1) * width]


def pick_blocks(kept, branched, spectra, pair_sides, pair_owner, block_members, case_table):
    _, freqs, parts, stations = spectra.shape
    block_count, width = block_members.shape
    columns = -(-freqs // LANES) * 2 * LANES
    rows = kept * width
    vmem = pl.BlockSpec(memory_space=pltpu.VMEM)
    smem = pl.BlockSpec(memory_space=pltpu.SMEM)
    out_shape = [jax.ShapeDtypeStruct((width, columns), BF16)] * REACH
    out_shape += [jax.ShapeDtypeStruct((1,), jnp.int32)] * branched
    return pl.pallas_call(
        functools.partial(pick_kernel, kept, branched, "sta"),
        out_shape=out_shape,
        in_specs=[pl.BlockSpec(memory_space=pltpu.HBM)] * 5,
        out_specs=[vmem] * REACH + [smem] * branched,
        scratch_shapes=[
            pltpu.SMEM(pair_sides.shape, jnp.int32),
            pltpu.SMEM(pair_owner.shape, jnp.int32),
            pltpu.VMEM(block_members.shape, jnp.int32),
            pltpu.SMEM(case_table.shape, jnp.int32),
            pltpu.VMEM((freqs, parts, stations), BF16),
            pltpu.VMEM((columns, rows), F32),
            pltpu.VMEM((rows, columns), BF16),
            pltpu.SemaphoreType.DMA((COPIES + 4,)),
        ],
        compiler_params=pltpu.CompilerParams(vmem_limit_bytes=PICK_VMEM_LIMIT),
        cost_estimate=pl.CostEstimate(
            flops=2 * rows * stations * freqs * parts,
            bytes_accessed=2 * spectra.size + 4 * rows * columns,
            transcendentals=0,
        ),
        name="pick_and_whiten",
    )(pair_sides, pair_owner, block_members, case_table, spectra)


def case_number(first, second, needs, sta_count):
    return (first * sta_count + second) * (1 << (REACH - 1)) + needs // 2


def routes(sta_count):
    def load(first, second, sent):
        links = {}
        flows = [(first, reach) for reach in range(1, REACH)]
        flows += [(second, reach) for reach in range(1, REACH) if sent >> reach & 1]
        for owner, reach in flows:
            source = (owner + reach) % sta_count
            step = 1 if owner > source else -1
            for place in range(source, owner, step):
                links[place, step] = links.get((place, step), 0) + 1
        return max(links.values())

    every = (1 << REACH) - 2
    sets = [every] + [every - (1 << reach) for reach in range(REACH - 1, 0, -1)]
    branches = []
    cases = [0] * case_number(sta_count, 0, 0, sta_count)
    for first, second in itertools.permutations(range(sta_count), 2):
        for named in itertools.combinations(range(REACH), 2):
            needs = sum(1 << reach for reach in named) & every
            fits = [sent for sent in sets if needs & ~sent == 0]
            sent = min(fits, key=lambda sent: load(first, second, sent))
            branch = (first, second, sent)
            if branch not in branches:
                branches.append(branch)
            number = branches.index(branch)
            cases[case_number(first, second, needs, sta_count)] = (number << REACH) + sent
    return branches, cases


def phase_tables(sub_count, sub_freqs, groups, lag_rows):
    chunks = -(-sub_freqs // LANES)
    total = sub_count * sub_freqs
    freq = np.arange(total, dtype=np.int64).reshape(sub_count, 1, sub_freqs)
    middle = [2 * (group * lag_rows - LAGS // 2) + lag_rows - 1 for group in range(groups)]
    away = [step for step in range(1, lag_rows) if step % 2 != lag_rows % 2]

    def table(twice, forms, tile, dtype):
        twice = np.array(twice or [0], dtype=np.int64).reshape(1, -1, 1)
        angle = np.mod(freq * twice, 2 * total) * (math.pi / total)
        rows = np.stack([form(angle) for form in forms], axis=2)
        rows = rows.reshape(sub_count, -1, sub_freqs)
        pad = ((0, 0), (0, -rows.shape[1] % tile), (0, chunks * LANES - sub_freqs))
        return np.pad(rows, pad).astype(np.float32).astype(dtype)

    turns = table(middle, (np.cos, np.sin), 8, np.float32)
    offsets = table(away, (np.cos, np.sin, lambda angle: -np.sin(angle)), 16, BF16)
    return turns, offsets, len(away)


def lag_kernel(hops, slots, lag_rows, away, block_count, branched, pair_ref, owner_ref, case_ref, turn_ref, offset_ref, *refs):
    sub_count = lax.axis_size("sub")
    hr_count = lax.axis_size("hr")
    blocks = refs[: REACH * sub_count]
    outs = refs[REACH * sub_count : REACH * sub_count + len(hops)]
    buf, sems = refs[REACH * sub_count + len(hops) :]
    width = buf.shape[3]
    span = buf.shape[4] // 2
    middle_lag = lag_rows % 2
    my_sub = lax.axis_index("sub")
    my_hr = lax.axis_index("hr")
    my_sta = lax.axis_index("sta")
    sta_count = lax.axis_size("sta")

    pairs = read_pairs(pair_ref, owner_ref, block_count)
    order = [jnp.int32(reach) for reach in range(REACH)]
    if branched:
        first, second, case = case_of(pairs, case_ref, sta_count)
        keys = send_keys(first, second, case, sta_count, jnp.where)
        for reach, key in enumerate(keys):
            order[1 + reach] = 1 + sum((other < key).astype(jnp.int32) for other in keys)
    owned = []
    for owner, _, homes in pairs:
        places = []
        for home in homes:
            reach_here = lax.rem(home - my_sta + sta_count, sta_count)
            place_here = order[0]
            for reach in range(1, REACH):
                place_here = jnp.where(reach_here == reach, order[reach], place_here)
            places.append(place_here)
        owned.append((owner == my_sta, places))
    ends = []
    for slot in slots:
        count = jnp.int32(0)
        slot_ends = [jnp.int32(-1)] * 2
        for mine, places in owned:
            hit = mine & (count == slot)
            count = count + mine.astype(jnp.int32)
            slot_ends = [jnp.where(hit, new, old) for new, old in zip(places, slot_ends)]
        ends.append(slot_ends)

    def fetches(index, act):
        for side in range(2):
            for place in range(REACH):

                @pl.when(ends[index][side] == place)
                def _():
                    for step in range(sub_count):
                        act(
                            pltpu.make_async_copy(
                                blocks[place * sub_count + step],
                                buf.at[index, side, step],
                                sems.at[index, side, step],
                            )
                        )

    for index in range(len(slots)):
        fetches(index, lambda copy: copy.start())

    for index in range(len(slots)):

        @pl.when(ends[index][0] < 0)
        def _():
            for out in outs:
                out[:, index] = jnp.zeros((lag_rows, width, width), out.dtype)

        fetches(index, lambda copy: copy.wait())

        @pl.when(ends[index][0] >= 0)
        def _():
            total = None
            for step in range(sub_count):
                sub = lax.rem(my_sub + step, sub_count)
                real = buf[index, 0, step, :, :span]
                imag = buf[index, 0, step, :, span:]
                scaled_real, scaled_imag = [real] * middle_lag, [imag] * middle_lag
                for near in range(away):
                    cosine, sine, minus = (
                        offset_ref[sub, 3 * near + form : 3 * near + form + 1, :]
                        for form in range(3)
                    )
                    scaled_real += [real * cosine, imag * minus]
                    scaled_imag += [imag * cosine, real * sine]
                real = buf[index, 1, step, :, :span].astype(F32)
                imag = buf[index, 1, step, :, span:].astype(F32)
                turned_real, turned_imag = [], []
                for hop in hops:
                    group = lax.rem(my_hr + hop, hr_count) * sub_count + my_sub
                    cosine = turn_ref[sub, pl.ds(2 * group, 1), :]
                    sine = turn_ref[sub, pl.ds(2 * group + 1, 1), :]
                    turned_real.append((real * cosine + imag * sine).astype(BF16))
                    turned_imag.append((imag * cosine - real * sine).astype(BF16))
                for scaled, turned in ((scaled_real, turned_real), (scaled_imag, turned_imag)):
                    part = dot_nt(jnp.concatenate(scaled, axis=0), jnp.concatenate(turned, axis=0))
                    total = part if total is None else total + part
            for place, out in enumerate(outs):
                columns = slice(place * width, (place + 1) * width)
                if middle_lag:
                    out[lag_rows // 2, index] = total[:width, columns].astype(out.dtype)
                for near in range(away):
                    start = (middle_lag + 2 * near) * width
                    even = total[start : start + width, columns]
                    odd = total[start + width : start + 2 * width, columns]
                    below = (lag_rows - 1) // 2 - near - middle_lag
                    above = lag_rows - 1 - below
                    out[above, index] = (even + odd).astype(out.dtype)
                    out[below, index] = (even - odd).astype(out.dtype)


def on_device(spectra, pair_blocks, pair_owner, block_members):
    hour_count, sub_freqs, _, _ = spectra.shape
    block_count, width = block_members.shape
    sta_count, hr_count, sub_count = (lax.axis_size(axis) for axis in ("sta", "hr", "sub"))
    groups = hr_count * sub_count
    lag_rows = LAGS // groups
    norming = 1.0 / math.sqrt(hour_count * hr_count * sub_count * sub_freqs)
    pair_sides = pair_blocks.T
    turns, offsets, away = phase_tables(sub_count, sub_freqs, groups, lag_rows)

    owners_at_most = pair_owner.shape[0] - CAP + 1
    branched = owners_at_most == 2 and sta_count == REACH
    kept = min(REACH, owners_at_most)
    branches, cases = routes(sta_count) if branched else ([], [])
    case_table = jnp.asarray(np.array(cases or [0], dtype=np.int32))
    picked = pick_blocks(
        kept, branched, spectra, pair_sides, pair_owner, block_members, case_table
    )

    def exchange(owners_of, order, *picked):
        arrived = [picked[0]]
        for reach in order:
            to_owner = [((owner + reach) % sta_count, owner) for owner in owners_of[reach - 1]]
            arrived.append(lax.ppermute(picked[reach], "sta", to_owner))
        blocks = []
        for block in arrived:
            blocks.append(block)
            for step in range(1, sub_count):
                swap = [((sub + step) % sub_count, sub) for sub in range(sub_count)]
                blocks.append(lax.ppermute(block, "sub", swap))
        return blocks

    if branched:
        steps = []
        for first, second, sent in branches:
            owners_of = [
                (first, second) if sent >> reach & 1 else (first,) for reach in range(1, REACH)
            ]
            keys = send_keys(first, second, sent, sta_count, lambda hit, yes, no: yes if hit else no)
            order = sorted(range(1, REACH), key=lambda reach: keys[reach - 1])
            steps.append(functools.partial(exchange, owners_of, order))
        blocks = lax.switch(picked[REACH][0], steps, *picked[:REACH])
    else:
        blocks = exchange([range(sta_count)] * (REACH - 1), range(1, REACH), *picked[:REACH])

    smem = pl.BlockSpec(memory_space=pltpu.SMEM)
    vmem = pl.BlockSpec(memory_space=pltpu.VMEM)
    hbm = pl.BlockSpec(memory_space=pltpu.HBM)
    row = picked[0].shape[1]
    versions = (lag_rows % 2 + 2 * away) * width

    def products(hops, slots, dtype, name):
        return pl.pallas_call(
            functools.partial(
                lag_kernel, hops, slots, lag_rows, away, block_count, branched
            ),
            out_shape=[jax.ShapeDtypeStruct((lag_rows, len(slots), width, width), dtype)]
            * len(hops),
            in_specs=[smem, smem, smem, vmem, vmem] + [hbm] * len(blocks),
            out_specs=[vmem] * len(hops),
            scratch_shapes=[
                pltpu.VMEM((len(slots), 2, sub_count, width, row), BF16),
                pltpu.SemaphoreType.DMA((len(slots), 2, sub_count)),
            ],
            compiler_params=pltpu.CompilerParams(vmem_limit_bytes=LAG_VMEM_LIMIT),
            cost_estimate=pl.CostEstimate(
                flops=2 * len(slots) * len(hops) * versions * width * sub_count * row,
                bytes_accessed=4 * len(slots) * sub_count * width * row,
                transcendentals=0,
            ),
            name=name,
        )(pair_sides, pair_owner, case_table, turns, offsets, *blocks)

    hops, slots = tuple(range(1, hr_count)), tuple(range(CAP))
    sent = products(hops, slots, BF16, "lags_to_send")
    received = []
    for hop, part in zip(hops, sent):
        to_device = [(hr, (hr + hop) % hr_count) for hr in range(hr_count)]
        received.append(lax.ppermute(part, "hr", to_device))
    (summed,) = products((0,), slots, F32, "lags_to_keep")
    for part in received:
        summed = summed + part.astype(F32)
    return (summed * norming).astype(BF16)


def solution(mesh):
    placed = (P(("grp", "hr"), "sub", None, "sta"), P(), P(), P("sta", None))
    return jax.shard_map(
        on_device,
        mesh=mesh,
        in_specs=placed,
        out_specs=P(("grp", "hr", "sub"), "sta", None, None),
        check_vma=False,
    )
```

```python
import functools
import itertools
import math

import jax
import jax.numpy as jnp
import numpy as np
from jax import lax
from jax.experimental import pallas as pl
from jax.experimental.pallas import tpu as pltpu
from jax.sharding import PartitionSpec as P

BAND = 50
LAGS = 16
CAP = 3
REACH = 4
COPIES = 2
EPSILON = 1e-05
LANES = 128
F32 = jnp.float32
BF16 = jnp.bfloat16
PICK_VMEM_LIMIT = 59 * 1024 * 1024
LAG_VMEM_LIMIT = 32 * 1024 * 1024

NT = (((1,), (1,)), ((), ()))


def dot_nt(left, right):
    return lax.dot_general(left, right, NT, preferred_element_type=F32)


def iota(shape, dim):
    return lax.broadcasted_iota(jnp.int32, shape, dim)


def read_pairs(pair_ref, owner_ref, block_count):
    pairs = []
    for pair in range(owner_ref.shape[0]):
        blocks = [pair_ref[side, pair] for side in range(2)]
        pairs.append((owner_ref[pair], blocks, [lax.div(block, block_count) for block in blocks]))
    return pairs


def owners_of(pairs, sta_count):
    first = second = jnp.int32(0)
    for owner, _, _ in pairs:
        count = sum((other == owner).astype(jnp.int32) for other, _, _ in pairs)
        first = jnp.where(count == CAP, owner, first)
        second = jnp.where(count < CAP, owner, second)
    named = [jnp.int32(0)] * REACH
    for owner, _, homes in pairs:
        for home in homes:
            reach_here = lax.rem(home - first + sta_count, sta_count)
            for reach in range(1, REACH):
                hit = (owner == first) & (reach_here == reach)
                named[reach] = named[reach] + hit.astype(jnp.int32)
    last = jnp.int32(1)
    for uses in (1, 0):
        for reach in range(REACH - 1, 0, -1):
            last = jnp.where(named[reach] == uses, reach, last)
    return first, second, last


def straight(first, second, last, sta_count, where):
    first_sends = (first - second) % sta_count
    places = [0]
    for reach in range(1, REACH):
        place = 1
        for other in range(1, REACH):
            if other != reach:
                ahead = 0 if other > reach else 1
                ahead = where(first_sends == reach, 1, where(first_sends == other, 0, ahead))
                if 1 in (reach, other):
                    ahead = int(other == 1)
                place = place + where(last == other, 0, ahead)
        places.append(place)
    return places


def slot_plan(pair_ref, owner_ref, block_count, staged):
    my_sta, sta_count = lax.axis_index("sta"), lax.axis_size("sta")
    pairs = read_pairs(pair_ref, owner_ref, block_count)
    order = [jnp.int32(reach) for reach in range(REACH)]
    if staged:
        first, second, last = owners_of(pairs, sta_count)
        is_first = my_sta == first
        order = straight(first, second, last, sta_count, jnp.where)
        for reach in range(1, REACH):
            away = REACH if reach == 1 else jnp.where(last == reach, REACH - 1, order[reach])
            order[reach] = jnp.where(
                is_first, jnp.where(last == reach, REACH, order[reach]), away
            )
    owned = []
    for owner, _, homes in pairs:
        places = []
        for home in homes:
            reach_here = lax.rem(home - my_sta + sta_count, sta_count)
            place_here = jnp.int32(0)
            for reach in range(1, REACH):
                place_here = jnp.where(reach_here == reach, order[reach], place_here)
            places.append(place_here)
        owned.append((owner == my_sta, places))
    early = later = jnp.int32(0)
    plan = []
    for slot in range(CAP):
        count = jnp.int32(0)
        left, right, filled = jnp.int32(-1), jnp.int32(-1), jnp.int32(0) > 0
        for mine, places in owned:
            hit = mine & (count == slot)
            count = count + mine.astype(jnp.int32)
            left, right = jnp.where(hit, places[0], left), jnp.where(hit, places[1], right)
            filled = filled | hit
        number = jnp.int32(slot)
        if staged:
            ready = filled & is_first & (left != REACH) & (right != REACH) & (early < CAP - 1)
            number = jnp.where(ready, early, CAP - 1 + later)
            early = early + ready.astype(jnp.int32)
            later = later + (filled & jnp.logical_not(ready)).astype(jnp.int32)
        plan.append((jnp.where(filled, number, -1), left, right))
    return plan


def pick_kernel(kept, staged, sta_axis, pair_hbm, owner_hbm, member_hbm, x_ref, *rest):
    outs = rest[:REACH]
    pair_ref, owner_ref, member_ref, x_buf, y_buf, white_buf, sems = rest[REACH + 2 * staged :]
    freqs, tiles = x_buf.shape[0], x_buf.shape[2] // LANES
    block_count, width = member_ref.shape
    rows = y_buf.shape[0]
    chunks = rows // (2 * LANES)

    def fetch(part):
        run = pl.ds(part * (freqs // COPIES), freqs // COPIES)
        return pltpu.make_async_copy(x_ref.at[0, run], x_buf.at[run], sems.at[part])

    small = [
        pltpu.make_async_copy(source, target, sems.at[COPIES + index])
        for index, (source, target) in enumerate(
            (
                (pair_hbm, pair_ref),
                (owner_hbm, owner_ref),
                (member_hbm, member_ref),
            )
        )
    ]
    for copy in small:
        copy.start()
    for part in range(COPIES):
        fetch(part).start()

    def bands(shape, part_dim):
        part, place = iota(shape, part_dim), iota(shape, 1 - part_dim)
        low = (place % 16) * (2 * BAND)
        hit = (part >= low) & (part < low + 2 * BAND) & (part < 2 * freqs) & (place < 48)
        return jnp.where(hit, 1.0, 0.0).astype(BF16)

    gather_bands, spread_bands = bands((48, rows), 1), bands((rows, LANES), 0)
    row, col = iota((2 * LANES, 2 * LANES), 0), iota((2 * LANES, 2 * LANES), 1)
    split = jnp.where(row == 2 * (col % LANES) + col // LANES, 1.0, 0.0).astype(BF16)
    y_buf[2 * freqs :] = jnp.zeros((rows - 2 * freqs, kept * width), F32)
    for copy in small:
        copy.wait()

    my_sta = lax.axis_index(sta_axis)
    sta_count = lax.axis_size(sta_axis)
    pairs = read_pairs(pair_ref, owner_ref, block_count)
    found, wanted = jnp.int32(0), []
    for reach in range(REACH):
        owner = lax.rem(my_sta - reach + REACH * sta_count, sta_count)
        chosen = jnp.int32(-1)
        for pair_owner, blocks, homes in pairs:
            for block, home in zip(blocks, homes):
                hit = (pair_owner == owner) & (home == my_sta)
                chosen = jnp.where(hit, lax.rem(block, block_count), chosen)
        wanted.append((found, chosen))
        found = found + (chosen >= 0).astype(jnp.int32)
    places, station = [], []
    for place in range(kept):
        reach_here, block_here = jnp.int32(-1), jnp.int32(0)
        for reach, (rank, chosen) in enumerate(wanted):
            hit = (rank == place) & (chosen >= 0)
            reach_here = jnp.where(hit, reach, reach_here)
            block_here = jnp.where(hit, chosen, block_here)
        places.append(reach_here)
        station.append(member_ref[pl.ds(block_here, 1), :])
    station = jnp.concatenate(station, axis=1)
    hot = jnp.where(station == iota((tiles * LANES, kept * width), 0), 1.0, 0.0).astype(BF16)

    if staged:
        branch_ref, rest_ref = rest[REACH : REACH + 2]
        first, second, last = owners_of(pairs, sta_count)
        second_rank = second - (second > first).astype(jnp.int32)
        branch_ref[0] = (first * (sta_count - 1) + second_rank) * (REACH - 1) + last - 1
        waiting = jnp.int32(0)
        for owner, _, homes in pairs:
            ends = [lax.rem(home - first + sta_count, sta_count) for home in homes]
            hit = (owner == first) & ((ends[0] == last) | (ends[1] == last))
            waiting = waiting + hit.astype(jnp.int32)
        rest_ref[0] = (waiting > 1).astype(jnp.int32)

    for part in range(COPIES):
        fetch(part).wait()
    x = jnp.concatenate(
        [
            x_buf[:, :, tile * LANES : (tile + 1) * LANES].reshape(2 * freqs, LANES)
            for tile in range(tiles)
        ],
        axis=1,
    )
    y_buf[: 2 * freqs] = jnp.dot(x, hot, preferred_element_type=F32)

    values = y_buf[...]
    square = values * values
    high = square.astype(BF16)
    low = (square - high.astype(F32)).astype(BF16)
    power = jnp.dot(gather_bands, high, preferred_element_type=F32)
    power += jnp.dot(gather_bands, low, preferred_element_type=F32)
    scale = lax.rsqrt(power * (1.0 / (2 * BAND)) + EPSILON)
    high = scale.astype(BF16).astype(F32)
    mid = (scale - high).astype(BF16).astype(F32)
    low = scale - high - mid
    third = iota(scale.shape, 0) // 16
    pieces = jnp.where(third == 0, high, jnp.where(third == 1, mid, low))
    pieces = jnp.concatenate(
        [pieces, jnp.zeros((LANES - pieces.shape[0], pieces.shape[1]), F32)], axis=0
    ).astype(BF16)
    white = y_buf[...] * jnp.dot(spread_bands, pieces, preferred_element_type=F32)
    white = white.astype(BF16)
    parted = []
    for chunk in range(chunks):
        mixed = white[chunk * 2 * LANES : (chunk + 1) * 2 * LANES]
        part = lax.dot_general(
            mixed, split, (((0,), (0,)), ((), ())), preferred_element_type=F32
        )
        parted.append(part.astype(BF16))
    white_buf[...] = jnp.concatenate(
        [part[:, :LANES] for part in parted] + [part[:, LANES:] for part in parted], axis=1
    )
    for place, reach_here in enumerate(places):
        for reach in range(REACH):

            @pl.when(reach_here == reach)
            def _():
                outs[reach][...] = white_buf[place * width : (place + 1) * width]


def pick_blocks(kept, staged, spectra, pair_sides, pair_owner, block_members):
    _, freqs, parts, stations = spectra.shape
    block_count, width = block_members.shape
    columns = -(-freqs // LANES) * 2 * LANES
    rows = kept * width
    vmem = pl.BlockSpec(memory_space=pltpu.VMEM)
    smem = pl.BlockSpec(memory_space=pltpu.SMEM)
    out_shape = [jax.ShapeDtypeStruct((width, columns), BF16)] * REACH
    out_shape += [jax.ShapeDtypeStruct((1,), jnp.int32)] * (2 * staged)
    return pl.pallas_call(
        functools.partial(pick_kernel, kept, staged, "sta"),
        out_shape=out_shape,
        in_specs=[pl.BlockSpec(memory_space=pltpu.HBM)] * 4,
        out_specs=[vmem] * REACH + [smem] * (2 * staged),
        scratch_shapes=[
            pltpu.SMEM(pair_sides.shape, jnp.int32),
            pltpu.SMEM(pair_owner.shape, jnp.int32),
            pltpu.VMEM(block_members.shape, jnp.int32),
            pltpu.VMEM((freqs, parts, stations), BF16),
            pltpu.VMEM((columns, rows), F32),
            pltpu.VMEM((rows, columns), BF16),
            pltpu.SemaphoreType.DMA((COPIES + 3,)),
        ],
        compiler_params=pltpu.CompilerParams(vmem_limit_bytes=PICK_VMEM_LIMIT),
        cost_estimate=pl.CostEstimate(
            flops=2 * rows * stations * freqs * parts,
            bytes_accessed=2 * spectra.size + 4 * rows * columns,
            transcendentals=0,
        ),
        name="pick_and_whiten",
    )(pair_sides, pair_owner, block_members, spectra)


def phase_tables(sub_count, sub_freqs, groups, lag_rows):
    chunks = -(-sub_freqs // LANES)
    total = sub_count * sub_freqs
    freq = np.arange(total, dtype=np.int64).reshape(sub_count, 1, sub_freqs)
    middle = [2 * (group * lag_rows - LAGS // 2) + lag_rows - 1 for group in range(groups)]
    away = [step for step in range(1, lag_rows) if step % 2 != lag_rows % 2]

    def table(twice, forms, tile, dtype):
        twice = np.array(twice or [0], dtype=np.int64).reshape(1, -1, 1)
        angle = np.mod(freq * twice, 2 * total) * (math.pi / total)
        rows = np.stack([form(angle) for form in forms], axis=2)
        rows = rows.reshape(sub_count, -1, sub_freqs)
        pad = ((0, 0), (0, -rows.shape[1] % tile), (0, chunks * LANES - sub_freqs))
        return np.pad(rows, pad).astype(np.float32).astype(dtype)

    turns = table(middle, (np.cos, np.sin), 8, np.float32)
    offsets = table(away, (np.cos, np.sin, lambda angle: -np.sin(angle)), 16, BF16)
    return turns, offsets, len(away)


def lag_kernel(hops, numbers, by_slot, lag_rows, away, block_count, staged, *refs):
    sub_count = lax.axis_size("sub")
    hr_count = lax.axis_size("hr")
    pair_ref, owner_ref, turn_ref, offset_ref = refs[:4]
    blocks, outs = refs[4 : -2 - len(hops)], refs[-2 - len(hops) : -2]
    buf, sems = refs[-2:]
    width = buf.shape[3]
    span = buf.shape[4] // 2
    middle_lag = lag_rows % 2
    my_sub = lax.axis_index("sub")
    my_hr = lax.axis_index("hr")
    plan = slot_plan(pair_ref, owner_ref, block_count, staged)
    ends = []
    for number in numbers:
        if by_slot:
            ends.append(plan[number][1:])
            continue
        left, right = jnp.int32(-1), jnp.int32(-1)
        for known, left_here, right_here in plan:
            left = jnp.where(known == number, left_here, left)
            right = jnp.where(known == number, right_here, right)
        ends.append((left, right))

    def fetches(index, act):
        for side in range(2):
            for place in range(len(blocks) // sub_count):

                @pl.when(ends[index][side] == place)
                def _():
                    for step in range(sub_count):
                        act(
                            pltpu.make_async_copy(
                                blocks[place * sub_count + step],
                                buf.at[index, side, step],
                                sems.at[index, side, step],
                            )
                        )

    for index in range(len(numbers)):
        fetches(index, lambda copy: copy.start())

    for index in range(len(numbers)):

        @pl.when(ends[index][0] < 0)
        def _():
            for out in outs:
                out[:, index] = jnp.zeros((lag_rows, width, width), out.dtype)

        fetches(index, lambda copy: copy.wait())

        @pl.when(ends[index][0] >= 0)
        def _():
            total = None
            for step in range(sub_count):
                sub = lax.rem(my_sub + step, sub_count)
                real = buf[index, 0, step, :, :span]
                imag = buf[index, 0, step, :, span:]
                scaled_real, scaled_imag = [real] * middle_lag, [imag] * middle_lag
                for near in range(away):
                    cosine, sine, minus = (
                        offset_ref[sub, 3 * near + form : 3 * near + form + 1, :]
                        for form in range(3)
                    )
                    scaled_real += [real * cosine, imag * minus]
                    scaled_imag += [imag * cosine, real * sine]
                real = buf[index, 1, step, :, :span].astype(F32)
                imag = buf[index, 1, step, :, span:].astype(F32)
                turned_real, turned_imag = [], []
                for hop in hops:
                    group = lax.rem(my_hr + hop, hr_count) * sub_count + my_sub
                    cosine = turn_ref[sub, pl.ds(2 * group, 1), :]
                    sine = turn_ref[sub, pl.ds(2 * group + 1, 1), :]
                    turned_real.append((real * cosine + imag * sine).astype(BF16))
                    turned_imag.append((imag * cosine - real * sine).astype(BF16))
                for scaled, turned in ((scaled_real, turned_real), (scaled_imag, turned_imag)):
                    part = dot_nt(jnp.concatenate(scaled, axis=0), jnp.concatenate(turned, axis=0))
                    total = part if total is None else total + part
            for place, out in enumerate(outs):
                columns = slice(place * width, (place + 1) * width)
                if middle_lag:
                    out[lag_rows // 2, index] = total[:width, columns].astype(out.dtype)
                for near in range(away):
                    start = (middle_lag + 2 * near) * width
                    even = total[start : start + width, columns]
                    odd = total[start + width : start + 2 * width, columns]
                    below = (lag_rows - 1) // 2 - near - middle_lag
                    above = lag_rows - 1 - below
                    out[above, index] = (even + odd).astype(out.dtype)
                    out[below, index] = (even - odd).astype(out.dtype)


def join_kernel(stages, norming, block_count, staged, pair_ref, owner_ref, own_ref, *refs):
    out = refs[-1]
    for slot, (number, _, _) in enumerate(slot_plan(pair_ref, owner_ref, block_count, staged)):

        @pl.when(number < 0)
        def _():
            out[:, slot] = jnp.zeros(out.shape[:1] + out.shape[2:], out.dtype)

        taken = 0
        for numbers, count in stages:
            for place, known in enumerate(numbers):

                @pl.when(number == known)
                def _():
                    total = own_ref[:, slot]
                    for ref in refs[taken : taken + count]:
                        total += ref[:, place].astype(F32)
                    out[:, slot] = (total * norming).astype(out.dtype)

            taken += count


def on_device(spectra, pair_blocks, pair_owner, block_members):
    hour_count, sub_freqs, _, _ = spectra.shape
    block_count, width = block_members.shape
    sta_count, hr_count, sub_count = (lax.axis_size(axis) for axis in ("sta", "hr", "sub"))
    groups = hr_count * sub_count
    lag_rows = LAGS // groups
    norming = 1.0 / math.sqrt(hour_count * hr_count * sub_count * sub_freqs)
    pair_sides = pair_blocks.T
    turns, offsets, away = phase_tables(sub_count, sub_freqs, groups, lag_rows)

    owners_at_most = pair_owner.shape[0] - CAP + 1
    staged = owners_at_most == 2 and sta_count == REACH
    kept = min(REACH, owners_at_most)
    picked = pick_blocks(kept, staged, spectra, pair_sides, pair_owner, block_members)

    def halves(block):
        others = []
        for step in range(1, sub_count):
            swap = [((sub + step) % sub_count, sub) for sub in range(sub_count)]
            others.append(lax.ppermute(block, "sub", swap))
        return [block] + others

    def to_owners(reach, owners):
        pairs = [((owner + reach) % sta_count, owner) for owner in owners]
        return lax.ppermute(picked[reach], "sta", pairs)

    def first_stage(first, second, last, *picked):
        places = straight(first, second, last, sta_count, lambda hit, yes, no: yes if hit else no)
        direct = [reach for reach in range(1, REACH) if reach != last]
        straight_blocks = []
        for reach in sorted(direct, key=lambda reach: places[reach]):
            owners = [first] if reach == 1 else [first, second]
            pairs = [((owner + reach) % sta_count, owner) for owner in owners]
            straight_blocks.append(lax.ppermute(picked[reach], "sta", pairs))
        if last == 1:
            return *straight_blocks, picked[1], jnp.zeros_like(picked[1])
        relay = (first + 1) % sta_count
        relayed = lax.ppermute(picked[last], "sta", [((first + last) % sta_count, relay)])
        ring = jnp.where(lax.axis_index("sta") == relay, relayed, picked[1])
        aside = lax.ppermute(picked[last], "sta", [((second + last) % sta_count, second)])
        return *straight_blocks, ring, aside

    smem = pl.BlockSpec(memory_space=pltpu.SMEM)
    vmem = pl.BlockSpec(memory_space=pltpu.VMEM)
    hbm = pl.BlockSpec(memory_space=pltpu.HBM)
    row = picked[0].shape[1]
    versions = (lag_rows % 2 + 2 * away) * width

    def products(hops, numbers, by_slot, dtype, blocks, name):
        return pl.pallas_call(
            functools.partial(
                lag_kernel, hops, numbers, by_slot, lag_rows, away, block_count, staged
            ),
            out_shape=[jax.ShapeDtypeStruct((lag_rows, len(numbers), width, width), dtype)]
            * len(hops),
            in_specs=[smem, smem, vmem, vmem] + [hbm] * len(blocks),
            out_specs=[vmem] * len(hops),
            scratch_shapes=[
                pltpu.VMEM((len(numbers), 2, sub_count, width, row), BF16),
                pltpu.SemaphoreType.DMA((len(numbers), 2, sub_count)),
            ],
            compiler_params=pltpu.CompilerParams(vmem_limit_bytes=LAG_VMEM_LIMIT),
            cost_estimate=pl.CostEstimate(
                flops=2 * len(numbers) * len(hops) * versions * width * sub_count * row,
                bytes_accessed=4 * len(numbers) * sub_count * width * row,
                transcendentals=0,
            ),
            name=name,
        )(pair_sides, pair_owner, turns, offsets, *blocks)

    hops, slots = tuple(range(1, hr_count)), tuple(range(CAP))

    def sums(numbers, blocks, name):
        sent = products(hops, numbers, False, BF16, blocks, name)
        received = []
        for hop, part in zip(hops, sent):
            to_device = [(hr, (hr + hop) % hr_count) for hr in range(hr_count)]
            received.append(lax.ppermute(part, "hr", to_device))
        return sent, received

    own = halves(picked[0])
    if staged:
        cases = [
            (first, second, last)
            for first in range(sta_count)
            for second in range(sta_count)
            if second != first
            for last in range(1, REACH)
        ]
        steps = [functools.partial(first_stage, *case) for case in cases]
        near, far, ring, aside = lax.switch(picked[REACH][0], steps, *picked[:REACH])
        late = lax.ppermute(
            ring, "sta", [((home + 1) % sta_count, home) for home in range(sta_count)]
        )
        blocks = own + halves(near) + halves(far)
        early_sent, early = sums((0, 1), blocks, "lags_of_two")
        late, aside, _ = lax.optimization_barrier((late, aside, early_sent))
        blocks = blocks + halves(aside) + halves(late)
        _, third = sums((2,), blocks, "lags_of_third")
        (mine,) = products((0,), slots, True, F32, blocks, "lags_to_keep")
        more, mine = lax.optimization_barrier((picked[REACH + 1], mine))
        blank = jnp.zeros((lag_rows, 1, width, width), BF16)
        fourth = lax.switch(
            more[0],
            [
                lambda *blocks: [blank] * len(hops),
                lambda *blocks: sums((3,), blocks, "lags_of_fourth")[1],
            ],
            *blocks,
        )
        stages, received = [((0, 1), len(hops)), ((2,), len(hops)), ((3,), len(hops))], [
            *early, *third, *fourth
        ]
    else:
        blocks = own
        for reach in range(1, REACH):
            blocks = blocks + halves(to_owners(reach, range(sta_count)))
        _, received = sums(slots, blocks, "lags_to_send")
        (mine,) = products((0,), slots, True, F32, blocks, "lags_to_keep")
        stages = [(slots, len(hops))]
    return pl.pallas_call(
        functools.partial(join_kernel, stages, norming, block_count, staged),
        out_shape=jax.ShapeDtypeStruct((lag_rows, CAP, width, width), BF16),
        in_specs=[smem, smem] + [vmem] * (1 + len(received)),
        out_specs=vmem,
        compiler_params=pltpu.CompilerParams(vmem_limit_bytes=LAG_VMEM_LIMIT),
        name="join",
    )(pair_sides, pair_owner, mine, *received)


def solution(mesh):
    placed = (P(("grp", "hr"), "sub", None, "sta"), P(), P(), P("sta", None))
    return jax.shard_map(
        on_device,
        mesh=mesh,
        in_specs=placed,
        out_specs=P(("grp", "hr", "sub"), "sta", None, None),
        check_vma=False,
    )
```

```python
import functools
import itertools
import math

import jax
import jax.numpy as jnp
import numpy as np
from jax import lax
from jax.experimental import pallas as pl
from jax.experimental.pallas import tpu as pltpu
from jax.sharding import PartitionSpec as P

BAND = 50
LAGS = 16
CAP = 3
REACH = 4
COPIES = 2
EPSILON = 1e-05
LANES = 128
F32 = jnp.float32
BF16 = jnp.bfloat16
PICK_VMEM_LIMIT = 59 * 1024 * 1024
LAG_VMEM_LIMIT = 32 * 1024 * 1024

NT = (((1,), (1,)), ((), ()))


def dot_nt(left, right):
    return lax.dot_general(left, right, NT, preferred_element_type=F32)


def iota(shape, dim):
    return lax.broadcasted_iota(jnp.int32, shape, dim)


def send_keys(first, second, sta_count, where):
    keys = [0]
    for reach in range(2, REACH):
        first_sends = (first - second - reach) % sta_count == 0
        keys.append(where(first_sends, REACH, 0) + reach)
    return keys


def read_pairs(pair_ref, owner_ref, block_count):
    pairs = []
    for pair in range(owner_ref.shape[0]):
        blocks = [pair_ref[side, pair] for side in range(2)]
        pairs.append((owner_ref[pair], blocks, [lax.div(block, block_count) for block in blocks]))
    return pairs


def case_of(pairs, sta_count):
    first = second = needs = jnp.int32(0)
    for owner, _, homes in pairs:
        count = jnp.int32(0)
        for other, _, _ in pairs:
            count = count + (other == owner).astype(jnp.int32)
        ends = [lax.rem(home - owner + sta_count, sta_count) for home in homes]
        first = jnp.where(count == CAP, owner, first)
        second = jnp.where(count < CAP, owner, second)
        needs = jnp.where(count < CAP, (1 << ends[0]) | (1 << ends[1]), needs)
    return first, second, case_number(first, second, needs, sta_count)


def pick_kernel(kept, branched, sta_axis, pair_hbm, owner_hbm, member_hbm, case_hbm, x_ref, *rest):
    outs = rest[:REACH]
    pair_ref, owner_ref, member_ref, case_ref, number_ref, x_buf, y_buf, white_buf, sems = rest[
        REACH + branched :
    ]
    if branched:
        branch_copy = pltpu.make_async_copy(number_ref, rest[REACH], sems.at[COPIES + 4])
    freqs, tiles = x_buf.shape[0], x_buf.shape[2] // LANES
    block_count, width = member_ref.shape
    rows = y_buf.shape[0]
    chunks = rows // (2 * LANES)

    def fetch(part):
        run = pl.ds(part * (freqs // COPIES), freqs // COPIES)
        return pltpu.make_async_copy(x_ref.at[0, run], x_buf.at[run], sems.at[part])

    small = [
        pltpu.make_async_copy(source, target, sems.at[COPIES + index])
        for index, (source, target) in enumerate(
            (
                (pair_hbm, pair_ref),
                (owner_hbm, owner_ref),
                (member_hbm, member_ref),
                (case_hbm, case_ref),
            )
        )
    ]
    for copy in small:
        copy.start()
    for part in range(COPIES):
        fetch(part).start()

    def bands(shape, part_dim):
        part, place = iota(shape, part_dim), iota(shape, 1 - part_dim)
        low = (place % 16) * (2 * BAND)
        hit = (part >= low) & (part < low + 2 * BAND) & (part < 2 * freqs) & (place < 48)
        return jnp.where(hit, 1.0, 0.0).astype(BF16)

    gather_bands, spread_bands = bands((48, rows), 1), bands((rows, LANES), 0)
    row, col = iota((2 * LANES, 2 * LANES), 0), iota((2 * LANES, 2 * LANES), 1)
    split = jnp.where(row == 2 * (col % LANES) + col // LANES, 1.0, 0.0).astype(BF16)
    y_buf[2 * freqs :] = jnp.zeros((rows - 2 * freqs, kept * width), F32)
    for copy in small:
        copy.wait()

    my_sta = lax.axis_index(sta_axis)
    sta_count = lax.axis_size(sta_axis)
    pairs = read_pairs(pair_ref, owner_ref, block_count)
    found, wanted = jnp.int32(0), []
    for reach in range(REACH):
        owner = lax.rem(my_sta - reach + REACH * sta_count, sta_count)
        chosen = jnp.int32(-1)
        for pair_owner, blocks, homes in pairs:
            for block, home in zip(blocks, homes):
                hit = (pair_owner == owner) & (home == my_sta)
                chosen = jnp.where(hit, lax.rem(block, block_count), chosen)
        wanted.append((found, chosen))
        found = found + (chosen >= 0).astype(jnp.int32)
    places, station = [], []
    for place in range(kept):
        reach_here, block_here = jnp.int32(-1), jnp.int32(0)
        for reach, (rank, chosen) in enumerate(wanted):
            hit = (rank == place) & (chosen >= 0)
            reach_here = jnp.where(hit, reach, reach_here)
            block_here = jnp.where(hit, chosen, block_here)
        places.append(reach_here)
        station.append(member_ref[pl.ds(block_here, 1), :])
    station = jnp.concatenate(station, axis=1)
    hot = jnp.where(station == iota((tiles * LANES, kept * width), 0), 1.0, 0.0).astype(BF16)

    if branched:
        number_ref[0] = case_ref[case_of(pairs, sta_count)[2]]
        branch_copy.start()

    for part in range(COPIES):
        fetch(part).wait()
    x = jnp.concatenate(
        [
            x_buf[:, :, tile * LANES : (tile + 1) * LANES].reshape(2 * freqs, LANES)
            for tile in range(tiles)
        ],
        axis=1,
    )
    y_buf[: 2 * freqs] = jnp.dot(x, hot, preferred_element_type=F32)

    values = y_buf[...]
    square = values * values
    high = square.astype(BF16)
    low = (square - high.astype(F32)).astype(BF16)
    power = jnp.dot(gather_bands, high, preferred_element_type=F32)
    power += jnp.dot(gather_bands, low, preferred_element_type=F32)
    scale = lax.rsqrt(power * (1.0 / (2 * BAND)) + EPSILON)
    high = scale.astype(BF16).astype(F32)
    mid = (scale - high).astype(BF16).astype(F32)
    low = scale - high - mid
    third = iota(scale.shape, 0) // 16
    pieces = jnp.where(third == 0, high, jnp.where(third == 1, mid, low))
    pieces = jnp.concatenate(
        [pieces, jnp.zeros((LANES - pieces.shape[0], pieces.shape[1]), F32)], axis=0
    ).astype(BF16)
    white = y_buf[...] * jnp.dot(spread_bands, pieces, preferred_element_type=F32)
    white = white.astype(BF16)
    parted = []
    for chunk in range(chunks):
        mixed = white[chunk * 2 * LANES : (chunk + 1) * 2 * LANES]
        part = lax.dot_general(
            mixed, split, (((0,), (0,)), ((), ())), preferred_element_type=F32
        )
        parted.append(part.astype(BF16))
    white_buf[...] = jnp.concatenate(
        [part[:, :LANES] for part in parted] + [part[:, LANES:] for part in parted], axis=1
    )
    for place, reach_here in enumerate(places):
        for reach in range(REACH):

            @pl.when(reach_here == reach)
            def _():
                outs[reach][...] = white_buf[place * width : (place + 1) * width]

    if branched:
        branch_copy.wait()


def pick_blocks(kept, branched, spectra, pair_sides, pair_owner, block_members, case_table):
    _, freqs, parts, stations = spectra.shape
    block_count, width = block_members.shape
    columns = -(-freqs // LANES) * 2 * LANES
    rows = kept * width
    vmem = pl.BlockSpec(memory_space=pltpu.VMEM)
    out_shape = [jax.ShapeDtypeStruct((width, columns), BF16)] * REACH
    out_shape += [jax.ShapeDtypeStruct((1,), jnp.int32)] * branched
    return pl.pallas_call(
        functools.partial(pick_kernel, kept, branched, "sta"),
        out_shape=out_shape,
        in_specs=[pl.BlockSpec(memory_space=pltpu.HBM)] * 5,
        out_specs=[vmem] * REACH + [pl.BlockSpec(memory_space=pltpu.HBM)] * branched,
        scratch_shapes=[
            pltpu.SMEM(pair_sides.shape, jnp.int32),
            pltpu.SMEM(pair_owner.shape, jnp.int32),
            pltpu.VMEM(block_members.shape, jnp.int32),
            pltpu.SMEM(case_table.shape, jnp.int32),
            pltpu.SMEM((1,), jnp.int32),
            pltpu.VMEM((freqs, parts, stations), BF16),
            pltpu.VMEM((columns, rows), F32),
            pltpu.VMEM((rows, columns), BF16),
            pltpu.SemaphoreType.DMA((COPIES + 5,)),
        ],
        compiler_params=pltpu.CompilerParams(vmem_limit_bytes=PICK_VMEM_LIMIT),
        cost_estimate=pl.CostEstimate(
            flops=2 * rows * stations * freqs * parts,
            bytes_accessed=2 * spectra.size + 4 * rows * columns,
            transcendentals=0,
        ),
        name="pick_and_whiten",
    )(pair_sides, pair_owner, block_members, case_table, spectra)


def case_number(first, second, needs, sta_count):
    return (first * sta_count + second) * (1 << (REACH - 1)) + needs // 2


def routes(sta_count):
    def load(first, second, sent):
        links = {}
        flows = [((home + 1) % sta_count, home) for home in range(sta_count)]
        flows += [((first + reach) % sta_count, first) for reach in range(2, REACH)]
        flows += [((second + reach) % sta_count, second) for reach in sent]
        for source, owner in flows:
            step = 1 if owner > source else -1
            for place in range(source, owner, step):
                links[place, step] = links.get((place, step), 0) + 1
        return max(links.values())

    far = range(2, REACH)
    sets = [sent for count in range(len(far), -1, -1) for sent in itertools.combinations(far, count)]
    branches = []
    cases = [0] * case_number(sta_count, 0, 0, sta_count)
    for first, second in itertools.permutations(range(sta_count), 2):
        for named in itertools.combinations(range(REACH), 2):
            fits = [sent for sent in sets if set(named) - {0, 1} <= set(sent)]
            branch = (first, second, min(fits, key=lambda sent: load(first, second, sent)))
            if branch not in branches:
                branches.append(branch)
            needs = sum(1 << reach for reach in named)
            cases[case_number(first, second, needs, sta_count)] = branches.index(branch)
    return branches, cases


def phase_tables(sub_count, sub_freqs, groups, lag_rows):
    chunks = -(-sub_freqs // LANES)
    total = sub_count * sub_freqs
    freq = np.arange(total, dtype=np.int64).reshape(sub_count, 1, sub_freqs)
    middle = [2 * (group * lag_rows - LAGS // 2) + lag_rows - 1 for group in range(groups)]
    away = [step for step in range(1, lag_rows) if step % 2 != lag_rows % 2]

    def table(twice, forms, tile, dtype):
        twice = np.array(twice or [0], dtype=np.int64).reshape(1, -1, 1)
        angle = np.mod(freq * twice, 2 * total) * (math.pi / total)
        rows = np.stack([form(angle) for form in forms], axis=2)
        rows = rows.reshape(sub_count, -1, sub_freqs)
        pad = ((0, 0), (0, -rows.shape[1] % tile), (0, chunks * LANES - sub_freqs))
        return np.pad(rows, pad).astype(np.float32).astype(dtype)

    turns = table(middle, (np.cos, np.sin), 8, np.float32)
    offsets = table(away, (np.cos, np.sin, lambda angle: -np.sin(angle)), 16, BF16)
    return turns, offsets, len(away)


def lag_kernel(hops, slots, lag_rows, away, block_count, branched, *refs):
    sub_count = lax.axis_size("sub")
    hr_count = lax.axis_size("hr")
    pair_ref, owner_ref, turn_ref, offset_ref = refs[:4]
    blocks, outs = refs[4 : -2 - len(hops)], refs[-2 - len(hops) : -2]
    buf, sems = refs[-2:]
    width = buf.shape[3]
    span = buf.shape[4] // 2
    middle_lag = lag_rows % 2
    my_sub = lax.axis_index("sub")
    my_hr = lax.axis_index("hr")
    my_sta = lax.axis_index("sta")
    sta_count = lax.axis_size("sta")

    pairs = read_pairs(pair_ref, owner_ref, block_count)
    order = [jnp.int32(reach) for reach in range(REACH)]
    if branched:
        first, second, _ = case_of(pairs, sta_count)
        keys = send_keys(first, second, sta_count, jnp.where)
        for reach, key in enumerate(keys):
            order[1 + reach] = 1 + sum(jnp.int32(other < key) for other in keys)
    owned = []
    for owner, _, homes in pairs:
        places = []
        for home in homes:
            reach_here = lax.rem(home - my_sta + sta_count, sta_count)
            place_here = order[0]
            for reach in range(1, REACH):
                place_here = jnp.where(reach_here == reach, order[reach], place_here)
            places.append(place_here)
        owned.append((owner == my_sta, places))
    ends = []
    for slot in slots:
        count = jnp.int32(0)
        slot_ends = [jnp.int32(-1)] * 2
        for mine, places in owned:
            hit = mine & (count == slot)
            count = count + mine.astype(jnp.int32)
            slot_ends = [jnp.where(hit, new, old) for new, old in zip(places, slot_ends)]
        ends.append(slot_ends)

    def fetches(index, act):
        for side in range(2):
            for place in range(REACH):

                @pl.when(ends[index][side] == place)
                def _():
                    for step in range(sub_count):
                        act(
                            pltpu.make_async_copy(
                                blocks[place * sub_count + step],
                                buf.at[index, side, step],
                                sems.at[index, side, step],
                            )
                        )

    for index in range(len(slots)):
        fetches(index, lambda copy: copy.start())

    for index in range(len(slots)):

        @pl.when(ends[index][0] < 0)
        def _():
            for out in outs:
                out[:, index] = jnp.zeros((lag_rows, width, width), out.dtype)

        fetches(index, lambda copy: copy.wait())

        @pl.when(ends[index][0] >= 0)
        def _():
            total = None
            for step in range(sub_count):
                sub = lax.rem(my_sub + step, sub_count)
                real = buf[index, 0, step, :, :span]
                imag = buf[index, 0, step, :, span:]
                scaled_real, scaled_imag = [real] * middle_lag, [imag] * middle_lag
                for near in range(away):
                    cosine, sine, minus = (
                        offset_ref[sub, 3 * near + form : 3 * near + form + 1, :]
                        for form in range(3)
                    )
                    scaled_real += [real * cosine, imag * minus]
                    scaled_imag += [imag * cosine, real * sine]
                real = buf[index, 1, step, :, :span].astype(F32)
                imag = buf[index, 1, step, :, span:].astype(F32)
                turned_real, turned_imag = [], []
                for hop in hops:
                    group = lax.rem(my_hr + hop, hr_count) * sub_count + my_sub
                    cosine = turn_ref[sub, pl.ds(2 * group, 1), :]
                    sine = turn_ref[sub, pl.ds(2 * group + 1, 1), :]
                    turned_real.append((real * cosine + imag * sine).astype(BF16))
                    turned_imag.append((imag * cosine - real * sine).astype(BF16))
                for scaled, turned in ((scaled_real, turned_real), (scaled_imag, turned_imag)):
                    part = dot_nt(jnp.concatenate(scaled, axis=0), jnp.concatenate(turned, axis=0))
                    total = part if total is None else total + part
            for place, out in enumerate(outs):
                columns = slice(place * width, (place + 1) * width)
                if middle_lag:
                    out[lag_rows // 2, index] = total[:width, columns].astype(out.dtype)
                for near in range(away):
                    start = (middle_lag + 2 * near) * width
                    even = total[start : start + width, columns]
                    odd = total[start + width : start + 2 * width, columns]
                    below = (lag_rows - 1) // 2 - near - middle_lag
                    above = lag_rows - 1 - below
                    out[above, index] = (even + odd).astype(out.dtype)
                    out[below, index] = (even - odd).astype(out.dtype)


def on_device(spectra, pair_blocks, pair_owner, block_members):
    hour_count, sub_freqs, _, _ = spectra.shape
    block_count, width = block_members.shape
    sta_count, hr_count, sub_count = (lax.axis_size(axis) for axis in ("sta", "hr", "sub"))
    groups = hr_count * sub_count
    lag_rows = LAGS // groups
    norming = 1.0 / math.sqrt(hour_count * hr_count * sub_count * sub_freqs)
    pair_sides = pair_blocks.T
    turns, offsets, away = phase_tables(sub_count, sub_freqs, groups, lag_rows)

    owners_at_most = pair_owner.shape[0] - CAP + 1
    branched = owners_at_most == 2 and sta_count == REACH
    kept = min(REACH, owners_at_most)
    branches, cases = routes(sta_count) if branched else ([], [])
    case_table = jnp.asarray(np.array(cases or [0], dtype=np.int32))
    picked = pick_blocks(
        kept, branched, spectra, pair_sides, pair_owner, block_members, case_table
    )

    def exchange(owners_of, order, *picked):
        arrived = [picked[0]]
        for reach in order:
            to_owner = [((owner + reach) % sta_count, owner) for owner in owners_of[reach - 1]]
            arrived.append(lax.ppermute(picked[reach], "sta", to_owner))
        blocks = []
        for block in arrived:
            blocks.append(block)
            for step in range(1, sub_count):
                swap = [((sub + step) % sub_count, sub) for sub in range(sub_count)]
                blocks.append(lax.ppermute(block, "sub", swap))
        return blocks

    if branched:
        steps = []
        for first, second, sent in branches:
            owners_of = [range(sta_count)] + [
                (first, second) if reach in sent else (first,) for reach in range(2, REACH)
            ]
            keys = send_keys(first, second, sta_count, lambda hit, yes, no: yes if hit else no)
            order = sorted(range(1, REACH), key=lambda reach: keys[reach - 1])
            steps.append(functools.partial(exchange, owners_of, order))
        blocks = lax.switch(picked[REACH][0], steps, *picked[:REACH])
    else:
        blocks = exchange([range(sta_count)] * (REACH - 1), range(1, REACH), *picked[:REACH])

    smem = pl.BlockSpec(memory_space=pltpu.SMEM)
    vmem = pl.BlockSpec(memory_space=pltpu.VMEM)
    hbm = pl.BlockSpec(memory_space=pltpu.HBM)
    row = picked[0].shape[1]
    versions = (lag_rows % 2 + 2 * away) * width

    def products(hops, slots, dtype, name):
        return pl.pallas_call(
            functools.partial(
                lag_kernel, hops, slots, lag_rows, away, block_count, branched
            ),
            out_shape=[jax.ShapeDtypeStruct((lag_rows, len(slots), width, width), dtype)]
            * len(hops),
            in_specs=[smem, smem, vmem, vmem] + [hbm] * len(blocks),
            out_specs=[vmem] * len(hops),
            scratch_shapes=[
                pltpu.VMEM((len(slots), 2, sub_count, width, row), BF16),
                pltpu.SemaphoreType.DMA((len(slots), 2, sub_count)),
            ],
            compiler_params=pltpu.CompilerParams(vmem_limit_bytes=LAG_VMEM_LIMIT),
            cost_estimate=pl.CostEstimate(
                flops=2 * len(slots) * len(hops) * versions * width * sub_count * row,
                bytes_accessed=4 * len(slots) * sub_count * width * row,
                transcendentals=0,
            ),
            name=name,
        )(pair_sides, pair_owner, turns, offsets, *blocks)

    hops, slots = tuple(range(1, hr_count)), tuple(range(CAP))
    sent = products(hops, slots, BF16, "lags_to_send")
    received = []
    for hop, part in zip(hops, sent):
        to_device = [(hr, (hr + hop) % hr_count) for hr in range(hr_count)]
        received.append(lax.ppermute(part, "hr", to_device))
    (summed,) = products((0,), slots, F32, "lags_to_keep")
    for part in received:
        summed = summed + part.astype(F32)
    return (summed * norming).astype(BF16)


def solution(mesh):
    placed = (P(("grp", "hr"), "sub", None, "sta"), P(), P(), P("sta", None))
    return jax.shard_map(
        on_device,
        mesh=mesh,
        in_specs=placed,
        out_specs=P(("grp", "hr", "sub"), "sta", None, None),
        check_vma=False,
    )
```

```python
import functools
import itertools
import math

import jax
import jax.numpy as jnp
import numpy as np
from jax import lax
from jax.experimental import pallas as pl
from jax.experimental.pallas import tpu as pltpu
from jax.sharding import PartitionSpec as P

BAND = 50
LAGS = 16
CAP = 3
REACH = 4
COPIES = 2
EPSILON = 1e-05
LANES = 128
F32 = jnp.float32
BF16 = jnp.bfloat16
PICK_VMEM_LIMIT = 59 * 1024 * 1024
LAG_VMEM_LIMIT = 32 * 1024 * 1024

NT = (((1,), (1,)), ((), ()))


def dot_nt(left, right):
    return lax.dot_general(left, right, NT, preferred_element_type=F32)


def iota(shape, dim):
    return lax.broadcasted_iota(jnp.int32, shape, dim)


def send_keys(first, second, sta_count, where):
    keys = []
    for reach in range(1, REACH):
        distance = abs((first + reach) % sta_count - first)
        alone = (first - second - reach) % sta_count == 0
        keys.append((2 * distance + where(alone, 0, 1)) * REACH + reach)
    return keys


def read_pairs(pair_ref, owner_ref, block_count):
    pairs = []
    for pair in range(owner_ref.shape[0]):
        blocks = [pair_ref[side, pair] for side in range(2)]
        pairs.append((owner_ref[pair], blocks, [lax.div(block, block_count) for block in blocks]))
    return pairs


def case_of(pairs, sta_count):
    first = second = needs = jnp.int32(0)
    for owner, _, homes in pairs:
        count = jnp.int32(0)
        for other, _, _ in pairs:
            count = count + (other == owner).astype(jnp.int32)
        ends = [lax.rem(home - owner + sta_count, sta_count) for home in homes]
        first = jnp.where(count == CAP, owner, first)
        second = jnp.where(count < CAP, owner, second)
        needs = jnp.where(count < CAP, (1 << ends[0]) | (1 << ends[1]), needs)
    return first, second, case_number(first, second, needs, sta_count)


def pick_kernel(kept, branched, sta_axis, pair_hbm, owner_hbm, member_hbm, case_hbm, x_ref, *rest):
    outs = rest[:REACH]
    pair_ref, owner_ref, member_ref, case_ref, number_ref, x_buf, y_buf, white_buf, sems = rest[
        REACH + branched :
    ]
    if branched:
        branch_copy = pltpu.make_async_copy(number_ref, rest[REACH], sems.at[COPIES + 4])
    freqs, tiles = x_buf.shape[0], x_buf.shape[2] // LANES
    block_count, width = member_ref.shape
    rows = y_buf.shape[0]
    chunks = rows // (2 * LANES)

    def fetch(part):
        run = pl.ds(part * (freqs // COPIES), freqs // COPIES)
        return pltpu.make_async_copy(x_ref.at[0, run], x_buf.at[run], sems.at[part])

    small = [
        pltpu.make_async_copy(source, target, sems.at[COPIES + index])
        for index, (source, target) in enumerate(
            (
                (pair_hbm, pair_ref),
                (owner_hbm, owner_ref),
                (member_hbm, member_ref),
                (case_hbm, case_ref),
            )
        )
    ]
    for copy in small:
        copy.start()
    for part in range(COPIES):
        fetch(part).start()

    def bands(shape, part_dim):
        part, place = iota(shape, part_dim), iota(shape, 1 - part_dim)
        low = (place % 16) * (2 * BAND)
        hit = (part >= low) & (part < low + 2 * BAND) & (part < 2 * freqs) & (place < 48)
        return jnp.where(hit, 1.0, 0.0).astype(BF16)

    gather_bands, spread_bands = bands((48, rows), 1), bands((rows, LANES), 0)
    row, col = iota((2 * LANES, 2 * LANES), 0), iota((2 * LANES, 2 * LANES), 1)
    split = jnp.where(row == 2 * (col % LANES) + col // LANES, 1.0, 0.0).astype(BF16)
    y_buf[2 * freqs :] = jnp.zeros((rows - 2 * freqs, kept * width), F32)
    for copy in small:
        copy.wait()

    my_sta = lax.axis_index(sta_axis)
    sta_count = lax.axis_size(sta_axis)
    pairs = read_pairs(pair_ref, owner_ref, block_count)
    found, wanted = jnp.int32(0), []
    for reach in range(REACH):
        owner = lax.rem(my_sta - reach + REACH * sta_count, sta_count)
        chosen = jnp.int32(-1)
        for pair_owner, blocks, homes in pairs:
            for block, home in zip(blocks, homes):
                hit = (pair_owner == owner) & (home == my_sta)
                chosen = jnp.where(hit, lax.rem(block, block_count), chosen)
        wanted.append((found, chosen))
        found = found + (chosen >= 0).astype(jnp.int32)
    places, station = [], []
    for place in range(kept):
        reach_here, block_here = jnp.int32(-1), jnp.int32(0)
        for reach, (rank, chosen) in enumerate(wanted):
            hit = (rank == place) & (chosen >= 0)
            reach_here = jnp.where(hit, reach, reach_here)
            block_here = jnp.where(hit, chosen, block_here)
        places.append(reach_here)
        station.append(member_ref[pl.ds(block_here, 1), :])
    station = jnp.concatenate(station, axis=1)
    hot = jnp.where(station == iota((tiles * LANES, kept * width), 0), 1.0, 0.0).astype(BF16)

    if branched:
        number_ref[0] = case_ref[case_of(pairs, sta_count)[2]]
        branch_copy.start()

    for part in range(COPIES):
        fetch(part).wait()
    x = jnp.concatenate(
        [
            x_buf[:, :, tile * LANES : (tile + 1) * LANES].reshape(2 * freqs, LANES)
            for tile in range(tiles)
        ],
        axis=1,
    )
    y_buf[: 2 * freqs] = jnp.dot(x, hot, preferred_element_type=F32)

    values = y_buf[...]
    square = values * values
    high = square.astype(BF16)
    low = (square - high.astype(F32)).astype(BF16)
    power = jnp.dot(gather_bands, high, preferred_element_type=F32)
    power += jnp.dot(gather_bands, low, preferred_element_type=F32)
    scale = lax.rsqrt(power * (1.0 / (2 * BAND)) + EPSILON)
    high = scale.astype(BF16).astype(F32)
    mid = (scale - high).astype(BF16).astype(F32)
    low = scale - high - mid
    third = iota(scale.shape, 0) // 16
    pieces = jnp.where(third == 0, high, jnp.where(third == 1, mid, low))
    pieces = jnp.concatenate(
        [pieces, jnp.zeros((LANES - pieces.shape[0], pieces.shape[1]), F32)], axis=0
    ).astype(BF16)
    white = y_buf[...] * jnp.dot(spread_bands, pieces, preferred_element_type=F32)
    white = white.astype(BF16)
    parted = []
    for chunk in range(chunks):
        mixed = white[chunk * 2 * LANES : (chunk + 1) * 2 * LANES]
        part = lax.dot_general(
            mixed, split, (((0,), (0,)), ((), ())), preferred_element_type=F32
        )
        parted.append(part.astype(BF16))
    white_buf[...] = jnp.concatenate(
        [part[:, :LANES] for part in parted] + [part[:, LANES:] for part in parted], axis=1
    )
    for place, reach_here in enumerate(places):
        for reach in range(REACH):

            @pl.when(reach_here == reach)
            def _():
                outs[reach][...] = white_buf[place * width : (place + 1) * width]

    if branched:
        branch_copy.wait()


def pick_blocks(kept, branched, spectra, pair_sides, pair_owner, block_members, case_table):
    _, freqs, parts, stations = spectra.shape
    block_count, width = block_members.shape
    columns = -(-freqs // LANES) * 2 * LANES
    rows = kept * width
    vmem = pl.BlockSpec(memory_space=pltpu.VMEM)
    out_shape = [jax.ShapeDtypeStruct((width, columns), BF16)] * REACH
    out_shape += [jax.ShapeDtypeStruct((1,), jnp.int32)] * branched
    return pl.pallas_call(
        functools.partial(pick_kernel, kept, branched, "sta"),
        out_shape=out_shape,
        in_specs=[pl.BlockSpec(memory_space=pltpu.HBM)] * 5,
        out_specs=[vmem] * REACH + [pl.BlockSpec(memory_space=pltpu.HBM)] * branched,
        scratch_shapes=[
            pltpu.SMEM(pair_sides.shape, jnp.int32),
            pltpu.SMEM(pair_owner.shape, jnp.int32),
            pltpu.VMEM(block_members.shape, jnp.int32),
            pltpu.SMEM(case_table.shape, jnp.int32),
            pltpu.SMEM((1,), jnp.int32),
            pltpu.VMEM((freqs, parts, stations), BF16),
            pltpu.VMEM((columns, rows), F32),
            pltpu.VMEM((rows, columns), BF16),
            pltpu.SemaphoreType.DMA((COPIES + 5,)),
        ],
        compiler_params=pltpu.CompilerParams(vmem_limit_bytes=PICK_VMEM_LIMIT),
        cost_estimate=pl.CostEstimate(
            flops=2 * rows * stations * freqs * parts,
            bytes_accessed=2 * spectra.size + 4 * rows * columns,
            transcendentals=0,
        ),
        name="pick_and_whiten",
    )(pair_sides, pair_owner, block_members, case_table, spectra)


def case_number(first, second, needs, sta_count):
    return (first * sta_count + second) * (1 << (REACH - 1)) + needs // 2


def routes(sta_count):
    def load(first, second, sent):
        links = {}
        flows = [((first + reach) % sta_count, first) for reach in range(1, REACH)]
        flows += [((second + reach) % sta_count, second) for reach in sent]
        for source, owner in flows:
            step = 1 if owner > source else -1
            for place in range(source, owner, step):
                links[place, step] = links.get((place, step), 0) + 1
        return max(links.values())

    every = range(1, REACH)
    sets = [every, *itertools.combinations(every, len(every) - 1)]
    branches = []
    cases = [0] * case_number(sta_count, 0, 0, sta_count)
    for first, second in itertools.permutations(range(sta_count), 2):
        own = (first - second) % sta_count
        for named in itertools.combinations(range(REACH), 2):
            fits = [sent for sent in sets if set(named) - {0} <= set(sent)]
            fits = [sent for sent in fits if own in named or own not in sent] or fits
            branch = (first, second, min(fits, key=lambda sent: load(first, second, sent)))
            if branch not in branches:
                branches.append(branch)
            needs = sum(1 << reach for reach in named)
            cases[case_number(first, second, needs, sta_count)] = branches.index(branch)
    return branches, cases


def phase_tables(sub_count, sub_freqs, groups, lag_rows):
    chunks = -(-sub_freqs // LANES)
    total = sub_count * sub_freqs
    freq = np.arange(total, dtype=np.int64).reshape(sub_count, 1, sub_freqs)
    middle = [2 * (group * lag_rows - LAGS // 2) + lag_rows - 1 for group in range(groups)]
    away = [step for step in range(1, lag_rows) if step % 2 != lag_rows % 2]

    def table(twice, forms, tile, dtype):
        twice = np.array(twice or [0], dtype=np.int64).reshape(1, -1, 1)
        angle = np.mod(freq * twice, 2 * total) * (math.pi / total)
        rows = np.stack([form(angle) for form in forms], axis=2)
        rows = rows.reshape(sub_count, -1, sub_freqs)
        pad = ((0, 0), (0, -rows.shape[1] % tile), (0, chunks * LANES - sub_freqs))
        return np.pad(rows, pad).astype(np.float32).astype(dtype)

    turns = table(middle, (np.cos, np.sin), 8, np.float32)
    offsets = table(away, (np.cos, np.sin, lambda angle: -np.sin(angle)), 16, BF16)
    return turns, offsets, len(away)


def lag_kernel(hops, slots, lag_rows, away, block_count, branched, *refs):
    sub_count = lax.axis_size("sub")
    hr_count = lax.axis_size("hr")
    pair_ref, owner_ref, turn_ref, offset_ref = refs[:4]
    blocks, outs = refs[4 : -2 - len(hops)], refs[-2 - len(hops) : -2]
    buf, sems = refs[-2:]
    width = buf.shape[3]
    span = buf.shape[4] // 2
    middle_lag = lag_rows % 2
    my_sub = lax.axis_index("sub")
    my_hr = lax.axis_index("hr")
    my_sta = lax.axis_index("sta")
    sta_count = lax.axis_size("sta")

    pairs = read_pairs(pair_ref, owner_ref, block_count)
    order = [jnp.int32(reach) for reach in range(REACH)]
    if branched:
        first, second, _ = case_of(pairs, sta_count)
        keys = send_keys(first, second, sta_count, jnp.where)
        for reach, key in enumerate(keys):
            order[1 + reach] = 1 + sum(jnp.int32(other < key) for other in keys)
    owned = []
    for owner, _, homes in pairs:
        places = []
        for home in homes:
            reach_here = lax.rem(home - my_sta + sta_count, sta_count)
            place_here = order[0]
            for reach in range(1, REACH):
                place_here = jnp.where(reach_here == reach, order[reach], place_here)
            places.append(place_here)
        owned.append((owner == my_sta, places))
    ends = []
    for slot in slots:
        count = jnp.int32(0)
        slot_ends = [jnp.int32(-1)] * 2
        for mine, places in owned:
            hit = mine & (count == slot)
            count = count + mine.astype(jnp.int32)
            slot_ends = [jnp.where(hit, new, old) for new, old in zip(places, slot_ends)]
        ends.append(slot_ends)

    def fetches(index, act):
        for side in range(2):
            for place in range(REACH):

                @pl.when(ends[index][side] == place)
                def _():
                    for step in range(sub_count):
                        act(
                            pltpu.make_async_copy(
                                blocks[place * sub_count + step],
                                buf.at[index, side, step],
                                sems.at[index, side, step],
                            )
                        )

    for index in range(len(slots)):
        fetches(index, lambda copy: copy.start())

    for index in range(len(slots)):

        @pl.when(ends[index][0] < 0)
        def _():
            for out in outs:
                out[:, index] = jnp.zeros((lag_rows, width, width), out.dtype)

        fetches(index, lambda copy: copy.wait())

        @pl.when(ends[index][0] >= 0)
        def _():
            total = None
            for step in range(sub_count):
                sub = lax.rem(my_sub + step, sub_count)
                real = buf[index, 0, step, :, :span]
                imag = buf[index, 0, step, :, span:]
                scaled_real, scaled_imag = [real] * middle_lag, [imag] * middle_lag
                for near in range(away):
                    cosine, sine, minus = (
                        offset_ref[sub, 3 * near + form : 3 * near + form + 1, :]
                        for form in range(3)
                    )
                    scaled_real += [real * cosine, imag * minus]
                    scaled_imag += [imag * cosine, real * sine]
                real = buf[index, 1, step, :, :span].astype(F32)
                imag = buf[index, 1, step, :, span:].astype(F32)
                turned_real, turned_imag = [], []
                for hop in hops:
                    group = lax.rem(my_hr + hop, hr_count) * sub_count + my_sub
                    cosine = turn_ref[sub, pl.ds(2 * group, 1), :]
                    sine = turn_ref[sub, pl.ds(2 * group + 1, 1), :]
                    turned_real.append((real * cosine + imag * sine).astype(BF16))
                    turned_imag.append((imag * cosine - real * sine).astype(BF16))
                for scaled, turned in ((scaled_real, turned_real), (scaled_imag, turned_imag)):
                    part = dot_nt(jnp.concatenate(scaled, axis=0), jnp.concatenate(turned, axis=0))
                    total = part if total is None else total + part
            for place, out in enumerate(outs):
                columns = slice(place * width, (place + 1) * width)
                if middle_lag:
                    out[lag_rows // 2, index] = total[:width, columns].astype(out.dtype)
                for near in range(away):
                    start = (middle_lag + 2 * near) * width
                    even = total[start : start + width, columns]
                    odd = total[start + width : start + 2 * width, columns]
                    below = (lag_rows - 1) // 2 - near - middle_lag
                    above = lag_rows - 1 - below
                    out[above, index] = (even + odd).astype(out.dtype)
                    out[below, index] = (even - odd).astype(out.dtype)


def on_device(spectra, pair_blocks, pair_owner, block_members):
    hour_count, sub_freqs, _, _ = spectra.shape
    block_count, width = block_members.shape
    sta_count, hr_count, sub_count = (lax.axis_size(axis) for axis in ("sta", "hr", "sub"))
    groups = hr_count * sub_count
    lag_rows = LAGS // groups
    norming = 1.0 / math.sqrt(hour_count * hr_count * sub_count * sub_freqs)
    pair_sides = pair_blocks.T
    turns, offsets, away = phase_tables(sub_count, sub_freqs, groups, lag_rows)

    owners_at_most = pair_owner.shape[0] - CAP + 1
    branched = owners_at_most == 2 and sta_count == REACH
    kept = min(REACH, owners_at_most)
    branches, cases = routes(sta_count) if branched else ([], [])
    case_table = jnp.asarray(np.array(cases or [0], dtype=np.int32))
    picked = pick_blocks(
        kept, branched, spectra, pair_sides, pair_owner, block_members, case_table
    )

    def halves(block):
        blocks = [block]
        for step in range(1, sub_count):
            swap = [((sub + step) % sub_count, sub) for sub in range(sub_count)]
            blocks.append(lax.ppermute(block, "sub", swap))
        return blocks

    def to_owners(block, reach, owners):
        pairs = [((owner + reach) % sta_count, owner) for owner in owners]
        return lax.ppermute(block, "sta", pairs)

    def exchange(*picked):
        blocks = []
        for reach in range(1, REACH):
            blocks += halves(to_owners(picked[reach], reach, range(sta_count)))
        return halves(picked[0]) + blocks

    def exchange_two(first, second, sent, *picked):
        own = (first - second) % sta_count
        keys = send_keys(first, second, sta_count, lambda hit, yes, no: yes if hit else no)
        order = sorted(range(1, REACH), key=lambda reach: keys[reach - 1])
        arrived = {}
        for reach in order:
            owners = (first, second) if reach in sent and reach != own else (first,)
            arrived[reach] = to_owners(picked[reach], reach, owners)
        if own in sent:
            block, _ = lax.optimization_barrier((picked[own], arrived[order[0]]))
            block = to_owners(block, own, (second,))
            here = lax.axis_index("sta") == second
            arrived[own] = jnp.where(here, block, arrived[own])
        blocks = halves(picked[0])
        for reach in order:
            blocks += halves(arrived[reach])
        return blocks

    if branched:
        steps = [functools.partial(exchange_two, *branch) for branch in branches]
        blocks = lax.switch(picked[REACH][0], steps, *picked[:REACH])
    else:
        blocks = exchange(*picked[:REACH])

    smem = pl.BlockSpec(memory_space=pltpu.SMEM)
    vmem = pl.BlockSpec(memory_space=pltpu.VMEM)
    hbm = pl.BlockSpec(memory_space=pltpu.HBM)
    row = picked[0].shape[1]
    versions = (lag_rows % 2 + 2 * away) * width

    def products(hops, slots, dtype, name):
        return pl.pallas_call(
            functools.partial(
                lag_kernel, hops, slots, lag_rows, away, block_count, branched
            ),
            out_shape=[jax.ShapeDtypeStruct((lag_rows, len(slots), width, width), dtype)]
            * len(hops),
            in_specs=[smem, smem, vmem, vmem] + [hbm] * len(blocks),
            out_specs=[vmem] * len(hops),
            scratch_shapes=[
                pltpu.VMEM((len(slots), 2, sub_count, width, row), BF16),
                pltpu.SemaphoreType.DMA((len(slots), 2, sub_count)),
            ],
            compiler_params=pltpu.CompilerParams(vmem_limit_bytes=LAG_VMEM_LIMIT),
            cost_estimate=pl.CostEstimate(
                flops=2 * len(slots) * len(hops) * versions * width * sub_count * row,
                bytes_accessed=4 * len(slots) * sub_count * width * row,
                transcendentals=0,
            ),
            name=name,
        )(pair_sides, pair_owner, turns, offsets, *blocks)

    hops, slots = tuple(range(1, hr_count)), tuple(range(CAP))
    sent = products(hops, slots, BF16, "lags_to_send")
    received = []
    for hop, part in zip(hops, sent):
        to_device = [(hr, (hr + hop) % hr_count) for hr in range(hr_count)]
        received.append(lax.ppermute(part, "hr", to_device))
    (summed,) = products((0,), slots, F32, "lags_to_keep")
    for part in received:
        summed = summed + part.astype(F32)
    return (summed * norming).astype(BF16)


def solution(mesh):
    placed = (P(("grp", "hr"), "sub", None, "sta"), P(), P(), P("sta", None))
    return jax.shard_map(
        on_device,
        mesh=mesh,
        in_specs=placed,
        out_specs=P(("grp", "hr", "sub"), "sta", None, None),
        check_vma=False,
    )
```

```python
import functools
import itertools
import math

import jax
import jax.numpy as jnp
import numpy as np
from jax import lax
from jax.experimental import pallas as pl
from jax.experimental.pallas import tpu as pltpu
from jax.sharding import PartitionSpec as P

BAND = 50
LAGS = 16
CAP = 3
REACH = 4
COPIES = 2
EPSILON = 1e-05
LANES = 128
F32 = jnp.float32
BF16 = jnp.bfloat16
PICK_VMEM_LIMIT = 59 * 1024 * 1024
LAG_VMEM_LIMIT = 32 * 1024 * 1024

NT = (((1,), (1,)), ((), ()))


def dot_nt(left, right):
    return lax.dot_general(left, right, NT, preferred_element_type=F32)


def iota(shape, dim):
    return lax.broadcasted_iota(jnp.int32, shape, dim)


def choose(hit, yes, no):
    return yes if hit else no


def ring_reach(first, where):
    return where(first % 2 == 1, 1, REACH - 1)


def send_keys(first, second, sta_count, where):
    ring = ring_reach(first, where)
    keys = []
    for reach in range(1, REACH):
        first_sends = (first - second - reach) % sta_count == 0
        keys.append(where(ring == reach, 0, where(first_sends, REACH, 0) + reach))
    return keys


def read_pairs(pair_ref, owner_ref, block_count):
    pairs = []
    for pair in range(owner_ref.shape[0]):
        blocks = [pair_ref[side, pair] for side in range(2)]
        pairs.append((owner_ref[pair], blocks, [lax.div(block, block_count) for block in blocks]))
    return pairs


def case_of(pairs, sta_count):
    first = second = needs = jnp.int32(0)
    for owner, _, homes in pairs:
        count = jnp.int32(0)
        for other, _, _ in pairs:
            count = count + (other == owner).astype(jnp.int32)
        ends = [lax.rem(home - owner + sta_count, sta_count) for home in homes]
        first = jnp.where(count == CAP, owner, first)
        second = jnp.where(count < CAP, owner, second)
        needs = jnp.where(count < CAP, (1 << ends[0]) | (1 << ends[1]), needs)
    return first, second, case_number(first, second, needs, sta_count)


def pick_kernel(kept, branched, sta_axis, pair_hbm, owner_hbm, member_hbm, case_hbm, x_ref, *rest):
    outs = rest[:REACH]
    pair_ref, owner_ref, member_ref, case_ref, number_ref, x_buf, y_buf, white_buf, sems = rest[
        REACH + branched :
    ]
    if branched:
        branch_copy = pltpu.make_async_copy(number_ref, rest[REACH], sems.at[COPIES + 4])
    freqs, tiles = x_buf.shape[0], x_buf.shape[2] // LANES
    block_count, width = member_ref.shape
    rows = y_buf.shape[0]
    chunks = rows // (2 * LANES)

    def fetch(part):
        run = pl.ds(part * (freqs // COPIES), freqs // COPIES)
        return pltpu.make_async_copy(x_ref.at[0, run], x_buf.at[run], sems.at[part])

    small = [
        pltpu.make_async_copy(source, target, sems.at[COPIES + index])
        for index, (source, target) in enumerate(
            (
                (pair_hbm, pair_ref),
                (owner_hbm, owner_ref),
                (member_hbm, member_ref),
                (case_hbm, case_ref),
            )
        )
    ]
    for copy in small:
        copy.start()
    for part in range(COPIES):
        fetch(part).start()

    def bands(shape, part_dim):
        part, place = iota(shape, part_dim), iota(shape, 1 - part_dim)
        low = (place % 16) * (2 * BAND)
        hit = (part >= low) & (part < low + 2 * BAND) & (part < 2 * freqs) & (place < 48)
        return jnp.where(hit, 1.0, 0.0).astype(BF16)

    gather_bands, spread_bands = bands((48, rows), 1), bands((rows, LANES), 0)
    row, col = iota((2 * LANES, 2 * LANES), 0), iota((2 * LANES, 2 * LANES), 1)
    split = jnp.where(row == 2 * (col % LANES) + col // LANES, 1.0, 0.0).astype(BF16)
    y_buf[2 * freqs :] = jnp.zeros((rows - 2 * freqs, kept * width), F32)
    for copy in small:
        copy.wait()

    my_sta = lax.axis_index(sta_axis)
    sta_count = lax.axis_size(sta_axis)
    pairs = read_pairs(pair_ref, owner_ref, block_count)
    found, wanted = jnp.int32(0), []
    for reach in range(REACH):
        owner = lax.rem(my_sta - reach + REACH * sta_count, sta_count)
        chosen = jnp.int32(-1)
        for pair_owner, blocks, homes in pairs:
            for block, home in zip(blocks, homes):
                hit = (pair_owner == owner) & (home == my_sta)
                chosen = jnp.where(hit, lax.rem(block, block_count), chosen)
        wanted.append((found, chosen))
        found = found + (chosen >= 0).astype(jnp.int32)
    places, station = [], []
    for place in range(kept):
        reach_here, block_here = jnp.int32(-1), jnp.int32(0)
        for reach, (rank, chosen) in enumerate(wanted):
            hit = (rank == place) & (chosen >= 0)
            reach_here = jnp.where(hit, reach, reach_here)
            block_here = jnp.where(hit, chosen, block_here)
        places.append(reach_here)
        station.append(member_ref[pl.ds(block_here, 1), :])
    station = jnp.concatenate(station, axis=1)
    hot = jnp.where(station == iota((tiles * LANES, kept * width), 0), 1.0, 0.0).astype(BF16)

    if branched:
        number_ref[0] = case_ref[case_of(pairs, sta_count)[2]]
        branch_copy.start()

    for part in range(COPIES):
        fetch(part).wait()
    x = jnp.concatenate(
        [
            x_buf[:, :, tile * LANES : (tile + 1) * LANES].reshape(2 * freqs, LANES)
            for tile in range(tiles)
        ],
        axis=1,
    )
    y_buf[: 2 * freqs] = jnp.dot(x, hot, preferred_element_type=F32)

    values = y_buf[...]
    square = values * values
    high = square.astype(BF16)
    low = (square - high.astype(F32)).astype(BF16)
    power = jnp.dot(gather_bands, high, preferred_element_type=F32)
    power += jnp.dot(gather_bands, low, preferred_element_type=F32)
    scale = lax.rsqrt(power * (1.0 / (2 * BAND)) + EPSILON)
    high = scale.astype(BF16).astype(F32)
    mid = (scale - high).astype(BF16).astype(F32)
    low = scale - high - mid
    third = iota(scale.shape, 0) // 16
    pieces = jnp.where(third == 0, high, jnp.where(third == 1, mid, low))
    pieces = jnp.concatenate(
        [pieces, jnp.zeros((LANES - pieces.shape[0], pieces.shape[1]), F32)], axis=0
    ).astype(BF16)
    white = y_buf[...] * jnp.dot(spread_bands, pieces, preferred_element_type=F32)
    white = white.astype(BF16)
    parted = []
    for chunk in range(chunks):
        mixed = white[chunk * 2 * LANES : (chunk + 1) * 2 * LANES]
        part = lax.dot_general(
            mixed, split, (((0,), (0,)), ((), ())), preferred_element_type=F32
        )
        parted.append(part.astype(BF16))
    white_buf[...] = jnp.concatenate(
        [part[:, :LANES] for part in parted] + [part[:, LANES:] for part in parted], axis=1
    )
    for place, reach_here in enumerate(places):
        for reach in range(REACH):

            @pl.when(reach_here == reach)
            def _():
                outs[reach][...] = white_buf[place * width : (place + 1) * width]

    if branched:
        branch_copy.wait()


def pick_blocks(kept, branched, spectra, pair_sides, pair_owner, block_members, case_table):
    _, freqs, parts, stations = spectra.shape
    block_count, width = block_members.shape
    columns = -(-freqs // LANES) * 2 * LANES
    rows = kept * width
    vmem = pl.BlockSpec(memory_space=pltpu.VMEM)
    out_shape = [jax.ShapeDtypeStruct((width, columns), BF16)] * REACH
    out_shape += [jax.ShapeDtypeStruct((1,), jnp.int32)] * branched
    return pl.pallas_call(
        functools.partial(pick_kernel, kept, branched, "sta"),
        out_shape=out_shape,
        in_specs=[pl.BlockSpec(memory_space=pltpu.HBM)] * 5,
        out_specs=[vmem] * REACH + [pl.BlockSpec(memory_space=pltpu.HBM)] * branched,
        scratch_shapes=[
            pltpu.SMEM(pair_sides.shape, jnp.int32),
            pltpu.SMEM(pair_owner.shape, jnp.int32),
            pltpu.VMEM(block_members.shape, jnp.int32),
            pltpu.SMEM(case_table.shape, jnp.int32),
            pltpu.SMEM((1,), jnp.int32),
            pltpu.VMEM((freqs, parts, stations), BF16),
            pltpu.VMEM((columns, rows), F32),
            pltpu.VMEM((rows, columns), BF16),
            pltpu.SemaphoreType.DMA((COPIES + 5,)),
        ],
        compiler_params=pltpu.CompilerParams(vmem_limit_bytes=PICK_VMEM_LIMIT),
        cost_estimate=pl.CostEstimate(
            flops=2 * rows * stations * freqs * parts,
            bytes_accessed=2 * spectra.size + 4 * rows * columns,
            transcendentals=0,
        ),
        name="pick_and_whiten",
    )(pair_sides, pair_owner, block_members, case_table, spectra)


def case_number(first, second, needs, sta_count):
    return (first * sta_count + second) * (1 << (REACH - 1)) + needs // 2


def routes(sta_count):
    def load(first, second, sent):
        links = {}
        ring = ring_reach(first, choose)
        flows = [((home + ring) % sta_count, home) for home in range(sta_count)]
        flows += [((first + reach) % sta_count, first) for reach in range(1, REACH) if reach != ring]
        flows += [((second + reach) % sta_count, second) for reach in sent]
        for source, owner in flows:
            step = 1 if owner > source else -1
            for place in range(source, owner, step):
                links[place, step] = links.get((place, step), 0) + 1
        return max(links.values())

    branches = []
    cases = [0] * case_number(sta_count, 0, 0, sta_count)
    for first, second in itertools.permutations(range(sta_count), 2):
        ring = ring_reach(first, choose)
        others = [reach for reach in range(1, REACH) if reach != ring]
        sets = [
            sent
            for count in range(len(others), -1, -1)
            for sent in itertools.combinations(others, count)
        ]
        for named in itertools.combinations(range(REACH), 2):
            fits = [sent for sent in sets if set(named) - {0, ring} <= set(sent)]
            branch = (first, second, min(fits, key=lambda sent: load(first, second, sent)))
            if branch not in branches:
                branches.append(branch)
            needs = sum(1 << reach for reach in named)
            cases[case_number(first, second, needs, sta_count)] = branches.index(branch)
    return branches, cases


def phase_tables(sub_count, sub_freqs, groups, lag_rows):
    chunks = -(-sub_freqs // LANES)
    total = sub_count * sub_freqs
    freq = np.arange(total, dtype=np.int64).reshape(sub_count, 1, sub_freqs)
    middle = [2 * (group * lag_rows - LAGS // 2) + lag_rows - 1 for group in range(groups)]
    away = [step for step in range(1, lag_rows) if step % 2 != lag_rows % 2]

    def table(twice, forms, tile, dtype):
        twice = np.array(twice or [0], dtype=np.int64).reshape(1, -1, 1)
        angle = np.mod(freq * twice, 2 * total) * (math.pi / total)
        rows = np.stack([form(angle) for form in forms], axis=2)
        rows = rows.reshape(sub_count, -1, sub_freqs)
        pad = ((0, 0), (0, -rows.shape[1] % tile), (0, chunks * LANES - sub_freqs))
        return np.pad(rows, pad).astype(np.float32).astype(dtype)

    turns = table(middle, (np.cos, np.sin), 8, np.float32)
    offsets = table(away, (np.cos, np.sin, lambda angle: -np.sin(angle)), 16, BF16)
    return turns, offsets, len(away)


def lag_kernel(hops, slots, lag_rows, away, block_count, branched, *refs):
    sub_count = lax.axis_size("sub")
    hr_count = lax.axis_size("hr")
    pair_ref, owner_ref, turn_ref, offset_ref = refs[:4]
    blocks, outs = refs[4 : -2 - len(hops)], refs[-2 - len(hops) : -2]
    buf, sems = refs[-2:]
    width = buf.shape[3]
    span = buf.shape[4] // 2
    middle_lag = lag_rows % 2
    my_sub = lax.axis_index("sub")
    my_hr = lax.axis_index("hr")
    my_sta = lax.axis_index("sta")
    sta_count = lax.axis_size("sta")

    pairs = read_pairs(pair_ref, owner_ref, block_count)
    order = [jnp.int32(reach) for reach in range(REACH)]
    if branched:
        first, second, _ = case_of(pairs, sta_count)
        keys = send_keys(first, second, sta_count, jnp.where)
        for reach, key in enumerate(keys):
            order[1 + reach] = 1 + sum(jnp.int32(other < key) for other in keys)
    owned = []
    for owner, _, homes in pairs:
        places = []
        for home in homes:
            reach_here = lax.rem(home - my_sta + sta_count, sta_count)
            place_here = order[0]
            for reach in range(1, REACH):
                place_here = jnp.where(reach_here == reach, order[reach], place_here)
            places.append(place_here)
        owned.append((owner == my_sta, places))
    ends = []
    for slot in slots:
        count = jnp.int32(0)
        slot_ends = [jnp.int32(-1)] * 2
        for mine, places in owned:
            hit = mine & (count == slot)
            count = count + mine.astype(jnp.int32)
            slot_ends = [jnp.where(hit, new, old) for new, old in zip(places, slot_ends)]
        ends.append(slot_ends)

    def fetches(index, act):
        for side in range(2):
            for place in range(REACH):

                @pl.when(ends[index][side] == place)
                def _():
                    for step in range(sub_count):
                        act(
                            pltpu.make_async_copy(
                                blocks[place * sub_count + step],
                                buf.at[index, side, step],
                                sems.at[index, side, step],
                            )
                        )

    for index in range(len(slots)):
        fetches(index, lambda copy: copy.start())

    for index in range(len(slots)):

        @pl.when(ends[index][0] < 0)
        def _():
            for out in outs:
                out[:, index] = jnp.zeros((lag_rows, width, width), out.dtype)

        fetches(index, lambda copy: copy.wait())

        @pl.when(ends[index][0] >= 0)
        def _():
            total = None
            for step in range(sub_count):
                sub = lax.rem(my_sub + step, sub_count)
                real = buf[index, 0, step, :, :span]
                imag = buf[index, 0, step, :, span:]
                scaled_real, scaled_imag = [real] * middle_lag, [imag] * middle_lag
                for near in range(away):
                    cosine, sine, minus = (
                        offset_ref[sub, 3 * near + form : 3 * near + form + 1, :]
                        for form in range(3)
                    )
                    scaled_real += [real * cosine, imag * minus]
                    scaled_imag += [imag * cosine, real * sine]
                real = buf[index, 1, step, :, :span].astype(F32)
                imag = buf[index, 1, step, :, span:].astype(F32)
                turned_real, turned_imag = [], []
                for hop in hops:
                    group = lax.rem(my_hr + hop, hr_count) * sub_count + my_sub
                    cosine = turn_ref[sub, pl.ds(2 * group, 1), :]
                    sine = turn_ref[sub, pl.ds(2 * group + 1, 1), :]
                    turned_real.append((real * cosine + imag * sine).astype(BF16))
                    turned_imag.append((imag * cosine - real * sine).astype(BF16))
                for scaled, turned in ((scaled_real, turned_real), (scaled_imag, turned_imag)):
                    part = dot_nt(jnp.concatenate(scaled, axis=0), jnp.concatenate(turned, axis=0))
                    total = part if total is None else total + part
            for place, out in enumerate(outs):
                columns = slice(place * width, (place + 1) * width)
                if middle_lag:
                    out[lag_rows // 2, index] = total[:width, columns].astype(out.dtype)
                for near in range(away):
                    start = (middle_lag + 2 * near) * width
                    even = total[start : start + width, columns]
                    odd = total[start + width : start + 2 * width, columns]
                    below = (lag_rows - 1) // 2 - near - middle_lag
                    above = lag_rows - 1 - below
                    out[above, index] = (even + odd).astype(out.dtype)
                    out[below, index] = (even - odd).astype(out.dtype)


def on_device(spectra, pair_blocks, pair_owner, block_members):
    hour_count, sub_freqs, _, _ = spectra.shape
    block_count, width = block_members.shape
    sta_count, hr_count, sub_count = (lax.axis_size(axis) for axis in ("sta", "hr", "sub"))
    groups = hr_count * sub_count
    lag_rows = LAGS // groups
    norming = 1.0 / math.sqrt(hour_count * hr_count * sub_count * sub_freqs)
    pair_sides = pair_blocks.T
    turns, offsets, away = phase_tables(sub_count, sub_freqs, groups, lag_rows)

    owners_at_most = pair_owner.shape[0] - CAP + 1
    branched = owners_at_most == 2 and sta_count == REACH
    kept = min(REACH, owners_at_most)
    branches, cases = routes(sta_count) if branched else ([], [])
    case_table = jnp.asarray(np.array(cases or [0], dtype=np.int32))
    picked = pick_blocks(
        kept, branched, spectra, pair_sides, pair_owner, block_members, case_table
    )

    def exchange(owners_of, order, *picked):
        arrived = [picked[0]]
        for reach in order:
            to_owner = [((owner + reach) % sta_count, owner) for owner in owners_of[reach - 1]]
            arrived.append(lax.ppermute(picked[reach], "sta", to_owner))
        blocks = []
        for block in arrived:
            blocks.append(block)
            for step in range(1, sub_count):
                swap = [((sub + step) % sub_count, sub) for sub in range(sub_count)]
                blocks.append(lax.ppermute(block, "sub", swap))
        return blocks

    if branched:
        steps = []
        for first, second, sent in branches:
            ring = ring_reach(first, choose)
            owners_of = [
                range(sta_count) if reach == ring else (first, second) if reach in sent else (first,)
                for reach in range(1, REACH)
            ]
            keys = send_keys(first, second, sta_count, choose)
            order = sorted(range(1, REACH), key=lambda reach: keys[reach - 1])
            steps.append(functools.partial(exchange, owners_of, order))
        blocks = lax.switch(picked[REACH][0], steps, *picked[:REACH])
    else:
        blocks = exchange([range(sta_count)] * (REACH - 1), range(1, REACH), *picked[:REACH])

    smem = pl.BlockSpec(memory_space=pltpu.SMEM)
    vmem = pl.BlockSpec(memory_space=pltpu.VMEM)
    hbm = pl.BlockSpec(memory_space=pltpu.HBM)
    row = picked[0].shape[1]
    versions = (lag_rows % 2 + 2 * away) * width

    def products(hops, slots, dtype, name):
        return pl.pallas_call(
            functools.partial(
                lag_kernel, hops, slots, lag_rows, away, block_count, branched
            ),
            out_shape=[jax.ShapeDtypeStruct((lag_rows, len(slots), width, width), dtype)]
            * len(hops),
            in_specs=[smem, smem, vmem, vmem] + [hbm] * len(blocks),
            out_specs=[vmem] * len(hops),
            scratch_shapes=[
                pltpu.VMEM((len(slots), 2, sub_count, width, row), BF16),
                pltpu.SemaphoreType.DMA((len(slots), 2, sub_count)),
            ],
            compiler_params=pltpu.CompilerParams(vmem_limit_bytes=LAG_VMEM_LIMIT),
            cost_estimate=pl.CostEstimate(
                flops=2 * len(slots) * len(hops) * versions * width * sub_count * row,
                bytes_accessed=4 * len(slots) * sub_count * width * row,
                transcendentals=0,
            ),
            name=name,
        )(pair_sides, pair_owner, turns, offsets, *blocks)

    hops, slots = tuple(range(1, hr_count)), tuple(range(CAP))
    sent = products(hops, slots, BF16, "lags_to_send")
    received = []
    for hop, part in zip(hops, sent):
        to_device = [(hr, (hr + hop) % hr_count) for hr in range(hr_count)]
        received.append(lax.ppermute(part, "hr", to_device))
    (summed,) = products((0,), slots, F32, "lags_to_keep")
    for part in received:
        summed = summed + part.astype(F32)
    return (summed * norming).astype(BF16)


def solution(mesh):
    placed = (P(("grp", "hr"), "sub", None, "sta"), P(), P(), P("sta", None))
    return jax.shard_map(
        on_device,
        mesh=mesh,
        in_specs=placed,
        out_specs=P(("grp", "hr", "sub"), "sta", None, None),
        check_vma=False,
    )
```

```python
import functools
import itertools
import math

import jax
import jax.numpy as jnp
import numpy as np
from jax import lax
from jax.experimental import pallas as pl
from jax.experimental.pallas import tpu as pltpu
from jax.sharding import PartitionSpec as P

BAND = 50
LAGS = 16
CAP = 3
REACH = 4
COPIES = 2
EPSILON = 1e-05
LANES = 128
F32 = jnp.float32
BF16 = jnp.bfloat16
PICK_VMEM_LIMIT = 59 * 1024 * 1024
LAG_VMEM_LIMIT = 32 * 1024 * 1024

NT = (((1,), (1,)), ((), ()))


def dot_nt(left, right):
    return lax.dot_general(left, right, NT, preferred_element_type=F32)


def iota(shape, dim):
    return lax.broadcasted_iota(jnp.int32, shape, dim)


def schedule(first, second, sta_count):
    every = range(1, REACH)
    if 0 < first < sta_count - 1:
        ring = 1 if 2 * first < sta_count else REACH - 1
        pairs = [((home + ring) % sta_count, home) for home in range(sta_count)]
    else:
        pairs = [(home ^ 1, home) for home in range(sta_count)]
    source = {target: start for start, target in pairs}
    reaches = [[(source[owner] - owner) % sta_count] for owner in (first, second)]
    both = [reach for reach in every if [reach] not in reaches]
    for taken in reaches:
        taken += both + [reach for reach in every if reach not in taken + both]
    plan = [(True, pairs, reaches[0][0], reaches[1][0])]
    for one, other in zip(reaches[0][1:], reaches[1][1:]):
        flows = [((first + one) % sta_count, first), ((second + other) % sta_count, second)]
        plan.append((False, flows, one, other))
    return plan[:1] + sorted(plan[1:], key=lambda step: step[1][1][0] == first)


def place_table(sta_count):
    table = []
    for first, second in itertools.product(range(sta_count), repeat=2):
        places = [0] * (2 * REACH)
        if first != second:
            for place, step in enumerate(schedule(first, second, sta_count)):
                places[step[2]], places[REACH + step[3]] = place + 1, place + 1
        table += places
    return table


def read_pairs(pair_ref, owner_ref, block_count):
    pairs = []
    for pair in range(owner_ref.shape[0]):
        blocks = [pair_ref[side, pair] for side in range(2)]
        pairs.append((owner_ref[pair], blocks, [lax.div(block, block_count) for block in blocks]))
    return pairs


def case_of(pairs, sta_count):
    first = second = needs = jnp.int32(0)
    for owner, _, homes in pairs:
        count = jnp.int32(0)
        for other, _, _ in pairs:
            count = count + (other == owner).astype(jnp.int32)
        ends = [lax.rem(home - owner + sta_count, sta_count) for home in homes]
        first = jnp.where(count == CAP, owner, first)
        second = jnp.where(count < CAP, owner, second)
        needs = jnp.where(count < CAP, (1 << ends[0]) | (1 << ends[1]), needs)
    return first, second, case_number(first, second, needs, sta_count)


def pick_kernel(kept, branched, sta_axis, pair_hbm, owner_hbm, member_hbm, case_hbm, x_ref, *rest):
    outs = rest[:REACH]
    pair_ref, owner_ref, member_ref, case_ref, number_ref, x_buf, y_buf, white_buf, sems = rest[
        REACH + branched :
    ]
    if branched:
        branch_copy = pltpu.make_async_copy(number_ref, rest[REACH], sems.at[COPIES + 4])
    freqs, tiles = x_buf.shape[0], x_buf.shape[2] // LANES
    block_count, width = member_ref.shape
    rows = y_buf.shape[0]
    chunks = rows // (2 * LANES)

    def fetch(part):
        run = pl.ds(part * (freqs // COPIES), freqs // COPIES)
        return pltpu.make_async_copy(x_ref.at[0, run], x_buf.at[run], sems.at[part])

    small = [
        pltpu.make_async_copy(source, target, sems.at[COPIES + index])
        for index, (source, target) in enumerate(
            (
                (pair_hbm, pair_ref),
                (owner_hbm, owner_ref),
                (member_hbm, member_ref),
                (case_hbm, case_ref),
            )
        )
    ]
    for copy in small:
        copy.start()
    for part in range(COPIES):
        fetch(part).start()

    def bands(shape, part_dim):
        part, place = iota(shape, part_dim), iota(shape, 1 - part_dim)
        low = (place % 16) * (2 * BAND)
        hit = (part >= low) & (part < low + 2 * BAND) & (part < 2 * freqs) & (place < 48)
        return jnp.where(hit, 1.0, 0.0).astype(BF16)

    gather_bands, spread_bands = bands((48, rows), 1), bands((rows, LANES), 0)
    row, col = iota((2 * LANES, 2 * LANES), 0), iota((2 * LANES, 2 * LANES), 1)
    split = jnp.where(row == 2 * (col % LANES) + col // LANES, 1.0, 0.0).astype(BF16)
    y_buf[2 * freqs :] = jnp.zeros((rows - 2 * freqs, kept * width), F32)
    for copy in small:
        copy.wait()

    my_sta = lax.axis_index(sta_axis)
    sta_count = lax.axis_size(sta_axis)
    pairs = read_pairs(pair_ref, owner_ref, block_count)
    found, wanted = jnp.int32(0), []
    for reach in range(REACH):
        owner = lax.rem(my_sta - reach + REACH * sta_count, sta_count)
        chosen = jnp.int32(-1)
        for pair_owner, blocks, homes in pairs:
            for block, home in zip(blocks, homes):
                hit = (pair_owner == owner) & (home == my_sta)
                chosen = jnp.where(hit, lax.rem(block, block_count), chosen)
        wanted.append((found, chosen))
        found = found + (chosen >= 0).astype(jnp.int32)
    places, station = [], []
    for place in range(kept):
        reach_here, block_here = jnp.int32(-1), jnp.int32(0)
        for reach, (rank, chosen) in enumerate(wanted):
            hit = (rank == place) & (chosen >= 0)
            reach_here = jnp.where(hit, reach, reach_here)
            block_here = jnp.where(hit, chosen, block_here)
        places.append(reach_here)
        station.append(member_ref[pl.ds(block_here, 1), :])
    station = jnp.concatenate(station, axis=1)
    hot = jnp.where(station == iota((tiles * LANES, kept * width), 0), 1.0, 0.0).astype(BF16)

    if branched:
        first, second, case = case_of(pairs, sta_count)
        number_ref[0] = case_ref[case]
        branch_copy.start()
        base = case_number(sta_count, 0, 0, sta_count) + (first * sta_count + second) * 2 * REACH
        for place, reach_here in enumerate(places):
            reach = jnp.maximum(reach_here, 0)
            owner = lax.rem(my_sta - reach + REACH * sta_count, sta_count)
            step = case_ref[base + jnp.where(owner == first, 0, REACH) + reach]
            places[place] = jnp.where(reach_here < 0, -1, step)

    for part in range(COPIES):
        fetch(part).wait()
    x = jnp.concatenate(
        [
            x_buf[:, :, tile * LANES : (tile + 1) * LANES].reshape(2 * freqs, LANES)
            for tile in range(tiles)
        ],
        axis=1,
    )
    y_buf[: 2 * freqs] = jnp.dot(x, hot, preferred_element_type=F32)

    values = y_buf[...]
    square = values * values
    high = square.astype(BF16)
    low = (square - high.astype(F32)).astype(BF16)
    power = jnp.dot(gather_bands, high, preferred_element_type=F32)
    power += jnp.dot(gather_bands, low, preferred_element_type=F32)
    scale = lax.rsqrt(power * (1.0 / (2 * BAND)) + EPSILON)
    high = scale.astype(BF16).astype(F32)
    mid = (scale - high).astype(BF16).astype(F32)
    low = scale - high - mid
    third = iota(scale.shape, 0) // 16
    pieces = jnp.where(third == 0, high, jnp.where(third == 1, mid, low))
    pieces = jnp.concatenate(
        [pieces, jnp.zeros((LANES - pieces.shape[0], pieces.shape[1]), F32)], axis=0
    ).astype(BF16)
    white = y_buf[...] * jnp.dot(spread_bands, pieces, preferred_element_type=F32)
    white = white.astype(BF16)
    parted = []
    for chunk in range(chunks):
        mixed = white[chunk * 2 * LANES : (chunk + 1) * 2 * LANES]
        part = lax.dot_general(
            mixed, split, (((0,), (0,)), ((), ())), preferred_element_type=F32
        )
        parted.append(part.astype(BF16))
    white_buf[...] = jnp.concatenate(
        [part[:, :LANES] for part in parted] + [part[:, LANES:] for part in parted], axis=1
    )
    for place, reach_here in enumerate(places):
        for reach in range(REACH):

            @pl.when(reach_here == reach)
            def _():
                outs[reach][...] = white_buf[place * width : (place + 1) * width]

    if branched:
        branch_copy.wait()


def pick_blocks(kept, branched, spectra, pair_sides, pair_owner, block_members, case_table):
    _, freqs, parts, stations = spectra.shape
    block_count, width = block_members.shape
    columns = -(-freqs // LANES) * 2 * LANES
    rows = kept * width
    vmem = pl.BlockSpec(memory_space=pltpu.VMEM)
    out_shape = [jax.ShapeDtypeStruct((width, columns), BF16)] * REACH
    out_shape += [jax.ShapeDtypeStruct((1,), jnp.int32)] * branched
    return pl.pallas_call(
        functools.partial(pick_kernel, kept, branched, "sta"),
        out_shape=out_shape,
        in_specs=[pl.BlockSpec(memory_space=pltpu.HBM)] * 5,
        out_specs=[vmem] * REACH + [pl.BlockSpec(memory_space=pltpu.HBM)] * branched,
        scratch_shapes=[
            pltpu.SMEM(pair_sides.shape, jnp.int32),
            pltpu.SMEM(pair_owner.shape, jnp.int32),
            pltpu.VMEM(block_members.shape, jnp.int32),
            pltpu.SMEM(case_table.shape, jnp.int32),
            pltpu.SMEM((1,), jnp.int32),
            pltpu.VMEM((freqs, parts, stations), BF16),
            pltpu.VMEM((columns, rows), F32),
            pltpu.VMEM((rows, columns), BF16),
            pltpu.SemaphoreType.DMA((COPIES + 5,)),
        ],
        compiler_params=pltpu.CompilerParams(vmem_limit_bytes=PICK_VMEM_LIMIT),
        cost_estimate=pl.CostEstimate(
            flops=2 * rows * stations * freqs * parts,
            bytes_accessed=2 * spectra.size + 4 * rows * columns,
            transcendentals=0,
        ),
        name="pick_and_whiten",
    )(pair_sides, pair_owner, block_members, case_table, spectra)


def case_number(first, second, needs, sta_count):
    return (first * sta_count + second) * (1 << (REACH - 1)) + needs // 2


def routes(sta_count):
    def load(first, second, sent):
        links = {}
        for full, flows, _, other in schedule(first, second, sta_count):
            for source, owner in flows if full or other in sent else flows[:1]:
                step = 1 if owner > source else -1
                for place in range(source, owner, step):
                    links[place, step] = links.get((place, step), 0) + 1
        return max(links.values())

    branches = []
    cases = [0] * case_number(sta_count, 0, 0, sta_count)
    for first, second in itertools.permutations(range(sta_count), 2):
        others = [step[3] for step in schedule(first, second, sta_count) if not step[0]]
        sets = [
            sent
            for count in range(len(others), -1, -1)
            for sent in itertools.combinations(others, count)
        ]
        for named in itertools.combinations(range(REACH), 2):
            fits = [sent for sent in sets if set(named) & set(others) <= set(sent)]
            branch = (first, second, min(fits, key=lambda sent: load(first, second, sent)))
            if branch not in branches:
                branches.append(branch)
            needs = sum(1 << reach for reach in named)
            cases[case_number(first, second, needs, sta_count)] = branches.index(branch)
    return branches, cases


def phase_tables(sub_count, sub_freqs, groups, lag_rows):
    chunks = -(-sub_freqs // LANES)
    total = sub_count * sub_freqs
    freq = np.arange(total, dtype=np.int64).reshape(sub_count, 1, sub_freqs)
    middle = [2 * (group * lag_rows - LAGS // 2) + lag_rows - 1 for group in range(groups)]
    away = [step for step in range(1, lag_rows) if step % 2 != lag_rows % 2]

    def table(twice, forms, tile, dtype):
        twice = np.array(twice or [0], dtype=np.int64).reshape(1, -1, 1)
        angle = np.mod(freq * twice, 2 * total) * (math.pi / total)
        rows = np.stack([form(angle) for form in forms], axis=2)
        rows = rows.reshape(sub_count, -1, sub_freqs)
        pad = ((0, 0), (0, -rows.shape[1] % tile), (0, chunks * LANES - sub_freqs))
        return np.pad(rows, pad).astype(np.float32).astype(dtype)

    turns = table(middle, (np.cos, np.sin), 8, np.float32)
    offsets = table(away, (np.cos, np.sin, lambda angle: -np.sin(angle)), 16, BF16)
    return turns, offsets, len(away)


def lag_kernel(hops, slots, lag_rows, away, block_count, branched, *refs):
    sub_count = lax.axis_size("sub")
    hr_count = lax.axis_size("hr")
    pair_ref, owner_ref, place_ref, turn_ref, offset_ref = refs[:5]
    blocks, outs = refs[5 : -2 - len(hops)], refs[-2 - len(hops) : -2]
    buf, sems = refs[-2:]
    width = buf.shape[3]
    span = buf.shape[4] // 2
    middle_lag = lag_rows % 2
    my_sub = lax.axis_index("sub")
    my_hr = lax.axis_index("hr")
    my_sta = lax.axis_index("sta")
    sta_count = lax.axis_size("sta")

    pairs = read_pairs(pair_ref, owner_ref, block_count)
    order = [jnp.int32(reach) for reach in range(REACH)]
    if branched:
        first, second, _ = case_of(pairs, sta_count)
        entry = (first * sta_count + second) * 2 + (my_sta != first).astype(jnp.int32)
        order = [place_ref[entry * REACH + reach] for reach in range(REACH)]
    owned = []
    for owner, _, homes in pairs:
        places = []
        for home in homes:
            reach_here = lax.rem(home - my_sta + sta_count, sta_count)
            place_here = order[0]
            for reach in range(1, REACH):
                place_here = jnp.where(reach_here == reach, order[reach], place_here)
            places.append(place_here)
        owned.append((owner == my_sta, places))
    ends = []
    for slot in slots:
        count = jnp.int32(0)
        slot_ends = [jnp.int32(-1)] * 2
        for mine, places in owned:
            hit = mine & (count == slot)
            count = count + mine.astype(jnp.int32)
            slot_ends = [jnp.where(hit, new, old) for new, old in zip(places, slot_ends)]
        ends.append(slot_ends)

    def fetches(index, act):
        for side in range(2):
            for place in range(REACH):

                @pl.when(ends[index][side] == place)
                def _():
                    for step in range(sub_count):
                        act(
                            pltpu.make_async_copy(
                                blocks[place * sub_count + step],
                                buf.at[index, side, step],
                                sems.at[index, side, step],
                            )
                        )

    for index in range(len(slots)):
        fetches(index, lambda copy: copy.start())

    for index in range(len(slots)):

        @pl.when(ends[index][0] < 0)
        def _():
            for out in outs:
                out[:, index] = jnp.zeros((lag_rows, width, width), out.dtype)

        fetches(index, lambda copy: copy.wait())

        @pl.when(ends[index][0] >= 0)
        def _():
            total = None
            for step in range(sub_count):
                sub = lax.rem(my_sub + step, sub_count)
                real = buf[index, 0, step, :, :span]
                imag = buf[index, 0, step, :, span:]
                scaled_real, scaled_imag = [real] * middle_lag, [imag] * middle_lag
                for near in range(away):
                    cosine, sine, minus = (
                        offset_ref[sub, 3 * near + form : 3 * near + form + 1, :]
                        for form in range(3)
                    )
                    scaled_real += [real * cosine, imag * minus]
                    scaled_imag += [imag * cosine, real * sine]
                real = buf[index, 1, step, :, :span].astype(F32)
                imag = buf[index, 1, step, :, span:].astype(F32)
                turned_real, turned_imag = [], []
                for hop in hops:
                    group = lax.rem(my_hr + hop, hr_count) * sub_count + my_sub
                    cosine = turn_ref[sub, pl.ds(2 * group, 1), :]
                    sine = turn_ref[sub, pl.ds(2 * group + 1, 1), :]
                    turned_real.append((real * cosine + imag * sine).astype(BF16))
                    turned_imag.append((imag * cosine - real * sine).astype(BF16))
                for scaled, turned in ((scaled_real, turned_real), (scaled_imag, turned_imag)):
                    part = dot_nt(jnp.concatenate(scaled, axis=0), jnp.concatenate(turned, axis=0))
                    total = part if total is None else total + part
            for place, out in enumerate(outs):
                columns = slice(place * width, (place + 1) * width)
                if middle_lag:
                    out[lag_rows // 2, index] = total[:width, columns].astype(out.dtype)
                for near in range(away):
                    start = (middle_lag + 2 * near) * width
                    even = total[start : start + width, columns]
                    odd = total[start + width : start + 2 * width, columns]
                    below = (lag_rows - 1) // 2 - near - middle_lag
                    above = lag_rows - 1 - below
                    out[above, index] = (even + odd).astype(out.dtype)
                    out[below, index] = (even - odd).astype(out.dtype)


def on_device(spectra, pair_blocks, pair_owner, block_members):
    hour_count, sub_freqs, _, _ = spectra.shape
    block_count, width = block_members.shape
    sta_count, hr_count, sub_count = (lax.axis_size(axis) for axis in ("sta", "hr", "sub"))
    groups = hr_count * sub_count
    lag_rows = LAGS // groups
    norming = 1.0 / math.sqrt(hour_count * hr_count * sub_count * sub_freqs)
    pair_sides = pair_blocks.T
    turns, offsets, away = phase_tables(sub_count, sub_freqs, groups, lag_rows)

    owners_at_most = pair_owner.shape[0] - CAP + 1
    branched = owners_at_most == 2 and sta_count == REACH
    kept = min(REACH, owners_at_most)
    branches, cases = routes(sta_count) if branched else ([], [0])
    places = place_table(sta_count) if branched else [0]
    case_table = jnp.asarray(np.array(cases + places, dtype=np.int32))
    places = jnp.asarray(np.array(places, dtype=np.int32))
    picked = pick_blocks(
        kept, branched, spectra, pair_sides, pair_owner, block_members, case_table
    )

    def halves(block):
        blocks = [block]
        for step in range(1, sub_count):
            swap = [((sub + step) % sub_count, sub) for sub in range(sub_count)]
            blocks.append(lax.ppermute(block, "sub", swap))
        return blocks

    def exchange(*picked):
        blocks = halves(picked[0])
        for reach in range(1, REACH):
            shift = [((home + reach) % sta_count, home) for home in range(sta_count)]
            blocks += halves(lax.ppermute(picked[reach], "sta", shift))
        return blocks

    def exchange_two(first, second, sent, *picked):
        blocks = halves(picked[0])
        for block, (full, flows, _, other) in zip(picked[1:], schedule(first, second, sta_count)):
            flows = flows if full or other in sent else flows[:1]
            blocks += halves(lax.ppermute(block, "sta", flows))
        return blocks

    if branched:
        steps = [functools.partial(exchange_two, *branch) for branch in branches]
        blocks = lax.switch(picked[REACH][0], steps, *picked[:REACH])
    else:
        blocks = exchange(*picked[:REACH])

    smem = pl.BlockSpec(memory_space=pltpu.SMEM)
    vmem = pl.BlockSpec(memory_space=pltpu.VMEM)
    hbm = pl.BlockSpec(memory_space=pltpu.HBM)
    row = picked[0].shape[1]
    versions = (lag_rows % 2 + 2 * away) * width

    def products(hops, slots, dtype, name):
        return pl.pallas_call(
            functools.partial(
                lag_kernel, hops, slots, lag_rows, away, block_count, branched
            ),
            out_shape=[jax.ShapeDtypeStruct((lag_rows, len(slots), width, width), dtype)]
            * len(hops),
            in_specs=[smem, smem, smem, vmem, vmem] + [hbm] * len(blocks),
            out_specs=[vmem] * len(hops),
            scratch_shapes=[
                pltpu.VMEM((len(slots), 2, sub_count, width, row), BF16),
                pltpu.SemaphoreType.DMA((len(slots), 2, sub_count)),
            ],
            compiler_params=pltpu.CompilerParams(vmem_limit_bytes=LAG_VMEM_LIMIT),
            cost_estimate=pl.CostEstimate(
                flops=2 * len(slots) * len(hops) * versions * width * sub_count * row,
                bytes_accessed=4 * len(slots) * sub_count * width * row,
                transcendentals=0,
            ),
            name=name,
        )(pair_sides, pair_owner, places, turns, offsets, *blocks)

    hops, slots = tuple(range(1, hr_count)), tuple(range(CAP))
    sent = products(hops, slots, BF16, "lags_to_send")
    received = []
    for hop, part in zip(hops, sent):
        to_device = [(hr, (hr + hop) % hr_count) for hr in range(hr_count)]
        received.append(lax.ppermute(part, "hr", to_device))
    (summed,) = products((0,), slots, F32, "lags_to_keep")
    for part in received:
        summed = summed + part.astype(F32)
    return (summed * norming).astype(BF16)


def solution(mesh):
    placed = (P(("grp", "hr"), "sub", None, "sta"), P(), P(), P("sta", None))
    return jax.shard_map(
        on_device,
        mesh=mesh,
        in_specs=placed,
        out_specs=P(("grp", "hr", "sub"), "sta", None, None),
        check_vma=False,
    )
```

```python
import functools
import itertools
import math

import jax
import jax.numpy as jnp
import numpy as np
from jax import lax
from jax.experimental import pallas as pl
from jax.experimental.pallas import tpu as pltpu
from jax.sharding import PartitionSpec as P

BAND = 50
LAGS = 16
CAP = 3
REACH = 4
COPIES = 2
EPSILON = 1e-05
LANES = 128
F32 = jnp.float32
BF16 = jnp.bfloat16
PICK_VMEM_LIMIT = 59 * 1024 * 1024
LAG_VMEM_LIMIT = 32 * 1024 * 1024

NT = (((1,), (1,)), ((), ()))


def dot_nt(left, right):
    return lax.dot_general(left, right, NT, preferred_element_type=F32)


def iota(shape, dim):
    return lax.broadcasted_iota(jnp.int32, shape, dim)


def schedule(first, second, sta_count):
    every = range(1, REACH)
    if 0 < first < sta_count - 1:
        ring = 1 if 2 * first < sta_count else REACH - 1
        pairs = [((home + ring) % sta_count, home) for home in range(sta_count)]
    else:
        pairs = [(home ^ 1, home) for home in range(sta_count)]
    source = {target: start for start, target in pairs}
    reaches = [[(source[owner] - owner) % sta_count] for owner in (first, second)]
    both = [reach for reach in every if [reach] not in reaches]
    for taken in reaches:
        taken += both + [reach for reach in every if reach not in taken + both]
    plan = [(True, pairs, reaches[0][0], reaches[1][0])]
    for one, other in zip(reaches[0][1:], reaches[1][1:]):
        flows = [((first + one) % sta_count, first), ((second + other) % sta_count, second)]
        plan.append((False, flows, one, other))
    return plan[:1] + sorted(plan[1:], key=lambda step: step[1][1][0] == first)


def place_table(sta_count):
    table = []
    for first, second in itertools.product(range(sta_count), repeat=2):
        places = [0] * (2 * REACH)
        if first != second:
            for place, step in enumerate(schedule(first, second, sta_count)):
                places[step[2]], places[REACH + step[3]] = place + 1, place + 1
        table += places
    return table


def read_pairs(pair_ref, owner_ref, block_count):
    pairs = []
    for pair in range(owner_ref.shape[0]):
        blocks = [pair_ref[side, pair] for side in range(2)]
        pairs.append((owner_ref[pair], blocks, [lax.div(block, block_count) for block in blocks]))
    return pairs


def case_of(pairs, sta_count):
    first = second = needs = jnp.int32(0)
    for owner, _, homes in pairs:
        count = jnp.int32(0)
        for other, _, _ in pairs:
            count = count + (other == owner).astype(jnp.int32)
        ends = [lax.rem(home - owner + sta_count, sta_count) for home in homes]
        first = jnp.where(count == CAP, owner, first)
        second = jnp.where(count < CAP, owner, second)
        needs = jnp.where(count < CAP, (1 << ends[0]) | (1 << ends[1]), needs)
    return first, second, case_number(first, second, needs, sta_count)


def pick_kernel(kept, branched, sta_axis, pair_hbm, owner_hbm, member_hbm, case_hbm, x_ref, *rest):
    outs = rest[:REACH]
    pair_ref, owner_ref, member_ref, case_ref, number_ref, x_buf, y_buf, white_buf, sems = rest[
        REACH + branched :
    ]
    if branched:
        branch_copy = pltpu.make_async_copy(number_ref, rest[REACH], sems.at[COPIES + 4])
    freqs, tiles = x_buf.shape[0], x_buf.shape[2] // LANES
    block_count, width = member_ref.shape
    rows = y_buf.shape[0]
    chunks = rows // (2 * LANES)

    cut = freqs // (4 * LANES) * 2 * LANES or freqs // LANES // 2 * LANES
    runs = [(0, cut), (cut, freqs - cut)]

    def fetch(part):
        run = pl.ds(*runs[part])
        return pltpu.make_async_copy(x_ref.at[0, run], x_buf.at[run], sems.at[part])

    small = [
        pltpu.make_async_copy(source, target, sems.at[COPIES + index])
        for index, (source, target) in enumerate(
            (
                (pair_hbm, pair_ref),
                (owner_hbm, owner_ref),
                (member_hbm, member_ref),
                (case_hbm, case_ref),
            )
        )
    ]
    for copy in small:
        copy.start()
    for part in range(COPIES):
        fetch(part).start()

    def bands(shape, part_dim):
        part, place = iota(shape, part_dim), iota(shape, 1 - part_dim)
        low = (place % 16) * (2 * BAND)
        hit = (part >= low) & (part < low + 2 * BAND) & (part < 2 * freqs) & (place < 48)
        return jnp.where(hit, 1.0, 0.0).astype(BF16)

    gather_bands, spread_bands = bands((48, rows), 1), bands((rows, LANES), 0)
    row, col = iota((2 * LANES, 2 * LANES), 0), iota((2 * LANES, 2 * LANES), 1)
    split = jnp.where(row == 2 * (col % LANES) + col // LANES, 1.0, 0.0).astype(BF16)
    y_buf[2 * freqs :] = jnp.zeros((rows - 2 * freqs, kept * width), F32)
    for copy in small:
        copy.wait()

    my_sta = lax.axis_index(sta_axis)
    sta_count = lax.axis_size(sta_axis)
    pairs = read_pairs(pair_ref, owner_ref, block_count)
    found, wanted = jnp.int32(0), []
    for reach in range(REACH):
        owner = lax.rem(my_sta - reach + REACH * sta_count, sta_count)
        chosen = jnp.int32(-1)
        for pair_owner, blocks, homes in pairs:
            for block, home in zip(blocks, homes):
                hit = (pair_owner == owner) & (home == my_sta)
                chosen = jnp.where(hit, lax.rem(block, block_count), chosen)
        wanted.append((found, chosen))
        found = found + (chosen >= 0).astype(jnp.int32)
    places, station = [], []
    for place in range(kept):
        reach_here, block_here = jnp.int32(-1), jnp.int32(0)
        for reach, (rank, chosen) in enumerate(wanted):
            hit = (rank == place) & (chosen >= 0)
            reach_here = jnp.where(hit, reach, reach_here)
            block_here = jnp.where(hit, chosen, block_here)
        places.append(reach_here)
        station.append(member_ref[pl.ds(block_here, 1), :])
    station = jnp.concatenate(station, axis=1)
    hot = jnp.where(station == iota((tiles * LANES, kept * width), 0), 1.0, 0.0).astype(BF16)

    if branched:
        first, second, case = case_of(pairs, sta_count)
        number_ref[0] = case_ref[case]
        branch_copy.start()
        base = case_number(sta_count, 0, 0, sta_count) + (first * sta_count + second) * 2 * REACH
        for place, reach_here in enumerate(places):
            reach = jnp.maximum(reach_here, 0)
            owner = lax.rem(my_sta - reach + REACH * sta_count, sta_count)
            step = case_ref[base + jnp.where(owner == first, 0, REACH) + reach]
            places[place] = jnp.where(reach_here < 0, -1, step)

    power = None
    for part, (start, count) in enumerate(runs):
        fetch(part).wait()
        x = jnp.concatenate(
            [
                x_buf[start : start + count, :, tile * LANES : (tile + 1) * LANES].reshape(
                    2 * count, LANES
                )
                for tile in range(tiles)
            ],
            axis=1,
        )
        values = jnp.dot(x, hot, preferred_element_type=F32)
        y_buf[2 * start : 2 * (start + count)] = values
        stop = 2 * (start + count) if part + 1 < len(runs) else rows
        values = y_buf[2 * start : stop]
        square = values * values
        high = square.astype(BF16)
        low = (square - high.astype(F32)).astype(BF16)
        for piece in (high, low):
            sums = jnp.dot(gather_bands[:, 2 * start : stop], piece, preferred_element_type=F32)
            power = sums if power is None else power + sums
    scale = lax.rsqrt(power * (1.0 / (2 * BAND)) + EPSILON)
    high = scale.astype(BF16).astype(F32)
    mid = (scale - high).astype(BF16).astype(F32)
    low = scale - high - mid
    third = iota(scale.shape, 0) // 16
    pieces = jnp.where(third == 0, high, jnp.where(third == 1, mid, low))
    pieces = jnp.concatenate(
        [pieces, jnp.zeros((LANES - pieces.shape[0], pieces.shape[1]), F32)], axis=0
    ).astype(BF16)
    white = y_buf[...] * jnp.dot(spread_bands, pieces, preferred_element_type=F32)
    white = white.astype(BF16)
    parted = []
    for chunk in range(chunks):
        mixed = white[chunk * 2 * LANES : (chunk + 1) * 2 * LANES]
        part = lax.dot_general(
            mixed, split, (((0,), (0,)), ((), ())), preferred_element_type=F32
        )
        parted.append(part.astype(BF16))
    white_buf[...] = jnp.concatenate(
        [part[:, :LANES] for part in parted] + [part[:, LANES:] for part in parted], axis=1
    )
    for place, reach_here in enumerate(places):
        for reach in range(REACH):

            @pl.when(reach_here == reach)
            def _():
                outs[reach][...] = white_buf[place * width : (place + 1) * width]

    if branched:
        branch_copy.wait()


def pick_blocks(kept, branched, spectra, pair_sides, pair_owner, block_members, case_table):
    _, freqs, parts, stations = spectra.shape
    block_count, width = block_members.shape
    columns = -(-freqs // LANES) * 2 * LANES
    rows = kept * width
    vmem = pl.BlockSpec(memory_space=pltpu.VMEM)
    out_shape = [jax.ShapeDtypeStruct((width, columns), BF16)] * REACH
    out_shape += [jax.ShapeDtypeStruct((1,), jnp.int32)] * branched
    return pl.pallas_call(
        functools.partial(pick_kernel, kept, branched, "sta"),
        out_shape=out_shape,
        in_specs=[pl.BlockSpec(memory_space=pltpu.HBM)] * 5,
        out_specs=[vmem] * REACH + [pl.BlockSpec(memory_space=pltpu.HBM)] * branched,
        scratch_shapes=[
            pltpu.SMEM(pair_sides.shape, jnp.int32),
            pltpu.SMEM(pair_owner.shape, jnp.int32),
            pltpu.VMEM(block_members.shape, jnp.int32),
            pltpu.SMEM(case_table.shape, jnp.int32),
            pltpu.SMEM((1,), jnp.int32),
            pltpu.VMEM((freqs, parts, stations), BF16),
            pltpu.VMEM((columns, rows), F32),
            pltpu.VMEM((rows, columns), BF16),
            pltpu.SemaphoreType.DMA((COPIES + 5,)),
        ],
        compiler_params=pltpu.CompilerParams(vmem_limit_bytes=PICK_VMEM_LIMIT),
        cost_estimate=pl.CostEstimate(
            flops=2 * rows * stations * freqs * parts,
            bytes_accessed=2 * spectra.size + 4 * rows * columns,
            transcendentals=0,
        ),
        name="pick_and_whiten",
    )(pair_sides, pair_owner, block_members, case_table, spectra)


def case_number(first, second, needs, sta_count):
    return (first * sta_count + second) * (1 << (REACH - 1)) + needs // 2


def routes(sta_count):
    def load(first, second, sent):
        links = {}
        for full, flows, _, other in schedule(first, second, sta_count):
            for source, owner in flows if full or other in sent else flows[:1]:
                step = 1 if owner > source else -1
                for place in range(source, owner, step):
                    links[place, step] = links.get((place, step), 0) + 1
        return max(links.values())

    branches = []
    cases = [0] * case_number(sta_count, 0, 0, sta_count)
    for first, second in itertools.permutations(range(sta_count), 2):
        others = [step[3] for step in schedule(first, second, sta_count) if not step[0]]
        sets = [
            sent
            for count in range(len(others), -1, -1)
            for sent in itertools.combinations(others, count)
        ]
        for named in itertools.combinations(range(REACH), 2):
            fits = [sent for sent in sets if set(named) & set(others) <= set(sent)]
            branch = (first, second, min(fits, key=lambda sent: load(first, second, sent)))
            if branch not in branches:
                branches.append(branch)
            needs = sum(1 << reach for reach in named)
            cases[case_number(first, second, needs, sta_count)] = branches.index(branch)
    return branches, cases


def phase_tables(sub_count, sub_freqs, groups, lag_rows):
    chunks = -(-sub_freqs // LANES)
    total = sub_count * sub_freqs
    freq = np.arange(total, dtype=np.int64).reshape(sub_count, 1, sub_freqs)
    middle = [2 * (group * lag_rows - LAGS // 2) + lag_rows - 1 for group in range(groups)]
    away = [step for step in range(1, lag_rows) if step % 2 != lag_rows % 2]

    def table(twice, forms, tile, dtype):
        twice = np.array(twice or [0], dtype=np.int64).reshape(1, -1, 1)
        angle = np.mod(freq * twice, 2 * total) * (math.pi / total)
        rows = np.stack([form(angle) for form in forms], axis=2)
        rows = rows.reshape(sub_count, -1, sub_freqs)
        pad = ((0, 0), (0, -rows.shape[1] % tile), (0, chunks * LANES - sub_freqs))
        return np.pad(rows, pad).astype(np.float32).astype(dtype)

    turns = table(middle, (np.cos, np.sin), 8, np.float32)
    offsets = table(away, (np.cos, np.sin, lambda angle: -np.sin(angle)), 16, BF16)
    return turns, offsets, len(away)


def lag_kernel(hops, slots, lag_rows, away, block_count, branched, *refs):
    sub_count = lax.axis_size("sub")
    hr_count = lax.axis_size("hr")
    pair_ref, owner_ref, place_ref, turn_ref, offset_ref = refs[:5]
    blocks, outs = refs[5 : -2 - len(hops)], refs[-2 - len(hops) : -2]
    buf, sems = refs[-2:]
    width = buf.shape[3]
    span = buf.shape[4] // 2
    middle_lag = lag_rows % 2
    my_sub = lax.axis_index("sub")
    my_hr = lax.axis_index("hr")
    my_sta = lax.axis_index("sta")
    sta_count = lax.axis_size("sta")

    pairs = read_pairs(pair_ref, owner_ref, block_count)
    order = [jnp.int32(reach) for reach in range(REACH)]
    if branched:
        first, second, _ = case_of(pairs, sta_count)
        entry = (first * sta_count + second) * 2 + (my_sta != first).astype(jnp.int32)
        order = [place_ref[entry * REACH + reach] for reach in range(REACH)]
    owned = []
    for owner, _, homes in pairs:
        places = []
        for home in homes:
            reach_here = lax.rem(home - my_sta + sta_count, sta_count)
            place_here = order[0]
            for reach in range(1, REACH):
                place_here = jnp.where(reach_here == reach, order[reach], place_here)
            places.append(place_here)
        owned.append((owner == my_sta, places))
    ends = []
    for slot in slots:
        count = jnp.int32(0)
        slot_ends = [jnp.int32(-1)] * 2
        for mine, places in owned:
            hit = mine & (count == slot)
            count = count + mine.astype(jnp.int32)
            slot_ends = [jnp.where(hit, new, old) for new, old in zip(places, slot_ends)]
        ends.append(slot_ends)

    def fetches(index, act):
        for side in range(2):
            for place in range(REACH):

                @pl.when(ends[index][side] == place)
                def _():
                    for step in range(sub_count):
                        act(
                            pltpu.make_async_copy(
                                blocks[place * sub_count + step],
                                buf.at[index, side, step],
                                sems.at[index, side, step],
                            )
                        )

    for index in range(len(slots)):
        fetches(index, lambda copy: copy.start())

    for index in range(len(slots)):

        @pl.when(ends[index][0] < 0)
        def _():
            for out in outs:
                out[:, index] = jnp.zeros((lag_rows, width, width), out.dtype)

        fetches(index, lambda copy: copy.wait())

        @pl.when(ends[index][0] >= 0)
        def _():
            total = None
            for step in range(sub_count):
                sub = lax.rem(my_sub + step, sub_count)
                real = buf[index, 0, step, :, :span]
                imag = buf[index, 0, step, :, span:]
                scaled_real, scaled_imag = [real] * middle_lag, [imag] * middle_lag
                for near in range(away):
                    cosine, sine, minus = (
                        offset_ref[sub, 3 * near + form : 3 * near + form + 1, :]
                        for form in range(3)
                    )
                    scaled_real += [real * cosine, imag * minus]
                    scaled_imag += [imag * cosine, real * sine]
                real = buf[index, 1, step, :, :span].astype(F32)
                imag = buf[index, 1, step, :, span:].astype(F32)
                turned_real, turned_imag = [], []
                for hop in hops:
                    group = lax.rem(my_hr + hop, hr_count) * sub_count + my_sub
                    cosine = turn_ref[sub, pl.ds(2 * group, 1), :]
                    sine = turn_ref[sub, pl.ds(2 * group + 1, 1), :]
                    turned_real.append((real * cosine + imag * sine).astype(BF16))
                    turned_imag.append((imag * cosine - real * sine).astype(BF16))
                for scaled, turned in ((scaled_real, turned_real), (scaled_imag, turned_imag)):
                    part = dot_nt(jnp.concatenate(scaled, axis=0), jnp.concatenate(turned, axis=0))
                    total = part if total is None else total + part
            for place, out in enumerate(outs):
                columns = slice(place * width, (place + 1) * width)
                if middle_lag:
                    out[lag_rows // 2, index] = total[:width, columns].astype(out.dtype)
                for near in range(away):
                    start = (middle_lag + 2 * near) * width
                    even = total[start : start + width, columns]
                    odd = total[start + width : start + 2 * width, columns]
                    below = (lag_rows - 1) // 2 - near - middle_lag
                    above = lag_rows - 1 - below
                    out[above, index] = (even + odd).astype(out.dtype)
                    out[below, index] = (even - odd).astype(out.dtype)


def on_device(spectra, pair_blocks, pair_owner, block_members):
    hour_count, sub_freqs, _, _ = spectra.shape
    block_count, width = block_members.shape
    sta_count, hr_count, sub_count = (lax.axis_size(axis) for axis in ("sta", "hr", "sub"))
    groups = hr_count * sub_count
    lag_rows = LAGS // groups
    norming = 1.0 / math.sqrt(hour_count * hr_count * sub_count * sub_freqs)
    pair_sides = pair_blocks.T
    turns, offsets, away = phase_tables(sub_count, sub_freqs, groups, lag_rows)

    owners_at_most = pair_owner.shape[0] - CAP + 1
    branched = owners_at_most == 2 and sta_count == REACH
    kept = min(REACH, owners_at_most)
    branches, cases = routes(sta_count) if branched else ([], [0])
    places = place_table(sta_count) if branched else [0]
    case_table = jnp.asarray(np.array(cases + places, dtype=np.int32))
    places = jnp.asarray(np.array(places, dtype=np.int32))
    picked = pick_blocks(
        kept, branched, spectra, pair_sides, pair_owner, block_members, case_table
    )

    def halves(block):
        blocks = [block]
        for step in range(1, sub_count):
            swap = [((sub + step) % sub_count, sub) for sub in range(sub_count)]
            blocks.append(lax.ppermute(block, "sub", swap))
        return blocks

    def exchange(*picked):
        blocks = halves(picked[0])
        for reach in range(1, REACH):
            shift = [((home + reach) % sta_count, home) for home in range(sta_count)]
            blocks += halves(lax.ppermute(picked[reach], "sta", shift))
        return blocks

    def exchange_two(first, second, sent, *picked):
        blocks = halves(picked[0])
        for block, (full, flows, _, other) in zip(picked[1:], schedule(first, second, sta_count)):
            flows = flows if full or other in sent else flows[:1]
            blocks += halves(lax.ppermute(block, "sta", flows))
        return blocks

    if branched:
        steps = [functools.partial(exchange_two, *branch) for branch in branches]
        blocks = lax.switch(picked[REACH][0], steps, *picked[:REACH])
    else:
        blocks = exchange(*picked[:REACH])

    smem = pl.BlockSpec(memory_space=pltpu.SMEM)
    vmem = pl.BlockSpec(memory_space=pltpu.VMEM)
    hbm = pl.BlockSpec(memory_space=pltpu.HBM)
    row = picked[0].shape[1]
    versions = (lag_rows % 2 + 2 * away) * width

    def products(hops, slots, dtype, name):
        return pl.pallas_call(
            functools.partial(
                lag_kernel, hops, slots, lag_rows, away, block_count, branched
            ),
            out_shape=[jax.ShapeDtypeStruct((lag_rows, len(slots), width, width), dtype)]
            * len(hops),
            in_specs=[smem, smem, smem, vmem, vmem] + [hbm] * len(blocks),
            out_specs=[vmem] * len(hops),
            scratch_shapes=[
                pltpu.VMEM((len(slots), 2, sub_count, width, row), BF16),
                pltpu.SemaphoreType.DMA((len(slots), 2, sub_count)),
            ],
            compiler_params=pltpu.CompilerParams(vmem_limit_bytes=LAG_VMEM_LIMIT),
            cost_estimate=pl.CostEstimate(
                flops=2 * len(slots) * len(hops) * versions * width * sub_count * row,
                bytes_accessed=4 * len(slots) * sub_count * width * row,
                transcendentals=0,
            ),
            name=name,
        )(pair_sides, pair_owner, places, turns, offsets, *blocks)

    hops, slots = tuple(range(1, hr_count)), tuple(range(CAP))
    sent = products(hops, slots, BF16, "lags_to_send")
    received = []
    for hop, part in zip(hops, sent):
        to_device = [(hr, (hr + hop) % hr_count) for hr in range(hr_count)]
        received.append(lax.ppermute(part, "hr", to_device))
    (summed,) = products((0,), slots, F32, "lags_to_keep")
    for part in received:
        summed = summed + part.astype(F32)
    return (summed * norming).astype(BF16)


def solution(mesh):
    placed = (P(("grp", "hr"), "sub", None, "sta"), P(), P(), P("sta", None))
    return jax.shard_map(
        on_device,
        mesh=mesh,
        in_specs=placed,
        out_specs=P(("grp", "hr", "sub"), "sta", None, None),
        check_vma=False,
    )
```

```python
import functools
import itertools
import math

import jax
import jax.numpy as jnp
import numpy as np
from jax import lax
from jax.experimental import pallas as pl
from jax.experimental.pallas import tpu as pltpu
from jax.sharding import PartitionSpec as P

BAND = 50
LAGS = 16
CAP = 3
REACH = 4
EPSILON = 1e-05
LANES = 128
F32 = jnp.float32
BF16 = jnp.bfloat16
PICK_VMEM_LIMIT = 59 * 1024 * 1024
LAG_VMEM_LIMIT = 32 * 1024 * 1024

NT = (((1,), (1,)), ((), ()))


def dot_nt(left, right):
    return lax.dot_general(left, right, NT, preferred_element_type=F32)


def iota(shape, dim):
    return lax.broadcasted_iota(jnp.int32, shape, dim)


def schedule(first, second, sta_count):
    every = range(1, REACH)
    if 0 < first < sta_count - 1:
        ring = 1 if 2 * first < sta_count else REACH - 1
        pairs = [((home + ring) % sta_count, home) for home in range(sta_count)]
    else:
        pairs = [(home ^ 1, home) for home in range(sta_count)]
    source = {target: start for start, target in pairs}
    reaches = [[(source[owner] - owner) % sta_count] for owner in (first, second)]
    both = [reach for reach in every if [reach] not in reaches]
    for taken in reaches:
        taken += both + [reach for reach in every if reach not in taken + both]
    plan = [(True, pairs, reaches[0][0], reaches[1][0])]
    for one, other in zip(reaches[0][1:], reaches[1][1:]):
        flows = [((first + one) % sta_count, first), ((second + other) % sta_count, second)]
        plan.append((False, flows, one, other))
    return plan[:1] + sorted(plan[1:], key=lambda step: step[1][1][0] == first)


def place_table(sta_count):
    table = []
    for first, second in itertools.product(range(sta_count), repeat=2):
        places = [0] * (2 * REACH)
        if first != second:
            for place, step in enumerate(schedule(first, second, sta_count)):
                places[step[2]], places[REACH + step[3]] = place + 1, place + 1
        table += places
    return table


def read_pairs(pair_ref, owner_ref, block_count):
    pairs = []
    for pair in range(owner_ref.shape[0]):
        blocks = [pair_ref[side, pair] for side in range(2)]
        pairs.append((owner_ref[pair], blocks, [lax.div(block, block_count) for block in blocks]))
    return pairs


def case_of(pairs, sta_count):
    first = second = needs = jnp.int32(0)
    for owner, _, homes in pairs:
        count = jnp.int32(0)
        for other, _, _ in pairs:
            count = count + (other == owner).astype(jnp.int32)
        ends = [lax.rem(home - owner + sta_count, sta_count) for home in homes]
        first = jnp.where(count == CAP, owner, first)
        second = jnp.where(count < CAP, owner, second)
        needs = jnp.where(count < CAP, (1 << ends[0]) | (1 << ends[1]), needs)
    return first, second, case_number(first, second, needs, sta_count)


def pick_kernel(kept, branched, sta_axis, pair_hbm, owner_hbm, member_hbm, case_hbm, x_ref, *rest):
    outs = rest[:REACH]
    pair_ref, owner_ref, member_ref, case_ref, number_ref, x_buf, y_buf, white_buf, sems = rest[
        REACH + branched :
    ]
    freqs, tiles = x_buf.shape[0], x_buf.shape[2] // LANES
    block_count, width = member_ref.shape
    rows = y_buf.shape[0]
    chunks = rows // (2 * LANES)

    runs = [(start, min(LANES, freqs - start)) for start in range(0, freqs, LANES)]

    if branched:
        branch_copy = pltpu.make_async_copy(number_ref, rest[REACH], sems.at[len(runs) + 4])

    def fetch(part):
        run = pl.ds(*runs[part])
        return pltpu.make_async_copy(x_ref.at[0, run], x_buf.at[run], sems.at[part])

    small = [
        pltpu.make_async_copy(source, target, sems.at[len(runs) + index])
        for index, (source, target) in enumerate(
            (
                (pair_hbm, pair_ref),
                (owner_hbm, owner_ref),
                (member_hbm, member_ref),
                (case_hbm, case_ref),
            )
        )
    ]
    for copy in small:
        copy.start()
    for part in range(len(runs)):
        fetch(part).start()

    def bands(shape, part_dim):
        part, place = iota(shape, part_dim), iota(shape, 1 - part_dim)
        low = (place % 16) * (2 * BAND)
        hit = (part >= low) & (part < low + 2 * BAND) & (part < 2 * freqs) & (place < 48)
        return jnp.where(hit, 1.0, 0.0).astype(BF16)

    gather_bands, spread_bands = bands((48, rows), 1), bands((rows, LANES), 0)
    row, col = iota((2 * LANES, 2 * LANES), 0), iota((2 * LANES, 2 * LANES), 1)
    split = jnp.where(row == 2 * (col % LANES) + col // LANES, 1.0, 0.0).astype(BF16)
    y_buf[2 * freqs :] = jnp.zeros((rows - 2 * freqs, kept * width), F32)
    for copy in small:
        copy.wait()

    my_sta = lax.axis_index(sta_axis)
    sta_count = lax.axis_size(sta_axis)
    pairs = read_pairs(pair_ref, owner_ref, block_count)
    found, wanted = jnp.int32(0), []
    for reach in range(REACH):
        owner = lax.rem(my_sta - reach + REACH * sta_count, sta_count)
        chosen = jnp.int32(-1)
        for pair_owner, blocks, homes in pairs:
            for block, home in zip(blocks, homes):
                hit = (pair_owner == owner) & (home == my_sta)
                chosen = jnp.where(hit, lax.rem(block, block_count), chosen)
        wanted.append((found, chosen))
        found = found + (chosen >= 0).astype(jnp.int32)
    places, station = [], []
    for place in range(kept):
        reach_here, block_here = jnp.int32(-1), jnp.int32(0)
        for reach, (rank, chosen) in enumerate(wanted):
            hit = (rank == place) & (chosen >= 0)
            reach_here = jnp.where(hit, reach, reach_here)
            block_here = jnp.where(hit, chosen, block_here)
        places.append(reach_here)
        station.append(member_ref[pl.ds(block_here, 1), :])
    station = jnp.concatenate(station, axis=1)
    hot = jnp.where(station == iota((tiles * LANES, kept * width), 0), 1.0, 0.0).astype(BF16)

    if branched:
        first, second, case = case_of(pairs, sta_count)
        number_ref[0] = case_ref[case]
        branch_copy.start()
        base = case_number(sta_count, 0, 0, sta_count) + (first * sta_count + second) * 2 * REACH
        for place, reach_here in enumerate(places):
            reach = jnp.maximum(reach_here, 0)
            owner = lax.rem(my_sta - reach + REACH * sta_count, sta_count)
            step = case_ref[base + jnp.where(owner == first, 0, REACH) + reach]
            places[place] = jnp.where(reach_here < 0, -1, step)

    power = None
    for part, (start, count) in enumerate(runs):
        fetch(part).wait()
        x = jnp.concatenate(
            [
                x_buf[start : start + count, :, tile * LANES : (tile + 1) * LANES].reshape(
                    2 * count, LANES
                )
                for tile in range(tiles)
            ],
            axis=1,
        )
        values = jnp.dot(x, hot, preferred_element_type=F32)
        y_buf[2 * start : 2 * (start + count)] = values
        stop = 2 * (start + count) if part + 1 < len(runs) else rows
        values = y_buf[2 * start : stop]
        square = values * values
        high = square.astype(BF16)
        low = (square - high.astype(F32)).astype(BF16)
        for piece in (high, low):
            sums = jnp.dot(gather_bands[:, 2 * start : stop], piece, preferred_element_type=F32)
            power = sums if power is None else power + sums
    scale = lax.rsqrt(power * (1.0 / (2 * BAND)) + EPSILON)
    high = scale.astype(BF16).astype(F32)
    mid = (scale - high).astype(BF16).astype(F32)
    low = scale - high - mid
    third = iota(scale.shape, 0) // 16
    pieces = jnp.where(third == 0, high, jnp.where(third == 1, mid, low))
    pieces = jnp.concatenate(
        [pieces, jnp.zeros((LANES - pieces.shape[0], pieces.shape[1]), F32)], axis=0
    ).astype(BF16)
    white = y_buf[...] * jnp.dot(spread_bands, pieces, preferred_element_type=F32)
    white = white.astype(BF16)
    parted = []
    for chunk in range(chunks):
        mixed = white[chunk * 2 * LANES : (chunk + 1) * 2 * LANES]
        part = lax.dot_general(
            mixed, split, (((0,), (0,)), ((), ())), preferred_element_type=F32
        )
        parted.append(part.astype(BF16))
    white_buf[...] = jnp.concatenate(
        [part[:, :LANES] for part in parted] + [part[:, LANES:] for part in parted], axis=1
    )
    for place, reach_here in enumerate(places):
        for reach in range(REACH):

            @pl.when(reach_here == reach)
            def _():
                outs[reach][...] = white_buf[place * width : (place + 1) * width]

    if branched:
        branch_copy.wait()


def pick_blocks(kept, branched, spectra, pair_sides, pair_owner, block_members, case_table):
    _, freqs, parts, stations = spectra.shape
    block_count, width = block_members.shape
    columns = -(-freqs // LANES) * 2 * LANES
    rows = kept * width
    vmem = pl.BlockSpec(memory_space=pltpu.VMEM)
    out_shape = [jax.ShapeDtypeStruct((width, columns), BF16)] * REACH
    out_shape += [jax.ShapeDtypeStruct((1,), jnp.int32)] * branched
    return pl.pallas_call(
        functools.partial(pick_kernel, kept, branched, "sta"),
        out_shape=out_shape,
        in_specs=[pl.BlockSpec(memory_space=pltpu.HBM)] * 5,
        out_specs=[vmem] * REACH + [pl.BlockSpec(memory_space=pltpu.HBM)] * branched,
        scratch_shapes=[
            pltpu.SMEM(pair_sides.shape, jnp.int32),
            pltpu.SMEM(pair_owner.shape, jnp.int32),
            pltpu.VMEM(block_members.shape, jnp.int32),
            pltpu.SMEM(case_table.shape, jnp.int32),
            pltpu.SMEM((1,), jnp.int32),
            pltpu.VMEM((freqs, parts, stations), BF16),
            pltpu.VMEM((columns, rows), F32),
            pltpu.VMEM((rows, columns), BF16),
            pltpu.SemaphoreType.DMA((-(-freqs // LANES) + 5,)),
        ],
        compiler_params=pltpu.CompilerParams(vmem_limit_bytes=PICK_VMEM_LIMIT),
        cost_estimate=pl.CostEstimate(
            flops=2 * rows * stations * freqs * parts,
            bytes_accessed=2 * spectra.size + 4 * rows * columns,
            transcendentals=0,
        ),
        name="pick_and_whiten",
    )(pair_sides, pair_owner, block_members, case_table, spectra)


def case_number(first, second, needs, sta_count):
    return (first * sta_count + second) * (1 << (REACH - 1)) + needs // 2


def routes(sta_count):
    def load(first, second, sent):
        links = {}
        for full, flows, _, other in schedule(first, second, sta_count):
            for source, owner in flows if full or other in sent else flows[:1]:
                step = 1 if owner > source else -1
                for place in range(source, owner, step):
                    links[place, step] = links.get((place, step), 0) + 1
        return max(links.values())

    branches = []
    cases = [0] * case_number(sta_count, 0, 0, sta_count)
    for first, second in itertools.permutations(range(sta_count), 2):
        others = [step[3] for step in schedule(first, second, sta_count) if not step[0]]
        sets = [
            sent
            for count in range(len(others), -1, -1)
            for sent in itertools.combinations(others, count)
        ]
        for named in itertools.combinations(range(REACH), 2):
            fits = [sent for sent in sets if set(named) & set(others) <= set(sent)]
            branch = (first, second, min(fits, key=lambda sent: load(first, second, sent)))
            if branch not in branches:
                branches.append(branch)
            needs = sum(1 << reach for reach in named)
            cases[case_number(first, second, needs, sta_count)] = branches.index(branch)
    return branches, cases


def phase_tables(sub_count, sub_freqs, groups, lag_rows):
    chunks = -(-sub_freqs // LANES)
    total = sub_count * sub_freqs
    freq = np.arange(total, dtype=np.int64).reshape(sub_count, 1, sub_freqs)
    middle = [2 * (group * lag_rows - LAGS // 2) + lag_rows - 1 for group in range(groups)]
    away = [step for step in range(1, lag_rows) if step % 2 != lag_rows % 2]

    def table(twice, forms, tile, dtype):
        twice = np.array(twice or [0], dtype=np.int64).reshape(1, -1, 1)
        angle = np.mod(freq * twice, 2 * total) * (math.pi / total)
        rows = np.stack([form(angle) for form in forms], axis=2)
        rows = rows.reshape(sub_count, -1, sub_freqs)
        pad = ((0, 0), (0, -rows.shape[1] % tile), (0, chunks * LANES - sub_freqs))
        return np.pad(rows, pad).astype(np.float32).astype(dtype)

    turns = table(middle, (np.cos, np.sin), 8, np.float32)
    offsets = table(away, (np.cos, np.sin, lambda angle: -np.sin(angle)), 16, BF16)
    return turns, offsets, len(away)


def lag_kernel(hops, slots, lag_rows, away, block_count, branched, *refs):
    sub_count = lax.axis_size("sub")
    hr_count = lax.axis_size("hr")
    pair_ref, owner_ref, place_ref, turn_ref, offset_ref = refs[:5]
    blocks, outs = refs[5 : -2 - len(hops)], refs[-2 - len(hops) : -2]
    buf, sems = refs[-2:]
    width = buf.shape[3]
    span = buf.shape[4] // 2
    middle_lag = lag_rows % 2
    my_sub = lax.axis_index("sub")
    my_hr = lax.axis_index("hr")
    my_sta = lax.axis_index("sta")
    sta_count = lax.axis_size("sta")

    pairs = read_pairs(pair_ref, owner_ref, block_count)
    order = [jnp.int32(reach) for reach in range(REACH)]
    if branched:
        first, second, _ = case_of(pairs, sta_count)
        entry = (first * sta_count + second) * 2 + (my_sta != first).astype(jnp.int32)
        order = [place_ref[entry * REACH + reach] for reach in range(REACH)]
    owned = []
    for owner, _, homes in pairs:
        places = []
        for home in homes:
            reach_here = lax.rem(home - my_sta + sta_count, sta_count)
            place_here = order[0]
            for reach in range(1, REACH):
                place_here = jnp.where(reach_here == reach, order[reach], place_here)
            places.append(place_here)
        owned.append((owner == my_sta, places))
    ends = []
    for slot in slots:
        count = jnp.int32(0)
        slot_ends = [jnp.int32(-1)] * 2
        for mine, places in owned:
            hit = mine & (count == slot)
            count = count + mine.astype(jnp.int32)
            slot_ends = [jnp.where(hit, new, old) for new, old in zip(places, slot_ends)]
        ends.append(slot_ends)

    def fetch(index, side, step, place=0):
        return pltpu.make_async_copy(
            blocks[place * sub_count + step], buf.at[index, side, step], sems.at[index, side, step]
        )

    for index, slot_ends in enumerate(ends):
        for side, end in enumerate(slot_ends):
            for place in range(REACH):

                @pl.when(jnp.maximum(end, 0) == place)
                def _():
                    for step in range(sub_count):
                        fetch(index, side, step, place).start()

    for index, (left, _) in enumerate(ends):

        def keep(value):
            return jnp.where(left >= 0, value, 0.0)

        total = None
        for step in range(sub_count):
            for side in range(2):
                fetch(index, side, step).wait()
            sub = lax.rem(my_sub + step, sub_count)
            real = buf[index, 0, step, :, :span]
            imag = buf[index, 0, step, :, span:]
            scaled_real, scaled_imag = [real] * middle_lag, [imag] * middle_lag
            for near in range(away):
                cosine, sine, minus = (
                    offset_ref[sub, 3 * near + form : 3 * near + form + 1, :]
                    for form in range(3)
                )
                scaled_real += [real * cosine, imag * minus]
                scaled_imag += [imag * cosine, real * sine]
            real = buf[index, 1, step, :, :span].astype(F32)
            imag = buf[index, 1, step, :, span:].astype(F32)
            turned_real, turned_imag = [], []
            for hop in hops:
                group = lax.rem(my_hr + hop, hr_count) * sub_count + my_sub
                cosine = turn_ref[sub, pl.ds(2 * group, 1), :]
                sine = turn_ref[sub, pl.ds(2 * group + 1, 1), :]
                turned_real.append((real * cosine + imag * sine).astype(BF16))
                turned_imag.append((imag * cosine - real * sine).astype(BF16))
            for scaled, turned in ((scaled_real, turned_real), (scaled_imag, turned_imag)):
                part = dot_nt(jnp.concatenate(scaled, axis=0), jnp.concatenate(turned, axis=0))
                total = part if total is None else total + part
        for place, out in enumerate(outs):
            columns = slice(place * width, (place + 1) * width)
            if middle_lag:
                out[lag_rows // 2, index] = keep(total[:width, columns]).astype(out.dtype)
            for near in range(away):
                start = (middle_lag + 2 * near) * width
                even = total[start : start + width, columns]
                odd = total[start + width : start + 2 * width, columns]
                below = (lag_rows - 1) // 2 - near - middle_lag
                above = lag_rows - 1 - below
                out[above, index] = keep(even + odd).astype(out.dtype)
                out[below, index] = keep(even - odd).astype(out.dtype)


def on_device(spectra, pair_blocks, pair_owner, block_members):
    hour_count, sub_freqs, _, _ = spectra.shape
    block_count, width = block_members.shape
    sta_count, hr_count, sub_count = (lax.axis_size(axis) for axis in ("sta", "hr", "sub"))
    groups = hr_count * sub_count
    lag_rows = LAGS // groups
    norming = 1.0 / math.sqrt(hour_count * hr_count * sub_count * sub_freqs)
    pair_sides = pair_blocks.T
    turns, offsets, away = phase_tables(sub_count, sub_freqs, groups, lag_rows)

    owners_at_most = pair_owner.shape[0] - CAP + 1
    branched = owners_at_most == 2 and sta_count == REACH
    kept = min(REACH, owners_at_most)
    branches, cases = routes(sta_count) if branched else ([], [0])
    places = place_table(sta_count) if branched else [0]
    case_table = jnp.asarray(np.array(cases + places, dtype=np.int32))
    places = jnp.asarray(np.array(places, dtype=np.int32))
    picked = pick_blocks(
        kept, branched, spectra, pair_sides, pair_owner, block_members, case_table
    )

    def halves(block):
        blocks = [block]
        for step in range(1, sub_count):
            swap = [((sub + step) % sub_count, sub) for sub in range(sub_count)]
            blocks.append(lax.ppermute(block, "sub", swap))
        return blocks

    def exchange(*picked):
        blocks = halves(picked[0])
        for reach in range(1, REACH):
            shift = [((home + reach) % sta_count, home) for home in range(sta_count)]
            blocks += halves(lax.ppermute(picked[reach], "sta", shift))
        return blocks

    def exchange_two(first, second, sent, *picked):
        blocks = halves(picked[0])
        for block, (full, flows, _, other) in zip(picked[1:], schedule(first, second, sta_count)):
            flows = flows if full or other in sent else flows[:1]
            blocks += halves(lax.ppermute(block, "sta", flows))
        return blocks

    if branched:
        steps = [functools.partial(exchange_two, *branch) for branch in branches]
        blocks = lax.switch(picked[REACH][0], steps, *picked[:REACH])
    else:
        blocks = exchange(*picked[:REACH])

    smem = pl.BlockSpec(memory_space=pltpu.SMEM)
    vmem = pl.BlockSpec(memory_space=pltpu.VMEM)
    hbm = pl.BlockSpec(memory_space=pltpu.HBM)
    row = picked[0].shape[1]
    versions = (lag_rows % 2 + 2 * away) * width

    def products(hops, slots, dtype, name):
        return pl.pallas_call(
            functools.partial(
                lag_kernel, hops, slots, lag_rows, away, block_count, branched
            ),
            out_shape=[jax.ShapeDtypeStruct((lag_rows, len(slots), width, width), dtype)]
            * len(hops),
            in_specs=[smem, smem, smem, vmem, vmem] + [hbm] * len(blocks),
            out_specs=[vmem] * len(hops),
            scratch_shapes=[
                pltpu.VMEM((len(slots), 2, sub_count, width, row), BF16),
                pltpu.SemaphoreType.DMA((len(slots), 2, sub_count)),
            ],
            compiler_params=pltpu.CompilerParams(vmem_limit_bytes=LAG_VMEM_LIMIT),
            cost_estimate=pl.CostEstimate(
                flops=2 * len(slots) * len(hops) * versions * width * sub_count * row,
                bytes_accessed=4 * len(slots) * sub_count * width * row,
                transcendentals=0,
            ),
            name=name,
        )(pair_sides, pair_owner, places, turns, offsets, *blocks)

    hops, slots = tuple(range(1, hr_count)), tuple(range(CAP))
    sent = products(hops, slots, BF16, "lags_to_send")
    received = []
    for hop, part in zip(hops, sent):
        to_device = [(hr, (hr + hop) % hr_count) for hr in range(hr_count)]
        received.append(lax.ppermute(part, "hr", to_device))
    (summed,) = products((0,), slots, F32, "lags_to_keep")
    for part in received:
        summed = summed + part.astype(F32)
    return (summed * norming).astype(BF16)


def solution(mesh):
    placed = (P(("grp", "hr"), "sub", None, "sta"), P(), P(), P("sta", None))
    return jax.shard_map(
        on_device,
        mesh=mesh,
        in_specs=placed,
        out_specs=P(("grp", "hr", "sub"), "sta", None, None),
        check_vma=False,
    )
```

```python
import functools
import itertools
import math

import jax
import jax.numpy as jnp
import numpy as np
from jax import lax
from jax.experimental import pallas as pl
from jax.experimental.pallas import tpu as pltpu
from jax.sharding import PartitionSpec as P

BAND = 50
LAGS = 16
CAP = 3
REACH = 4
COPIES = 2
EPSILON = 1e-05
LANES = 128
F32 = jnp.float32
BF16 = jnp.bfloat16
PICK_VMEM_LIMIT = 59 * 1024 * 1024
LAG_VMEM_LIMIT = 32 * 1024 * 1024

NT = (((1,), (1,)), ((), ()))


def dot_nt(left, right):
    return lax.dot_general(left, right, NT, preferred_element_type=F32)


def iota(shape, dim):
    return lax.broadcasted_iota(jnp.int32, shape, dim)


def schedule(first, second, sta_count):
    every = range(1, REACH)
    if 0 < first < sta_count - 1:
        ring = 1 if 2 * first < sta_count else REACH - 1
        pairs = [((home + ring) % sta_count, home) for home in range(sta_count)]
    else:
        pairs = [(home ^ 1, home) for home in range(sta_count)]
    source = {target: start for start, target in pairs}
    reaches = [[(source[owner] - owner) % sta_count] for owner in (first, second)]
    both = [reach for reach in every if [reach] not in reaches]
    for taken in reaches:
        taken += both + [reach for reach in every if reach not in taken + both]
    plan = [(True, pairs, reaches[0][0], reaches[1][0])]
    for one, other in zip(reaches[0][1:], reaches[1][1:]):
        flows = [((first + one) % sta_count, first), ((second + other) % sta_count, second)]
        plan.append((False, flows, one, other))
    return plan[:1] + sorted(plan[1:], key=lambda step: step[1][1][0] == first)


def place_table(sta_count):
    table = []
    for first, second in itertools.product(range(sta_count), repeat=2):
        places = [0] * (2 * REACH)
        if first != second:
            for place, step in enumerate(schedule(first, second, sta_count)):
                places[step[2]], places[REACH + step[3]] = place + 1, place + 1
        table += places
    return table


def read_pairs(pair_ref, owner_ref, block_count):
    pairs = []
    for pair in range(owner_ref.shape[0]):
        blocks = [pair_ref[side, pair] for side in range(2)]
        pairs.append((owner_ref[pair], blocks, [lax.div(block, block_count) for block in blocks]))
    return pairs


def case_of(pairs, sta_count):
    first = second = needs = jnp.int32(0)
    for owner, _, homes in pairs:
        count = jnp.int32(0)
        for other, _, _ in pairs:
            count = count + (other == owner).astype(jnp.int32)
        ends = [lax.rem(home - owner + sta_count, sta_count) for home in homes]
        first = jnp.where(count == CAP, owner, first)
        second = jnp.where(count < CAP, owner, second)
        needs = jnp.where(count < CAP, (1 << ends[0]) | (1 << ends[1]), needs)
    return first, second, case_number(first, second, needs, sta_count)


def pick_kernel(kept, branched, sta_axis, pair_hbm, owner_hbm, member_hbm, case_hbm, x_ref, *rest):
    outs = rest[:REACH]
    pair_ref, owner_ref, member_ref, case_ref, number_ref, x_buf, y_buf, white_buf, sems = rest[
        REACH + branched :
    ]
    if branched:
        branch_copy = pltpu.make_async_copy(number_ref, rest[REACH], sems.at[COPIES + 4])
    freqs, tiles = x_buf.shape[0], x_buf.shape[2] // LANES
    block_count, width = member_ref.shape
    rows = y_buf.shape[0]
    chunks = rows // (2 * LANES)

    cut = (freqs // LANES + 1) // 2 * LANES
    runs = [(0, cut), (cut, freqs - cut)]

    def fetch(part):
        run = pl.ds(*runs[part])
        return pltpu.make_async_copy(x_ref.at[0, run], x_buf.at[run], sems.at[part])

    small = [
        pltpu.make_async_copy(source, target, sems.at[COPIES + index])
        for index, (source, target) in enumerate(
            (
                (pair_hbm, pair_ref),
                (owner_hbm, owner_ref),
                (member_hbm, member_ref),
                (case_hbm, case_ref),
            )
        )
    ]
    for copy in small:
        copy.start()
    for part in range(COPIES):
        fetch(part).start()

    def bands(shape, part_dim):
        part, place = iota(shape, part_dim), iota(shape, 1 - part_dim)
        low = (place % 16) * (2 * BAND)
        hit = (part >= low) & (part < low + 2 * BAND) & (part < 2 * freqs) & (place < 48)
        return jnp.where(hit, 1.0, 0.0).astype(BF16)

    gather_bands, spread_bands = bands((48, rows), 1), bands((rows, LANES), 0)
    row, col = iota((2 * LANES, 2 * LANES), 0), iota((2 * LANES, 2 * LANES), 1)
    split = jnp.where(row == 2 * (col % LANES) + col // LANES, 1.0, 0.0).astype(BF16)
    y_buf[2 * freqs :] = jnp.zeros((rows - 2 * freqs, kept * width), F32)
    for copy in small:
        copy.wait()

    my_sta = lax.axis_index(sta_axis)
    sta_count = lax.axis_size(sta_axis)
    pairs = read_pairs(pair_ref, owner_ref, block_count)
    found, wanted = jnp.int32(0), []
    for reach in range(REACH):
        owner = lax.rem(my_sta - reach + REACH * sta_count, sta_count)
        chosen = jnp.int32(-1)
        for pair_owner, blocks, homes in pairs:
            for block, home in zip(blocks, homes):
                hit = (pair_owner == owner) & (home == my_sta)
                chosen = jnp.where(hit, lax.rem(block, block_count), chosen)
        wanted.append((found, chosen))
        found = found + (chosen >= 0).astype(jnp.int32)
    places, station = [], []
    for place in range(kept):
        reach_here, block_here = jnp.int32(-1), jnp.int32(0)
        for reach, (rank, chosen) in enumerate(wanted):
            hit = (rank == place) & (chosen >= 0)
            reach_here = jnp.where(hit, reach, reach_here)
            block_here = jnp.where(hit, chosen, block_here)
        places.append(reach_here)
        station.append(member_ref[pl.ds(block_here, 1), :])
    station = jnp.concatenate(station, axis=1)
    hot = jnp.where(station == iota((tiles * LANES, kept * width), 0), 1.0, 0.0).astype(BF16)

    if branched:
        first, second, case = case_of(pairs, sta_count)
        number_ref[0] = case_ref[case]
        branch_copy.start()
        base = case_number(sta_count, 0, 0, sta_count) + (first * sta_count + second) * 2 * REACH
        for place, reach_here in enumerate(places):
            reach = jnp.maximum(reach_here, 0)
            owner = lax.rem(my_sta - reach + REACH * sta_count, sta_count)
            step = case_ref[base + jnp.where(owner == first, 0, REACH) + reach]
            places[place] = jnp.where(reach_here < 0, -1, step)

    power = None
    for part, (start, count) in enumerate(runs):
        fetch(part).wait()
        x = jnp.concatenate(
            [
                x_buf[start : start + count, :, tile * LANES : (tile + 1) * LANES].reshape(
                    2 * count, LANES
                )
                for tile in range(tiles)
            ],
            axis=1,
        )
        values = jnp.dot(x, hot, preferred_element_type=F32)
        y_buf[2 * start : 2 * (start + count)] = values
        stop = 2 * (start + count) if part + 1 < len(runs) else rows
        values = y_buf[2 * start : stop]
        square = values * values
        high = square.astype(BF16)
        low = (square - high.astype(F32)).astype(BF16)
        for piece in (high, low):
            sums = jnp.dot(gather_bands[:, 2 * start : stop], piece, preferred_element_type=F32)
            power = sums if power is None else power + sums
    scale = lax.rsqrt(power * (1.0 / (2 * BAND)) + EPSILON)
    high = scale.astype(BF16).astype(F32)
    mid = (scale - high).astype(BF16).astype(F32)
    low = scale - high - mid
    third = iota(scale.shape, 0) // 16
    pieces = jnp.where(third == 0, high, jnp.where(third == 1, mid, low))
    pieces = jnp.concatenate(
        [pieces, jnp.zeros((LANES - pieces.shape[0], pieces.shape[1]), F32)], axis=0
    ).astype(BF16)
    white = y_buf[...] * jnp.dot(spread_bands, pieces, preferred_element_type=F32)
    white = white.astype(BF16)
    parted = []
    for chunk in range(chunks):
        mixed = white[chunk * 2 * LANES : (chunk + 1) * 2 * LANES]
        part = lax.dot_general(
            mixed, split, (((0,), (0,)), ((), ())), preferred_element_type=F32
        )
        parted.append(part.astype(BF16))
    white_buf[...] = jnp.concatenate(
        [part[:, :LANES] for part in parted] + [part[:, LANES:] for part in parted], axis=1
    )
    for place, reach_here in enumerate(places):
        for reach in range(REACH):

            @pl.when(reach_here == reach)
            def _():
                outs[reach][...] = white_buf[place * width : (place + 1) * width]

    if branched:
        branch_copy.wait()


def pick_blocks(kept, branched, spectra, pair_sides, pair_owner, block_members, case_table):
    _, freqs, parts, stations = spectra.shape
    block_count, width = block_members.shape
    columns = -(-freqs // LANES) * 2 * LANES
    rows = kept * width
    vmem = pl.BlockSpec(memory_space=pltpu.VMEM)
    out_shape = [jax.ShapeDtypeStruct((width, columns), BF16)] * REACH
    out_shape += [jax.ShapeDtypeStruct((1,), jnp.int32)] * branched
    return pl.pallas_call(
        functools.partial(pick_kernel, kept, branched, "sta"),
        out_shape=out_shape,
        in_specs=[pl.BlockSpec(memory_space=pltpu.HBM)] * 5,
        out_specs=[vmem] * REACH + [pl.BlockSpec(memory_space=pltpu.HBM)] * branched,
        scratch_shapes=[
            pltpu.SMEM(pair_sides.shape, jnp.int32),
            pltpu.SMEM(pair_owner.shape, jnp.int32),
            pltpu.VMEM(block_members.shape, jnp.int32),
            pltpu.SMEM(case_table.shape, jnp.int32),
            pltpu.SMEM((1,), jnp.int32),
            pltpu.VMEM((freqs, parts, stations), BF16),
            pltpu.VMEM((columns, rows), F32),
            pltpu.VMEM((rows, columns), BF16),
            pltpu.SemaphoreType.DMA((COPIES + 5,)),
        ],
        compiler_params=pltpu.CompilerParams(vmem_limit_bytes=PICK_VMEM_LIMIT),
        cost_estimate=pl.CostEstimate(
            flops=2 * rows * stations * freqs * parts,
            bytes_accessed=2 * spectra.size + 4 * rows * columns,
            transcendentals=0,
        ),
        name="pick_and_whiten",
    )(pair_sides, pair_owner, block_members, case_table, spectra)


def case_number(first, second, needs, sta_count):
    return (first * sta_count + second) * (1 << (REACH - 1)) + needs // 2


def routes(sta_count):
    def load(first, second, sent):
        links = {}
        for full, flows, _, other in schedule(first, second, sta_count):
            for source, owner in flows if full or other in sent else flows[:1]:
                step = 1 if owner > source else -1
                for place in range(source, owner, step):
                    links[place, step] = links.get((place, step), 0) + 1
        return max(links.values())

    branches = []
    cases = [0] * case_number(sta_count, 0, 0, sta_count)
    for first, second in itertools.permutations(range(sta_count), 2):
        others = [step[3] for step in schedule(first, second, sta_count) if not step[0]]
        sets = [
            sent
            for count in range(len(others), -1, -1)
            for sent in itertools.combinations(others, count)
        ]
        for named in itertools.combinations(range(REACH), 2):
            fits = [sent for sent in sets if set(named) & set(others) <= set(sent)]
            branch = (first, second, min(fits, key=lambda sent: load(first, second, sent)))
            if branch not in branches:
                branches.append(branch)
            needs = sum(1 << reach for reach in named)
            cases[case_number(first, second, needs, sta_count)] = branches.index(branch)
    return branches, cases


def phase_tables(sub_count, sub_freqs, groups, lag_rows):
    chunks = -(-sub_freqs // LANES)
    total = sub_count * sub_freqs
    freq = np.arange(total, dtype=np.int64).reshape(sub_count, 1, sub_freqs)
    middle = [2 * (group * lag_rows - LAGS // 2) + lag_rows - 1 for group in range(groups)]
    away = [step for step in range(1, lag_rows) if step % 2 != lag_rows % 2]

    def table(twice, forms, tile, dtype):
        twice = np.array(twice or [0], dtype=np.int64).reshape(1, -1, 1)
        angle = np.mod(freq * twice, 2 * total) * (math.pi / total)
        rows = np.stack([form(angle) for form in forms], axis=2)
        rows = rows.reshape(sub_count, -1, sub_freqs)
        pad = ((0, 0), (0, -rows.shape[1] % tile), (0, chunks * LANES - sub_freqs))
        return np.pad(rows, pad).astype(np.float32).astype(dtype)

    turns = table(middle, (np.cos, np.sin), 8, np.float32)
    offsets = table(away, (np.cos, np.sin, lambda angle: -np.sin(angle)), 16, BF16)
    return turns, offsets, len(away)


def lag_kernel(hops, slots, lag_rows, away, block_count, branched, *refs):
    sub_count = lax.axis_size("sub")
    hr_count = lax.axis_size("hr")
    pair_ref, owner_ref, place_ref, turn_ref, offset_ref = refs[:5]
    blocks, outs = refs[5 : -2 - len(hops)], refs[-2 - len(hops) : -2]
    buf, sems = refs[-2:]
    width = buf.shape[3]
    span = buf.shape[4] // 2
    middle_lag = lag_rows % 2
    my_sub = lax.axis_index("sub")
    my_hr = lax.axis_index("hr")
    my_sta = lax.axis_index("sta")
    sta_count = lax.axis_size("sta")

    pairs = read_pairs(pair_ref, owner_ref, block_count)
    order = [jnp.int32(reach) for reach in range(REACH)]
    if branched:
        first, second, _ = case_of(pairs, sta_count)
        entry = (first * sta_count + second) * 2 + (my_sta != first).astype(jnp.int32)
        order = [place_ref[entry * REACH + reach] for reach in range(REACH)]
    owned = []
    for owner, _, homes in pairs:
        places = []
        for home in homes:
            reach_here = lax.rem(home - my_sta + sta_count, sta_count)
            place_here = order[0]
            for reach in range(1, REACH):
                place_here = jnp.where(reach_here == reach, order[reach], place_here)
            places.append(place_here)
        owned.append((owner == my_sta, places))
    ends = []
    for slot in slots:
        count = jnp.int32(0)
        slot_ends = [jnp.int32(-1)] * 2
        for mine, places in owned:
            hit = mine & (count == slot)
            count = count + mine.astype(jnp.int32)
            slot_ends = [jnp.where(hit, new, old) for new, old in zip(places, slot_ends)]
        ends.append(slot_ends)

    def fetches(index, act):
        for side in range(2):
            for place in range(REACH):

                @pl.when(ends[index][side] == place)
                def _():
                    for step in range(sub_count):
                        act(
                            pltpu.make_async_copy(
                                blocks[place * sub_count + step],
                                buf.at[index, side, step],
                                sems.at[index, side, step],
                            )
                        )

    for index in range(len(slots)):
        fetches(index, lambda copy: copy.start())

    for index in range(len(slots)):

        @pl.when(ends[index][0] < 0)
        def _():
            for out in outs:
                out[:, index] = jnp.zeros((lag_rows, width, width), out.dtype)

        fetches(index, lambda copy: copy.wait())

        @pl.when(ends[index][0] >= 0)
        def _():
            total = None
            for step in range(sub_count):
                sub = lax.rem(my_sub + step, sub_count)
                real = buf[index, 0, step, :, :span]
                imag = buf[index, 0, step, :, span:]
                scaled_real, scaled_imag = [real] * middle_lag, [imag] * middle_lag
                for near in range(away):
                    cosine, sine, minus = (
                        offset_ref[sub, 3 * near + form : 3 * near + form + 1, :]
                        for form in range(3)
                    )
                    scaled_real += [real * cosine, imag * minus]
                    scaled_imag += [imag * cosine, real * sine]
                real = buf[index, 1, step, :, :span].astype(F32)
                imag = buf[index, 1, step, :, span:].astype(F32)
                turned_real, turned_imag = [], []
                for hop in hops:
                    group = lax.rem(my_hr + hop, hr_count) * sub_count + my_sub
                    cosine = turn_ref[sub, pl.ds(2 * group, 1), :]
                    sine = turn_ref[sub, pl.ds(2 * group + 1, 1), :]
                    turned_real.append((real * cosine + imag * sine).astype(BF16))
                    turned_imag.append((imag * cosine - real * sine).astype(BF16))
                for scaled, turned in ((scaled_real, turned_real), (scaled_imag, turned_imag)):
                    part = dot_nt(jnp.concatenate(scaled, axis=0), jnp.concatenate(turned, axis=0))
                    total = part if total is None else total + part
            for place, out in enumerate(outs):
                columns = slice(place * width, (place + 1) * width)
                if middle_lag:
                    out[lag_rows // 2, index] = total[:width, columns].astype(out.dtype)
                for near in range(away):
                    start = (middle_lag + 2 * near) * width
                    even = total[start : start + width, columns]
                    odd = total[start + width : start + 2 * width, columns]
                    below = (lag_rows - 1) // 2 - near - middle_lag
                    above = lag_rows - 1 - below
                    out[above, index] = (even + odd).astype(out.dtype)
                    out[below, index] = (even - odd).astype(out.dtype)


def on_device(spectra, pair_blocks, pair_owner, block_members):
    hour_count, sub_freqs, _, _ = spectra.shape
    block_count, width = block_members.shape
    sta_count, hr_count, sub_count = (lax.axis_size(axis) for axis in ("sta", "hr", "sub"))
    groups = hr_count * sub_count
    lag_rows = LAGS // groups
    norming = 1.0 / math.sqrt(hour_count * hr_count * sub_count * sub_freqs)
    pair_sides = pair_blocks.T
    turns, offsets, away = phase_tables(sub_count, sub_freqs, groups, lag_rows)

    owners_at_most = pair_owner.shape[0] - CAP + 1
    branched = owners_at_most == 2 and sta_count == REACH
    kept = min(REACH, owners_at_most)
    branches, cases = routes(sta_count) if branched else ([], [0])
    places = place_table(sta_count) if branched else [0]
    case_table = jnp.asarray(np.array(cases + places, dtype=np.int32))
    places = jnp.asarray(np.array(places, dtype=np.int32))
    picked = pick_blocks(
        kept, branched, spectra, pair_sides, pair_owner, block_members, case_table
    )

    def halves(block):
        blocks = [block]
        for step in range(1, sub_count):
            swap = [((sub + step) % sub_count, sub) for sub in range(sub_count)]
            blocks.append(lax.ppermute(block, "sub", swap))
        return blocks

    def exchange(*picked):
        shifts = [
            [((home + reach) % sta_count, home) for home in range(sta_count)]
            for reach in range(1, REACH)
        ]
        return [lax.ppermute(block, "sta", shift) for block, shift in zip(picked, shifts)]

    def exchange_two(first, second, sent, *picked):
        arrived = []
        for block, (full, flows, _, other) in zip(picked, schedule(first, second, sta_count)):
            flows = flows if full or other in sent else flows[:1]
            arrived.append(lax.ppermute(block, "sta", flows))
        return arrived

    blocks = halves(picked[0])
    if branched:
        steps = [functools.partial(exchange_two, *branch) for branch in branches]
        arrived = lax.switch(picked[REACH][0], steps, *picked[1:REACH])
    else:
        arrived = exchange(*picked[1:REACH])
    for block in arrived:
        blocks += halves(block)

    smem = pl.BlockSpec(memory_space=pltpu.SMEM)
    vmem = pl.BlockSpec(memory_space=pltpu.VMEM)
    hbm = pl.BlockSpec(memory_space=pltpu.HBM)
    row = picked[0].shape[1]
    versions = (lag_rows % 2 + 2 * away) * width

    def products(hops, slots, dtype, name):
        return pl.pallas_call(
            functools.partial(
                lag_kernel, hops, slots, lag_rows, away, block_count, branched
            ),
            out_shape=[jax.ShapeDtypeStruct((lag_rows, len(slots), width, width), dtype)]
            * len(hops),
            in_specs=[smem, smem, smem, vmem, vmem] + [hbm] * len(blocks),
            out_specs=[vmem] * len(hops),
            scratch_shapes=[
                pltpu.VMEM((len(slots), 2, sub_count, width, row), BF16),
                pltpu.SemaphoreType.DMA((len(slots), 2, sub_count)),
            ],
            compiler_params=pltpu.CompilerParams(vmem_limit_bytes=LAG_VMEM_LIMIT),
            cost_estimate=pl.CostEstimate(
                flops=2 * len(slots) * len(hops) * versions * width * sub_count * row,
                bytes_accessed=4 * len(slots) * sub_count * width * row,
                transcendentals=0,
            ),
            name=name,
        )(pair_sides, pair_owner, places, turns, offsets, *blocks)

    hops, slots = tuple(range(1, hr_count)), tuple(range(CAP))
    sent = products(hops, slots, BF16, "lags_to_send")
    received = []
    for hop, part in zip(hops, sent):
        to_device = [(hr, (hr + hop) % hr_count) for hr in range(hr_count)]
        received.append(lax.ppermute(part, "hr", to_device))
    (summed,) = products((0,), slots, F32, "lags_to_keep")
    for part in received:
        summed = summed + part.astype(F32)
    return (summed * norming).astype(BF16)


def solution(mesh):
    placed = (P(("grp", "hr"), "sub", None, "sta"), P(), P(), P("sta", None))
    return jax.shard_map(
        on_device,
        mesh=mesh,
        in_specs=placed,
        out_specs=P(("grp", "hr", "sub"), "sta", None, None),
        check_vma=False,
    )
```

```python
import functools
import itertools
import math

import jax
import jax.numpy as jnp
import numpy as np
from jax import lax
from jax.experimental import pallas as pl
from jax.experimental.pallas import tpu as pltpu
from jax.sharding import PartitionSpec as P

BAND = 50
LAGS = 16
CAP = 3
REACH = 4
COPIES = 2
EPSILON = 1e-05
LANES = 128
F32 = jnp.float32
BF16 = jnp.bfloat16
PICK_VMEM_LIMIT = 59 * 1024 * 1024
LAG_VMEM_LIMIT = 32 * 1024 * 1024

NT = (((1,), (1,)), ((), ()))


def dot_nt(left, right):
    return lax.dot_general(left, right, NT, preferred_element_type=F32)


def iota(shape, dim):
    return lax.broadcasted_iota(jnp.int32, shape, dim)


def schedule(first, second, sta_count, ring_needed=True):
    every = range(1, REACH)
    if 0 < first < sta_count - 1:
        ring = 1 if 2 * first < sta_count else REACH - 1
        pairs = [((home + ring) % sta_count, home) for home in range(sta_count)]
    else:
        pairs = [(home ^ 1, home) for home in range(sta_count)]
    source = {target: start for start, target in pairs}
    reaches = [[(source[owner] - owner) % sta_count] for owner in (first, second)]
    both = [reach for reach in every if [reach] not in reaches]
    for taken in reaches:
        taken += both + [reach for reach in every if reach not in taken + both]
    if not ring_needed and 0 < first < sta_count - 1:
        swap = {first: source[first], source[first]: first}
        pairs = [(swap.get(home, home), home) for home in range(sta_count)]
    plan = [(True, pairs, reaches[0][0], reaches[1][0])]
    for one, other in zip(reaches[0][1:], reaches[1][1:]):
        flows = [((first + one) % sta_count, first), ((second + other) % sta_count, second)]
        plan.append((False, flows, one, other))
    return plan[:1] + sorted(plan[1:], key=lambda step: step[1][1][0] == first)


def place_table(sta_count):
    table = []
    for first, second in itertools.product(range(sta_count), repeat=2):
        places = [0] * (2 * REACH)
        if first != second:
            for place, step in enumerate(schedule(first, second, sta_count)):
                places[step[2]], places[REACH + step[3]] = place + 1, place + 1
        table += places
    return table


def read_pairs(pair_ref, owner_ref, block_count):
    pairs = []
    for pair in range(owner_ref.shape[0]):
        blocks = [pair_ref[side, pair] for side in range(2)]
        pairs.append((owner_ref[pair], blocks, [lax.div(block, block_count) for block in blocks]))
    return pairs


def case_of(pairs, sta_count):
    first = second = needs = jnp.int32(0)
    for owner, _, homes in pairs:
        count = jnp.int32(0)
        for other, _, _ in pairs:
            count = count + (other == owner).astype(jnp.int32)
        ends = [lax.rem(home - owner + sta_count, sta_count) for home in homes]
        first = jnp.where(count == CAP, owner, first)
        second = jnp.where(count < CAP, owner, second)
        needs = jnp.where(count < CAP, (1 << ends[0]) | (1 << ends[1]), needs)
    return first, second, case_number(first, second, needs, sta_count)


def pick_kernel(kept, branched, sta_axis, pair_hbm, owner_hbm, member_hbm, case_hbm, x_ref, *rest):
    outs = rest[:REACH]
    pair_ref, owner_ref, member_ref, case_ref, number_ref, x_buf, y_buf, white_buf, sems = rest[
        REACH + branched :
    ]
    if branched:
        branch_copy = pltpu.make_async_copy(number_ref, rest[REACH], sems.at[COPIES + 4])
    freqs, tiles = x_buf.shape[0], x_buf.shape[2] // LANES
    block_count, width = member_ref.shape
    rows = y_buf.shape[0]
    chunks = rows // (2 * LANES)

    cut = freqs // (4 * LANES) * 2 * LANES or freqs // LANES // 2 * LANES
    runs = [(0, cut), (cut, freqs - cut)]

    def fetch(part):
        run = pl.ds(*runs[part])
        return pltpu.make_async_copy(x_ref.at[0, run], x_buf.at[run], sems.at[part])

    small = [
        pltpu.make_async_copy(source, target, sems.at[COPIES + index])
        for index, (source, target) in enumerate(
            (
                (pair_hbm, pair_ref),
                (owner_hbm, owner_ref),
                (member_hbm, member_ref),
                (case_hbm, case_ref),
            )
        )
    ]
    for copy in small:
        copy.start()
    for part in range(COPIES):
        fetch(part).start()

    def bands(shape, part_dim):
        part, place = iota(shape, part_dim), iota(shape, 1 - part_dim)
        low = (place % 16) * (2 * BAND)
        hit = (part >= low) & (part < low + 2 * BAND) & (part < 2 * freqs) & (place < 48)
        return jnp.where(hit, 1.0, 0.0).astype(BF16)

    gather_bands, spread_bands = bands((48, rows), 1), bands((rows, LANES), 0)
    row, col = iota((2 * LANES, 2 * LANES), 0), iota((2 * LANES, 2 * LANES), 1)
    split = jnp.where(row == 2 * (col % LANES) + col // LANES, 1.0, 0.0).astype(BF16)
    y_buf[2 * freqs :] = jnp.zeros((rows - 2 * freqs, kept * width), F32)
    for copy in small:
        copy.wait()

    my_sta = lax.axis_index(sta_axis)
    sta_count = lax.axis_size(sta_axis)
    pairs = read_pairs(pair_ref, owner_ref, block_count)
    found, wanted = jnp.int32(0), []
    for reach in range(REACH):
        owner = lax.rem(my_sta - reach + REACH * sta_count, sta_count)
        chosen = jnp.int32(-1)
        for pair_owner, blocks, homes in pairs:
            for block, home in zip(blocks, homes):
                hit = (pair_owner == owner) & (home == my_sta)
                chosen = jnp.where(hit, lax.rem(block, block_count), chosen)
        wanted.append((found, chosen))
        found = found + (chosen >= 0).astype(jnp.int32)
    places, station = [], []
    for place in range(kept):
        reach_here, block_here = jnp.int32(-1), jnp.int32(0)
        for reach, (rank, chosen) in enumerate(wanted):
            hit = (rank == place) & (chosen >= 0)
            reach_here = jnp.where(hit, reach, reach_here)
            block_here = jnp.where(hit, chosen, block_here)
        places.append(reach_here)
        station.append(member_ref[pl.ds(block_here, 1), :])
    station = jnp.concatenate(station, axis=1)
    hot = jnp.where(station == iota((tiles * LANES, kept * width), 0), 1.0, 0.0).astype(BF16)

    if branched:
        first, second, case = case_of(pairs, sta_count)
        number_ref[0] = case_ref[case]
        branch_copy.start()
        base = case_number(sta_count, 0, 0, sta_count) + (first * sta_count + second) * 2 * REACH
        for place, reach_here in enumerate(places):
            reach = jnp.maximum(reach_here, 0)
            owner = lax.rem(my_sta - reach + REACH * sta_count, sta_count)
            step = case_ref[base + jnp.where(owner == first, 0, REACH) + reach]
            places[place] = jnp.where(reach_here < 0, -1, step)

    power = None
    for part, (start, count) in enumerate(runs):
        fetch(part).wait()
        x = jnp.concatenate(
            [
                x_buf[start : start + count, :, tile * LANES : (tile + 1) * LANES].reshape(
                    2 * count, LANES
                )
                for tile in range(tiles)
            ],
            axis=1,
        )
        values = jnp.dot(x, hot, preferred_element_type=F32)
        y_buf[2 * start : 2 * (start + count)] = values
        stop = 2 * (start + count) if part + 1 < len(runs) else rows
        values = y_buf[2 * start : stop]
        square = values * values
        high = square.astype(BF16)
        low = (square - high.astype(F32)).astype(BF16)
        for piece in (high, low):
            sums = jnp.dot(gather_bands[:, 2 * start : stop], piece, preferred_element_type=F32)
            power = sums if power is None else power + sums
    scale = lax.rsqrt(power * (1.0 / (2 * BAND)) + EPSILON)
    high = scale.astype(BF16).astype(F32)
    mid = (scale - high).astype(BF16).astype(F32)
    low = scale - high - mid
    third = iota(scale.shape, 0) // 16
    pieces = jnp.where(third == 0, high, jnp.where(third == 1, mid, low))
    pieces = jnp.concatenate(
        [pieces, jnp.zeros((LANES - pieces.shape[0], pieces.shape[1]), F32)], axis=0
    ).astype(BF16)
    white = y_buf[...] * jnp.dot(spread_bands, pieces, preferred_element_type=F32)
    white = white.astype(BF16)
    parted = []
    for chunk in range(chunks):
        mixed = white[chunk * 2 * LANES : (chunk + 1) * 2 * LANES]
        part = lax.dot_general(
            mixed, split, (((0,), (0,)), ((), ())), preferred_element_type=F32
        )
        parted.append(part.astype(BF16))
    white_buf[...] = jnp.concatenate(
        [part[:, :LANES] for part in parted] + [part[:, LANES:] for part in parted], axis=1
    )
    for place, reach_here in enumerate(places):
        for reach in range(REACH):

            @pl.when(reach_here == reach)
            def _():
                outs[reach][...] = white_buf[place * width : (place + 1) * width]

    if branched:
        branch_copy.wait()


def pick_blocks(kept, branched, spectra, pair_sides, pair_owner, block_members, case_table):
    _, freqs, parts, stations = spectra.shape
    block_count, width = block_members.shape
    columns = -(-freqs // LANES) * 2 * LANES
    rows = kept * width
    vmem = pl.BlockSpec(memory_space=pltpu.VMEM)
    out_shape = [jax.ShapeDtypeStruct((width, columns), BF16)] * REACH
    out_shape += [jax.ShapeDtypeStruct((1,), jnp.int32)] * branched
    return pl.pallas_call(
        functools.partial(pick_kernel, kept, branched, "sta"),
        out_shape=out_shape,
        in_specs=[pl.BlockSpec(memory_space=pltpu.HBM)] * 5,
        out_specs=[vmem] * REACH + [pl.BlockSpec(memory_space=pltpu.HBM)] * branched,
        scratch_shapes=[
            pltpu.SMEM(pair_sides.shape, jnp.int32),
            pltpu.SMEM(pair_owner.shape, jnp.int32),
            pltpu.VMEM(block_members.shape, jnp.int32),
            pltpu.SMEM(case_table.shape, jnp.int32),
            pltpu.SMEM((1,), jnp.int32),
            pltpu.VMEM((freqs, parts, stations), BF16),
            pltpu.VMEM((columns, rows), F32),
            pltpu.VMEM((rows, columns), BF16),
            pltpu.SemaphoreType.DMA((COPIES + 5,)),
        ],
        compiler_params=pltpu.CompilerParams(vmem_limit_bytes=PICK_VMEM_LIMIT),
        cost_estimate=pl.CostEstimate(
            flops=2 * rows * stations * freqs * parts,
            bytes_accessed=2 * spectra.size + 4 * rows * columns,
            transcendentals=0,
        ),
        name="pick_and_whiten",
    )(pair_sides, pair_owner, block_members, case_table, spectra)


def case_number(first, second, needs, sta_count):
    return (first * sta_count + second) * (1 << (REACH - 1)) + needs // 2


def routes(sta_count):
    def load(first, second, ring, sent):
        links = {}
        for full, flows, _, other in schedule(first, second, sta_count, ring):
            for source, owner in flows if full or other in sent else flows[:1]:
                step = 1 if owner > source else -1
                for place in range(source, owner, step):
                    links[place, step] = links.get((place, step), 0) + 1
        return max(links.values())

    branches = []
    cases = [0] * case_number(sta_count, 0, 0, sta_count)
    for first, second in itertools.permutations(range(sta_count), 2):
        plan = schedule(first, second, sta_count)
        others = [step[3] for step in plan if not step[0]]
        sets = [
            sent
            for count in range(len(others), -1, -1)
            for sent in itertools.combinations(others, count)
        ]
        for named in itertools.combinations(range(REACH), 2):
            ring = plan[0][3] in named or not 0 < first < sta_count - 1
            fits = [sent for sent in sets if set(named) & set(others) <= set(sent)]
            best = min(fits, key=lambda sent: load(first, second, ring, sent))
            branch = (first, second, ring, best)
            if branch not in branches:
                branches.append(branch)
            needs = sum(1 << reach for reach in named)
            cases[case_number(first, second, needs, sta_count)] = branches.index(branch)
    return branches, cases


def phase_tables(sub_count, sub_freqs, groups, lag_rows):
    chunks = -(-sub_freqs // LANES)
    total = sub_count * sub_freqs
    freq = np.arange(total, dtype=np.int64).reshape(sub_count, 1, sub_freqs)
    middle = [2 * (group * lag_rows - LAGS // 2) + lag_rows - 1 for group in range(groups)]
    away = [step for step in range(1, lag_rows) if step % 2 != lag_rows % 2]

    def table(twice, forms, tile, dtype):
        twice = np.array(twice or [0], dtype=np.int64).reshape(1, -1, 1)
        angle = np.mod(freq * twice, 2 * total) * (math.pi / total)
        rows = np.stack([form(angle) for form in forms], axis=2)
        rows = rows.reshape(sub_count, -1, sub_freqs)
        pad = ((0, 0), (0, -rows.shape[1] % tile), (0, chunks * LANES - sub_freqs))
        return np.pad(rows, pad).astype(np.float32).astype(dtype)

    turns = table(middle, (np.cos, np.sin), 8, np.float32)
    offsets = table(away, (np.cos, np.sin, lambda angle: -np.sin(angle)), 16, BF16)
    return turns, offsets, len(away)


def lag_kernel(hops, slots, lag_rows, away, block_count, branched, *refs):
    sub_count = lax.axis_size("sub")
    hr_count = lax.axis_size("hr")
    pair_ref, owner_ref, place_ref, turn_ref, offset_ref = refs[:5]
    blocks, outs = refs[5 : -2 - len(hops)], refs[-2 - len(hops) : -2]
    buf, sems = refs[-2:]
    width = buf.shape[3]
    span = buf.shape[4] // 2
    middle_lag = lag_rows % 2
    my_sub = lax.axis_index("sub")
    my_hr = lax.axis_index("hr")
    my_sta = lax.axis_index("sta")
    sta_count = lax.axis_size("sta")

    pairs = read_pairs(pair_ref, owner_ref, block_count)
    order = [jnp.int32(reach) for reach in range(REACH)]
    if branched:
        first, second, _ = case_of(pairs, sta_count)
        entry = (first * sta_count + second) * 2 + (my_sta != first).astype(jnp.int32)
        order = [place_ref[entry * REACH + reach] for reach in range(REACH)]
    owned = []
    for owner, _, homes in pairs:
        places = []
        for home in homes:
            reach_here = lax.rem(home - my_sta + sta_count, sta_count)
            place_here = order[0]
            for reach in range(1, REACH):
                place_here = jnp.where(reach_here == reach, order[reach], place_here)
            places.append(place_here)
        owned.append((owner == my_sta, places))
    ends = []
    for slot in slots:
        count = jnp.int32(0)
        slot_ends = [jnp.int32(-1)] * 2
        for mine, places in owned:
            hit = mine & (count == slot)
            count = count + mine.astype(jnp.int32)
            slot_ends = [jnp.where(hit, new, old) for new, old in zip(places, slot_ends)]
        ends.append(slot_ends)

    def fetches(index, act):
        for side in range(2):
            for place in range(REACH):

                @pl.when(ends[index][side] == place)
                def _():
                    for step in range(sub_count):
                        act(
                            pltpu.make_async_copy(
                                blocks[place * sub_count + step],
                                buf.at[index, side, step],
                                sems.at[index, side, step],
                            )
                        )

    for index in range(len(slots)):
        fetches(index, lambda copy: copy.start())

    for index in range(len(slots)):

        @pl.when(ends[index][0] < 0)
        def _():
            for out in outs:
                out[:, index] = jnp.zeros((lag_rows, width, width), out.dtype)

        fetches(index, lambda copy: copy.wait())

        @pl.when(ends[index][0] >= 0)
        def _():
            total = None
            for step in range(sub_count):
                sub = lax.rem(my_sub + step, sub_count)
                real = buf[index, 0, step, :, :span]
                imag = buf[index, 0, step, :, span:]
                scaled_real, scaled_imag = [real] * middle_lag, [imag] * middle_lag
                for near in range(away):
                    cosine, sine, minus = (
                        offset_ref[sub, 3 * near + form : 3 * near + form + 1, :]
                        for form in range(3)
                    )
                    scaled_real += [real * cosine, imag * minus]
                    scaled_imag += [imag * cosine, real * sine]
                real = buf[index, 1, step, :, :span].astype(F32)
                imag = buf[index, 1, step, :, span:].astype(F32)
                turned_real, turned_imag = [], []
                for hop in hops:
                    group = lax.rem(my_hr + hop, hr_count) * sub_count + my_sub
                    cosine = turn_ref[sub, pl.ds(2 * group, 1), :]
                    sine = turn_ref[sub, pl.ds(2 * group + 1, 1), :]
                    turned_real.append((real * cosine + imag * sine).astype(BF16))
                    turned_imag.append((imag * cosine - real * sine).astype(BF16))
                for scaled, turned in ((scaled_real, turned_real), (scaled_imag, turned_imag)):
                    part = dot_nt(jnp.concatenate(scaled, axis=0), jnp.concatenate(turned, axis=0))
                    total = part if total is None else total + part
            for place, out in enumerate(outs):
                columns = slice(place * width, (place + 1) * width)
                if middle_lag:
                    out[lag_rows // 2, index] = total[:width, columns].astype(out.dtype)
                for near in range(away):
                    start = (middle_lag + 2 * near) * width
                    even = total[start : start + width, columns]
                    odd = total[start + width : start + 2 * width, columns]
                    below = (lag_rows - 1) // 2 - near - middle_lag
                    above = lag_rows - 1 - below
                    out[above, index] = (even + odd).astype(out.dtype)
                    out[below, index] = (even - odd).astype(out.dtype)


def on_device(spectra, pair_blocks, pair_owner, block_members):
    hour_count, sub_freqs, _, _ = spectra.shape
    block_count, width = block_members.shape
    sta_count, hr_count, sub_count = (lax.axis_size(axis) for axis in ("sta", "hr", "sub"))
    groups = hr_count * sub_count
    lag_rows = LAGS // groups
    norming = 1.0 / math.sqrt(hour_count * hr_count * sub_count * sub_freqs)
    pair_sides = pair_blocks.T
    turns, offsets, away = phase_tables(sub_count, sub_freqs, groups, lag_rows)

    owners_at_most = pair_owner.shape[0] - CAP + 1
    branched = owners_at_most == 2 and sta_count == REACH
    kept = min(REACH, owners_at_most)
    branches, cases = routes(sta_count) if branched else ([], [0])
    places = place_table(sta_count) if branched else [0]
    case_table = jnp.asarray(np.array(cases + places, dtype=np.int32))
    places = jnp.asarray(np.array(places, dtype=np.int32))
    picked = pick_blocks(
        kept, branched, spectra, pair_sides, pair_owner, block_members, case_table
    )

    def halves(block):
        blocks = [block]
        for step in range(1, sub_count):
            swap = [((sub + step) % sub_count, sub) for sub in range(sub_count)]
            blocks.append(lax.ppermute(block, "sub", swap))
        return blocks

    def exchange(*picked):
        blocks = halves(picked[0])
        for reach in range(1, REACH):
            shift = [((home + reach) % sta_count, home) for home in range(sta_count)]
            blocks += halves(lax.ppermute(picked[reach], "sta", shift))
        return blocks

    def exchange_two(first, second, ring, sent, *picked):
        blocks = halves(picked[0])
        plan = schedule(first, second, sta_count, ring)
        for block, (full, flows, _, other) in zip(picked[1:], plan):
            flows = flows if full or other in sent else flows[:1]
            blocks += halves(lax.ppermute(block, "sta", flows))
        return blocks

    if branched:
        steps = [functools.partial(exchange_two, *branch) for branch in branches]
        blocks = lax.switch(picked[REACH][0], steps, *picked[:REACH])
    else:
        blocks = exchange(*picked[:REACH])

    smem = pl.BlockSpec(memory_space=pltpu.SMEM)
    vmem = pl.BlockSpec(memory_space=pltpu.VMEM)
    hbm = pl.BlockSpec(memory_space=pltpu.HBM)
    row = picked[0].shape[1]
    versions = (lag_rows % 2 + 2 * away) * width

    def products(hops, slots, dtype, name):
        return pl.pallas_call(
            functools.partial(
                lag_kernel, hops, slots, lag_rows, away, block_count, branched
            ),
            out_shape=[jax.ShapeDtypeStruct((lag_rows, len(slots), width, width), dtype)]
            * len(hops),
            in_specs=[smem, smem, smem, vmem, vmem] + [hbm] * len(blocks),
            out_specs=[vmem] * len(hops),
            scratch_shapes=[
                pltpu.VMEM((len(slots), 2, sub_count, width, row), BF16),
                pltpu.SemaphoreType.DMA((len(slots), 2, sub_count)),
            ],
            compiler_params=pltpu.CompilerParams(vmem_limit_bytes=LAG_VMEM_LIMIT),
            cost_estimate=pl.CostEstimate(
                flops=2 * len(slots) * len(hops) * versions * width * sub_count * row,
                bytes_accessed=4 * len(slots) * sub_count * width * row,
                transcendentals=0,
            ),
            name=name,
        )(pair_sides, pair_owner, places, turns, offsets, *blocks)

    hops, slots = tuple(range(1, hr_count)), tuple(range(CAP))
    sent = products(hops, slots, BF16, "lags_to_send")
    received = []
    for hop, part in zip(hops, sent):
        to_device = [(hr, (hr + hop) % hr_count) for hr in range(hr_count)]
        received.append(lax.ppermute(part, "hr", to_device))
    (summed,) = products((0,), slots, F32, "lags_to_keep")
    for part in received:
        summed = summed + part.astype(F32)
    return (summed * norming).astype(BF16)


def solution(mesh):
    placed = (P(("grp", "hr"), "sub", None, "sta"), P(), P(), P("sta", None))
    return jax.shard_map(
        on_device,
        mesh=mesh,
        in_specs=placed,
        out_specs=P(("grp", "hr", "sub"), "sta", None, None),
        check_vma=False,
    )
```

```python
import functools
import itertools
import math

import jax
import jax.numpy as jnp
import numpy as np
from jax import lax
from jax.experimental import pallas as pl
from jax.experimental.pallas import tpu as pltpu
from jax.sharding import PartitionSpec as P

BAND = 50
LAGS = 16
CAP = 3
REACH = 4
COPIES = 2
EPSILON = 1e-05
LANES = 128
F32 = jnp.float32
BF16 = jnp.bfloat16
PICK_VMEM_LIMIT = 59 * 1024 * 1024
LAG_VMEM_LIMIT = 32 * 1024 * 1024

NT = (((1,), (1,)), ((), ()))


def dot_nt(left, right):
    return lax.dot_general(left, right, NT, preferred_element_type=F32)


def iota(shape, dim):
    return lax.broadcasted_iota(jnp.int32, shape, dim)


def schedule(first, second, sta_count):
    every = range(1, REACH)
    pairs = [(home ^ 1, home) for home in range(sta_count)]
    source = {target: start for start, target in pairs}
    reaches = [[(source[owner] - owner) % sta_count] for owner in (first, second)]
    both = [reach for reach in every if [reach] not in reaches]
    for taken in reaches:
        taken += both + [reach for reach in every if reach not in taken + both]
    plan = [(True, pairs, reaches[0][0], reaches[1][0])]
    for one, other in zip(reaches[0][1:], reaches[1][1:]):
        flows = [((first + one) % sta_count, first), ((second + other) % sta_count, second)]
        plan.append((False, flows, one, other))
    return plan[:1] + sorted(plan[1:], key=lambda step: step[1][1][0] == first)


def place_table(sta_count):
    table = []
    for first, second in itertools.product(range(sta_count), repeat=2):
        places = [0] * (2 * REACH)
        if first != second:
            for place, step in enumerate(schedule(first, second, sta_count)):
                places[step[2]], places[REACH + step[3]] = place + 1, place + 1
        table += places
    return table


def read_pairs(pair_ref, owner_ref, block_count):
    pairs = []
    for pair in range(owner_ref.shape[0]):
        blocks = [pair_ref[side, pair] for side in range(2)]
        pairs.append((owner_ref[pair], blocks, [lax.div(block, block_count) for block in blocks]))
    return pairs


def case_of(pairs, sta_count):
    first = second = needs = jnp.int32(0)
    for owner, _, homes in pairs:
        count = jnp.int32(0)
        for other, _, _ in pairs:
            count = count + (other == owner).astype(jnp.int32)
        ends = [lax.rem(home - owner + sta_count, sta_count) for home in homes]
        first = jnp.where(count == CAP, owner, first)
        second = jnp.where(count < CAP, owner, second)
        needs = jnp.where(count < CAP, (1 << ends[0]) | (1 << ends[1]), needs)
    return first, second, case_number(first, second, needs, sta_count)


def pick_kernel(kept, branched, sta_axis, pair_hbm, owner_hbm, member_hbm, case_hbm, x_ref, *rest):
    outs = rest[:REACH]
    pair_ref, owner_ref, member_ref, case_ref, number_ref, x_buf, y_buf, white_buf, sems = rest[
        REACH + branched :
    ]
    if branched:
        branch_copy = pltpu.make_async_copy(number_ref, rest[REACH], sems.at[COPIES + 4])
    freqs, tiles = x_buf.shape[0], x_buf.shape[2] // LANES
    block_count, width = member_ref.shape
    rows = y_buf.shape[0]
    chunks = rows // (2 * LANES)

    cut = freqs // (4 * LANES) * 2 * LANES or freqs // LANES // 2 * LANES
    runs = [(0, cut), (cut, freqs - cut)]

    def fetch(part):
        run = pl.ds(*runs[part])
        return pltpu.make_async_copy(x_ref.at[0, run], x_buf.at[run], sems.at[part])

    small = [
        pltpu.make_async_copy(source, target, sems.at[COPIES + index])
        for index, (source, target) in enumerate(
            (
                (pair_hbm, pair_ref),
                (owner_hbm, owner_ref),
                (member_hbm, member_ref),
                (case_hbm, case_ref),
            )
        )
    ]
    for copy in small:
        copy.start()
    for part in range(COPIES):
        fetch(part).start()

    def bands(shape, part_dim):
        part, place = iota(shape, part_dim), iota(shape, 1 - part_dim)
        low = (place % 16) * (2 * BAND)
        hit = (part >= low) & (part < low + 2 * BAND) & (part < 2 * freqs) & (place < 48)
        return jnp.where(hit, 1.0, 0.0).astype(BF16)

    gather_bands, spread_bands = bands((48, rows), 1), bands((rows, LANES), 0)
    row, col = iota((2 * LANES, 2 * LANES), 0), iota((2 * LANES, 2 * LANES), 1)
    split = jnp.where(row == 2 * (col % LANES) + col // LANES, 1.0, 0.0).astype(BF16)
    y_buf[2 * freqs :] = jnp.zeros((rows - 2 * freqs, kept * width), F32)
    for copy in small:
        copy.wait()

    my_sta = lax.axis_index(sta_axis)
    sta_count = lax.axis_size(sta_axis)
    pairs = read_pairs(pair_ref, owner_ref, block_count)
    found, wanted = jnp.int32(0), []
    for reach in range(REACH):
        owner = lax.rem(my_sta - reach + REACH * sta_count, sta_count)
        chosen = jnp.int32(-1)
        for pair_owner, blocks, homes in pairs:
            for block, home in zip(blocks, homes):
                hit = (pair_owner == owner) & (home == my_sta)
                chosen = jnp.where(hit, lax.rem(block, block_count), chosen)
        wanted.append((found, chosen))
        found = found + (chosen >= 0).astype(jnp.int32)
    places, station = [], []
    for place in range(kept):
        reach_here, block_here = jnp.int32(-1), jnp.int32(0)
        for reach, (rank, chosen) in enumerate(wanted):
            hit = (rank == place) & (chosen >= 0)
            reach_here = jnp.where(hit, reach, reach_here)
            block_here = jnp.where(hit, chosen, block_here)
        places.append(reach_here)
        station.append(member_ref[pl.ds(block_here, 1), :])
    station = jnp.concatenate(station, axis=1)
    hot = jnp.where(station == iota((tiles * LANES, kept * width), 0), 1.0, 0.0).astype(BF16)

    if branched:
        first, second, case = case_of(pairs, sta_count)
        number_ref[0] = case_ref[case]
        branch_copy.start()
        base = case_number(sta_count, 0, 0, sta_count) + (first * sta_count + second) * 2 * REACH
        for place, reach_here in enumerate(places):
            reach = jnp.maximum(reach_here, 0)
            owner = lax.rem(my_sta - reach + REACH * sta_count, sta_count)
            step = case_ref[base + jnp.where(owner == first, 0, REACH) + reach]
            places[place] = jnp.where(reach_here < 0, -1, step)

    power = None
    for part, (start, count) in enumerate(runs):
        fetch(part).wait()
        x = jnp.concatenate(
            [
                x_buf[start : start + count, :, tile * LANES : (tile + 1) * LANES].reshape(
                    2 * count, LANES
                )
                for tile in range(tiles)
            ],
            axis=1,
        )
        values = jnp.dot(x, hot, preferred_element_type=F32)
        y_buf[2 * start : 2 * (start + count)] = values
        stop = 2 * (start + count) if part + 1 < len(runs) else rows
        values = y_buf[2 * start : stop]
        square = values * values
        high = square.astype(BF16)
        low = (square - high.astype(F32)).astype(BF16)
        for piece in (high, low):
            sums = jnp.dot(gather_bands[:, 2 * start : stop], piece, preferred_element_type=F32)
            power = sums if power is None else power + sums
    scale = lax.rsqrt(power * (1.0 / (2 * BAND)) + EPSILON)
    high = scale.astype(BF16).astype(F32)
    mid = (scale - high).astype(BF16).astype(F32)
    low = scale - high - mid
    third = iota(scale.shape, 0) // 16
    pieces = jnp.where(third == 0, high, jnp.where(third == 1, mid, low))
    pieces = jnp.concatenate(
        [pieces, jnp.zeros((LANES - pieces.shape[0], pieces.shape[1]), F32)], axis=0
    ).astype(BF16)
    white = y_buf[...] * jnp.dot(spread_bands, pieces, preferred_element_type=F32)
    white = white.astype(BF16)
    parted = []
    for chunk in range(chunks):
        mixed = white[chunk * 2 * LANES : (chunk + 1) * 2 * LANES]
        part = lax.dot_general(
            mixed, split, (((0,), (0,)), ((), ())), preferred_element_type=F32
        )
        parted.append(part.astype(BF16))
    white_buf[...] = jnp.concatenate(
        [part[:, :LANES] for part in parted] + [part[:, LANES:] for part in parted], axis=1
    )
    for place, reach_here in enumerate(places):
        for reach in range(REACH):

            @pl.when(reach_here == reach)
            def _():
                outs[reach][...] = white_buf[place * width : (place + 1) * width]

    if branched:
        branch_copy.wait()


def pick_blocks(kept, branched, spectra, pair_sides, pair_owner, block_members, case_table):
    _, freqs, parts, stations = spectra.shape
    block_count, width = block_members.shape
    columns = -(-freqs // LANES) * 2 * LANES
    rows = kept * width
    vmem = pl.BlockSpec(memory_space=pltpu.VMEM)
    out_shape = [jax.ShapeDtypeStruct((width, columns), BF16)] * REACH
    out_shape += [jax.ShapeDtypeStruct((1,), jnp.int32)] * branched
    return pl.pallas_call(
        functools.partial(pick_kernel, kept, branched, "sta"),
        out_shape=out_shape,
        in_specs=[pl.BlockSpec(memory_space=pltpu.HBM)] * 5,
        out_specs=[vmem] * REACH + [pl.BlockSpec(memory_space=pltpu.HBM)] * branched,
        scratch_shapes=[
            pltpu.SMEM(pair_sides.shape, jnp.int32),
            pltpu.SMEM(pair_owner.shape, jnp.int32),
            pltpu.VMEM(block_members.shape, jnp.int32),
            pltpu.SMEM(case_table.shape, jnp.int32),
            pltpu.SMEM((1,), jnp.int32),
            pltpu.VMEM((freqs, parts, stations), BF16),
            pltpu.VMEM((columns, rows), F32),
            pltpu.VMEM((rows, columns), BF16),
            pltpu.SemaphoreType.DMA((COPIES + 5,)),
        ],
        compiler_params=pltpu.CompilerParams(vmem_limit_bytes=PICK_VMEM_LIMIT),
        cost_estimate=pl.CostEstimate(
            flops=2 * rows * stations * freqs * parts,
            bytes_accessed=2 * spectra.size + 4 * rows * columns,
            transcendentals=0,
        ),
        name="pick_and_whiten",
    )(pair_sides, pair_owner, block_members, case_table, spectra)


def case_number(first, second, needs, sta_count):
    return (first * sta_count + second) * (1 << (REACH - 1)) + needs // 2


def routes(sta_count):
    def load(first, second, sent):
        links = {}
        for full, flows, _, other in schedule(first, second, sta_count):
            for source, owner in flows if full or other in sent else flows[:1]:
                step = 1 if owner > source else -1
                for place in range(source, owner, step):
                    links[place, step] = links.get((place, step), 0) + 1
        return max(links.values())

    branches = []
    cases = [0] * case_number(sta_count, 0, 0, sta_count)
    for first, second in itertools.permutations(range(sta_count), 2):
        others = [step[3] for step in schedule(first, second, sta_count) if not step[0]]
        sets = [
            sent
            for count in range(len(others), -1, -1)
            for sent in itertools.combinations(others, count)
        ]
        for named in itertools.combinations(range(REACH), 2):
            fits = [sent for sent in sets if set(named) & set(others) <= set(sent)]
            branch = (first, second, min(fits, key=lambda sent: load(first, second, sent)))
            if branch not in branches:
                branches.append(branch)
            needs = sum(1 << reach for reach in named)
            cases[case_number(first, second, needs, sta_count)] = branches.index(branch)
    return branches, cases


def phase_tables(sub_count, sub_freqs, groups, lag_rows):
    chunks = -(-sub_freqs // LANES)
    total = sub_count * sub_freqs
    freq = np.arange(total, dtype=np.int64).reshape(sub_count, 1, sub_freqs)
    middle = [2 * (group * lag_rows - LAGS // 2) + lag_rows - 1 for group in range(groups)]
    away = [step for step in range(1, lag_rows) if step % 2 != lag_rows % 2]

    def table(twice, forms, tile, dtype):
        twice = np.array(twice or [0], dtype=np.int64).reshape(1, -1, 1)
        angle = np.mod(freq * twice, 2 * total) * (math.pi / total)
        rows = np.stack([form(angle) for form in forms], axis=2)
        rows = rows.reshape(sub_count, -1, sub_freqs)
        pad = ((0, 0), (0, -rows.shape[1] % tile), (0, chunks * LANES - sub_freqs))
        return np.pad(rows, pad).astype(np.float32).astype(dtype)

    turns = table(middle, (np.cos, np.sin), 8, np.float32)
    offsets = table(away, (np.cos, np.sin, lambda angle: -np.sin(angle)), 16, BF16)
    return turns, offsets, len(away)


def lag_kernel(hops, slots, lag_rows, away, block_count, branched, *refs):
    sub_count = lax.axis_size("sub")
    hr_count = lax.axis_size("hr")
    pair_ref, owner_ref, place_ref, turn_ref, offset_ref = refs[:5]
    blocks, outs = refs[5 : -2 - len(hops)], refs[-2 - len(hops) : -2]
    buf, sems = refs[-2:]
    width = buf.shape[3]
    span = buf.shape[4] // 2
    middle_lag = lag_rows % 2
    my_sub = lax.axis_index("sub")
    my_hr = lax.axis_index("hr")
    my_sta = lax.axis_index("sta")
    sta_count = lax.axis_size("sta")

    pairs = read_pairs(pair_ref, owner_ref, block_count)
    order = [jnp.int32(reach) for reach in range(REACH)]
    if branched:
        first, second, _ = case_of(pairs, sta_count)
        entry = (first * sta_count + second) * 2 + (my_sta != first).astype(jnp.int32)
        order = [place_ref[entry * REACH + reach] for reach in range(REACH)]
    owned = []
    for owner, _, homes in pairs:
        places = []
        for home in homes:
            reach_here = lax.rem(home - my_sta + sta_count, sta_count)
            place_here = order[0]
            for reach in range(1, REACH):
                place_here = jnp.where(reach_here == reach, order[reach], place_here)
            places.append(place_here)
        owned.append((owner == my_sta, places))
    ends = []
    for slot in slots:
        count = jnp.int32(0)
        slot_ends = [jnp.int32(-1)] * 2
        for mine, places in owned:
            hit = mine & (count == slot)
            count = count + mine.astype(jnp.int32)
            slot_ends = [jnp.where(hit, new, old) for new, old in zip(places, slot_ends)]
        ends.append(slot_ends)

    def fetches(index, act):
        for side in range(2):
            for place in range(REACH):

                @pl.when(ends[index][side] == place)
                def _():
                    for step in range(sub_count):
                        act(
                            pltpu.make_async_copy(
                                blocks[place * sub_count + step],
                                buf.at[index, side, step],
                                sems.at[index, side, step],
                            )
                        )

    for index in range(len(slots)):
        fetches(index, lambda copy: copy.start())

    for index in range(len(slots)):

        @pl.when(ends[index][0] < 0)
        def _():
            for out in outs:
                out[:, index] = jnp.zeros((lag_rows, width, width), out.dtype)

        fetches(index, lambda copy: copy.wait())

        @pl.when(ends[index][0] >= 0)
        def _():
            total = None
            for step in range(sub_count):
                sub = lax.rem(my_sub + step, sub_count)
                real = buf[index, 0, step, :, :span]
                imag = buf[index, 0, step, :, span:]
                scaled_real, scaled_imag = [real] * middle_lag, [imag] * middle_lag
                for near in range(away):
                    cosine, sine, minus = (
                        offset_ref[sub, 3 * near + form : 3 * near + form + 1, :]
                        for form in range(3)
                    )
                    scaled_real += [real * cosine, imag * minus]
                    scaled_imag += [imag * cosine, real * sine]
                real = buf[index, 1, step, :, :span].astype(F32)
                imag = buf[index, 1, step, :, span:].astype(F32)
                turned_real, turned_imag = [], []
                for hop in hops:
                    group = lax.rem(my_hr + hop, hr_count) * sub_count + my_sub
                    cosine = turn_ref[sub, pl.ds(2 * group, 1), :]
                    sine = turn_ref[sub, pl.ds(2 * group + 1, 1), :]
                    turned_real.append((real * cosine + imag * sine).astype(BF16))
                    turned_imag.append((imag * cosine - real * sine).astype(BF16))
                for scaled, turned in ((scaled_real, turned_real), (scaled_imag, turned_imag)):
                    part = dot_nt(jnp.concatenate(scaled, axis=0), jnp.concatenate(turned, axis=0))
                    total = part if total is None else total + part
            for place, out in enumerate(outs):
                columns = slice(place * width, (place + 1) * width)
                if middle_lag:
                    out[lag_rows // 2, index] = total[:width, columns].astype(out.dtype)
                for near in range(away):
                    start = (middle_lag + 2 * near) * width
                    even = total[start : start + width, columns]
                    odd = total[start + width : start + 2 * width, columns]
                    below = (lag_rows - 1) // 2 - near - middle_lag
                    above = lag_rows - 1 - below
                    out[above, index] = (even + odd).astype(out.dtype)
                    out[below, index] = (even - odd).astype(out.dtype)


def on_device(spectra, pair_blocks, pair_owner, block_members):
    hour_count, sub_freqs, _, _ = spectra.shape
    block_count, width = block_members.shape
    sta_count, hr_count, sub_count = (lax.axis_size(axis) for axis in ("sta", "hr", "sub"))
    groups = hr_count * sub_count
    lag_rows = LAGS // groups
    norming = 1.0 / math.sqrt(hour_count * hr_count * sub_count * sub_freqs)
    pair_sides = pair_blocks.T
    turns, offsets, away = phase_tables(sub_count, sub_freqs, groups, lag_rows)

    owners_at_most = pair_owner.shape[0] - CAP + 1
    branched = owners_at_most == 2 and sta_count == REACH
    kept = min(REACH, owners_at_most)
    branches, cases = routes(sta_count) if branched else ([], [0])
    places = place_table(sta_count) if branched else [0]
    case_table = jnp.asarray(np.array(cases + places, dtype=np.int32))
    places = jnp.asarray(np.array(places, dtype=np.int32))
    picked = pick_blocks(
        kept, branched, spectra, pair_sides, pair_owner, block_members, case_table
    )

    def halves(block):
        blocks = [block]
        for step in range(1, sub_count):
            swap = [((sub + step) % sub_count, sub) for sub in range(sub_count)]
            blocks.append(lax.ppermute(block, "sub", swap))
        return blocks

    def exchange(*picked):
        blocks = halves(picked[0])
        for reach in range(1, REACH):
            shift = [((home + reach) % sta_count, home) for home in range(sta_count)]
            blocks += halves(lax.ppermute(picked[reach], "sta", shift))
        return blocks

    def exchange_two(first, second, sent, *picked):
        blocks = halves(picked[0])
        for block, (full, flows, _, other) in zip(picked[1:], schedule(first, second, sta_count)):
            flows = flows if full or other in sent else flows[:1]
            blocks += halves(lax.ppermute(block, "sta", flows))
        return blocks

    if branched:
        steps = [functools.partial(exchange_two, *branch) for branch in branches]
        blocks = lax.switch(picked[REACH][0], steps, *picked[:REACH])
    else:
        blocks = exchange(*picked[:REACH])

    smem = pl.BlockSpec(memory_space=pltpu.SMEM)
    vmem = pl.BlockSpec(memory_space=pltpu.VMEM)
    hbm = pl.BlockSpec(memory_space=pltpu.HBM)
    row = picked[0].shape[1]
    versions = (lag_rows % 2 + 2 * away) * width

    def products(hops, slots, dtype, name):
        return pl.pallas_call(
            functools.partial(
                lag_kernel, hops, slots, lag_rows, away, block_count, branched
            ),
            out_shape=[jax.ShapeDtypeStruct((lag_rows, len(slots), width, width), dtype)]
            * len(hops),
            in_specs=[smem, smem, smem, vmem, vmem] + [hbm] * len(blocks),
            out_specs=[vmem] * len(hops),
            scratch_shapes=[
                pltpu.VMEM((len(slots), 2, sub_count, width, row), BF16),
                pltpu.SemaphoreType.DMA((len(slots), 2, sub_count)),
            ],
            compiler_params=pltpu.CompilerParams(vmem_limit_bytes=LAG_VMEM_LIMIT),
            cost_estimate=pl.CostEstimate(
                flops=2 * len(slots) * len(hops) * versions * width * sub_count * row,
                bytes_accessed=4 * len(slots) * sub_count * width * row,
                transcendentals=0,
            ),
            name=name,
        )(pair_sides, pair_owner, places, turns, offsets, *blocks)

    hops, slots = tuple(range(1, hr_count)), tuple(range(CAP))
    sent = products(hops, slots, BF16, "lags_to_send")
    received = []
    for hop, part in zip(hops, sent):
        to_device = [(hr, (hr + hop) % hr_count) for hr in range(hr_count)]
        received.append(lax.ppermute(part, "hr", to_device))
    (summed,) = products((0,), slots, F32, "lags_to_keep")
    for part in received:
        summed = summed + part.astype(F32)
    return (summed * norming).astype(BF16)


def solution(mesh):
    placed = (P(("grp", "hr"), "sub", None, "sta"), P(), P(), P("sta", None))
    return jax.shard_map(
        on_device,
        mesh=mesh,
        in_specs=placed,
        out_specs=P(("grp", "hr", "sub"), "sta", None, None),
        check_vma=False,
    )
```

```python
import functools
import itertools
import math

import jax
import jax.numpy as jnp
import numpy as np
from jax import lax
from jax.experimental import pallas as pl
from jax.experimental.pallas import tpu as pltpu
from jax.sharding import PartitionSpec as P

BAND = 50
LAGS = 16
CAP = 3
REACH = 4
COPIES = 2
EPSILON = 1e-05
LANES = 128
F32 = jnp.float32
BF16 = jnp.bfloat16
PICK_VMEM_LIMIT = 59 * 1024 * 1024
LAG_VMEM_LIMIT = 32 * 1024 * 1024

NT = (((1,), (1,)), ((), ()))


def dot_nt(left, right):
    return lax.dot_general(left, right, NT, preferred_element_type=F32)


def iota(shape, dim):
    return lax.broadcasted_iota(jnp.int32, shape, dim)


def schedule(first, second, sta_count):
    every = range(1, REACH)
    if 0 < first < sta_count - 1:
        ring = 1 if 2 * first < sta_count else REACH - 1
        pairs = [((home + ring) % sta_count, home) for home in range(sta_count)]
    else:
        pairs = [(home ^ 1, home) for home in range(sta_count)]
    source = {target: start for start, target in pairs}
    reaches = [[(source[owner] - owner) % sta_count] for owner in (first, second)]
    both = [reach for reach in every if [reach] not in reaches]
    for taken in reaches:
        taken += both + [reach for reach in every if reach not in taken + both]
    plan = [(True, pairs, reaches[0][0], reaches[1][0])]
    for one, other in zip(reaches[0][1:], reaches[1][1:]):
        flows = [((first + one) % sta_count, first), ((second + other) % sta_count, second)]
        plan.append((False, flows, one, other))
    return plan[:1] + sorted(plan[1:], key=lambda step: step[1][1][0] == first)


def place_table(sta_count):
    table = []
    for first, second in itertools.product(range(sta_count), repeat=2):
        places = [0] * (2 * REACH)
        if first != second:
            for place, step in enumerate(schedule(first, second, sta_count)):
                places[step[2]], places[REACH + step[3]] = place + 1, place + 1
        table += places
    return table


def read_pairs(pair_ref, owner_ref, block_count):
    pairs = []
    for pair in range(owner_ref.shape[0]):
        blocks = [pair_ref[side, pair] for side in range(2)]
        pairs.append((owner_ref[pair], blocks, [lax.div(block, block_count) for block in blocks]))
    return pairs


def case_of(pairs, sta_count):
    first = second = needs = jnp.int32(0)
    for owner, _, homes in pairs:
        count = jnp.int32(0)
        for other, _, _ in pairs:
            count = count + (other == owner).astype(jnp.int32)
        ends = [lax.rem(home - owner + sta_count, sta_count) for home in homes]
        first = jnp.where(count == CAP, owner, first)
        second = jnp.where(count < CAP, owner, second)
        needs = jnp.where(count < CAP, (1 << ends[0]) | (1 << ends[1]), needs)
    return first, second, case_number(first, second, needs, sta_count)


def pick_kernel(kept, branched, sta_axis, pair_hbm, owner_hbm, member_hbm, case_hbm, x_ref, *rest):
    outs = rest[:REACH]
    pair_ref, owner_ref, member_ref, case_ref, number_ref, x_buf, y_buf, white_buf, sems = rest[
        REACH + branched :
    ]
    if branched:
        branch_copy = pltpu.make_async_copy(number_ref, rest[REACH], sems.at[COPIES + 4])
    freqs, tiles = x_buf.shape[0], x_buf.shape[2] // LANES
    block_count, width = member_ref.shape
    rows = y_buf.shape[0]
    chunks = rows // (2 * LANES)

    cut = freqs // (4 * LANES) * 2 * LANES or freqs // LANES // 2 * LANES
    runs = [(0, cut), (cut, freqs - cut)]

    def fetch(part):
        run = pl.ds(*runs[part])
        return pltpu.make_async_copy(x_ref.at[0, run], x_buf.at[run], sems.at[part])

    small = [
        pltpu.make_async_copy(source, target, sems.at[COPIES + index])
        for index, (source, target) in enumerate(
            (
                (pair_hbm, pair_ref),
                (owner_hbm, owner_ref),
                (member_hbm, member_ref),
                (case_hbm, case_ref),
            )
        )
    ]
    for copy in small:
        copy.start()
    for part in range(COPIES):
        fetch(part).start()

    def bands(shape, part_dim):
        part, place = iota(shape, part_dim), iota(shape, 1 - part_dim)
        low = (place % 16) * (2 * BAND)
        hit = (part >= low) & (part < low + 2 * BAND) & (part < 2 * freqs) & (place < 48)
        return jnp.where(hit, 1.0, 0.0).astype(BF16)

    gather_bands, spread_bands = bands((48, rows), 1), bands((rows, LANES), 0)
    row, col = iota((2 * LANES, 2 * LANES), 0), iota((2 * LANES, 2 * LANES), 1)
    split = jnp.where(row == 2 * (col % LANES) + col // LANES, 1.0, 0.0).astype(BF16)
    y_buf[2 * freqs :] = jnp.zeros((rows - 2 * freqs, kept * width), F32)
    for copy in small:
        copy.wait()

    my_sta = lax.axis_index(sta_axis)
    sta_count = lax.axis_size(sta_axis)
    pairs = read_pairs(pair_ref, owner_ref, block_count)
    found, wanted = jnp.int32(0), []
    for reach in range(REACH):
        owner = lax.rem(my_sta - reach + REACH * sta_count, sta_count)
        chosen = jnp.int32(-1)
        for pair_owner, blocks, homes in pairs:
            for block, home in zip(blocks, homes):
                hit = (pair_owner == owner) & (home == my_sta)
                chosen = jnp.where(hit, lax.rem(block, block_count), chosen)
        wanted.append((found, chosen))
        found = found + (chosen >= 0).astype(jnp.int32)
    places, station = [], []
    for place in range(kept):
        reach_here, block_here = jnp.int32(-1), jnp.int32(0)
        for reach, (rank, chosen) in enumerate(wanted):
            hit = (rank == place) & (chosen >= 0)
            reach_here = jnp.where(hit, reach, reach_here)
            block_here = jnp.where(hit, chosen, block_here)
        places.append(reach_here)
        station.append(member_ref[pl.ds(block_here, 1), :])
    station = jnp.concatenate(station, axis=1)
    hot = jnp.where(station == iota((tiles * LANES, kept * width), 0), 1.0, 0.0).astype(BF16)

    if branched:
        first, second, case = case_of(pairs, sta_count)
        number_ref[0] = case_ref[case]
        branch_copy.start()
        base = case_number(sta_count, 0, 0, sta_count) + (first * sta_count + second) * 2 * REACH
        for place, reach_here in enumerate(places):
            reach = jnp.maximum(reach_here, 0)
            owner = lax.rem(my_sta - reach + REACH * sta_count, sta_count)
            step = case_ref[base + jnp.where(owner == first, 0, REACH) + reach]
            places[place] = jnp.where(reach_here < 0, -1, step)

    power = None
    for part, (start, count) in enumerate(runs):
        fetch(part).wait()
        x = jnp.concatenate(
            [
                x_buf[start : start + count, :, tile * LANES : (tile + 1) * LANES].reshape(
                    2 * count, LANES
                )
                for tile in range(tiles)
            ],
            axis=1,
        )
        values = jnp.dot(x, hot, preferred_element_type=F32)
        y_buf[2 * start : 2 * (start + count)] = values
        stop = 2 * (start + count) if part + 1 < len(runs) else rows
        values = y_buf[2 * start : stop]
        square = values * values
        high = square.astype(BF16)
        low = (square - high.astype(F32)).astype(BF16)
        for piece in (high, low):
            sums = jnp.dot(gather_bands[:, 2 * start : stop], piece, preferred_element_type=F32)
            power = sums if power is None else power + sums
    scale = lax.rsqrt(power * (1.0 / (2 * BAND)) + EPSILON)
    high = scale.astype(BF16).astype(F32)
    mid = (scale - high).astype(BF16).astype(F32)
    low = scale - high - mid
    third = iota(scale.shape, 0) // 16
    pieces = jnp.where(third == 0, high, jnp.where(third == 1, mid, low))
    pieces = jnp.concatenate(
        [pieces, jnp.zeros((LANES - pieces.shape[0], pieces.shape[1]), F32)], axis=0
    ).astype(BF16)
    white = y_buf[...] * jnp.dot(spread_bands, pieces, preferred_element_type=F32)
    white = white.astype(BF16)
    parted = []
    for chunk in range(chunks):
        mixed = white[chunk * 2 * LANES : (chunk + 1) * 2 * LANES]
        part = lax.dot_general(
            mixed, split, (((0,), (0,)), ((), ())), preferred_element_type=F32
        )
        parted.append(part.astype(BF16))
    white_buf[...] = jnp.concatenate(
        [part[:, :LANES] for part in parted] + [part[:, LANES:] for part in parted], axis=1
    )
    for place, reach_here in enumerate(places):
        for reach in range(REACH):

            @pl.when(reach_here == reach)
            def _():
                outs[reach][...] = white_buf[place * width : (place + 1) * width]

    if branched:
        branch_copy.wait()


def pick_blocks(kept, branched, spectra, pair_sides, pair_owner, block_members, case_table):
    _, freqs, parts, stations = spectra.shape
    block_count, width = block_members.shape
    columns = -(-freqs // LANES) * 2 * LANES
    rows = kept * width
    vmem = pl.BlockSpec(memory_space=pltpu.VMEM)
    out_shape = [jax.ShapeDtypeStruct((width, columns), BF16)] * REACH
    out_shape += [jax.ShapeDtypeStruct((1,), jnp.int32)] * branched
    return pl.pallas_call(
        functools.partial(pick_kernel, kept, branched, "sta"),
        out_shape=out_shape,
        in_specs=[pl.BlockSpec(memory_space=pltpu.HBM)] * 5,
        out_specs=[vmem] * REACH + [pl.BlockSpec(memory_space=pltpu.HBM)] * branched,
        scratch_shapes=[
            pltpu.SMEM(pair_sides.shape, jnp.int32),
            pltpu.SMEM(pair_owner.shape, jnp.int32),
            pltpu.VMEM(block_members.shape, jnp.int32),
            pltpu.SMEM(case_table.shape, jnp.int32),
            pltpu.SMEM((1,), jnp.int32),
            pltpu.VMEM((freqs, parts, stations), BF16),
            pltpu.VMEM((columns, rows), F32),
            pltpu.VMEM((rows, columns), BF16),
            pltpu.SemaphoreType.DMA((COPIES + 5,)),
        ],
        compiler_params=pltpu.CompilerParams(vmem_limit_bytes=PICK_VMEM_LIMIT),
        cost_estimate=pl.CostEstimate(
            flops=2 * rows * stations * freqs * parts,
            bytes_accessed=2 * spectra.size + 4 * rows * columns,
            transcendentals=0,
        ),
        name="pick_and_whiten",
    )(pair_sides, pair_owner, block_members, case_table, spectra)


def case_number(first, second, needs, sta_count):
    return (first * sta_count + second) * (1 << (REACH - 1)) + needs // 2


def routes(sta_count):
    def load(first, second, sent):
        links = {}
        for full, flows, _, other in schedule(first, second, sta_count):
            for source, owner in flows if full or other in sent else flows[:1]:
                step = 1 if owner > source else -1
                for place in range(source, owner, step):
                    links[place, step] = links.get((place, step), 0) + 1
        return max(links.values())

    branches = []
    cases = [0] * case_number(sta_count, 0, 0, sta_count)
    for first, second in itertools.permutations(range(sta_count), 2):
        others = [step[3] for step in schedule(first, second, sta_count) if not step[0]]
        sets = [
            sent
            for count in range(len(others), -1, -1)
            for sent in itertools.combinations(others, count)
        ]
        for named in itertools.combinations(range(REACH), 2):
            fits = [sent for sent in sets if set(named) & set(others) <= set(sent)]
            branch = (first, second, min(fits, key=lambda sent: load(first, second, sent)))
            if branch not in branches:
                branches.append(branch)
            needs = sum(1 << reach for reach in named)
            cases[case_number(first, second, needs, sta_count)] = branches.index(branch)
    return branches, cases


def phase_tables(sub_count, sub_freqs, groups, lag_rows):
    chunks = -(-sub_freqs // LANES)
    total = sub_count * sub_freqs
    freq = np.arange(total, dtype=np.int64).reshape(sub_count, 1, sub_freqs)
    middle = [2 * (group * lag_rows - LAGS // 2) + lag_rows - 1 for group in range(groups)]
    away = [step for step in range(1, lag_rows) if step % 2 != lag_rows % 2]

    def table(twice, forms, tile, dtype):
        twice = np.array(twice or [0], dtype=np.int64).reshape(1, -1, 1)
        angle = np.mod(freq * twice, 2 * total) * (math.pi / total)
        rows = np.stack([form(angle) for form in forms], axis=2)
        rows = rows.reshape(sub_count, -1, sub_freqs)
        pad = ((0, 0), (0, -rows.shape[1] % tile), (0, chunks * LANES - sub_freqs))
        return np.pad(rows, pad).astype(np.float32).astype(dtype)

    turns = table(middle, (np.cos, np.sin), 8, np.float32)
    offsets = table(away, (np.cos, np.sin, lambda angle: -np.sin(angle)), 16, BF16)
    return turns, offsets, len(away)


def lag_kernel(hops, slots, lag_rows, away, block_count, branched, *refs):
    sub_count = lax.axis_size("sub")
    hr_count = lax.axis_size("hr")
    pair_ref, owner_ref, place_ref, turn_ref, offset_ref = refs[:5]
    blocks, outs = refs[5 : -2 - len(hops)], refs[-2 - len(hops) : -2]
    buf, sems = refs[-2:]
    width = buf.shape[3]
    span = buf.shape[4] // 2
    middle_lag = lag_rows % 2
    my_sub = lax.axis_index("sub")
    my_hr = lax.axis_index("hr")
    my_sta = lax.axis_index("sta")
    sta_count = lax.axis_size("sta")

    pairs = read_pairs(pair_ref, owner_ref, block_count)
    order = [jnp.int32(reach) for reach in range(REACH)]
    if branched:
        first, second, _ = case_of(pairs, sta_count)
        entry = (first * sta_count + second) * 2 + (my_sta != first).astype(jnp.int32)
        order = [place_ref[entry * REACH + reach] for reach in range(REACH)]
    owned = []
    for owner, _, homes in pairs:
        places = []
        for home in homes:
            reach_here = lax.rem(home - my_sta + sta_count, sta_count)
            place_here = order[0]
            for reach in range(1, REACH):
                place_here = jnp.where(reach_here == reach, order[reach], place_here)
            places.append(place_here)
        owned.append((owner == my_sta, places))
    ends = []
    for slot in slots:
        count = jnp.int32(0)
        slot_ends = [jnp.int32(-1)] * 2
        for mine, places in owned:
            hit = mine & (count == slot)
            count = count + mine.astype(jnp.int32)
            slot_ends = [jnp.where(hit, new, old) for new, old in zip(places, slot_ends)]
        ends.append(slot_ends)

    def fetches(index, act):
        for side in range(2):
            for place in range(REACH):

                @pl.when(ends[index][side] == place)
                def _():
                    for step in range(sub_count):
                        act(
                            pltpu.make_async_copy(
                                blocks[place * sub_count + step],
                                buf.at[index, side, step],
                                sems.at[index, side, step],
                            )
                        )

    for index in range(len(slots)):
        fetches(index, lambda copy: copy.start())

    for index in range(len(slots)):

        @pl.when(ends[index][0] < 0)
        def _():
            for out in outs:
                out[:, index] = jnp.zeros((lag_rows, width, width), out.dtype)

        fetches(index, lambda copy: copy.wait())

        @pl.when(ends[index][0] >= 0)
        def _():
            total = None
            for step in range(sub_count):
                sub = lax.rem(my_sub + step, sub_count)
                real = buf[index, 0, step, :, :span]
                imag = buf[index, 0, step, :, span:]
                scaled_real, scaled_imag = [real] * middle_lag, [imag] * middle_lag
                for near in range(away):
                    cosine, sine, minus = (
                        offset_ref[sub, 3 * near + form : 3 * near + form + 1, :]
                        for form in range(3)
                    )
                    scaled_real += [real * cosine, imag * minus]
                    scaled_imag += [imag * cosine, real * sine]
                real = buf[index, 1, step, :, :span].astype(F32)
                imag = buf[index, 1, step, :, span:].astype(F32)
                turned_real, turned_imag = [], []
                for hop in hops:
                    group = lax.rem(my_hr + hop, hr_count) * sub_count + my_sub
                    cosine = turn_ref[sub, pl.ds(2 * group, 1), :]
                    sine = turn_ref[sub, pl.ds(2 * group + 1, 1), :]
                    turned_real.append((real * cosine + imag * sine).astype(BF16))
                    turned_imag.append((imag * cosine - real * sine).astype(BF16))
                for scaled, turned in ((scaled_real, turned_real), (scaled_imag, turned_imag)):
                    part = dot_nt(jnp.concatenate(scaled, axis=0), jnp.concatenate(turned, axis=0))
                    total = part if total is None else total + part
            for place, out in enumerate(outs):
                columns = slice(place * width, (place + 1) * width)
                if middle_lag:
                    out[lag_rows // 2, index] = total[:width, columns].astype(out.dtype)
                for near in range(away):
                    start = (middle_lag + 2 * near) * width
                    even = total[start : start + width, columns]
                    odd = total[start + width : start + 2 * width, columns]
                    below = (lag_rows - 1) // 2 - near - middle_lag
                    above = lag_rows - 1 - below
                    out[above, index] = (even + odd).astype(out.dtype)
                    out[below, index] = (even - odd).astype(out.dtype)


def on_device(spectra, pair_blocks, pair_owner, block_members):
    hour_count, sub_freqs, _, _ = spectra.shape
    block_count, width = block_members.shape
    sta_count, hr_count, sub_count = (lax.axis_size(axis) for axis in ("sta", "hr", "sub"))
    groups = hr_count * sub_count
    lag_rows = LAGS // groups
    norming = 1.0 / math.sqrt(hour_count * hr_count * sub_count * sub_freqs)
    pair_sides = pair_blocks.T
    turns, offsets, away = phase_tables(sub_count, sub_freqs, groups, lag_rows)

    owners_at_most = pair_owner.shape[0] - CAP + 1
    branched = owners_at_most == 2 and sta_count == REACH
    kept = min(REACH, owners_at_most)
    branches, cases = routes(sta_count) if branched else ([], [0])
    places = place_table(sta_count) if branched else [0]
    case_table = jnp.asarray(np.array(cases + places, dtype=np.int32))
    places = jnp.asarray(np.array(places, dtype=np.int32))
    picked = pick_blocks(
        kept, branched, spectra, pair_sides, pair_owner, block_members, case_table
    )

    def halves(block):
        blocks = [block]
        for step in range(1, sub_count):
            swap = [((sub + step) % sub_count, sub) for sub in range(sub_count)]
            blocks.append(lax.ppermute(block, "sub", swap))
        return blocks

    def exchange(*picked):
        blocks = halves(picked[0])
        for reach in range(1, REACH):
            shift = [((home + reach) % sta_count, home) for home in range(sta_count)]
            blocks += halves(lax.ppermute(picked[reach], "sta", shift))
        return blocks

    def exchange_two(first, second, sent, *picked):
        blocks = halves(picked[0])
        for block, (full, flows, _, other) in zip(picked[1:], schedule(first, second, sta_count)):
            flows = flows if full or other in sent else flows[:1]
            blocks += halves(lax.ppermute(block, "sta", flows))
        return blocks

    if branched:
        steps = [functools.partial(exchange_two, *branch) for branch in branches]
        blocks = lax.switch(picked[REACH][0], steps, *picked[:REACH])
    else:
        blocks = exchange(*picked[:REACH])

    smem = pl.BlockSpec(memory_space=pltpu.SMEM)
    vmem = pl.BlockSpec(memory_space=pltpu.VMEM)
    hbm = pl.BlockSpec(memory_space=pltpu.HBM)
    row = picked[0].shape[1]
    versions = (lag_rows % 2 + 2 * away) * width

    def products(hops, slots, dtype, name):
        return pl.pallas_call(
            functools.partial(
                lag_kernel, hops, slots, lag_rows, away, block_count, branched
            ),
            out_shape=[jax.ShapeDtypeStruct((lag_rows, len(slots), width, width), dtype)]
            * len(hops),
            in_specs=[smem, smem, smem, vmem, vmem] + [hbm] * len(blocks),
            out_specs=[vmem] * len(hops),
            scratch_shapes=[
                pltpu.VMEM((len(slots), 2, sub_count, width, row), BF16),
                pltpu.SemaphoreType.DMA((len(slots), 2, sub_count)),
            ],
            compiler_params=pltpu.CompilerParams(vmem_limit_bytes=LAG_VMEM_LIMIT),
            cost_estimate=pl.CostEstimate(
                flops=2 * len(slots) * len(hops) * versions * width * sub_count * row,
                bytes_accessed=4 * len(slots) * sub_count * width * row,
                transcendentals=0,
            ),
            name=name,
        )(pair_sides, pair_owner, places, turns, offsets, *blocks)

    hops, slots = tuple(range(1, hr_count)), tuple(range(CAP))
    received = []
    for group in (slots[:-1], slots[-1:]):
        sent = products(hops, group, BF16, f"lags_to_send_{len(group)}")
        for hop, part in zip(hops, sent):
            to_device = [(hr, (hr + hop) % hr_count) for hr in range(hr_count)]
            received.append(lax.ppermute(part, "hr", to_device))
    (summed,) = products((0,), slots, F32, "lags_to_keep")
    for early, late in zip(received[: len(hops)], received[len(hops) :]):
        summed = summed + jnp.concatenate([early, late], axis=1).astype(F32)
    return (summed * norming).astype(BF16)


def solution(mesh):
    placed = (P(("grp", "hr"), "sub", None, "sta"), P(), P(), P("sta", None))
    return jax.shard_map(
        on_device,
        mesh=mesh,
        in_specs=placed,
        out_specs=P(("grp", "hr", "sub"), "sta", None, None),
        check_vma=False,
    )
```

```python
import functools
import itertools
import math

import jax
import jax.numpy as jnp
import numpy as np
from jax import lax
from jax.experimental import pallas as pl
from jax.experimental.pallas import tpu as pltpu
from jax.sharding import PartitionSpec as P

BAND = 50
LAGS = 16
CAP = 3
REACH = 4
COPIES = 2
EPSILON = 1e-05
LANES = 128
F32 = jnp.float32
BF16 = jnp.bfloat16
PICK_VMEM_LIMIT = 59 * 1024 * 1024
LAG_VMEM_LIMIT = 32 * 1024 * 1024

NT = (((1,), (1,)), ((), ()))


def dot_nt(left, right):
    return lax.dot_general(left, right, NT, preferred_element_type=F32)


def iota(shape, dim):
    return lax.broadcasted_iota(jnp.int32, shape, dim)


def schedule(first, second, sta_count):
    every = range(1, REACH)
    if 0 < first < sta_count - 1:
        ring = 1 if 2 * first < sta_count else REACH - 1
        pairs = [((home + ring) % sta_count, home) for home in range(sta_count)]
    else:
        pairs = [(home ^ 1, home) for home in range(sta_count)]
    source = {target: start for start, target in pairs}
    reaches = [[(source[owner] - owner) % sta_count] for owner in (first, second)]
    both = [reach for reach in every if [reach] not in reaches]
    for taken in reaches:
        taken += both + [reach for reach in every if reach not in taken + both]
    plan = [(True, pairs, reaches[0][0], reaches[1][0])]
    for one, other in zip(reaches[0][1:], reaches[1][1:]):
        flows = [((first + one) % sta_count, first), ((second + other) % sta_count, second)]
        plan.append((False, flows, one, other))
    return plan[:1] + sorted(plan[1:], key=lambda step: step[1][1][0] == first)


def place_table(sta_count):
    table = []
    for first, second in itertools.product(range(sta_count), repeat=2):
        places = [0] * (2 * REACH)
        if first != second:
            for place, step in enumerate(schedule(first, second, sta_count)):
                places[step[2]], places[REACH + step[3]] = place + 1, place + 1
        table += places
    return table


def read_pairs(pair_ref, owner_ref, block_count):
    pairs = []
    for pair in range(owner_ref.shape[0]):
        blocks = [pair_ref[side, pair] for side in range(2)]
        pairs.append((owner_ref[pair], blocks, [lax.div(block, block_count) for block in blocks]))
    return pairs


def case_of(pairs, sta_count):
    first = second = needs = jnp.int32(0)
    for owner, _, homes in pairs:
        count = jnp.int32(0)
        for other, _, _ in pairs:
            count = count + (other == owner).astype(jnp.int32)
        ends = [lax.rem(home - owner + sta_count, sta_count) for home in homes]
        first = jnp.where(count == CAP, owner, first)
        second = jnp.where(count < CAP, owner, second)
        needs = jnp.where(count < CAP, (1 << ends[0]) | (1 << ends[1]), needs)
    return first, second, case_number(first, second, needs, sta_count)


def pick_kernel(kept, branched, sta_axis, pair_hbm, owner_hbm, member_hbm, case_hbm, x_ref, *rest):
    outs = rest[:REACH]
    pair_ref, owner_ref, member_ref, case_ref, number_ref, x_buf, y_buf, white_buf, sems = rest[
        REACH + branched :
    ]
    if branched:
        branch_copy = pltpu.make_async_copy(number_ref, rest[REACH], sems.at[COPIES + 4])
    freqs, tiles = x_buf.shape[0], x_buf.shape[2] // LANES
    block_count, width = member_ref.shape
    rows = y_buf.shape[0]
    chunks = rows // (2 * LANES)

    cut = freqs // (4 * LANES) * 2 * LANES or freqs // LANES // 2 * LANES
    runs = [(0, cut), (cut, freqs - cut)]

    def fetch(part):
        run = pl.ds(*runs[part])
        return pltpu.make_async_copy(x_ref.at[0, run], x_buf.at[run], sems.at[part])

    small = [
        pltpu.make_async_copy(source, target, sems.at[COPIES + index])
        for index, (source, target) in enumerate(
            (
                (pair_hbm, pair_ref),
                (owner_hbm, owner_ref),
                (member_hbm, member_ref),
                (case_hbm, case_ref),
            )
        )
    ]
    for copy in small:
        copy.start()
    for part in range(COPIES):
        fetch(part).start(priority=part % 2)

    def bands(shape, part_dim):
        part, place = iota(shape, part_dim), iota(shape, 1 - part_dim)
        low = (place % 16) * (2 * BAND)
        hit = (part >= low) & (part < low + 2 * BAND) & (part < 2 * freqs) & (place < 48)
        return jnp.where(hit, 1.0, 0.0).astype(BF16)

    gather_bands, spread_bands = bands((48, rows), 1), bands((rows, LANES), 0)
    row, col = iota((2 * LANES, 2 * LANES), 0), iota((2 * LANES, 2 * LANES), 1)
    split = jnp.where(row == 2 * (col % LANES) + col // LANES, 1.0, 0.0).astype(BF16)
    y_buf[2 * freqs :] = jnp.zeros((rows - 2 * freqs, kept * width), F32)
    for copy in small:
        copy.wait()

    my_sta = lax.axis_index(sta_axis)
    sta_count = lax.axis_size(sta_axis)
    pairs = read_pairs(pair_ref, owner_ref, block_count)
    found, wanted = jnp.int32(0), []
    for reach in range(REACH):
        owner = lax.rem(my_sta - reach + REACH * sta_count, sta_count)
        chosen = jnp.int32(-1)
        for pair_owner, blocks, homes in pairs:
            for block, home in zip(blocks, homes):
                hit = (pair_owner == owner) & (home == my_sta)
                chosen = jnp.where(hit, lax.rem(block, block_count), chosen)
        wanted.append((found, chosen))
        found = found + (chosen >= 0).astype(jnp.int32)
    places, station = [], []
    for place in range(kept):
        reach_here, block_here = jnp.int32(-1), jnp.int32(0)
        for reach, (rank, chosen) in enumerate(wanted):
            hit = (rank == place) & (chosen >= 0)
            reach_here = jnp.where(hit, reach, reach_here)
            block_here = jnp.where(hit, chosen, block_here)
        places.append(reach_here)
        station.append(member_ref[pl.ds(block_here, 1), :])
    station = jnp.concatenate(station, axis=1)
    hot = jnp.where(station == iota((tiles * LANES, kept * width), 0), 1.0, 0.0).astype(BF16)

    if branched:
        first, second, case = case_of(pairs, sta_count)
        number_ref[0] = case_ref[case]
        branch_copy.start()
        base = case_number(sta_count, 0, 0, sta_count) + (first * sta_count + second) * 2 * REACH
        for place, reach_here in enumerate(places):
            reach = jnp.maximum(reach_here, 0)
            owner = lax.rem(my_sta - reach + REACH * sta_count, sta_count)
            step = case_ref[base + jnp.where(owner == first, 0, REACH) + reach]
            places[place] = jnp.where(reach_here < 0, -1, step)

    power = None
    for part, (start, count) in enumerate(runs):
        fetch(part).wait()
        x = jnp.concatenate(
            [
                x_buf[start : start + count, :, tile * LANES : (tile + 1) * LANES].reshape(
                    2 * count, LANES
                )
                for tile in range(tiles)
            ],
            axis=1,
        )
        values = jnp.dot(x, hot, preferred_element_type=F32)
        y_buf[2 * start : 2 * (start + count)] = values
        stop = 2 * (start + count) if part + 1 < len(runs) else rows
        values = y_buf[2 * start : stop]
        square = values * values
        high = square.astype(BF16)
        low = (square - high.astype(F32)).astype(BF16)
        for piece in (high, low):
            sums = jnp.dot(gather_bands[:, 2 * start : stop], piece, preferred_element_type=F32)
            power = sums if power is None else power + sums
    scale = lax.rsqrt(power * (1.0 / (2 * BAND)) + EPSILON)
    high = scale.astype(BF16).astype(F32)
    mid = (scale - high).astype(BF16).astype(F32)
    low = scale - high - mid
    third = iota(scale.shape, 0) // 16
    pieces = jnp.where(third == 0, high, jnp.where(third == 1, mid, low))
    pieces = jnp.concatenate(
        [pieces, jnp.zeros((LANES - pieces.shape[0], pieces.shape[1]), F32)], axis=0
    ).astype(BF16)
    white = y_buf[...] * jnp.dot(spread_bands, pieces, preferred_element_type=F32)
    white = white.astype(BF16)
    parted = []
    for chunk in range(chunks):
        mixed = white[chunk * 2 * LANES : (chunk + 1) * 2 * LANES]
        part = lax.dot_general(
            mixed, split, (((0,), (0,)), ((), ())), preferred_element_type=F32
        )
        parted.append(part.astype(BF16))
    white_buf[...] = jnp.concatenate(
        [part[:, :LANES] for part in parted] + [part[:, LANES:] for part in parted], axis=1
    )
    for place, reach_here in enumerate(places):
        for reach in range(REACH):

            @pl.when(reach_here == reach)
            def _():
                outs[reach][...] = white_buf[place * width : (place + 1) * width]

    if branched:
        branch_copy.wait()


def pick_blocks(kept, branched, spectra, pair_sides, pair_owner, block_members, case_table):
    _, freqs, parts, stations = spectra.shape
    block_count, width = block_members.shape
    columns = -(-freqs // LANES) * 2 * LANES
    rows = kept * width
    vmem = pl.BlockSpec(memory_space=pltpu.VMEM)
    out_shape = [jax.ShapeDtypeStruct((width, columns), BF16)] * REACH
    out_shape += [jax.ShapeDtypeStruct((1,), jnp.int32)] * branched
    return pl.pallas_call(
        functools.partial(pick_kernel, kept, branched, "sta"),
        out_shape=out_shape,
        in_specs=[pl.BlockSpec(memory_space=pltpu.HBM)] * 5,
        out_specs=[vmem] * REACH + [pl.BlockSpec(memory_space=pltpu.HBM)] * branched,
        scratch_shapes=[
            pltpu.SMEM(pair_sides.shape, jnp.int32),
            pltpu.SMEM(pair_owner.shape, jnp.int32),
            pltpu.VMEM(block_members.shape, jnp.int32),
            pltpu.SMEM(case_table.shape, jnp.int32),
            pltpu.SMEM((1,), jnp.int32),
            pltpu.VMEM((freqs, parts, stations), BF16),
            pltpu.VMEM((columns, rows), F32),
            pltpu.VMEM((rows, columns), BF16),
            pltpu.SemaphoreType.DMA((COPIES + 5,)),
        ],
        compiler_params=pltpu.CompilerParams(vmem_limit_bytes=PICK_VMEM_LIMIT),
        cost_estimate=pl.CostEstimate(
            flops=2 * rows * stations * freqs * parts,
            bytes_accessed=2 * spectra.size + 4 * rows * columns,
            transcendentals=0,
        ),
        name="pick_and_whiten",
    )(pair_sides, pair_owner, block_members, case_table, spectra)


def case_number(first, second, needs, sta_count):
    return (first * sta_count + second) * (1 << (REACH - 1)) + needs // 2


def routes(sta_count):
    def load(first, second, sent):
        links = {}
        for full, flows, _, other in schedule(first, second, sta_count):
            for source, owner in flows if full or other in sent else flows[:1]:
                step = 1 if owner > source else -1
                for place in range(source, owner, step):
                    links[place, step] = links.get((place, step), 0) + 1
        return max(links.values())

    branches = []
    cases = [0] * case_number(sta_count, 0, 0, sta_count)
    for first, second in itertools.permutations(range(sta_count), 2):
        others = [step[3] for step in schedule(first, second, sta_count) if not step[0]]
        sets = [
            sent
            for count in range(len(others), -1, -1)
            for sent in itertools.combinations(others, count)
        ]
        for named in itertools.combinations(range(REACH), 2):
            fits = [sent for sent in sets if set(named) & set(others) <= set(sent)]
            branch = (first, second, min(fits, key=lambda sent: load(first, second, sent)))
            if branch not in branches:
                branches.append(branch)
            needs = sum(1 << reach for reach in named)
            cases[case_number(first, second, needs, sta_count)] = branches.index(branch)
    return branches, cases


def phase_tables(sub_count, sub_freqs, groups, lag_rows):
    chunks = -(-sub_freqs // LANES)
    total = sub_count * sub_freqs
    freq = np.arange(total, dtype=np.int64).reshape(sub_count, 1, sub_freqs)
    middle = [2 * (group * lag_rows - LAGS // 2) + lag_rows - 1 for group in range(groups)]
    away = [step for step in range(1, lag_rows) if step % 2 != lag_rows % 2]

    def table(twice, forms, tile, dtype):
        twice = np.array(twice or [0], dtype=np.int64).reshape(1, -1, 1)
        angle = np.mod(freq * twice, 2 * total) * (math.pi / total)
        rows = np.stack([form(angle) for form in forms], axis=2)
        rows = rows.reshape(sub_count, -1, sub_freqs)
        pad = ((0, 0), (0, -rows.shape[1] % tile), (0, chunks * LANES - sub_freqs))
        return np.pad(rows, pad).astype(np.float32).astype(dtype)

    turns = table(middle, (np.cos, np.sin), 8, np.float32)
    offsets = table(away, (np.cos, np.sin, lambda angle: -np.sin(angle)), 16, BF16)
    return turns, offsets, len(away)


def lag_kernel(hops, slots, lag_rows, away, block_count, branched, *refs):
    sub_count = lax.axis_size("sub")
    hr_count = lax.axis_size("hr")
    pair_ref, owner_ref, place_ref, turn_ref, offset_ref = refs[:5]
    blocks, outs = refs[5 : -2 - len(hops)], refs[-2 - len(hops) : -2]
    buf, sems = refs[-2:]
    width = buf.shape[3]
    span = buf.shape[4] // 2
    middle_lag = lag_rows % 2
    my_sub = lax.axis_index("sub")
    my_hr = lax.axis_index("hr")
    my_sta = lax.axis_index("sta")
    sta_count = lax.axis_size("sta")

    pairs = read_pairs(pair_ref, owner_ref, block_count)
    order = [jnp.int32(reach) for reach in range(REACH)]
    if branched:
        first, second, _ = case_of(pairs, sta_count)
        entry = (first * sta_count + second) * 2 + (my_sta != first).astype(jnp.int32)
        order = [place_ref[entry * REACH + reach] for reach in range(REACH)]
    owned = []
    for owner, _, homes in pairs:
        places = []
        for home in homes:
            reach_here = lax.rem(home - my_sta + sta_count, sta_count)
            place_here = order[0]
            for reach in range(1, REACH):
                place_here = jnp.where(reach_here == reach, order[reach], place_here)
            places.append(place_here)
        owned.append((owner == my_sta, places))
    ends = []
    for slot in slots:
        count = jnp.int32(0)
        slot_ends = [jnp.int32(-1)] * 2
        for mine, places in owned:
            hit = mine & (count == slot)
            count = count + mine.astype(jnp.int32)
            slot_ends = [jnp.where(hit, new, old) for new, old in zip(places, slot_ends)]
        ends.append(slot_ends)

    def fetches(index, act):
        for side in range(2):
            for place in range(REACH):

                @pl.when(ends[index][side] == place)
                def _():
                    for step in range(sub_count):
                        act(
                            pltpu.make_async_copy(
                                blocks[place * sub_count + step],
                                buf.at[index, side, step],
                                sems.at[index, side, step],
                            ),
                            step,
                        )

    for index in range(len(slots)):
        fetches(index, lambda copy, step: copy.start(priority=step % 2))

    for index in range(len(slots)):

        @pl.when(ends[index][0] < 0)
        def _():
            for out in outs:
                out[:, index] = jnp.zeros((lag_rows, width, width), out.dtype)

        fetches(index, lambda copy, step: copy.wait())

        @pl.when(ends[index][0] >= 0)
        def _():
            total = None
            for step in range(sub_count):
                sub = lax.rem(my_sub + step, sub_count)
                real = buf[index, 0, step, :, :span]
                imag = buf[index, 0, step, :, span:]
                scaled_real, scaled_imag = [real] * middle_lag, [imag] * middle_lag
                for near in range(away):
                    cosine, sine, minus = (
                        offset_ref[sub, 3 * near + form : 3 * near + form + 1, :]
                        for form in range(3)
                    )
                    scaled_real += [real * cosine, imag * minus]
                    scaled_imag += [imag * cosine, real * sine]
                real = buf[index, 1, step, :, :span].astype(F32)
                imag = buf[index, 1, step, :, span:].astype(F32)
                turned_real, turned_imag = [], []
                for hop in hops:
                    group = lax.rem(my_hr + hop, hr_count) * sub_count + my_sub
                    cosine = turn_ref[sub, pl.ds(2 * group, 1), :]
                    sine = turn_ref[sub, pl.ds(2 * group + 1, 1), :]
                    turned_real.append((real * cosine + imag * sine).astype(BF16))
                    turned_imag.append((imag * cosine - real * sine).astype(BF16))
                for scaled, turned in ((scaled_real, turned_real), (scaled_imag, turned_imag)):
                    part = dot_nt(jnp.concatenate(scaled, axis=0), jnp.concatenate(turned, axis=0))
                    total = part if total is None else total + part
            for place, out in enumerate(outs):
                columns = slice(place * width, (place + 1) * width)
                if middle_lag:
                    out[lag_rows // 2, index] = total[:width, columns].astype(out.dtype)
                for near in range(away):
                    start = (middle_lag + 2 * near) * width
                    even = total[start : start + width, columns]
                    odd = total[start + width : start + 2 * width, columns]
                    below = (lag_rows - 1) // 2 - near - middle_lag
                    above = lag_rows - 1 - below
                    out[above, index] = (even + odd).astype(out.dtype)
                    out[below, index] = (even - odd).astype(out.dtype)


def on_device(spectra, pair_blocks, pair_owner, block_members):
    hour_count, sub_freqs, _, _ = spectra.shape
    block_count, width = block_members.shape
    sta_count, hr_count, sub_count = (lax.axis_size(axis) for axis in ("sta", "hr", "sub"))
    groups = hr_count * sub_count
    lag_rows = LAGS // groups
    norming = 1.0 / math.sqrt(hour_count * hr_count * sub_count * sub_freqs)
    pair_sides = pair_blocks.T
    turns, offsets, away = phase_tables(sub_count, sub_freqs, groups, lag_rows)

    owners_at_most = pair_owner.shape[0] - CAP + 1
    branched = owners_at_most == 2 and sta_count == REACH
    kept = min(REACH, owners_at_most)
    branches, cases = routes(sta_count) if branched else ([], [0])
    places = place_table(sta_count) if branched else [0]
    case_table = jnp.asarray(np.array(cases + places, dtype=np.int32))
    places = jnp.asarray(np.array(places, dtype=np.int32))
    picked = pick_blocks(
        kept, branched, spectra, pair_sides, pair_owner, block_members, case_table
    )

    def halves(block):
        blocks = [block]
        for step in range(1, sub_count):
            swap = [((sub + step) % sub_count, sub) for sub in range(sub_count)]
            blocks.append(lax.ppermute(block, "sub", swap))
        return blocks

    def exchange(*picked):
        blocks = halves(picked[0])
        for reach in range(1, REACH):
            shift = [((home + reach) % sta_count, home) for home in range(sta_count)]
            blocks += halves(lax.ppermute(picked[reach], "sta", shift))
        return blocks

    def exchange_two(first, second, sent, *picked):
        blocks = halves(picked[0])
        for block, (full, flows, _, other) in zip(picked[1:], schedule(first, second, sta_count)):
            flows = flows if full or other in sent else flows[:1]
            blocks += halves(lax.ppermute(block, "sta", flows))
        return blocks

    if branched:
        steps = [functools.partial(exchange_two, *branch) for branch in branches]
        blocks = lax.switch(picked[REACH][0], steps, *picked[:REACH])
    else:
        blocks = exchange(*picked[:REACH])

    smem = pl.BlockSpec(memory_space=pltpu.SMEM)
    vmem = pl.BlockSpec(memory_space=pltpu.VMEM)
    hbm = pl.BlockSpec(memory_space=pltpu.HBM)
    row = picked[0].shape[1]
    versions = (lag_rows % 2 + 2 * away) * width

    def products(hops, slots, dtype, name):
        return pl.pallas_call(
            functools.partial(
                lag_kernel, hops, slots, lag_rows, away, block_count, branched
            ),
            out_shape=[jax.ShapeDtypeStruct((lag_rows, len(slots), width, width), dtype)]
            * len(hops),
            in_specs=[smem, smem, smem, vmem, vmem] + [hbm] * len(blocks),
            out_specs=[vmem] * len(hops),
            scratch_shapes=[
                pltpu.VMEM((len(slots), 2, sub_count, width, row), BF16),
                pltpu.SemaphoreType.DMA((len(slots), 2, sub_count)),
            ],
            compiler_params=pltpu.CompilerParams(vmem_limit_bytes=LAG_VMEM_LIMIT),
            cost_estimate=pl.CostEstimate(
                flops=2 * len(slots) * len(hops) * versions * width * sub_count * row,
                bytes_accessed=4 * len(slots) * sub_count * width * row,
                transcendentals=0,
            ),
            name=name,
        )(pair_sides, pair_owner, places, turns, offsets, *blocks)

    hops, slots = tuple(range(1, hr_count)), tuple(range(CAP))
    received = []
    for group in (slots[:-1], slots[-1:]):
        sent = products(hops, group, BF16, f"lags_to_send_{len(group)}")
        for hop, part in zip(hops, sent):
            to_device = [(hr, (hr + hop) % hr_count) for hr in range(hr_count)]
            received.append(lax.ppermute(part, "hr", to_device))
    (summed,) = products((0,), slots, F32, "lags_to_keep")
    for early, late in zip(received[: len(hops)], received[len(hops) :]):
        summed = summed + jnp.concatenate([early, late], axis=1).astype(F32)
    return (summed * norming).astype(BF16)


def solution(mesh):
    placed = (P(("grp", "hr"), "sub", None, "sta"), P(), P(), P("sta", None))
    return jax.shard_map(
        on_device,
        mesh=mesh,
        in_specs=placed,
        out_specs=P(("grp", "hr", "sub"), "sta", None, None),
        check_vma=False,
    )
```

```python
import functools
import itertools
import math

import jax
import jax.numpy as jnp
import numpy as np
from jax import lax
from jax.experimental import pallas as pl
from jax.experimental.pallas import tpu as pltpu
from jax.sharding import PartitionSpec as P

BAND = 50
LAGS = 16
CAP = 3
REACH = 4
COPIES = 2
EPSILON = 1e-05
LANES = 128
F32 = jnp.float32
BF16 = jnp.bfloat16
PICK_VMEM_LIMIT = 59 * 1024 * 1024
LAG_VMEM_LIMIT = 32 * 1024 * 1024

NT = (((1,), (1,)), ((), ()))


def dot_nt(left, right):
    return lax.dot_general(left, right, NT, preferred_element_type=F32)


def iota(shape, dim):
    return lax.broadcasted_iota(jnp.int32, shape, dim)


def schedule(first, second, sta_count):
    every = range(1, REACH)
    if 0 < first < sta_count - 1:
        ring = 1 if 2 * first < sta_count else REACH - 1
        pairs = [((home + ring) % sta_count, home) for home in range(sta_count)]
    else:
        pairs = [(home ^ 1, home) for home in range(sta_count)]
    source = {target: start for start, target in pairs}
    reaches = [[(source[owner] - owner) % sta_count] for owner in (first, second)]
    both = [reach for reach in every if [reach] not in reaches]
    for taken in reaches:
        taken += both + [reach for reach in every if reach not in taken + both]
    plan = [(True, pairs, reaches[0][0], reaches[1][0])]
    for one, other in zip(reaches[0][1:], reaches[1][1:]):
        flows = [((first + one) % sta_count, first), ((second + other) % sta_count, second)]
        plan.append((False, flows, one, other))
    return plan[:1] + sorted(plan[1:], key=lambda step: step[1][1][0] == first)


def place_table(sta_count):
    table = []
    for first, second in itertools.product(range(sta_count), repeat=2):
        places = [0] * (2 * REACH)
        if first != second:
            for place, step in enumerate(schedule(first, second, sta_count)):
                places[step[2]], places[REACH + step[3]] = place + 1, place + 1
        table += places
    return table


def read_pairs(pair_ref, owner_ref, block_count):
    pairs = []
    for pair in range(owner_ref.shape[0]):
        blocks = [pair_ref[side, pair] for side in range(2)]
        pairs.append((owner_ref[pair], blocks, [lax.div(block, block_count) for block in blocks]))
    return pairs


def case_of(pairs, sta_count):
    first = second = needs = jnp.int32(0)
    for owner, _, homes in pairs:
        count = jnp.int32(0)
        for other, _, _ in pairs:
            count = count + (other == owner).astype(jnp.int32)
        ends = [lax.rem(home - owner + sta_count, sta_count) for home in homes]
        first = jnp.where(count == CAP, owner, first)
        second = jnp.where(count < CAP, owner, second)
        needs = jnp.where(count < CAP, (1 << ends[0]) | (1 << ends[1]), needs)
    return first, second, case_number(first, second, needs, sta_count)


def pick_kernel(kept, branched, sta_axis, pair_hbm, owner_hbm, member_hbm, case_hbm, x_ref, *rest):
    outs = rest[:REACH]
    pair_ref, owner_ref, member_ref, case_ref, number_ref, x_buf, y_buf, white_buf, sems = rest[
        REACH + branched :
    ]
    if branched:
        branch_copy = pltpu.make_async_copy(number_ref, rest[REACH], sems.at[COPIES + 4])
    freqs, tiles = x_buf.shape[0], x_buf.shape[2] // LANES
    block_count, width = member_ref.shape
    rows = y_buf.shape[0]
    chunks = rows // (2 * LANES)

    cut = freqs // (4 * LANES) * 2 * LANES or freqs // LANES // 2 * LANES
    runs = [(0, cut), (cut, freqs - cut)]

    def fetch(part):
        run = pl.ds(*runs[part])
        return pltpu.make_async_copy(x_ref.at[0, run], x_buf.at[run], sems.at[part])

    small = [
        pltpu.make_async_copy(source, target, sems.at[COPIES + index])
        for index, (source, target) in enumerate(
            (
                (pair_hbm, pair_ref),
                (owner_hbm, owner_ref),
                (member_hbm, member_ref),
                (case_hbm, case_ref),
            )
        )
    ]
    for copy in small:
        copy.start()
    for part in range(COPIES):
        fetch(part).start()

    def bands(shape, part_dim):
        part, place = iota(shape, part_dim), iota(shape, 1 - part_dim)
        low = (place % 16) * (2 * BAND)
        hit = (part >= low) & (part < low + 2 * BAND) & (part < 2 * freqs) & (place < 48)
        return jnp.where(hit, 1.0, 0.0).astype(BF16)

    gather_bands, spread_bands = bands((48, rows), 1), bands((rows, LANES), 0)
    row, col = iota((2 * LANES, 2 * LANES), 0), iota((2 * LANES, 2 * LANES), 1)
    split = jnp.where(row == 2 * (col % LANES) + col // LANES, 1.0, 0.0).astype(BF16)
    y_buf[2 * freqs :] = jnp.zeros((rows - 2 * freqs, kept * width), F32)
    for copy in small:
        copy.wait()

    my_sta = lax.axis_index(sta_axis)
    sta_count = lax.axis_size(sta_axis)
    pairs = read_pairs(pair_ref, owner_ref, block_count)
    found, wanted = jnp.int32(0), []
    for reach in range(REACH):
        owner = lax.rem(my_sta - reach + REACH * sta_count, sta_count)
        chosen = jnp.int32(-1)
        for pair_owner, blocks, homes in pairs:
            for block, home in zip(blocks, homes):
                hit = (pair_owner == owner) & (home == my_sta)
                chosen = jnp.where(hit, lax.rem(block, block_count), chosen)
        wanted.append((found, chosen))
        found = found + (chosen >= 0).astype(jnp.int32)
    places, station = [], []
    for place in range(kept):
        reach_here, block_here = jnp.int32(-1), jnp.int32(0)
        for reach, (rank, chosen) in enumerate(wanted):
            hit = (rank == place) & (chosen >= 0)
            reach_here = jnp.where(hit, reach, reach_here)
            block_here = jnp.where(hit, chosen, block_here)
        places.append(reach_here)
        station.append(member_ref[pl.ds(block_here, 1), :])
    station = jnp.concatenate(station, axis=1)
    hot = jnp.where(station == iota((tiles * LANES, kept * width), 0), 1.0, 0.0).astype(BF16)

    if branched:
        first, second, case = case_of(pairs, sta_count)
        number_ref[0] = case_ref[case]
        branch_copy.start()
        base = case_number(sta_count, 0, 0, sta_count) + (first * sta_count + second) * 2 * REACH
        for place, reach_here in enumerate(places):
            reach = jnp.maximum(reach_here, 0)
            owner = lax.rem(my_sta - reach + REACH * sta_count, sta_count)
            step = case_ref[base + jnp.where(owner == first, 0, REACH) + reach]
            places[place] = jnp.where(reach_here < 0, -1, step)

    power = None
    for part, (start, count) in enumerate(runs):
        fetch(part).wait()
        x = jnp.concatenate(
            [
                x_buf[start : start + count, :, tile * LANES : (tile + 1) * LANES].reshape(
                    2 * count, LANES
                )
                for tile in range(tiles)
            ],
            axis=1,
        )
        values = jnp.dot(x, hot, preferred_element_type=F32)
        y_buf[2 * start : 2 * (start + count)] = values
        stop = 2 * (start + count) if part + 1 < len(runs) else rows
        values = y_buf[2 * start : stop]
        square = values * values
        high = square.astype(BF16)
        low = (square - high.astype(F32)).astype(BF16)
        for piece in (high, low):
            sums = jnp.dot(gather_bands[:, 2 * start : stop], piece, preferred_element_type=F32)
            power = sums if power is None else power + sums
    scale = lax.rsqrt(power * (1.0 / (2 * BAND)) + EPSILON)
    high = scale.astype(BF16).astype(F32)
    mid = (scale - high).astype(BF16).astype(F32)
    low = scale - high - mid
    third = iota(scale.shape, 0) // 16
    pieces = jnp.where(third == 0, high, jnp.where(third == 1, mid, low))
    pieces = jnp.concatenate(
        [pieces, jnp.zeros((LANES - pieces.shape[0], pieces.shape[1]), F32)], axis=0
    ).astype(BF16)
    white = y_buf[...] * jnp.dot(spread_bands, pieces, preferred_element_type=F32)
    white = white.astype(BF16)
    parted = []
    for chunk in range(chunks):
        mixed = white[chunk * 2 * LANES : (chunk + 1) * 2 * LANES]
        part = lax.dot_general(
            mixed, split, (((0,), (0,)), ((), ())), preferred_element_type=F32
        )
        parted.append(part.astype(BF16))
    white_buf[...] = jnp.concatenate(
        [part[:, :LANES] for part in parted] + [part[:, LANES:] for part in parted], axis=1
    )
    for place, reach_here in enumerate(places):
        for reach in range(REACH):

            @pl.when(reach_here == reach)
            def _():
                outs[reach][...] = white_buf[place * width : (place + 1) * width]

    if branched:
        branch_copy.wait()


def pick_blocks(kept, branched, spectra, pair_sides, pair_owner, block_members, case_table):
    _, freqs, parts, stations = spectra.shape
    block_count, width = block_members.shape
    columns = -(-freqs // LANES) * 2 * LANES
    rows = kept * width
    vmem = pl.BlockSpec(memory_space=pltpu.VMEM)
    out_shape = [jax.ShapeDtypeStruct((width, columns), BF16)] * REACH
    out_shape += [jax.ShapeDtypeStruct((1,), jnp.int32)] * branched
    return pl.pallas_call(
        functools.partial(pick_kernel, kept, branched, "sta"),
        out_shape=out_shape,
        in_specs=[pl.BlockSpec(memory_space=pltpu.HBM)] * 5,
        out_specs=[vmem] * REACH + [pl.BlockSpec(memory_space=pltpu.HBM)] * branched,
        scratch_shapes=[
            pltpu.SMEM(pair_sides.shape, jnp.int32),
            pltpu.SMEM(pair_owner.shape, jnp.int32),
            pltpu.VMEM(block_members.shape, jnp.int32),
            pltpu.SMEM(case_table.shape, jnp.int32),
            pltpu.SMEM((1,), jnp.int32),
            pltpu.VMEM((freqs, parts, stations), BF16),
            pltpu.VMEM((columns, rows), F32),
            pltpu.VMEM((rows, columns), BF16),
            pltpu.SemaphoreType.DMA((COPIES + 5,)),
        ],
        compiler_params=pltpu.CompilerParams(vmem_limit_bytes=PICK_VMEM_LIMIT),
        cost_estimate=pl.CostEstimate(
            flops=2 * rows * stations * freqs * parts,
            bytes_accessed=2 * spectra.size + 4 * rows * columns,
            transcendentals=0,
        ),
        name="pick_and_whiten",
    )(pair_sides, pair_owner, block_members, case_table, spectra)


def case_number(first, second, needs, sta_count):
    return (first * sta_count + second) * (1 << (REACH - 1)) + needs // 2


def routes(sta_count):
    def load(first, second, sent):
        links = {}
        for full, flows, _, other in schedule(first, second, sta_count):
            for source, owner in flows if full or other in sent else flows[:1]:
                step = 1 if owner > source else -1
                for place in range(source, owner, step):
                    links[place, step] = links.get((place, step), 0) + 1
        return max(links.values())

    branches = []
    cases = [0] * case_number(sta_count, 0, 0, sta_count)
    for first, second in itertools.permutations(range(sta_count), 2):
        others = [step[3] for step in schedule(first, second, sta_count) if not step[0]]
        sets = [
            sent
            for count in range(len(others), -1, -1)
            for sent in itertools.combinations(others, count)
        ]
        for named in itertools.combinations(range(REACH), 2):
            fits = [sent for sent in sets if set(named) & set(others) <= set(sent)]
            branch = (first, second, min(fits, key=lambda sent: load(first, second, sent)))
            if branch not in branches:
                branches.append(branch)
            needs = sum(1 << reach for reach in named)
            cases[case_number(first, second, needs, sta_count)] = branches.index(branch)
    return branches, cases


def phase_tables(sub_count, sub_freqs, groups, lag_rows):
    chunks = -(-sub_freqs // LANES)
    total = sub_count * sub_freqs
    freq = np.arange(total, dtype=np.int64).reshape(sub_count, 1, sub_freqs)
    middle = [2 * (group * lag_rows - LAGS // 2) + lag_rows - 1 for group in range(groups)]
    away = [step for step in range(1, lag_rows) if step % 2 != lag_rows % 2]

    def table(twice, forms, tile, dtype):
        twice = np.array(twice or [0], dtype=np.int64).reshape(1, -1, 1)
        angle = np.mod(freq * twice, 2 * total) * (math.pi / total)
        rows = np.stack([form(angle) for form in forms], axis=2)
        rows = rows.reshape(sub_count, -1, sub_freqs)
        pad = ((0, 0), (0, -rows.shape[1] % tile), (0, chunks * LANES - sub_freqs))
        return np.pad(rows, pad).astype(np.float32).astype(dtype)

    turns = table(middle, (np.cos, np.sin), 8, np.float32)
    offsets = table(away, (np.cos, np.sin, lambda angle: -np.sin(angle)), 16, BF16)
    return turns, offsets, len(away)


def lag_kernel(hops, slots, lag_rows, away, block_count, branched, *refs):
    sub_count = lax.axis_size("sub")
    hr_count = lax.axis_size("hr")
    pair_ref, owner_ref, place_ref, turn_ref, offset_ref = refs[:5]
    blocks, outs = refs[5 : -2 - len(hops)], refs[-2 - len(hops) : -2]
    buf, sems = refs[-2:]
    width = buf.shape[3]
    span = buf.shape[4] // 2
    middle_lag = lag_rows % 2
    my_sub = lax.axis_index("sub")
    my_hr = lax.axis_index("hr")
    my_sta = lax.axis_index("sta")
    sta_count = lax.axis_size("sta")

    pairs = read_pairs(pair_ref, owner_ref, block_count)
    order = [jnp.int32(reach) for reach in range(REACH)]
    if branched:
        first, second, _ = case_of(pairs, sta_count)
        entry = (first * sta_count + second) * 2 + (my_sta != first).astype(jnp.int32)
        order = [place_ref[entry * REACH + reach] for reach in range(REACH)]
    owned = []
    for owner, _, homes in pairs:
        places = []
        for home in homes:
            reach_here = lax.rem(home - my_sta + sta_count, sta_count)
            place_here = order[0]
            for reach in range(1, REACH):
                place_here = jnp.where(reach_here == reach, order[reach], place_here)
            places.append(place_here)
        owned.append((owner == my_sta, places))
    ends = []
    for slot in slots:
        count = jnp.int32(0)
        slot_ends = [jnp.int32(-1)] * 2
        for mine, places in owned:
            hit = mine & (count == slot)
            count = count + mine.astype(jnp.int32)
            slot_ends = [jnp.where(hit, new, old) for new, old in zip(places, slot_ends)]
        ends.append(slot_ends)

    def fetches(index, act):
        for side in range(2):
            for place in range(REACH):

                @pl.when(ends[index][side] == place)
                def _():
                    for step in range(sub_count):
                        act(
                            pltpu.make_async_copy(
                                blocks[place * sub_count + step],
                                buf.at[index, side, step],
                                sems.at[index, side, step],
                            )
                        )

    for index in range(len(slots)):
        fetches(index, lambda copy: copy.start())

    for index in range(len(slots)):

        @pl.when(ends[index][0] < 0)
        def _():
            for out in outs:
                out[:, index] = jnp.zeros((lag_rows, width, width), out.dtype)

        fetches(index, lambda copy: copy.wait())

        @pl.when(ends[index][0] >= 0)
        def _():
            total = None
            for step in range(sub_count):
                sub = lax.rem(my_sub + step, sub_count)
                real = buf[index, 0, step, :, :span]
                imag = buf[index, 0, step, :, span:]
                scaled_real, scaled_imag = [real] * middle_lag, [imag] * middle_lag
                for near in range(away):
                    cosine, sine, minus = (
                        offset_ref[sub, 3 * near + form : 3 * near + form + 1, :]
                        for form in range(3)
                    )
                    scaled_real += [real * cosine, imag * minus]
                    scaled_imag += [imag * cosine, real * sine]
                real = buf[index, 1, step, :, :span].astype(F32)
                imag = buf[index, 1, step, :, span:].astype(F32)
                turned_real, turned_imag = [], []
                for hop in hops:
                    group = lax.rem(my_hr + hop, hr_count) * sub_count + my_sub
                    cosine = turn_ref[sub, pl.ds(2 * group, 1), :]
                    sine = turn_ref[sub, pl.ds(2 * group + 1, 1), :]
                    turned_real.append((real * cosine + imag * sine).astype(BF16))
                    turned_imag.append((imag * cosine - real * sine).astype(BF16))
                for scaled, turned in ((scaled_real, turned_real), (scaled_imag, turned_imag)):
                    part = dot_nt(jnp.concatenate(scaled, axis=0), jnp.concatenate(turned, axis=0))
                    total = part if total is None else total + part
            for place, out in enumerate(outs):
                columns = slice(place * width, (place + 1) * width)
                if middle_lag:
                    out[lag_rows // 2, index] = total[:width, columns].astype(out.dtype)
                for near in range(away):
                    start = (middle_lag + 2 * near) * width
                    even = total[start : start + width, columns]
                    odd = total[start + width : start + 2 * width, columns]
                    below = (lag_rows - 1) // 2 - near - middle_lag
                    above = lag_rows - 1 - below
                    out[above, index] = (even + odd).astype(out.dtype)
                    out[below, index] = (even - odd).astype(out.dtype)


def on_device(spectra, pair_blocks, pair_owner, block_members):
    hour_count, sub_freqs, _, _ = spectra.shape
    block_count, width = block_members.shape
    sta_count, hr_count, sub_count = (lax.axis_size(axis) for axis in ("sta", "hr", "sub"))
    groups = hr_count * sub_count
    lag_rows = LAGS // groups
    norming = 1.0 / math.sqrt(hour_count * hr_count * sub_count * sub_freqs)
    pair_sides = pair_blocks.T
    turns, offsets, away = phase_tables(sub_count, sub_freqs, groups, lag_rows)

    owners_at_most = pair_owner.shape[0] - CAP + 1
    branched = owners_at_most == 2 and sta_count == REACH
    kept = min(REACH, owners_at_most)
    branches, cases = routes(sta_count) if branched else ([], [0])
    places = place_table(sta_count) if branched else [0]
    case_table = jnp.asarray(np.array(cases + places, dtype=np.int32))
    places = jnp.asarray(np.array(places, dtype=np.int32))
    picked = pick_blocks(
        kept, branched, spectra, pair_sides, pair_owner, block_members, case_table
    )

    def halves(block):
        blocks = [block]
        for step in range(1, sub_count):
            swap = [((sub + step) % sub_count, sub) for sub in range(sub_count)]
            blocks.append(lax.ppermute(block, "sub", swap))
        return blocks

    def exchange(*picked):
        blocks = halves(picked[0])
        for reach in range(1, REACH):
            shift = [((home + reach) % sta_count, home) for home in range(sta_count)]
            blocks += halves(lax.ppermute(picked[reach], "sta", shift))
        return blocks

    def exchange_two(first, second, sent, *picked):
        blocks = halves(picked[0])
        for block, (full, flows, _, other) in zip(picked[1:], schedule(first, second, sta_count)):
            flows = flows if full or other in sent else flows[:1]
            blocks += halves(lax.ppermute(block, "sta", flows))
        return blocks

    if branched:
        steps = [functools.partial(exchange_two, *branch) for branch in branches]
        blocks = lax.switch(picked[REACH][0], steps, *picked[:REACH])
    else:
        blocks = exchange(*picked[:REACH])

    smem = pl.BlockSpec(memory_space=pltpu.SMEM)
    vmem = pl.BlockSpec(memory_space=pltpu.VMEM)
    hbm = pl.BlockSpec(memory_space=pltpu.HBM)
    row = picked[0].shape[1]
    versions = (lag_rows % 2 + 2 * away) * width

    def products(hops, slots, dtype, name):
        return pl.pallas_call(
            functools.partial(
                lag_kernel, hops, slots, lag_rows, away, block_count, branched
            ),
            out_shape=[jax.ShapeDtypeStruct((lag_rows, len(slots), width, width), dtype)]
            * len(hops),
            in_specs=[smem, smem, smem, vmem, vmem] + [hbm] * len(blocks),
            out_specs=[vmem] * len(hops),
            scratch_shapes=[
                pltpu.VMEM((len(slots), 2, sub_count, width, row), BF16),
                pltpu.SemaphoreType.DMA((len(slots), 2, sub_count)),
            ],
            compiler_params=pltpu.CompilerParams(vmem_limit_bytes=LAG_VMEM_LIMIT),
            cost_estimate=pl.CostEstimate(
                flops=2 * len(slots) * len(hops) * versions * width * sub_count * row,
                bytes_accessed=4 * len(slots) * sub_count * width * row,
                transcendentals=0,
            ),
            name=name,
        )(pair_sides, pair_owner, places, turns, offsets, *blocks)

    hops, slots = tuple(range(1, hr_count)), tuple(range(CAP))
    received = []
    for slot in slots:
        sent = products(hops, (slot,), BF16, f"lags_to_send_{slot}")
        for hop, part in zip(hops, sent):
            to_device = [(hr, (hr + hop) % hr_count) for hr in range(hr_count)]
            received.append(lax.ppermute(part, "hr", to_device))
    (summed,) = products((0,), slots, F32, "lags_to_keep")
    for hop in range(len(hops)):
        joined = jnp.concatenate(received[hop :: len(hops)], axis=1)
        summed = summed + joined.astype(F32)
    return (summed * norming).astype(BF16)


def solution(mesh):
    placed = (P(("grp", "hr"), "sub", None, "sta"), P(), P(), P("sta", None))
    return jax.shard_map(
        on_device,
        mesh=mesh,
        in_specs=placed,
        out_specs=P(("grp", "hr", "sub"), "sta", None, None),
        check_vma=False,
    )
```
